32 devices in a mesh: groups: 2 (over x), expert: 16 (over z, y, core).
Axes of the slice: x: 2, y: 2, z: 4, core: 2. Of those that a mesh axis runs over, the one named last changes fastest.
Arguments:
- tokens: bfloat16 [4096, 4096], P(('groups', 'expert')), parts along dimension 0, may hold values from -6 to 6
- shift: float32 [4, 4096], P('groups'), parts along dimension 0, may hold values from -4 to 4
- scale: float32 [4, 4096], P('groups'), parts along dimension 0, may hold values from -4 to 4
- gate: float32 [4, 4096], P('groups'), parts along dimension 0, may hold values from -5 to 5
- w_up: bfloat16 [32768, 4096], P('expert'), may hold values from -0.09375 to 0.09375
- w_down: bfloat16 [32768, 4096], P('expert'), may hold values from -0.0625 to 0.0625
- pick: int32 [32, 4, 16], P(('groups', 'expert')), parts along dimension 0, may hold values from 0 to 127, as said below
- count: int32 [32, 4], P(('groups', 'expert')), parts along dimension 0, may hold values from 0 to 16, as said below
- combine: float32 [32, 4, 16], P(('groups', 'expert')), parts along dimension 0, may hold values from 0.1 to 1
Outputs:
- branch: bfloat16 [4096, 4096], P(('groups', 'expert')), parts along dimension 0
The draws below stay inside these ranges and needn't reach their ends.
There are 2 independent parts, one for each index of `groups`. The reference program is written for one: setup_inputs(seed, part) draws one part's arguments, and reference() takes and returns one part's arrays. A program takes and returns all parts, laid end to end along the dimension named above; an argument that names none is the same for every part. Nothing has to cross between parts.
Inputs may be any that keep to these rules, and one draw needn't show every extreme that they name: `pick`: for each device and expert the 16 entries are distinct. Only the first count[s, e] slots are live; in every draw some expert has 16 live slots on every device.
All inputs are finite; a program needn't handle non-finite values.
Results may differ from the reference program's by a relative error of at most 0.0065.
Values may be sent and summed in bfloat16 or wider, within the bound.
No kernel may reach another device: no remote copies, remote signals or barrier semaphores. Data moves between devices by JAX's collectives and lax.ppermute only.
A program may use at most 128 MiB of HBM per device.

```python
import jax
import jax.numpy as jnp
from jax import lax

D = 4096
FF = 8192
EXPERTS = 4
REQUESTS = 2
MOST = 16
TOK_DEV = 128
TOKENS = 2048
N_EXPERT = 16


def draw_pick(key, part):
    key = jax.random.fold_in(key, 11)
    keys = jax.random.split(key, N_EXPERT * EXPERTS)
    orders = jax.vmap(lambda k: jax.random.permutation(k, TOK_DEV))(keys)
    return orders[:, :MOST].reshape(N_EXPERT, EXPERTS, MOST).astype(jnp.int32)


def draw_count(key, part):
    key = jax.random.fold_in(key, 23)
    key_top, key_low, key_full = jax.random.split(key, 3)
    upper = jax.random.randint(key_top, (REQUESTS, EXPERTS), 1, MOST + 1)
    request = jnp.arange(N_EXPERT, dtype=jnp.int32) // (N_EXPERT // REQUESTS)
    upper_dev = upper[request]
    lower_dev = upper_dev // 2
    noise = jax.random.randint(key_low, (N_EXPERT, EXPERTS), 0, MOST + 1)
    counts = lower_dev + noise % (upper_dev - lower_dev + 1)
    full = jax.random.randint(key_full, (), 0, EXPERTS)
    expert_ids = jnp.arange(EXPERTS, dtype=jnp.int32)[None, :]
    counts = jnp.where(expert_ids == full, MOST, counts)
    return counts.astype(jnp.int32)


def steps_of(key, dims, cuts, least, high):
    def one(dim, blocks):
        heights = jax.random.uniform(jax.random.fold_in(jax.random.fold_in(key, 6), dim), (blocks,), jnp.float32, least / len(cuts), high / len(cuts))
        return jnp.repeat(jnp.exp(heights), dims[dim] // blocks).reshape((-1,) + (1,) * (len(dims) - dim - 1))

    gain = one(*cuts[0])
    for cut in cuts[1:]:
        gain = gain * one(*cut)
    return gain


def gaussian(own_key, shape, scale, reach, shards=(), kind=jnp.bfloat16):
    values = jax.random.normal(own_key, shape, jnp.float32) * scale
    if len(shards) > 0:
        values = steps_of(own_key, shape, shards, -0.22, 0.18) * values
    return jnp.clip(values, min=-reach, max=reach).astype(kind)


def setup_inputs(seed: int = 0, part: int = 0) -> dict:
    arg_keys = jax.random.split(jax.random.key(seed), 10)
    part_splits = jax.random.split(jax.random.fold_in(arg_keys[9], part), 10)
    return {
        "tokens": gaussian(part_splits[0], (TOKENS, D), 1.0, 6.0, ((0, 16),)),
        "shift": gaussian(part_splits[1], (REQUESTS, D), 0.5, 4.0, (), jnp.float32),
        "scale": gaussian(part_splits[2], (REQUESTS, D), 0.5, 4.0, (), jnp.float32),
        "gate": gaussian(part_splits[3], (REQUESTS, D), 1.0, 5.0, (), jnp.float32),
        "w_up": gaussian(arg_keys[4], (EXPERTS * FF, D), D ** -0.5, 0.09375, ((0, 16),)),
        "w_down": gaussian(arg_keys[5], (EXPERTS * FF, D), FF ** -0.5, 0.0625, ((0, 16),)),
        "pick": draw_pick(jax.random.fold_in(jax.random.fold_in(arg_keys[9], part), 71), part),
        "count": draw_count(jax.random.fold_in(jax.random.fold_in(arg_keys[9], part), 71), part),
        "combine": jnp.clip(0.1 + 0.9 * jax.random.uniform(part_splits[8], (N_EXPERT, EXPERTS, MOST), jnp.float32) ** steps_of(part_splits[8], (N_EXPERT, EXPERTS, MOST), ((0, 16),), -0.2, 0.2), 0.1, 1.0),
    }


def reference(tokens, shift, scale, gate, w_up, w_down, pick, count, combine):
    per_request = TOKENS // REQUESTS
    request = jnp.arange(TOKENS, dtype=jnp.int32) // per_request
    values = tokens.astype(jnp.float32)
    center = values - lax.optimization_barrier(jnp.mean(values, axis=1, keepdims=True))
    spread = lax.optimization_barrier(jnp.mean(center * center, axis=1, keepdims=True))
    normed = center / jnp.sqrt(spread + 1e-06)
    modulated = (normed * (1.0 + scale[request]) + shift[request]).astype(jnp.bfloat16)
    owners = jnp.arange(N_EXPERT, dtype=jnp.int32)[:, None, None] * TOK_DEV + pick.astype(jnp.int32)
    up_all = w_up.reshape(EXPERTS, FF, D)
    down_all = w_down.reshape(EXPERTS, FF, D)
    pieces = N_EXPERT // EXPERTS
    piece_width = FF // pieces
    results = []
    for expert in range(EXPERTS):
        rows = modulated[owners[:, expert, :].reshape(-1)]
        lifted = jnp.dot(rows, up_all[expert].T, preferred_element_type=jnp.float32)
        hidden = jax.nn.gelu(lifted, approximate=True).astype(jnp.bfloat16)
        lowered = jnp.zeros((rows.shape[0], D), jnp.float32)
        for piece in range(pieces):
            lo = piece * piece_width
            part_out = jnp.dot(hidden[:, lo:lo + piece_width], down_all[expert][lo:lo + piece_width], preferred_element_type=jnp.float32)
            lowered = lowered + part_out.astype(jnp.bfloat16).astype(jnp.float32)
        results.append(lowered.reshape(N_EXPERT, MOST, D))
    expert_out = jnp.stack(results, axis=1)
    live = jnp.arange(MOST, dtype=jnp.int32)[None, None, :] < count[:, :, None]
    weights = jnp.where(live, combine, jnp.zeros_like(combine))
    terms = (weights[..., None] * expert_out).reshape(-1, D)
    mixed = jax.ops.segment_sum(terms, owners.reshape(-1), num_segments=TOKENS)
    return (gate[request] * mixed).astype(jnp.bfloat16)
```

```python
import functools

import jax
import jax.numpy as jnp
from jax import lax
from jax.experimental import pallas as pl
from jax.experimental.pallas import tpu as pltpu
from jax.sharding import PartitionSpec as P

CHUNKS = 4
MIB = 1024 * 1024
F32 = jnp.float32
BF16 = jnp.bfloat16

SMEM = pl.BlockSpec(memory_space=pltpu.SMEM)


def params(mib):
    return pltpu.CompilerParams(vmem_limit_bytes=mib * MIB)


def token_rows(info_ref, pick_ref, tok_rows, experts):
    slots = pick_ref.shape[1]
    rows = [pick_ref[pl.ds(info_ref[0] ^ d, 1), :] for d in range(experts)]
    picks = jnp.concatenate(rows, axis=1)
    ids = lax.broadcasted_iota(jnp.int32, (tok_rows, experts * slots), 0)
    return ids == picks


def pre_kernel(info_ref, pick_ref, tok_ref, shift_ref, scale_ref, *outs, experts, slots, chunks):
    tok_rows, width = tok_ref.shape
    hot = token_rows(info_ref, pick_ref, tok_rows, experts).astype(F32).astype(BF16)
    values = lax.dot_general(hot, tok_ref[...], (((0,), (0,)), ((), ())), preferred_element_type=F32)
    center = values - jnp.mean(values, axis=1, keepdims=True)
    spread = jnp.mean(center * center, axis=1, keepdims=True)
    normed = center * (1.0 / jnp.sqrt(spread + 1e-06))
    scale = scale_ref[pl.ds(info_ref[1], 1), :]
    shift = shift_ref[pl.ds(info_ref[1], 1), :]
    modulated = (normed * (1.0 + scale) + shift).astype(BF16)
    step = width // chunks
    for d in range(experts):
        for c in range(chunks):
            outs[d * chunks + c][...] = modulated[d * slots:(d + 1) * slots, c * step:(c + 1) * step]


def up_kernel(*refs, blocks, first, last):
    parts = refs[:blocks]
    w_ref = refs[blocks]
    acc_ref = None if first else refs[blocks + 1]
    out_ref, rows_ref = refs[-2:]

    @pl.when(pl.program_id(0) == 0)
    def _():
        at = 0
        for part in parts:
            rows_ref[at:at + part.shape[0], :] = part[...]
            at += part.shape[0]

    lifted = lax.dot_general(
        rows_ref[...], w_ref[...], (((1,), (1,)), ((), ())), preferred_element_type=F32
    )
    if not first:
        lifted = lifted + acc_ref[...]
    if last:
        lifted = jax.nn.gelu(lifted, approximate=True)
    out_ref[...] = lifted.astype(out_ref.dtype)


def up(parts, w_up, acc, chunk, chunks, rows):
    hidden, width = w_up.shape
    step = width // chunks
    tile = min(256, hidden)
    first, last = chunk == 0, chunk == chunks - 1
    in_specs = [pl.BlockSpec(p.shape, lambda i: (0, 0)) for p in parts]
    in_specs.append(pl.BlockSpec((tile, step), lambda i: (i, chunk)))
    args = list(parts) + [w_up]
    if not first:
        in_specs.append(pl.BlockSpec((rows, tile), lambda i: (0, i)))
        args.append(acc)
    return pl.pallas_call(
        functools.partial(up_kernel, blocks=len(parts), first=first, last=last),
        grid=(hidden // tile,),
        in_specs=in_specs,
        out_specs=pl.BlockSpec((rows, tile), lambda i: (0, i)),
        out_shape=jax.ShapeDtypeStruct((rows, hidden), BF16 if last else F32),
        scratch_shapes=[pltpu.VMEM((rows, step), BF16)],
        compiler_params=params(20),
        cost_estimate=pl.CostEstimate(
            flops=2 * rows * hidden * step, bytes_accessed=2 * hidden * step, transcendentals=0
        ),
        name="up",
    )(*args)


def down_kernel(h_ref, w_ref, keep_ref, send_ref):
    half = keep_ref.shape[0]
    out = jnp.dot(h_ref[...], w_ref[...], preferred_element_type=F32)
    keep_ref[...] = out[:half]
    send_ref[...] = out[half:].astype(BF16)


def down(h, w_down, chunk, chunks):
    rows, hidden = h.shape
    width = w_down.shape[1]
    step = width // chunks
    tile = min(512, step)
    per = step // tile
    half = rows // 2
    return pl.pallas_call(
        down_kernel,
        grid=(per,),
        in_specs=[
            pl.BlockSpec((rows, hidden), lambda i: (0, 0)),
            pl.BlockSpec((hidden, tile), lambda i: (0, chunk * per + i)),
        ],
        out_specs=[
            pl.BlockSpec((half, tile), lambda i: (0, i)),
            pl.BlockSpec((half, tile), lambda i: (0, i)),
        ],
        out_shape=[
            jax.ShapeDtypeStruct((half, step), F32),
            jax.ShapeDtypeStruct((half, step), BF16),
        ],
        compiler_params=params(20),
        cost_estimate=pl.CostEstimate(
            flops=2 * rows * hidden * step, bytes_accessed=2 * hidden * step, transcendentals=0
        ),
        name="down",
    )(h, w_down)


def add_kernel(keep_ref, got_ref, *outs):
    total = keep_ref[...] + got_ref[...].astype(F32)
    at = 0
    for out in outs:
        out[...] = total[at:at + out.shape[0]].astype(out.dtype)
        at += out.shape[0]


def add(keep, got, heights, kinds):
    width = keep.shape[1]
    return pl.pallas_call(
        add_kernel,
        out_shape=[jax.ShapeDtypeStruct((h, width), k) for h, k in zip(heights, kinds)],
        compiler_params=params(12),
        name="add",
    )(keep, got)


def post_kernel(info_ref, count_ref, pick_ref, comb_ref, gate_ref, *refs, experts, filled):
    parts = refs[:experts]
    out_ref = refs[-1]
    tok_rows = out_ref.shape[0]
    slots = pick_ref.shape[1]
    hot = token_rows(info_ref, pick_ref, tok_rows, experts)
    lanes = lax.broadcasted_iota(jnp.int32, (1, slots), 1)
    weights = []
    for d in range(experts):
        e = info_ref[0] ^ d
        weights.append(jnp.where(lanes < count_ref[0, e], comb_ref[pl.ds(e, 1), :], 0.0))
    mix = jnp.where(hot, jnp.concatenate(weights, axis=1), 0.0)
    high = mix.astype(BF16)
    rest = mix - high.astype(F32)
    mid = rest.astype(BF16)
    low = (rest - mid.astype(F32)).astype(BF16)
    values = jnp.concatenate([p[...] for p in parts], axis=0)
    mixed = jnp.dot(high, values, preferred_element_type=F32)
    mixed = mixed + jnp.dot(mid, values, preferred_element_type=F32)
    mixed = mixed + jnp.dot(low, values, preferred_element_type=F32)
    out_ref[...] = (gate_ref[pl.ds(info_ref[1], 1), :] * mixed).astype(BF16)


def post(info, count, pick, comb, gate, parts, out, chunk, chunks, tok_rows):
    experts, slots = pick.shape
    requests, width = gate.shape
    step = width // chunks
    whole = lambda shape: pl.BlockSpec(shape, lambda i: (0,) * len(shape))
    in_specs = [
        SMEM,
        SMEM,
        whole(pick.shape),
        whole(comb.shape),
        pl.BlockSpec((requests, step), lambda i: (0, chunk)),
    ] + [whole(p.shape) for p in parts]
    args = [info, count, pick, comb, gate] + list(parts)
    aliases = {}
    if out is not None:
        aliases = {len(args): 0}
        in_specs.append(pl.BlockSpec(memory_space=pl.ANY))
        args.append(out)
    return pl.pallas_call(
        functools.partial(post_kernel, experts=experts, filled=out is not None),
        grid=(1,),
        in_specs=in_specs,
        out_specs=pl.BlockSpec((tok_rows, step), lambda i: (0, chunk)),
        out_shape=jax.ShapeDtypeStruct((tok_rows, width), BF16),
        input_output_aliases=aliases,
        compiler_params=params(12),
        name="post",
    )(*args)


def shards(tokens, shift, scale, gate, w_up, w_down, pick, count, combine):
    tok_rows, width = tokens.shape
    _, experts, slots = pick.shape
    devices = lax.axis_size("expert")
    place = lax.axis_index("expert")
    group = devices // experts
    requests = shift.shape[0]
    chunks = CHUNKS
    step = width // chunks
    rows = devices * slots
    info = jnp.stack([place // group, place // (devices // requests)]).astype(jnp.int32)
    pick = pick[0]
    comb = combine[0]

    far = [d * group for d in range(1, experts)]
    near = []
    bit = group // 2
    while bit:
        near.append(bit)
        bit //= 2

    def swap(x, mask):
        return lax.ppermute(x, "expert", [(i, i ^ mask) for i in range(devices)])

    flat = pl.pallas_call(
        functools.partial(pre_kernel, experts=experts, slots=slots, chunks=chunks),
        in_specs=[SMEM] + [pl.BlockSpec(memory_space=pltpu.VMEM)] * 4,
        out_shape=[jax.ShapeDtypeStruct((slots, step), BF16)] * (experts * chunks),
        compiler_params=params(20),
        name="pre",
    )(info, pick, tokens, shift, scale)

    acc = None
    for c in range(chunks):
        parts = [flat[c]] + [swap(flat[d * chunks + c], far[d - 1]) for d in range(1, experts)]
        for mask in near:
            whole = parts[0] if len(parts) == 1 else jnp.concatenate(parts, axis=0)
            parts = [whole, swap(whole, mask)]
        acc = up(parts, w_up, acc, c, chunks, rows)

    out = None
    for c in range(chunks):
        keep, send = down(acc, w_down, c, chunks)
        for at, mask in enumerate(reversed(near)):
            got = swap(send, mask)
            height = keep.shape[0]
            if at < len(near) - 1:
                keep, send = add(keep, got, [height // 2] * 2, [F32, BF16])
            else:
                parts = add(keep, got, [slots] * experts, [BF16] * experts)
        parts = [parts[0]] + [swap(parts[d], far[d - 1]) for d in range(1, experts)]
        out = post(info, count, pick, comb, gate, parts, out, c, chunks, tok_rows)
    return out


def solution(mesh):
    return jax.shard_map(
        shards,
        mesh=mesh,
        in_specs=(
            P(("groups", "expert"), None),
            P("groups", None),
            P("groups", None),
            P("groups", None),
            P("expert", None),
            P("expert", None),
            P(("groups", "expert"), None, None),
            P(("groups", "expert"), None),
            P(("groups", "expert"), None, None),
        ),
        out_specs=P(("groups", "expert"), None),
        check_vma=False,
    )
```

```python
import functools

import jax
import jax.numpy as jnp
from jax import lax
from jax.experimental import pallas as pl
from jax.experimental.pallas import tpu as pltpu
from jax.sharding import PartitionSpec as P

CHUNKS = 2
MIB = 1024 * 1024
F32 = jnp.float32
BF16 = jnp.bfloat16

SMEM = pl.BlockSpec(memory_space=pltpu.SMEM)


def params(mib):
    return pltpu.CompilerParams(vmem_limit_bytes=mib * MIB)


def token_rows(info_ref, pick_ref, tok_rows, experts):
    slots = pick_ref.shape[1]
    rows = [pick_ref[pl.ds(info_ref[0] ^ d, 1), :] for d in range(experts)]
    picks = jnp.concatenate(rows, axis=1)
    ids = lax.broadcasted_iota(jnp.int32, (tok_rows, experts * slots), 0)
    return ids == picks


def pre_kernel(info_ref, pick_ref, tok_ref, shift_ref, scale_ref, *outs, experts, slots, chunks):
    tok_rows, width = tok_ref.shape
    hot = token_rows(info_ref, pick_ref, tok_rows, experts).astype(F32).astype(BF16)
    values = lax.dot_general(hot, tok_ref[...], (((0,), (0,)), ((), ())), preferred_element_type=F32)
    center = values - jnp.mean(values, axis=1, keepdims=True)
    spread = jnp.mean(center * center, axis=1, keepdims=True)
    normed = center * (1.0 / jnp.sqrt(spread + 1e-06))
    scale = scale_ref[pl.ds(info_ref[1], 1), :]
    shift = shift_ref[pl.ds(info_ref[1], 1), :]
    modulated = (normed * (1.0 + scale) + shift).astype(BF16)
    step = width // chunks
    for d in range(experts):
        for c in range(chunks):
            outs[d * chunks + c][...] = modulated[d * slots:(d + 1) * slots, c * step:(c + 1) * step]


def up_kernel(*refs, blocks, first, last):
    parts = refs[:blocks]
    w_ref = refs[blocks]
    acc_ref = None if first else refs[blocks + 1]
    out_ref, rows_ref = refs[-2:]

    @pl.when(pl.program_id(0) == 0)
    def _():
        at = 0
        for part in parts:
            rows_ref[at:at + part.shape[0], :] = part[...]
            at += part.shape[0]

    lifted = lax.dot_general(
        rows_ref[...], w_ref[...], (((1,), (1,)), ((), ())), preferred_element_type=F32
    )
    if not first:
        lifted = lifted + acc_ref[...]
    if last:
        lifted = jax.nn.gelu(lifted, approximate=True)
    out_ref[...] = lifted.astype(out_ref.dtype)


def up(parts, w_up, acc, chunk, chunks, rows):
    hidden, width = w_up.shape
    step = width // chunks
    tile = min(256, hidden)
    first, last = chunk == 0, chunk == chunks - 1
    in_specs = [pl.BlockSpec(p.shape, lambda i: (0, 0)) for p in parts]
    in_specs.append(pl.BlockSpec((tile, step), lambda i: (i, chunk)))
    args = list(parts) + [w_up]
    if not first:
        in_specs.append(pl.BlockSpec((rows, tile), lambda i: (0, i)))
        args.append(acc)
    return pl.pallas_call(
        functools.partial(up_kernel, blocks=len(parts), first=first, last=last),
        grid=(hidden // tile,),
        in_specs=in_specs,
        out_specs=pl.BlockSpec((rows, tile), lambda i: (0, i)),
        out_shape=jax.ShapeDtypeStruct((rows, hidden), BF16 if last else F32),
        scratch_shapes=[pltpu.VMEM((rows, step), BF16)],
        compiler_params=params(48),
        cost_estimate=pl.CostEstimate(
            flops=2 * rows * hidden * step, bytes_accessed=2 * hidden * step, transcendentals=0
        ),
        name="up",
    )(*args)


def down_kernel(h_ref, w_ref, out_ref):
    out_ref[...] = jnp.dot(h_ref[...], w_ref[...], preferred_element_type=F32).astype(BF16)


def down(h, w_down, chunk, chunks):
    rows, hidden = h.shape
    width = w_down.shape[1]
    step = width // chunks
    tile = min(512, step)
    per = step // tile
    return pl.pallas_call(
        down_kernel,
        grid=(per,),
        in_specs=[
            pl.BlockSpec((rows, hidden), lambda i: (0, 0)),
            pl.BlockSpec((hidden, tile), lambda i: (0, chunk * per + i)),
        ],
        out_specs=pl.BlockSpec((rows, tile), lambda i: (0, i)),
        out_shape=jax.ShapeDtypeStruct((rows, step), BF16),
        compiler_params=params(48),
        cost_estimate=pl.CostEstimate(
            flops=2 * rows * hidden * step, bytes_accessed=2 * hidden * step, transcendentals=0
        ),
        name="down",
    )(h, w_down)


def post_kernel(info_ref, count_ref, pick_ref, comb_ref, gate_ref, *refs, experts, filled):
    parts = refs[:experts]
    out_ref = refs[-1]
    tok_rows = out_ref.shape[0]
    slots = pick_ref.shape[1]
    hot = token_rows(info_ref, pick_ref, tok_rows, experts)
    lanes = lax.broadcasted_iota(jnp.int32, (1, slots), 1)
    weights = []
    for d in range(experts):
        e = info_ref[0] ^ d
        weights.append(jnp.where(lanes < count_ref[0, e], comb_ref[pl.ds(e, 1), :], 0.0))
    mix = jnp.where(hot, jnp.concatenate(weights, axis=1), 0.0)
    high = mix.astype(BF16)
    rest = mix - high.astype(F32)
    mid = rest.astype(BF16)
    low = (rest - mid.astype(F32)).astype(BF16)
    values = jnp.concatenate([p[...] for p in parts], axis=0)
    mixed = jnp.dot(high, values, preferred_element_type=F32)
    mixed = mixed + jnp.dot(mid, values, preferred_element_type=F32)
    mixed = mixed + jnp.dot(low, values, preferred_element_type=F32)
    out_ref[...] = (gate_ref[pl.ds(info_ref[1], 1), :] * mixed).astype(BF16)


def post(info, count, pick, comb, gate, parts, out, chunk, chunks, tok_rows):
    experts, slots = pick.shape
    requests, width = gate.shape
    step = width // chunks
    whole = lambda shape: pl.BlockSpec(shape, lambda i: (0,) * len(shape))
    in_specs = [
        SMEM,
        SMEM,
        whole(pick.shape),
        whole(comb.shape),
        pl.BlockSpec((requests, step), lambda i: (0, chunk)),
    ] + [whole(p.shape) for p in parts]
    args = [info, count, pick, comb, gate] + list(parts)
    aliases = {}
    if out is not None:
        aliases = {len(args): 0}
        in_specs.append(pl.BlockSpec(memory_space=pl.ANY))
        args.append(out)
    return pl.pallas_call(
        functools.partial(post_kernel, experts=experts, filled=out is not None),
        grid=(1,),
        in_specs=in_specs,
        out_specs=pl.BlockSpec((tok_rows, step), lambda i: (0, chunk)),
        out_shape=jax.ShapeDtypeStruct((tok_rows, width), BF16),
        input_output_aliases=aliases,
        compiler_params=params(12),
        name="post",
    )(*args)


def shards(tokens, shift, scale, gate, w_up, w_down, pick, count, combine):
    tok_rows, width = tokens.shape
    _, experts, slots = pick.shape
    devices = lax.axis_size("expert")
    place = lax.axis_index("expert")
    group = devices // experts
    requests = shift.shape[0]
    chunks = CHUNKS
    step = width // chunks
    rows = devices * slots
    info = jnp.stack([place // group, place // (devices // requests)]).astype(jnp.int32)
    pick = pick[0]
    comb = combine[0]

    far = [d * group for d in range(1, experts)]

    def swap(x, mask):
        return lax.ppermute(x, "expert", [(i, i ^ mask) for i in range(devices)])

    flat = pl.pallas_call(
        functools.partial(pre_kernel, experts=experts, slots=slots, chunks=chunks),
        in_specs=[SMEM] + [pl.BlockSpec(memory_space=pltpu.VMEM)] * 4,
        out_shape=[jax.ShapeDtypeStruct((slots, step), BF16)] * (experts * chunks),
        compiler_params=params(20),
        name="pre",
    )(info, pick, tokens, shift, scale)

    groups = [[e * group + j for j in range(group)] for e in range(experts)]
    acc = None
    for c in range(chunks):
        parts = [flat[c]] + [swap(flat[d * chunks + c], far[d - 1]) for d in range(1, experts)]
        own = jnp.concatenate(parts, axis=0)
        every = lax.all_gather(own, "expert", axis_index_groups=groups, axis=0, tiled=True)
        acc = up([every], w_up, acc, c, chunks, rows)

    out = None
    for c in range(chunks):
        part = down(acc, w_down, c, chunks)
        got = lax.psum_scatter(part, "expert", scatter_dimension=0, axis_index_groups=groups, tiled=True)
        parts = [got[d * slots:(d + 1) * slots] for d in range(experts)]
        parts = [parts[0]] + [swap(parts[d], far[d - 1]) for d in range(1, experts)]
        out = post(info, count, pick, comb, gate, parts, out, c, chunks, tok_rows)
    return out


def solution(mesh):
    return jax.shard_map(
        shards,
        mesh=mesh,
        in_specs=(
            P(("groups", "expert"), None),
            P("groups", None),
            P("groups", None),
            P("groups", None),
            P("expert", None),
            P("expert", None),
            P(("groups", "expert"), None, None),
            P(("groups", "expert"), None),
            P(("groups", "expert"), None, None),
        ),
        out_specs=P(("groups", "expert"), None),
        check_vma=False,
    )
```

```python
import functools

import jax
import jax.numpy as jnp
from jax import lax
from jax.experimental import pallas as pl
from jax.experimental.pallas import tpu as pltpu
from jax.sharding import PartitionSpec as P

CHUNKS = 2
MIB = 1024 * 1024
F32 = jnp.float32
BF16 = jnp.bfloat16

SMEM = pl.BlockSpec(memory_space=pltpu.SMEM)
VMEM = pl.BlockSpec(memory_space=pltpu.VMEM)
HBM = pl.BlockSpec(memory_space=pltpu.HBM)
ANY = pl.BlockSpec(memory_space=pl.ANY)


FREE = pl.CostEstimate(flops=1, bytes_accessed=1, transcendentals=0)


def params(mib):
    return pltpu.CompilerParams(vmem_limit_bytes=mib * MIB)


def fetch(pairs, sems):
    copies = [pltpu.make_async_copy(src, dst, sems.at[i]) for i, (src, dst) in enumerate(pairs)]
    for copy in copies:
        copy.start()
    for copy in copies:
        copy.wait()


def slot_tokens(info_ref, pick_ref, tok_rows):
    experts, slots = pick_ref.shape
    rows = [pick_ref[pl.ds(info_ref[1] ^ d, 1), :] for d in range(experts)]
    picks = jnp.concatenate(rows, axis=1)
    return lax.broadcasted_iota(jnp.int32, (tok_rows, experts * slots), 0) == picks


def pre_kernel(info_ref, pick_hbm, tok_hbm, shift_hbm, scale_hbm, *refs, chunks):
    outs = refs[:-5]
    pick_ref, tok_ref, shift_ref, scale_ref, sems = refs[-5:]
    experts, slots = pick_ref.shape
    fetch(
        [(tok_hbm, tok_ref), (pick_hbm, pick_ref), (shift_hbm, shift_ref), (scale_hbm, scale_ref)],
        sems,
    )
    tok_rows, width = tok_ref.shape
    hot = slot_tokens(info_ref, pick_ref, tok_rows).astype(F32).astype(BF16)
    values = lax.dot_general(hot, tok_ref[...], (((0,), (0,)), ((), ())), preferred_element_type=F32)
    center = values - jnp.mean(values, axis=1, keepdims=True)
    spread = jnp.mean(center * center, axis=1, keepdims=True)
    normed = center * (1.0 / jnp.sqrt(spread + 1e-06))
    scale = scale_ref[pl.ds(info_ref[0], 1), :]
    shift = shift_ref[pl.ds(info_ref[0], 1), :]
    modulated = (normed * (1.0 + scale) + shift).astype(BF16)
    step = width // chunks
    outs[-1][...] = modulated[:slots]
    for c in range(chunks):
        for d in range(1, experts):
            outs[c * (experts - 1) + d - 1][...] = modulated[d * slots:(d + 1) * slots, c * step:(c + 1) * step]


def pre(info, pick, tokens, shift, scale, chunks):
    experts, slots = pick.shape
    width = tokens.shape[1]
    return pl.pallas_call(
        functools.partial(pre_kernel, chunks=chunks),
        in_specs=[SMEM] + [HBM] * 4,
        out_specs=[VMEM] * (chunks * (experts - 1) + 1),
        out_shape=[jax.ShapeDtypeStruct((slots, width // chunks), BF16)] * (chunks * (experts - 1))
        + [jax.ShapeDtypeStruct((slots, width), BF16)],
        scratch_shapes=[
            pltpu.VMEM(pick.shape, jnp.int32),
            pltpu.VMEM(tokens.shape, BF16),
            pltpu.VMEM(shift.shape, F32),
            pltpu.VMEM(scale.shape, F32),
            pltpu.SemaphoreType.DMA((4,)),
        ],
        compiler_params=params(16),
        cost_estimate=FREE,
        name="pre",
    )(info, pick, tokens, shift, scale)


def mixer_kernel(info_ref, count_ref, pick_hbm, comb_hbm, gate_hbm, after_ref, mix_ref, row_ref, pick_ref, comb_ref, gate_ref, sems):
    fetch([(pick_hbm, pick_ref), (comb_hbm, comb_ref), (gate_hbm, gate_ref)], sems)
    experts, slots = pick_ref.shape
    tok_rows = mix_ref.shape[0]
    hot = slot_tokens(info_ref, pick_ref, tok_rows)
    lanes = lax.broadcasted_iota(jnp.int32, (1, slots), 1)
    weights = []
    for d in range(experts):
        e = info_ref[1] ^ d
        weights.append(jnp.where(lanes < count_ref[0, e], comb_ref[pl.ds(e, 1), :], 0.0))
    mix = jnp.where(hot, jnp.concatenate(weights, axis=1), 0.0)
    high = mix.astype(BF16).astype(F32)
    rest = mix - high
    mid = rest.astype(BF16).astype(F32)
    mix_ref[...] = jnp.concatenate([high, mid, rest - mid], axis=1).astype(BF16)
    row_ref[...] = gate_ref[pl.ds(info_ref[0], 1), :]


def mixer(info, count, pick, comb, gate, after, tok_rows):
    experts, slots = pick.shape
    return pl.pallas_call(
        mixer_kernel,
        in_specs=[SMEM, SMEM] + [HBM] * 3 + [ANY],
        out_specs=[VMEM] * 2,
        out_shape=[
            jax.ShapeDtypeStruct((tok_rows, 3 * experts * slots), BF16),
            jax.ShapeDtypeStruct((1, gate.shape[1]), F32),
        ],
        scratch_shapes=[
            pltpu.VMEM(pick.shape, jnp.int32),
            pltpu.VMEM(comb.shape, F32),
            pltpu.VMEM(gate.shape, F32),
            pltpu.SemaphoreType.DMA((3,)),
        ],
        compiler_params=params(8),
        cost_estimate=FREE,
        name="mixer",
    )(info, count, pick, comb, gate, after)


def load_kernel(w_hbm, after_ref, out_ref, sems, *, chunk, pieces):
    rows, step = out_ref.shape
    part = rows // pieces
    fetch(
        [
            (
                w_hbm.at[pl.ds(p * part, part), pl.ds(chunk * step, step)],
                out_ref.at[pl.ds(p * part, part), :],
            )
            for p in range(pieces)
        ],
        sems,
    )


def load(w, after, chunk, chunks):
    rows, width = w.shape
    step = width // chunks
    pieces = 8
    return pl.pallas_call(
        functools.partial(load_kernel, chunk=chunk, pieces=pieces),
        in_specs=[HBM, ANY],
        out_specs=VMEM,
        out_shape=pltpu.VMEM((rows, step), w.dtype),
        scratch_shapes=[pltpu.SemaphoreType.DMA((pieces,))],
        compiler_params=params(4),
        cost_estimate=FREE,
        name="load",
    )(w, after)


def join_kernel(*refs, cuts):
    out_ref = refs[-1]
    at = 0
    for ref, cut in zip(refs, cuts):
        out_ref[at:at + ref.shape[0], :] = ref[...] if cut is None else ref[:, cut[0]:cut[1]]
        at += ref.shape[0]


def join(parts, after):
    arrays = [p[0] if isinstance(p, tuple) else p for p in parts]
    cuts = [p[1] if isinstance(p, tuple) else None for p in parts]
    step = min(a.shape[1] for a in arrays)
    return pl.pallas_call(
        functools.partial(join_kernel, cuts=cuts),
        in_specs=[VMEM] * len(arrays) + [ANY] * len(after),
        out_specs=VMEM,
        out_shape=jax.ShapeDtypeStruct((sum(a.shape[0] for a in arrays), step), BF16),
        compiler_params=params(4),
        cost_estimate=FREE,
        name="join",
    )(*arrays, *after)


def up_kernel(*refs, blocks, first, last):
    parts = refs[:blocks]
    w_ref = refs[blocks]
    acc_ref = None if first else refs[blocks + 1]
    out_ref, rows_ref = refs[-2:]
    at = 0
    for part in parts:
        rows_ref[at:at + part.shape[0], :] = part[...]
        at += part.shape[0]
    hidden = w_ref.shape[0]
    tile = min(256, hidden)

    @pl.loop(0, hidden // tile)
    def _(i):
        cut = pl.ds(pl.multiple_of(i * tile, tile), tile)
        lifted = lax.dot_general(
            rows_ref[...], w_ref[cut, :], (((1,), (1,)), ((), ())), preferred_element_type=F32
        )
        if not first:
            lifted = lifted + acc_ref[:, cut]
        if last:
            lifted = jax.nn.gelu(lifted, approximate=True)
        out_ref[:, cut] = lifted.astype(out_ref.dtype)


def up(parts, w, acc, first, last):
    hidden, step = w.shape
    rows = sum(p.shape[0] for p in parts)
    args = list(parts) + [w] + ([] if first else [acc])
    return pl.pallas_call(
        functools.partial(up_kernel, blocks=len(parts), first=first, last=last),
        in_specs=[VMEM] * len(args),
        out_specs=VMEM,
        out_shape=jax.ShapeDtypeStruct((rows, hidden), BF16 if last else F32),
        scratch_shapes=[pltpu.VMEM((rows, step), BF16)],
        compiler_params=params(16),
        cost_estimate=FREE,
        name="up",
    )(*args)


def down_kernel(h_ref, w_ref, after_ref, keep_ref, send_ref):
    half, step = keep_ref.shape
    tile = min(256, step)

    @pl.loop(0, step // tile)
    def _(i):
        cut = pl.ds(pl.multiple_of(i * tile, tile), tile)
        out = jnp.dot(h_ref[...], w_ref[:, cut], preferred_element_type=F32)
        keep_ref[:, cut] = out[:half]
        send_ref[:, cut] = out[half:].astype(BF16)


def down(h, w, after):
    rows, hidden = h.shape
    step = w.shape[1]
    half = rows // 2
    return pl.pallas_call(
        down_kernel,
        in_specs=[VMEM] * 2 + [ANY],
        out_specs=[VMEM] * 2,
        out_shape=[
            jax.ShapeDtypeStruct((half, step), F32),
            jax.ShapeDtypeStruct((half, step), BF16),
        ],
        compiler_params=params(16),
        cost_estimate=FREE,
        name="down",
    )(h, w, after)


def add_kernel(keep_ref, got_ref, *outs):
    at = 0
    for out in outs:
        cut = slice(at, at + out.shape[0])
        out[...] = (keep_ref[cut] + got_ref[cut].astype(F32)).astype(out.dtype)
        at += out.shape[0]


def add(keep, got, heights, kinds):
    width = keep.shape[1]
    return pl.pallas_call(
        add_kernel,
        in_specs=[VMEM] * 2,
        out_specs=[VMEM] * len(heights),
        out_shape=[jax.ShapeDtypeStruct((h, width), k) for h, k in zip(heights, kinds)],
        compiler_params=params(12),
        cost_estimate=FREE,
        name="add",
    )(keep, got)


def post_kernel(mix_ref, row_ref, *refs, experts):
    out_ref = refs[-1]
    values = jnp.concatenate([ref[...] for ref in refs[:experts]] * 3, axis=0)
    mixed = jnp.dot(mix_ref[...], values, preferred_element_type=F32)
    out_ref[...] = (row_ref[...] * mixed).astype(BF16)


def post(mix, row, parts, out, chunk, chunks):
    tok_rows = mix.shape[0]
    width = row.shape[1]
    step = width // chunks
    in_specs = [
        pl.BlockSpec(mix.shape, lambda i: (0, 0)),
        pl.BlockSpec((1, step), lambda i: (0, chunk)),
    ] + [pl.BlockSpec(p.shape, lambda i: (0, 0)) for p in parts]
    args = [mix, row] + list(parts)
    aliases = {}
    if out is not None:
        aliases = {len(args): 0}
        in_specs.append(ANY)
        args.append(out)
    return pl.pallas_call(
        functools.partial(post_kernel, experts=len(parts)),
        grid=(1,),
        in_specs=in_specs,
        out_specs=pl.BlockSpec((tok_rows, step), lambda i: (0, chunk)),
        out_shape=jax.ShapeDtypeStruct((tok_rows, width), BF16),
        input_output_aliases=aliases,
        compiler_params=params(12),
        cost_estimate=FREE,
        name="post",
    )(*args)


def shards(tokens, shift, scale, gate, w_up, w_down, pick, count, combine):
    tok_rows, width = tokens.shape
    _, experts, slots = pick.shape
    devices = lax.axis_size("expert")
    place = lax.axis_index("expert")
    group = devices // experts
    requests = shift.shape[0]
    chunks = CHUNKS
    step = width // chunks
    info = jnp.stack([place // (devices // requests), place // group]).astype(jnp.int32)
    pick = pick[0]
    comb = combine[0]

    far = [d * group for d in range(1, experts)]
    near = []
    bit = group // 2
    while bit:
        near.append(bit)
        bit //= 2

    def swap(x, mask):
        return lax.ppermute(x, "expert", [(i, i ^ mask) for i in range(devices)])

    tokens, shift, scale, gate, w_up, w_down, pick, comb = [
        pltpu.with_memory_space_constraint(x, pltpu.HBM)
        for x in (tokens, shift, scale, gate, w_up, w_down, pick, comb)
    ]
    *flat, own = pre(info, pick, tokens, shift, scale, chunks)
    got = []
    for c in range(chunks):
        got.append([swap(flat[c * (experts - 1) + d - 1], far[d - 1]) for d in range(1, experts)])
    own_near = swap(own, near[0])

    acc = None
    downs = []
    after = own
    mix, row = mixer(info, count, pick, comb, gate, own, tok_rows)
    for c in range(chunks):
        cut = (c * step, (c + 1) * step)
        w = load(w_up, after, c, chunks)
        block = join(got[c], [w, own_near])
        after = block
        parts = [(own, cut), block, (own_near, cut), swap(block, near[0])]
        for mask in near[1:]:
            block = join(parts, [])
            parts = [block, swap(block, mask)]
        downs.append(load(w_down, block, c, chunks))
        acc = up(parts, w, acc, c == 0, c == chunks - 1)

    out = None
    for c in range(chunks):
        keep, send = down(acc, downs[c], downs[-1])
        for at, mask in enumerate(reversed(near)):
            arrived = swap(send, mask)
            height = keep.shape[0]
            if at < len(near) - 1:
                keep, send = add(keep, arrived, [height // 2] * 2, [F32, BF16])
            else:
                parts = add(keep, arrived, [slots] * experts, [BF16] * experts)
        parts = [parts[0]] + [swap(parts[d], far[d - 1]) for d in range(1, experts)]
        out = post(mix, row, parts, out, c, chunks)
    return out


def solution(mesh):
    return jax.shard_map(
        shards,
        mesh=mesh,
        in_specs=(
            P(("groups", "expert"), None),
            P("groups", None),
            P("groups", None),
            P("groups", None),
            P("expert", None),
            P("expert", None),
            P(("groups", "expert"), None, None),
            P(("groups", "expert"), None),
            P(("groups", "expert"), None, None),
        ),
        out_specs=P(("groups", "expert"), None),
        check_vma=False,
    )
```

```python
import functools

import jax
import jax.numpy as jnp
from jax import lax
from jax.experimental import pallas as pl
from jax.experimental.pallas import tpu as pltpu
from jax.sharding import PartitionSpec as P

CHUNKS = 2
PIECES = 8
MIB = 1024 * 1024
F32 = jnp.float32
BF16 = jnp.bfloat16

SMEM = pl.BlockSpec(memory_space=pltpu.SMEM)
VMEM = pl.BlockSpec(memory_space=pltpu.VMEM)
HBM = pl.BlockSpec(memory_space=pltpu.HBM)
ANY = pl.BlockSpec(memory_space=pl.ANY)


FREE = pl.CostEstimate(flops=1, bytes_accessed=1, transcendentals=0)


def params(mib):
    return pltpu.CompilerParams(vmem_limit_bytes=mib * MIB)


def fetch(pairs, sems):
    copies = [pltpu.make_async_copy(src, dst, sems.at[i]) for i, (src, dst) in enumerate(pairs)]
    for copy in copies:
        copy.start()
    for copy in copies:
        copy.wait()


def turns(experts):
    return [0] + list(range(experts - 1, 0, -1))


def slot_tokens(info_ref, pick_ref, tok_rows):
    experts, slots = pick_ref.shape
    rows = [pick_ref[pl.ds(info_ref[1] ^ d, 1), :] for d in turns(experts)]
    picks = jnp.concatenate(rows, axis=1)
    return lax.broadcasted_iota(jnp.int32, (tok_rows, experts * slots), 0) == picks


def pre_kernel(info_ref, pick_hbm, tok_hbm, shift_hbm, scale_hbm, *refs, chunks):
    outs = refs[:-5]
    pick_ref, tok_ref, shift_ref, scale_ref, sems = refs[-5:]
    experts, slots = pick_ref.shape
    fetch(
        [(tok_hbm, tok_ref), (pick_hbm, pick_ref), (shift_hbm, shift_ref), (scale_hbm, scale_ref)],
        sems,
    )
    tok_rows, width = tok_ref.shape
    hot = slot_tokens(info_ref, pick_ref, tok_rows).astype(F32).astype(BF16)
    values = lax.dot_general(hot, tok_ref[...], (((0,), (0,)), ((), ())), preferred_element_type=F32)
    center = values - jnp.mean(values, axis=1, keepdims=True)
    spread = jnp.mean(center * center, axis=1, keepdims=True)
    normed = center * (1.0 / jnp.sqrt(spread + 1e-06))
    scale = scale_ref[pl.ds(info_ref[0], 1), :]
    shift = shift_ref[pl.ds(info_ref[0], 1), :]
    modulated = (normed * (1.0 + scale) + shift).astype(BF16)
    step = width // chunks
    outs[-1][...] = modulated[:slots]
    for c in range(chunks):
        for d in range(1, experts):
            outs[c * (experts - 1) + d - 1][...] = modulated[d * slots:(d + 1) * slots, c * step:(c + 1) * step]


def pre(info, pick, tokens, shift, scale, chunks):
    experts, slots = pick.shape
    width = tokens.shape[1]
    return pl.pallas_call(
        functools.partial(pre_kernel, chunks=chunks),
        in_specs=[SMEM] + [HBM] * 4,
        out_specs=[VMEM] * (chunks * (experts - 1) + 1),
        out_shape=[jax.ShapeDtypeStruct((slots, width // chunks), BF16)] * (chunks * (experts - 1))
        + [jax.ShapeDtypeStruct((slots, width), BF16)],
        scratch_shapes=[
            pltpu.VMEM(pick.shape, jnp.int32),
            pltpu.VMEM(tokens.shape, BF16),
            pltpu.VMEM(shift.shape, F32),
            pltpu.VMEM(scale.shape, F32),
            pltpu.SemaphoreType.DMA((4,)),
        ],
        compiler_params=params(16),
        cost_estimate=FREE,
        name="pre",
    )(info, pick, tokens, shift, scale)


def mixer_kernel(info_ref, count_ref, pick_hbm, comb_hbm, gate_hbm, after_ref, mix_ref, row_ref, pick_ref, comb_ref, gate_ref, sems):
    fetch([(pick_hbm, pick_ref), (comb_hbm, comb_ref), (gate_hbm, gate_ref)], sems)
    experts, slots = pick_ref.shape
    tok_rows = mix_ref.shape[0]
    hot = slot_tokens(info_ref, pick_ref, tok_rows)
    lanes = lax.broadcasted_iota(jnp.int32, (1, slots), 1)
    weights = []
    for d in turns(experts):
        e = info_ref[1] ^ d
        weights.append(jnp.where(lanes < count_ref[0, e], comb_ref[pl.ds(e, 1), :], 0.0))
    mix = jnp.where(hot, jnp.concatenate(weights, axis=1), 0.0)
    high = mix.astype(BF16).astype(F32)
    rest = mix - high
    mid = rest.astype(BF16).astype(F32)
    mix_ref[...] = jnp.concatenate([high, mid, rest - mid], axis=1).astype(BF16)
    row_ref[...] = gate_ref[pl.ds(info_ref[0], 1), :]


def mixer(info, count, pick, comb, gate, after, tok_rows):
    experts, slots = pick.shape
    return pl.pallas_call(
        mixer_kernel,
        in_specs=[SMEM, SMEM] + [HBM] * 3 + [ANY],
        out_specs=[VMEM] * 2,
        out_shape=[
            jax.ShapeDtypeStruct((tok_rows, 3 * experts * slots), BF16),
            jax.ShapeDtypeStruct((1, gate.shape[1]), F32),
        ],
        scratch_shapes=[
            pltpu.VMEM(pick.shape, jnp.int32),
            pltpu.VMEM(comb.shape, F32),
            pltpu.VMEM(gate.shape, F32),
            pltpu.SemaphoreType.DMA((3,)),
        ],
        compiler_params=params(8),
        cost_estimate=FREE,
        name="mixer",
    )(info, count, pick, comb, gate, after)


def join_kernel(*refs, cuts):
    out_ref = refs[-1]
    at = 0
    for ref, cut in zip(refs, cuts):
        out_ref[at:at + ref.shape[0], :] = ref[...] if cut is None else ref[:, cut[0]:cut[1]]
        at += ref.shape[0]


def join(parts, after):
    arrays = [p[0] if isinstance(p, tuple) else p for p in parts]
    cuts = [p[1] if isinstance(p, tuple) else None for p in parts]
    step = min(a.shape[1] for a in arrays)
    return pl.pallas_call(
        functools.partial(join_kernel, cuts=cuts),
        in_specs=[VMEM] * len(arrays) + [ANY] * len(after),
        out_specs=VMEM,
        out_shape=jax.ShapeDtypeStruct((sum(a.shape[0] for a in arrays), step), BF16),
        compiler_params=params(4),
        cost_estimate=FREE,
        name="join",
    )(*arrays, *after)


def stream(w_hbm, out_ref, sems, chunk):
    rows, step = out_ref.shape
    pieces = sems.shape[0]
    part = rows // pieces
    return [
        pltpu.make_async_copy(
            w_hbm.at[pl.ds(p * part, part), pl.ds(chunk * step, step)],
            out_ref.at[pl.ds(p * part, part), :],
            sems.at[p],
        )
        for p in range(pieces)
    ]


def load_kernel(w_hbm, after_ref, out_ref, sems, *, chunk):
    copies = stream(w_hbm, out_ref, sems, chunk)
    for copy in copies:
        copy.start()
    for copy in copies:
        copy.wait()


def load(w, after, chunk, chunks):
    rows, width = w.shape
    step = width // chunks
    return pl.pallas_call(
        functools.partial(load_kernel, chunk=chunk),
        in_specs=[HBM, ANY],
        out_specs=VMEM,
        out_shape=pltpu.VMEM((rows, step), w.dtype),
        scratch_shapes=[pltpu.SemaphoreType.DMA((PIECES,))],
        compiler_params=params(2),
        cost_estimate=FREE,
        name="load",
    )(w, after)


def up_kernel(*refs, blocks, first, last, chunk):
    parts = refs[:blocks]
    w_ref, next_hbm = refs[blocks:blocks + 2]
    acc_ref = None if first else refs[blocks + 2]
    out_ref, next_ref, rows_ref, sems = refs[-4:]
    copies = stream(next_hbm, next_ref, sems, chunk)
    for copy in copies:
        copy.start()
    at = 0
    for part in parts:
        rows_ref[at:at + part.shape[0], :] = part[...]
        at += part.shape[0]
    hidden = w_ref.shape[0]
    tile = min(1024, hidden)

    for i in range(hidden // tile):
        cut = slice(i * tile, (i + 1) * tile)
        lifted = lax.dot_general(
            w_ref[cut, :], rows_ref[...], (((1,), (1,)), ((), ())), preferred_element_type=F32
        )
        if not first:
            lifted = lifted + acc_ref[cut, :]
        if last:
            out_ref[:, cut] = jax.nn.gelu(lifted, approximate=True).astype(BF16).T
        else:
            out_ref[cut, :] = lifted
    for copy in copies:
        copy.wait()


def up(parts, w, acc, last, following, chunk, chunks):
    hidden, step = w.shape
    rows = sum(p.shape[0] for p in parts)
    first = acc is None
    args = list(parts) + [w, following] + ([] if first else [acc])
    out = jax.ShapeDtypeStruct((rows, hidden), BF16) if last else jax.ShapeDtypeStruct((hidden, rows), F32)
    return pl.pallas_call(
        functools.partial(up_kernel, blocks=len(parts), first=first, last=last, chunk=chunk),
        in_specs=[VMEM] * len(parts) + [VMEM, HBM] + [VMEM] * (0 if first else 1),
        out_specs=[VMEM] * 2,
        out_shape=[out, pltpu.VMEM((following.shape[0], following.shape[1] // chunks), BF16)],
        scratch_shapes=[pltpu.VMEM((rows, step), BF16), pltpu.SemaphoreType.DMA((PIECES,))],
        compiler_params=params(12),
        cost_estimate=FREE,
        name="up",
    )(*args)


def down_kernel(h_ref, w_ref, *refs, chunk):
    if chunk is not None:
        next_hbm, keep_ref, send_ref, next_ref, sems = refs
        copies = stream(next_hbm, next_ref, sems, chunk)
    else:
        keep_ref, send_ref = refs
        copies = []
    for copy in copies:
        copy.start()
    half, step = keep_ref.shape
    tile = min(512, step)

    @pl.loop(0, step // tile)
    def _(i):
        cut = pl.ds(pl.multiple_of(i * tile, tile), tile)
        out = jnp.dot(h_ref[...], w_ref[:, cut], preferred_element_type=F32)
        keep_ref[:, cut] = out[:half]
        send_ref[:, cut] = out[half:].astype(BF16)

    for copy in copies:
        copy.wait()


def down(h, w, following, chunk):
    rows = h.shape[0]
    step = w.shape[1]
    half = rows // 2
    more = chunk is not None
    return pl.pallas_call(
        functools.partial(down_kernel, chunk=chunk),
        in_specs=[VMEM] * 2 + [HBM] * more,
        out_specs=[VMEM] * (2 + more),
        out_shape=[
            jax.ShapeDtypeStruct((half, step), F32),
            jax.ShapeDtypeStruct((half, step), BF16),
        ]
        + [pltpu.VMEM(w.shape, BF16)] * more,
        scratch_shapes=[pltpu.SemaphoreType.DMA((PIECES,))] * more,
        compiler_params=params(8),
        cost_estimate=FREE,
        name="down",
    )(*([h, w] + [following] * more))


def add_kernel(keep_ref, got_ref, *outs):
    at = 0
    for out in outs:
        cut = slice(at, at + out.shape[0])
        out[...] = (keep_ref[cut] + got_ref[cut].astype(F32)).astype(out.dtype)
        at += out.shape[0]


def add(keep, got, heights, kinds):
    width = keep.shape[1]
    return pl.pallas_call(
        add_kernel,
        in_specs=[VMEM] * 2,
        out_specs=[VMEM] * len(heights),
        out_shape=[jax.ShapeDtypeStruct((h, width), k) for h, k in zip(heights, kinds)],
        compiler_params=params(12),
        cost_estimate=FREE,
        name="add",
    )(keep, got)


def post_kernel(mix_ref, row_ref, *refs, experts):
    out_ref = refs[-1]
    values = jnp.concatenate([ref[...] for ref in refs[:experts]] * 3, axis=0)
    mixed = jnp.dot(mix_ref[...], values, preferred_element_type=F32)
    out_ref[...] = (row_ref[...] * mixed).astype(BF16)


def post(mix, row, parts, out, chunk, chunks):
    tok_rows = mix.shape[0]
    width = row.shape[1]
    step = width // chunks
    in_specs = [
        pl.BlockSpec(mix.shape, lambda i: (0, 0)),
        pl.BlockSpec((1, step), lambda i: (0, chunk)),
    ] + [pl.BlockSpec(p.shape, lambda i: (0, 0)) for p in parts]
    args = [mix, row] + list(parts)
    aliases = {}
    if out is not None:
        aliases = {len(args): 0}
        in_specs.append(ANY)
        args.append(out)
    return pl.pallas_call(
        functools.partial(post_kernel, experts=len(parts)),
        grid=(1,),
        in_specs=in_specs,
        out_specs=pl.BlockSpec((tok_rows, step), lambda i: (0, chunk)),
        out_shape=jax.ShapeDtypeStruct((tok_rows, width), BF16),
        input_output_aliases=aliases,
        compiler_params=params(12),
        cost_estimate=FREE,
        name="post",
    )(*args)


def shards(tokens, shift, scale, gate, w_up, w_down, pick, count, combine):
    tok_rows, width = tokens.shape
    _, experts, slots = pick.shape
    devices = lax.axis_size("expert")
    place = lax.axis_index("expert")
    group = devices // experts
    requests = shift.shape[0]
    chunks = CHUNKS
    step = width // chunks
    info = jnp.stack([place // (devices // requests), place // group]).astype(jnp.int32)
    pick = pick[0]
    comb = combine[0]

    far = [d * group for d in turns(experts)[1:]]
    near = []
    bit = group // 2
    while bit:
        near.append(bit)
        bit //= 2

    def swap(x, mask):
        return lax.ppermute(x, "expert", [(i, i ^ mask) for i in range(devices)])

    tokens, shift, scale, gate, w_up, w_down, pick, comb = [
        pltpu.with_memory_space_constraint(x, pltpu.HBM)
        for x in (tokens, shift, scale, gate, w_up, w_down, pick, comb)
    ]
    *flat, own = pre(info, pick, tokens, shift, scale, chunks)
    got = []
    for c in range(chunks):
        got.append([swap(flat[c * (experts - 1) + i], mask) for i, mask in enumerate(far)])
    own_near = swap(own, near[0])

    mix, row = mixer(info, count, pick, comb, gate, own, tok_rows)
    w = load(w_up, mix, 0, chunks)
    acc = None
    for c in range(chunks):
        cut = (c * step, (c + 1) * step)
        block = join(got[c], [own_near, w] if c == 0 else [])
        parts = [(own, cut), block, (own_near, cut), swap(block, near[0])]
        for mask in near[1:]:
            block = join(parts, [])
            parts = [block, swap(block, mask)]
        last = c == chunks - 1
        acc, w = up(parts, w, acc, last, w_down if last else w_up, 0 if last else c + 1, chunks)

    out = None
    for c in range(chunks):
        if c < chunks - 1:
            keep, send, w = down(acc, w, w_down, c + 1)
        else:
            keep, send = down(acc, w, None, None)
        for at, mask in enumerate(reversed(near)):
            arrived = swap(send, mask)
            height = keep.shape[0]
            if at < len(near) - 1:
                keep, send = add(keep, arrived, [height // 2] * 2, [F32, BF16])
            else:
                parts = add(keep, arrived, [slots] * experts, [BF16] * experts)
        parts = [parts[0]] + [swap(part, mask) for part, mask in zip(parts[1:], far)]
        out = post(mix, row, parts, out, c, chunks)
    return out


def solution(mesh):
    return jax.shard_map(
        shards,
        mesh=mesh,
        in_specs=(
            P(("groups", "expert"), None),
            P("groups", None),
            P("groups", None),
            P("groups", None),
            P("expert", None),
            P("expert", None),
            P(("groups", "expert"), None, None),
            P(("groups", "expert"), None),
            P(("groups", "expert"), None, None),
        ),
        out_specs=P(("groups", "expert"), None),
        check_vma=False,
    )
```

```python
import functools

import jax
import jax.numpy as jnp
from jax import lax
from jax.experimental import pallas as pl
from jax.experimental.pallas import tpu as pltpu
from jax.sharding import PartitionSpec as P

CHUNKS = 2
PIECES = 16
MIB = 1024 * 1024
F32 = jnp.float32
BF16 = jnp.bfloat16

SMEM = pl.BlockSpec(memory_space=pltpu.SMEM)
VMEM = pl.BlockSpec(memory_space=pltpu.VMEM)
HBM = pl.BlockSpec(memory_space=pltpu.HBM)
ANY = pl.BlockSpec(memory_space=pl.ANY)


FREE = pl.CostEstimate(flops=1, bytes_accessed=1, transcendentals=0)


def params(mib):
    return pltpu.CompilerParams(vmem_limit_bytes=mib * MIB)


def fetch(pairs, sems):
    copies = [pltpu.make_async_copy(src, dst, sems.at[i]) for i, (src, dst) in enumerate(pairs)]
    for copy in copies:
        copy.start()
    for copy in copies:
        copy.wait()


def turns(experts):
    return [0] + list(range(experts - 1, 0, -1))


def slot_tokens(info_ref, pick_ref, tok_rows):
    experts, slots = pick_ref.shape
    rows = [pick_ref[pl.ds(info_ref[1] ^ d, 1), :] for d in turns(experts)]
    picks = jnp.concatenate(rows, axis=1)
    return lax.broadcasted_iota(jnp.int32, (tok_rows, experts * slots), 0) == picks


def pre_kernel(info_ref, pick_hbm, tok_hbm, shift_hbm, scale_hbm, *refs, chunks):
    outs = refs[:-5]
    pick_ref, tok_ref, shift_ref, scale_ref, sems = refs[-5:]
    experts, slots = pick_ref.shape
    fetch(
        [(tok_hbm, tok_ref), (pick_hbm, pick_ref), (shift_hbm, shift_ref), (scale_hbm, scale_ref)],
        sems,
    )
    tok_rows, width = tok_ref.shape
    hot = slot_tokens(info_ref, pick_ref, tok_rows).astype(F32).astype(BF16)
    values = lax.dot_general(hot, tok_ref[...], (((0,), (0,)), ((), ())), preferred_element_type=F32)
    center = values - jnp.mean(values, axis=1, keepdims=True)
    spread = jnp.mean(center * center, axis=1, keepdims=True)
    normed = center * (1.0 / jnp.sqrt(spread + 1e-06))
    scale = scale_ref[pl.ds(info_ref[0], 1), :]
    shift = shift_ref[pl.ds(info_ref[0], 1), :]
    modulated = (normed * (1.0 + scale) + shift).astype(BF16)
    step = width // chunks
    outs[-1][...] = modulated[:slots]
    for c in range(chunks):
        for d in range(1, experts):
            outs[c * (experts - 1) + d - 1][...] = modulated[d * slots:(d + 1) * slots, c * step:(c + 1) * step]


def pre(info, pick, tokens, shift, scale, chunks):
    experts, slots = pick.shape
    width = tokens.shape[1]
    return pl.pallas_call(
        functools.partial(pre_kernel, chunks=chunks),
        in_specs=[SMEM] + [HBM] * 4,
        out_specs=[VMEM] * (chunks * (experts - 1) + 1),
        out_shape=[jax.ShapeDtypeStruct((slots, width // chunks), BF16)] * (chunks * (experts - 1))
        + [jax.ShapeDtypeStruct((slots, width), BF16)],
        scratch_shapes=[
            pltpu.VMEM(pick.shape, jnp.int32),
            pltpu.VMEM(tokens.shape, BF16),
            pltpu.VMEM(shift.shape, F32),
            pltpu.VMEM(scale.shape, F32),
            pltpu.SemaphoreType.DMA((4,)),
        ],
        compiler_params=params(16),
        cost_estimate=FREE,
        name="pre",
    )(info, pick, tokens, shift, scale)


def mixer_kernel(info_ref, count_ref, pick_hbm, comb_hbm, gate_hbm, after_ref, mix_ref, row_ref, pick_ref, comb_ref, gate_ref, sems):
    fetch([(pick_hbm, pick_ref), (comb_hbm, comb_ref), (gate_hbm, gate_ref)], sems)
    experts, slots = pick_ref.shape
    tok_rows = mix_ref.shape[0]
    hot = slot_tokens(info_ref, pick_ref, tok_rows)
    lanes = lax.broadcasted_iota(jnp.int32, (1, slots), 1)
    weights = []
    for d in turns(experts):
        e = info_ref[1] ^ d
        weights.append(jnp.where(lanes < count_ref[0, e], comb_ref[pl.ds(e, 1), :], 0.0))
    mix = jnp.where(hot, jnp.concatenate(weights, axis=1), 0.0)
    high = mix.astype(BF16).astype(F32)
    rest = mix - high
    mid = rest.astype(BF16).astype(F32)
    mix_ref[...] = jnp.concatenate([high, mid, rest - mid], axis=1).astype(BF16)
    row_ref[...] = gate_ref[pl.ds(info_ref[0], 1), :]


def mixer(info, count, pick, comb, gate, after, tok_rows):
    experts, slots = pick.shape
    return pl.pallas_call(
        mixer_kernel,
        in_specs=[SMEM, SMEM] + [HBM] * 3 + [ANY],
        out_specs=[VMEM] * 2,
        out_shape=[
            jax.ShapeDtypeStruct((tok_rows, 3 * experts * slots), BF16),
            jax.ShapeDtypeStruct((1, gate.shape[1]), F32),
        ],
        scratch_shapes=[
            pltpu.VMEM(pick.shape, jnp.int32),
            pltpu.VMEM(comb.shape, F32),
            pltpu.VMEM(gate.shape, F32),
            pltpu.SemaphoreType.DMA((3,)),
        ],
        compiler_params=params(8),
        cost_estimate=FREE,
        name="mixer",
    )(info, count, pick, comb, gate, after)


def join_kernel(*refs, cuts):
    out_ref = refs[-1]
    at = 0
    for ref, cut in zip(refs, cuts):
        out_ref[at:at + ref.shape[0], :] = ref[...] if cut is None else ref[:, cut[0]:cut[1]]
        at += ref.shape[0]


def join(parts, after):
    arrays = [p[0] if isinstance(p, tuple) else p for p in parts]
    cuts = [p[1] if isinstance(p, tuple) else None for p in parts]
    step = min(a.shape[1] for a in arrays)
    return pl.pallas_call(
        functools.partial(join_kernel, cuts=cuts),
        in_specs=[VMEM] * len(arrays) + [ANY] * len(after),
        out_specs=VMEM,
        out_shape=jax.ShapeDtypeStruct((sum(a.shape[0] for a in arrays), step), BF16),
        compiler_params=params(4),
        cost_estimate=FREE,
        name="join",
    )(*arrays, *after)


def stream(w_hbm, out_ref, sems, chunk):
    rows, step = out_ref.shape
    pieces = sems.shape[0]
    part = rows // pieces
    return [
        pltpu.make_async_copy(
            w_hbm.at[pl.ds(p * part, part), pl.ds(chunk * step, step)],
            out_ref.at[pl.ds(p * part, part), :],
            sems.at[p],
        )
        for p in range(pieces)
    ]


def load_kernel(w_hbm, after_ref, out_ref, sems, *, chunk):
    copies = stream(w_hbm, out_ref, sems, chunk)
    for copy in copies:
        copy.start()
    for copy in copies:
        copy.wait()


def load(w, after, chunk, chunks):
    rows, width = w.shape
    step = width // chunks
    return pl.pallas_call(
        functools.partial(load_kernel, chunk=chunk),
        in_specs=[HBM, ANY],
        out_specs=VMEM,
        out_shape=pltpu.VMEM((rows, step), w.dtype),
        scratch_shapes=[pltpu.SemaphoreType.DMA((PIECES,))],
        compiler_params=params(2),
        cost_estimate=FREE,
        name="load",
    )(w, after)


def up_kernel(*refs, blocks, first, last, chunk):
    parts = refs[:blocks]
    w_ref, next_hbm, after_ref = refs[blocks:blocks + 3]
    acc_ref = None if first else refs[blocks + 3]
    out_ref, next_ref, rows_ref, sems = refs[-4:]
    copies = stream(next_hbm, next_ref, sems, chunk)
    for copy in copies:
        copy.start()
    at = 0
    for part in parts:
        rows_ref[at:at + part.shape[0], :] = part[...]
        at += part.shape[0]
    hidden = w_ref.shape[0]
    tile = min(2048, hidden)

    for i in range(hidden // tile):
        cut = slice(i * tile, (i + 1) * tile)
        lifted = lax.dot_general(
            w_ref[cut, :], rows_ref[...], (((1,), (1,)), ((), ())), preferred_element_type=F32
        )
        if not first:
            lifted = lifted + acc_ref[cut, :]
        if last:
            out_ref[:, cut] = jax.nn.gelu(lifted, approximate=True).astype(BF16).T
        else:
            out_ref[cut, :] = lifted
    for copy in copies:
        copy.wait()


def up(parts, w, acc, last, after, following, chunk, chunks):
    hidden, step = w.shape
    rows = sum(p.shape[0] for p in parts)
    first = acc is None
    args = list(parts) + [w, following, after] + ([] if first else [acc])
    out = jax.ShapeDtypeStruct((rows, hidden), BF16) if last else jax.ShapeDtypeStruct((hidden, rows), F32)
    return pl.pallas_call(
        functools.partial(up_kernel, blocks=len(parts), first=first, last=last, chunk=chunk),
        in_specs=[VMEM] * len(parts) + [VMEM, HBM, ANY] + [VMEM] * (0 if first else 1),
        out_specs=[VMEM] * 2,
        out_shape=[out, pltpu.VMEM((following.shape[0], following.shape[1] // chunks), BF16)],
        scratch_shapes=[pltpu.VMEM((rows, step), BF16), pltpu.SemaphoreType.DMA((PIECES,))],
        compiler_params=params(12),
        cost_estimate=FREE,
        name="up",
    )(*args)


def down_kernel(h_ref, w_ref, after_ref, *refs, chunk):
    if chunk is not None:
        next_hbm, keep_ref, send_ref, next_ref, sems = refs
        copies = stream(next_hbm, next_ref, sems, chunk)
    else:
        keep_ref, send_ref = refs
        copies = []
    for copy in copies:
        copy.start()
    half, step = keep_ref.shape
    tile = min(1024, step)
    for i in range(step // tile):
        cut = slice(i * tile, (i + 1) * tile)
        out = jnp.dot(h_ref[...], w_ref[:, cut], preferred_element_type=F32)
        keep_ref[:, cut] = out[:half]
        send_ref[:, cut] = out[half:].astype(BF16)

    for copy in copies:
        copy.wait()


def down(h, w, after, following, chunk):
    rows = h.shape[0]
    step = w.shape[1]
    half = rows // 2
    more = chunk is not None
    return pl.pallas_call(
        functools.partial(down_kernel, chunk=chunk),
        in_specs=[VMEM] * 2 + [ANY] + [HBM] * more,
        out_specs=[VMEM] * (2 + more),
        out_shape=[
            jax.ShapeDtypeStruct((half, step), F32),
            jax.ShapeDtypeStruct((half, step), BF16),
        ]
        + [pltpu.VMEM(w.shape, BF16)] * more,
        scratch_shapes=[pltpu.SemaphoreType.DMA((PIECES,))] * more,
        compiler_params=params(8),
        cost_estimate=FREE,
        name="down",
    )(*([h, w, after] + [following] * more))


def add_kernel(keep_ref, got_ref, *refs, cuts):
    width = keep_ref.shape[1]
    for ref, (low, high) in zip(refs[-len(cuts):], cuts):
        start = ref.shape[1] - width
        if start:
            ref[:, :start] = refs[0][...]
        total = keep_ref[low:high] + got_ref[low:high].astype(F32)
        ref[:, start:] = total.astype(ref.dtype)


def add(keep, got, cuts, kinds, before=None):
    width = keep.shape[1]
    shapes = [[high - low, width] for low, high in cuts]
    args = [keep, got]
    if before is not None:
        shapes[-1][1] += before.shape[1]
        args.append(before)
    return pl.pallas_call(
        functools.partial(add_kernel, cuts=cuts),
        in_specs=[VMEM] * len(args),
        out_specs=[VMEM] * len(cuts),
        out_shape=[jax.ShapeDtypeStruct(shape, k) for shape, k in zip(shapes, kinds)],
        compiler_params=params(12),
        cost_estimate=FREE,
        name="add",
    )(*args)


def post_kernel(mix_ref, row_ref, keep_ref, near_ref, *refs, experts):
    out_ref = refs[-1]
    own = (keep_ref[...] + near_ref[...].astype(F32)).astype(BF16)
    values = jnp.concatenate([own] + [ref[...] for ref in refs[:experts - 1]], axis=0)
    values = jnp.concatenate([values] * 3, axis=0)
    mixed = jnp.dot(mix_ref[...], values, preferred_element_type=F32)
    out_ref[...] = (row_ref[...] * mixed).astype(BF16)


def post(mix, row, keep, own, parts, out, chunk, chunks):
    tok_rows = mix.shape[0]
    width = row.shape[1]
    step = width // chunks
    in_specs = [
        pl.BlockSpec(mix.shape, lambda i: (0, 0)),
        pl.BlockSpec((1, step), lambda i: (0, chunk)),
        pl.BlockSpec((own.shape[0], step), lambda i: (0, 0)),
        pl.BlockSpec((own.shape[0], step), lambda i: (0, chunk)),
    ] + [pl.BlockSpec(p.shape, lambda i: (0, 0)) for p in parts]
    args = [mix, row, keep, own] + list(parts)
    aliases = {}
    if out is not None:
        aliases = {len(args): 0}
        in_specs.append(ANY)
        args.append(out)
    return pl.pallas_call(
        functools.partial(post_kernel, experts=len(parts) + 1),
        grid=(1,),
        in_specs=in_specs,
        out_specs=pl.BlockSpec((tok_rows, step), lambda i: (0, chunk)),
        out_shape=jax.ShapeDtypeStruct((tok_rows, width), BF16),
        input_output_aliases=aliases,
        compiler_params=params(12),
        cost_estimate=FREE,
        name="post",
    )(*args)


def shards(tokens, shift, scale, gate, w_up, w_down, pick, count, combine):
    tok_rows, width = tokens.shape
    _, experts, slots = pick.shape
    devices = lax.axis_size("expert")
    place = lax.axis_index("expert")
    group = devices // experts
    requests = shift.shape[0]
    chunks = CHUNKS
    step = width // chunks
    info = jnp.stack([place // (devices // requests), place // group]).astype(jnp.int32)
    pick = pick[0]
    comb = combine[0]

    far = [d * group for d in turns(experts)[1:]]
    near = []
    bit = group // 2
    while bit:
        near.append(bit)
        bit //= 2

    def swap(x, mask):
        return lax.ppermute(x, "expert", [(i, i ^ mask) for i in range(devices)])

    tokens, shift, scale, gate, w_up, w_down, pick, comb = [
        pltpu.with_memory_space_constraint(x, pltpu.HBM)
        for x in (tokens, shift, scale, gate, w_up, w_down, pick, comb)
    ]
    *flat, own = pre(info, pick, tokens, shift, scale, chunks)
    got = []
    for c in range(chunks):
        got.append([swap(flat[c * (experts - 1) + i], mask) for i, mask in enumerate(far)])
    own_near = swap(own, near[0])

    blocks = []
    w = None
    for c in range(chunks):
        blocks.append(join(got[c], [own_near] if c == 0 else [w]))
        if c == 0:
            w = load(w_up, blocks[0], 0, chunks)
    acc = None
    mix = None
    for c in range(chunks):
        cut = (c * step, (c + 1) * step)
        parts = [(own, cut), blocks[c], (own_near, cut), swap(blocks[c], near[0])]
        for mask in near[1:]:
            block = join(parts, [] if c == 0 else [acc])
            parts = [block, swap(block, mask)]
        if c == 0:
            mix, row = mixer(info, count, pick, comb, gate, parts[0], tok_rows)
        last = c == chunks - 1
        acc, w = up(parts, w, acc, last, mix, w_down if last else w_up, 0 if last else c + 1, chunks)

    halves = []
    after = mix
    before = None
    for c in range(chunks):
        if c < chunks - 1:
            keep, send, w = down(acc, w, after, w_down, c + 1)
        else:
            keep, send = down(acc, w, after, None, None)
        for mask in reversed(near[1:]):
            arrived = swap(send, mask)
            height = keep.shape[0] // 2
            if height > experts * slots:
                keep, send = add(keep, arrived, [(0, height), (height, 2 * height)], [F32, BF16])
            else:
                keep, send, before = add(
                    keep,
                    arrived,
                    [(0, height), (height + slots, 2 * height), (height, height + slots)],
                    [F32, BF16, BF16],
                    before,
                )
        halves.append((keep, send))
    own_near = swap(before, near[0])
    out = None
    for c, (keep, send) in enumerate(halves):
        arrived = swap(send, near[0])
        cuts = [(i * slots, (i + 1) * slots) for i in range(experts - 1)]
        parts = add(keep[slots:], arrived, cuts, [BF16] * (experts - 1))
        parts = [swap(part, mask) for part, mask in zip(parts, far)]
        out = post(mix, row, keep, own_near, parts, out, c, chunks)
    return out


def solution(mesh):
    return jax.shard_map(
        shards,
        mesh=mesh,
        in_specs=(
            P(("groups", "expert"), None),
            P("groups", None),
            P("groups", None),
            P("groups", None),
            P("expert", None),
            P("expert", None),
            P(("groups", "expert"), None, None),
            P(("groups", "expert"), None),
            P(("groups", "expert"), None, None),
        ),
        out_specs=P(("groups", "expert"), None),
        check_vma=False,
    )
```

```python
import functools

import jax
import jax.numpy as jnp
from jax import lax
from jax.experimental import pallas as pl
from jax.experimental.pallas import tpu as pltpu
from jax.sharding import PartitionSpec as P

PIECES = 8
MIB = 1024 * 1024
F32 = jnp.float32
BF16 = jnp.bfloat16

SMEM = pl.BlockSpec(memory_space=pltpu.SMEM)
VMEM = pl.BlockSpec(memory_space=pltpu.VMEM)
HBM = pl.BlockSpec(memory_space=pltpu.HBM)
ANY = pl.BlockSpec(memory_space=pl.ANY)


FREE = pl.CostEstimate(flops=1, bytes_accessed=1, transcendentals=0)


def params(mib):
    return pltpu.CompilerParams(vmem_limit_bytes=mib * MIB)


def fetch(pairs, sems):
    copies = [pltpu.make_async_copy(src, dst, sems.at[i]) for i, (src, dst) in enumerate(pairs)]
    for copy in copies:
        copy.start()
    for copy in copies:
        copy.wait()


def turns(experts):
    return [0] + list(range(experts - 1, 0, -1))


def slot_tokens(info_ref, pick_ref, tok_rows):
    experts, slots = pick_ref.shape
    rows = [pick_ref[pl.ds(info_ref[1] ^ d, 1), :] for d in turns(experts)]
    picks = jnp.concatenate(rows, axis=1)
    return lax.broadcasted_iota(jnp.int32, (tok_rows, experts * slots), 0) == picks


def pre_kernel(info_ref, pick_hbm, tok_hbm, shift_hbm, scale_hbm, *refs):
    outs = refs[:-5]
    pick_ref, tok_ref, shift_ref, scale_ref, sems = refs[-5:]
    slots = pick_ref.shape[1]
    fetch(
        [(tok_hbm, tok_ref), (pick_hbm, pick_ref), (shift_hbm, shift_ref), (scale_hbm, scale_ref)],
        sems,
    )
    hot = slot_tokens(info_ref, pick_ref, tok_ref.shape[0]).astype(F32).astype(BF16)
    values = lax.dot_general(hot, tok_ref[...], (((0,), (0,)), ((), ())), preferred_element_type=F32)
    center = values - jnp.mean(values, axis=1, keepdims=True)
    spread = jnp.mean(center * center, axis=1, keepdims=True)
    normed = center * (1.0 / jnp.sqrt(spread + 1e-06))
    scale = scale_ref[pl.ds(info_ref[0], 1), :]
    shift = shift_ref[pl.ds(info_ref[0], 1), :]
    modulated = (normed * (1.0 + scale) + shift).astype(BF16)
    for i, out in enumerate(outs):
        out[...] = modulated[i * slots:(i + 1) * slots]


def pre(info, pick, tokens, shift, scale):
    experts, slots = pick.shape
    width = tokens.shape[1]
    return pl.pallas_call(
        pre_kernel,
        in_specs=[SMEM] + [HBM] * 4,
        out_specs=[VMEM] * experts,
        out_shape=[jax.ShapeDtypeStruct((slots, width), BF16)] * experts,
        scratch_shapes=[
            pltpu.VMEM(pick.shape, jnp.int32),
            pltpu.VMEM(tokens.shape, BF16),
            pltpu.VMEM(shift.shape, F32),
            pltpu.VMEM(scale.shape, F32),
            pltpu.SemaphoreType.DMA((4,)),
        ],
        compiler_params=params(12),
        cost_estimate=FREE,
        name="pre",
    )(info, pick, tokens, shift, scale)


def mixer_kernel(info_ref, count_ref, pick_hbm, comb_hbm, gate_hbm, after_ref, mix_ref, row_ref, pick_ref, comb_ref, gate_ref, sems):
    fetch([(pick_hbm, pick_ref), (comb_hbm, comb_ref), (gate_hbm, gate_ref)], sems)
    experts, slots = pick_ref.shape
    tok_rows = mix_ref.shape[0]
    hot = slot_tokens(info_ref, pick_ref, tok_rows)
    lanes = lax.broadcasted_iota(jnp.int32, (1, slots), 1)
    weights = []
    for d in turns(experts):
        e = info_ref[1] ^ d
        weights.append(jnp.where(lanes < count_ref[0, e], comb_ref[pl.ds(e, 1), :], 0.0))
    mix = jnp.where(hot, jnp.concatenate(weights, axis=1), 0.0)
    high = mix.astype(BF16).astype(F32)
    rest = mix - high
    mid = rest.astype(BF16).astype(F32)
    mix_ref[...] = jnp.concatenate([high, mid, rest - mid], axis=1).astype(BF16)
    row_ref[...] = gate_ref[pl.ds(info_ref[0], 1), :]


def mixer(info, count, pick, comb, gate, after, tok_rows):
    experts, slots = pick.shape
    return pl.pallas_call(
        mixer_kernel,
        in_specs=[SMEM, SMEM] + [HBM] * 3 + [ANY],
        out_specs=[VMEM] * 2,
        out_shape=[
            jax.ShapeDtypeStruct((tok_rows, 3 * experts * slots), BF16),
            jax.ShapeDtypeStruct((1, gate.shape[1]), F32),
        ],
        scratch_shapes=[
            pltpu.VMEM(pick.shape, jnp.int32),
            pltpu.VMEM(comb.shape, F32),
            pltpu.VMEM(gate.shape, F32),
            pltpu.SemaphoreType.DMA((3,)),
        ],
        compiler_params=params(8),
        cost_estimate=FREE,
        name="mixer",
    )(info, count, pick, comb, gate, after)


def join_kernel(*refs, cuts):
    out_ref = refs[-1]
    at = 0
    for ref, cut in zip(refs, cuts):
        out_ref[at:at + ref.shape[0], :] = ref[...] if cut is None else ref[:, cut[0]:cut[1]]
        at += ref.shape[0]


def join(parts, after):
    arrays = [p[0] if isinstance(p, tuple) else p for p in parts]
    cuts = [p[1] if isinstance(p, tuple) else None for p in parts]
    step = min(a.shape[1] for a in arrays)
    return pl.pallas_call(
        functools.partial(join_kernel, cuts=cuts),
        in_specs=[VMEM] * len(arrays) + [ANY] * len(after),
        out_specs=VMEM,
        out_shape=jax.ShapeDtypeStruct((sum(a.shape[0] for a in arrays), step), BF16),
        compiler_params=params(4),
        cost_estimate=FREE,
        name="join",
    )(*arrays, *after)


def stream(w_hbm, out_ref, sems, at):
    rows, columns = out_ref.shape
    pieces = sems.shape[0]
    part = rows // pieces
    return [
        pltpu.make_async_copy(
            w_hbm.at[pl.ds(at[0] + p * part, part), pl.ds(at[1], columns)],
            out_ref.at[pl.ds(p * part, part), :],
            sems.at[p],
        )
        for p in range(pieces)
    ]


def load_kernel(w_hbm, *refs, at):
    out_ref, sems = refs[-2:]
    copies = stream(w_hbm, out_ref, sems, at)
    for copy in copies:
        copy.start()
    for copy in copies:
        copy.wait()


def load(w, at, shape, after):
    return pl.pallas_call(
        functools.partial(load_kernel, at=at),
        in_specs=[HBM] + [ANY] * len(after),
        out_specs=VMEM,
        out_shape=pltpu.VMEM(shape, w.dtype),
        scratch_shapes=[pltpu.SemaphoreType.DMA((PIECES,))],
        compiler_params=params(2),
        cost_estimate=FREE,
        name="load",
    )(w, *after)


def join_kernel(*refs, count):
    out_ref = refs[-1]
    at = 0
    for ref in refs[:count]:
        out_ref[at:at + ref.shape[0], :] = ref[...]
        at += ref.shape[0]


def join(parts, after):
    return pl.pallas_call(
        functools.partial(join_kernel, count=len(parts)),
        in_specs=[VMEM] * len(parts) + [ANY] * len(after),
        out_specs=VMEM,
        out_shape=jax.ShapeDtypeStruct((sum(p.shape[0] for p in parts), parts[0].shape[1]), BF16),
        compiler_params=params(2),
        cost_estimate=FREE,
        name="join",
    )(*parts, *after)


def up_kernel(*refs, sources, count, at):
    w_ref, next_hbm = refs[count:count + 2]
    if sources is None:
        rows_ref = refs[0]
        out_ref, next_ref, sems = refs[-3:]
    else:
        out_ref, next_ref, rows_ref, sems = refs[-4:]
    copies = stream(next_hbm, next_ref, sems, at)
    for copy in copies:
        copy.start()
    if sources is not None:
        to = 0
        for source, low, high in sources:
            rows_ref[to:to + high - low, :] = refs[source][low:high, :]
            to += high - low
    hidden = w_ref.shape[0]
    tile = min(512, hidden)

    @pl.loop(0, hidden // tile)
    def _(i):
        cut = pl.ds(pl.multiple_of(i * tile, tile), tile)
        lifted = lax.dot_general(
            rows_ref[...], w_ref[cut, :], (((1,), (1,)), ((), ())), preferred_element_type=F32
        )
        out_ref[:, cut] = jax.nn.gelu(lifted, approximate=True).astype(BF16)

    for copy in copies:
        copy.wait()


def up(parts, sources, w, following, at, shape):
    hidden, width = w.shape
    rows = parts[0].shape[0] if sources is None else sum(high - low for _, low, high in sources)
    out_shape = [jax.ShapeDtypeStruct((rows, hidden), BF16), pltpu.VMEM(shape, BF16)]
    if sources is not None:
        out_shape.append(jax.ShapeDtypeStruct((rows, width), BF16))
    return pl.pallas_call(
        functools.partial(up_kernel, sources=sources, count=len(parts), at=at),
        in_specs=[VMEM] * len(parts) + [VMEM, HBM],
        out_specs=[VMEM] * len(out_shape),
        out_shape=out_shape,
        scratch_shapes=[pltpu.SemaphoreType.DMA((PIECES,))],
        compiler_params=params(12),
        cost_estimate=FREE,
        name="up",
    )(*parts, w, following)


def down_kernel(*refs, count):
    w_ref, keep_ref, send_ref = refs[count:]
    half, step = keep_ref.shape
    tile = min(1024, step)

    @pl.loop(0, step // tile)
    def _(i):
        cut = pl.ds(pl.multiple_of(i * tile, tile), tile)
        at = 0
        out = None
        for h_ref in refs[:count]:
            part = jnp.dot(
                h_ref[...], w_ref[at:at + h_ref.shape[1], cut], preferred_element_type=F32
            )
            out = part if out is None else out + part
            at += h_ref.shape[1]
        keep_ref[:, cut] = out[:half]
        send_ref[:, cut] = out[half:].astype(BF16)


def down(hiddens, w):
    half = hiddens[0].shape[0] // 2
    step = w.shape[1]
    return pl.pallas_call(
        functools.partial(down_kernel, count=len(hiddens)),
        in_specs=[VMEM] * (len(hiddens) + 1),
        out_specs=[VMEM] * 2,
        out_shape=[
            jax.ShapeDtypeStruct((half, step), F32),
            jax.ShapeDtypeStruct((half, step), BF16),
        ],
        compiler_params=params(12),
        cost_estimate=FREE,
        name="down",
    )(*hiddens, w)


def add_kernel(*refs, count, cuts):
    at = 0
    for i in range(count):
        keep_ref, got_ref = refs[2 * i:2 * i + 2]
        step = keep_ref.shape[1]
        for ref, (low, high) in zip(refs[2 * count:], cuts):
            total = keep_ref[low:high] + got_ref[low:high].astype(F32)
            ref[:, at:at + step] = total.astype(ref.dtype)
        at += step


def add(pairs, cuts, kinds):
    width = sum(keep.shape[1] for keep, _ in pairs)
    args = [x for pair in pairs for x in pair]
    return pl.pallas_call(
        functools.partial(add_kernel, count=len(pairs), cuts=cuts),
        in_specs=[VMEM] * len(args),
        out_specs=[VMEM] * len(cuts),
        out_shape=[jax.ShapeDtypeStruct((high - low, width), k) for (low, high), k in zip(cuts, kinds)],
        compiler_params=params(8),
        cost_estimate=FREE,
        name="add",
    )(*args)


def post_kernel(mix_ref, row_ref, keep_ref, near_ref, *refs):
    out_ref = refs[-1]
    step = out_ref.shape[1]
    cut = pl.ds(pl.multiple_of(pl.program_id(0) * step, step), step)
    own = (keep_ref[:, cut] + near_ref[:, cut].astype(F32)).astype(BF16)
    values = jnp.concatenate([own] + [ref[:, cut] for ref in refs[:-1]], axis=0)
    values = jnp.concatenate([values] * 3, axis=0)
    mixed = jnp.dot(mix_ref[...], values, preferred_element_type=F32)
    out_ref[...] = (row_ref[:, cut] * mixed).astype(BF16)


def post(mix, row, keep, near, parts):
    tok_rows = mix.shape[0]
    width = row.shape[1]
    step = min(1024, width)
    return pl.pallas_call(
        post_kernel,
        grid=(width // step,),
        in_specs=[VMEM] * (4 + len(parts)),
        out_specs=pl.BlockSpec((tok_rows, step), lambda i: (0, i)),
        out_shape=jax.ShapeDtypeStruct((tok_rows, width), BF16),
        compiler_params=params(8),
        cost_estimate=FREE,
        name="post",
    )(mix, row, keep, near, *parts)


def shards(tokens, shift, scale, gate, w_up, w_down, pick, count, combine):
    tok_rows, width = tokens.shape
    _, experts, slots = pick.shape
    devices = lax.axis_size("expert")
    place = lax.axis_index("expert")
    group = devices // experts
    requests = shift.shape[0]
    hidden = w_up.shape[0]
    info = jnp.stack([place // (devices // requests), place // group]).astype(jnp.int32)
    pick = pick[0]
    comb = combine[0]

    far = [d * group for d in turns(experts)[1:]]
    near = []
    bit = group // 2
    while bit:
        near.append(bit)
        bit //= 2

    def swap(x, mask):
        return lax.ppermute(x, "expert", [(i, i ^ mask) for i in range(devices)])

    tokens, shift, scale, gate, w_up, w_down, pick, comb = [
        pltpu.with_memory_space_constraint(x, pltpu.HBM)
        for x in (tokens, shift, scale, gate, w_up, w_down, pick, comb)
    ]
    own, *flat = pre(info, pick, tokens, shift, scale)
    mix, row = mixer(info, count, pick, comb, gate, own, tok_rows)

    blocks = [own] + [swap(x, mask) for x, mask in zip(flat, far)]
    beside = [swap(block, near[0]) for block in blocks]
    block_up = (hidden // 2, width)
    ups = [load(w_up, (0, 0), block_up, [blocks[-1], mix])]
    ups.append(load(w_up, (hidden // 2, 0), block_up, [blocks[1], ups[0]]))
    early, late = [0, experts - 1], list(range(1, experts - 1))
    parts = []
    sources = []
    for members, after in ((early, []), (late, ups[1:])):
        pieces = [join([x for i in members for x in (blocks[i], beside[i])], after)]
        height = pieces[0].shape[0]
        for mask in near[1:]:
            block = pieces[0] if len(pieces) == 1 else join(pieces, [])
            pieces = [block, swap(block, mask)]
        cuts = []
        for piece in pieces:
            cuts += [(len(parts), at, at + height) for at in range(0, piece.shape[0], height)]
            parts.append(piece)
        sources.append(cuts)
    sources = [cut for pair in zip(*sources) for cut in pair]

    step = width // 2
    hid, down_a, rows = up(parts, sources, ups[0], w_down, (0, 0), (hidden, step))
    hid_b, down_b = up([rows], None, ups[1], w_down, (0, step), (hidden, step))

    pairs = []
    for w in (down_a, down_b):
        keep, send = down([hid, hid_b], w)
        for i, mask in enumerate(reversed(near[1:])):
            if i:
                half = keep.shape[0] // 2
                keep, send = add([(keep, got)], [(0, half), (half, 2 * half)], [F32, BF16])
            got = swap(send, mask)
        pairs.append((keep, got))
    places = {}
    for at, i in enumerate(early + late):
        places[i] = (2 * at * slots, (2 * at + 1) * slots)
    order = list(range(1, experts)) + [0]
    keeps = [places[i] for i in order]
    sends = [(high, high + slots) for _, high in keeps]
    summed = add(pairs, sends + keeps, [BF16] * experts + [F32] * experts)
    sends, keeps = summed[:experts], summed[experts:]
    arrived = [swap(send, near[0]) for send in sends]
    back = []
    for i, mask in enumerate(far):
        (part,) = add([(keeps[i], arrived[i])], [(0, slots)], [BF16])
        back.append(swap(part, mask))
    return post(mix, row, keeps[-1], arrived[-1], back)


def solution(mesh):
    return jax.shard_map(
        shards,
        mesh=mesh,
        in_specs=(
            P(("groups", "expert"), None),
            P("groups", None),
            P("groups", None),
            P("groups", None),
            P("expert", None),
            P("expert", None),
            P(("groups", "expert"), None, None),
            P(("groups", "expert"), None),
            P(("groups", "expert"), None, None),
        ),
        out_specs=P(("groups", "expert"), None),
        check_vma=False,
    )
```

```python
import functools

import jax
import jax.numpy as jnp
from jax import lax
from jax.experimental import pallas as pl
from jax.experimental.pallas import tpu as pltpu
from jax.sharding import PartitionSpec as P

PIECES = 8
MIB = 1024 * 1024
F32 = jnp.float32
BF16 = jnp.bfloat16

SMEM = pl.BlockSpec(memory_space=pltpu.SMEM)
VMEM = pl.BlockSpec(memory_space=pltpu.VMEM)
HBM = pl.BlockSpec(memory_space=pltpu.HBM)
ANY = pl.BlockSpec(memory_space=pl.ANY)


FREE = pl.CostEstimate(flops=1, bytes_accessed=1, transcendentals=0)


def params(mib):
    return pltpu.CompilerParams(vmem_limit_bytes=mib * MIB)


def fetch(pairs, sems):
    copies = [pltpu.make_async_copy(src, dst, sems.at[i]) for i, (src, dst) in enumerate(pairs)]
    for copy in copies:
        copy.start()
    for copy in copies:
        copy.wait()


def turns(experts):
    return [0] + list(range(experts - 1, 0, -1))


def hot_rows(picks, tok_rows):
    return lax.broadcasted_iota(jnp.int32, (tok_rows, picks.shape[1]), 0) == picks


def modulate(picks, tok_ref, table_ref):
    hot = hot_rows(picks, tok_ref.shape[0]).astype(F32).astype(BF16)
    values = lax.dot_general(hot, tok_ref[...], (((0,), (0,)), ((), ())), preferred_element_type=F32)
    center = values - jnp.mean(values, axis=1, keepdims=True)
    spread = jnp.mean(center * center, axis=1, keepdims=True)
    normed = center * (1.0 / jnp.sqrt(spread + 1e-06))
    return (normed * table_ref[0:1, :] + table_ref[1:2, :]).astype(BF16)


def first_kernel(info_ref, *refs):
    sources = refs[:7]
    far_ref, tok_ref, table_ref, picks_ref, weights_ref = refs[7:12]
    pick_ref, comb_ref, count_ref, shift_ref, scale_ref, gate_ref, sems = refs[12:]
    fetch(
        list(zip(sources, (tok_ref, pick_ref, shift_ref, scale_ref, gate_ref, comb_ref, count_ref))),
        sems,
    )
    experts, slots = pick_ref.shape
    which = pl.ds(info_ref[0], 1)
    table_ref[0:1, :] = 1.0 + scale_ref[which, :]
    table_ref[1:2, :] = shift_ref[which, :]
    table_ref[2:3, :] = gate_ref[which, :]
    lanes = lax.broadcasted_iota(jnp.int32, (1, slots), 1)
    for i, d in enumerate(turns(experts)):
        e = info_ref[1] ^ d
        picks_ref[i:i + 1, :] = pick_ref[pl.ds(e, 1), :]
        weights_ref[i:i + 1, :] = jnp.where(lanes < count_ref[0, e], comb_ref[pl.ds(e, 1), :], 0.0)
    far_ref[...] = modulate(picks_ref[1:2, :], tok_ref, table_ref)


def first(info, tokens, pick, shift, scale, gate, comb, count):
    experts, slots = pick.shape
    width = tokens.shape[1]
    return pl.pallas_call(
        first_kernel,
        in_specs=[SMEM] + [HBM] * 7,
        out_specs=[VMEM] * 5,
        out_shape=[
            jax.ShapeDtypeStruct((slots, width), BF16),
            jax.ShapeDtypeStruct(tokens.shape, BF16),
            jax.ShapeDtypeStruct((3, width), F32),
            jax.ShapeDtypeStruct(pick.shape, jnp.int32),
            jax.ShapeDtypeStruct(comb.shape, F32),
        ],
        scratch_shapes=[
            pltpu.VMEM(pick.shape, jnp.int32),
            pltpu.VMEM(comb.shape, F32),
            pltpu.SMEM(count.shape, jnp.int32),
            pltpu.VMEM(shift.shape, F32),
            pltpu.VMEM(scale.shape, F32),
            pltpu.VMEM(gate.shape, F32),
            pltpu.SemaphoreType.DMA((7,)),
        ],
        compiler_params=params(8),
        cost_estimate=FREE,
        name="first",
    )(info, tokens, pick, shift, scale, gate, comb, count)


def rest_kernel(tok_ref, table_ref, picks_ref, *outs):
    experts, slots = picks_ref.shape
    order = [0] + list(range(2, experts))
    picks = jnp.concatenate([picks_ref[i:i + 1, :] for i in order], axis=1)
    rows = modulate(picks, tok_ref, table_ref)
    for i, out in enumerate(outs):
        out[...] = rows[i * slots:(i + 1) * slots]


def rest(tok, table, picks):
    experts, slots = picks.shape
    return pl.pallas_call(
        rest_kernel,
        in_specs=[VMEM] * 3,
        out_specs=[VMEM] * (experts - 1),
        out_shape=[jax.ShapeDtypeStruct((slots, tok.shape[1]), BF16)] * (experts - 1),
        compiler_params=params(8),
        cost_estimate=FREE,
        name="rest",
    )(tok, table, picks)


def mixer_kernel(picks_ref, weights_ref, after_ref, *outs):
    for i, out in enumerate(outs):
        each = picks_ref.shape[0] // len(outs)
        rows = range(i * each, (i + 1) * each)
        picks = jnp.concatenate([picks_ref[r:r + 1, :] for r in rows], axis=1)
        weights = jnp.concatenate([weights_ref[r:r + 1, :] for r in rows], axis=1)
        mix = jnp.where(hot_rows(picks, out.shape[0]), weights, 0.0)
        high = mix.astype(BF16).astype(F32)
        out[...] = jnp.concatenate([high, mix - high], axis=1).astype(BF16)


def mixer(picks, weights, after, tok_rows):
    experts, slots = picks.shape
    return pl.pallas_call(
        mixer_kernel,
        in_specs=[VMEM] * 2 + [ANY],
        out_specs=[VMEM] * 2,
        out_shape=[jax.ShapeDtypeStruct((tok_rows, experts * slots), BF16)] * 2,
        compiler_params=params(4),
        cost_estimate=FREE,
        name="mixer",
    )(picks, weights, after)


def stream(w_hbm, out_ref, sems, at):
    rows, columns = out_ref.shape
    pieces = sems.shape[0]
    part = rows // pieces
    return [
        pltpu.make_async_copy(
            w_hbm.at[pl.ds(at[0] + p * part, part), pl.ds(at[1], columns)],
            out_ref.at[pl.ds(p * part, part), :],
            sems.at[p],
        )
        for p in range(pieces)
    ]


def load_kernel(w_hbm, *refs, at):
    out_ref, sems = refs[-2:]
    copies = stream(w_hbm, out_ref, sems, at)
    for copy in copies:
        copy.start()
    for copy in copies:
        copy.wait()


def load(w, at, shape, after):
    return pl.pallas_call(
        functools.partial(load_kernel, at=at),
        in_specs=[HBM] + [ANY] * len(after),
        out_specs=VMEM,
        out_shape=pltpu.VMEM(shape, w.dtype),
        scratch_shapes=[pltpu.SemaphoreType.DMA((PIECES,))],
        compiler_params=params(2),
        cost_estimate=FREE,
        name="load",
    )(w, *after)


def join_kernel(*refs, count):
    out_ref = refs[-1]
    at = 0
    for ref in refs[:count]:
        out_ref[at:at + ref.shape[0], :] = ref[...]
        at += ref.shape[0]


def join(parts, after):
    return pl.pallas_call(
        functools.partial(join_kernel, count=len(parts)),
        in_specs=[VMEM] * len(parts) + [ANY] * len(after),
        out_specs=VMEM,
        out_shape=jax.ShapeDtypeStruct((sum(p.shape[0] for p in parts), parts[0].shape[1]), BF16),
        compiler_params=params(2),
        cost_estimate=FREE,
        name="join",
    )(*parts, *after)


def up_kernel(*refs, sources, count, at):
    w_ref, next_hbm = refs[count:count + 2]
    if sources is None:
        rows_ref = refs[0]
        out_ref, next_ref, sems = refs[-3:]
    else:
        out_ref, next_ref, rows_ref, sems = refs[-4:]
    copies = stream(next_hbm, next_ref, sems, at)
    for copy in copies:
        copy.start()
    if sources is not None:
        to = 0
        for source, low, high in sources:
            rows_ref[to:to + high - low, :] = refs[source][low:high, :]
            to += high - low
    hidden = w_ref.shape[0]
    tile = min(512, hidden)

    @pl.loop(0, hidden // tile)
    def _(i):
        cut = pl.ds(pl.multiple_of(i * tile, tile), tile)
        lifted = lax.dot_general(
            rows_ref[...], w_ref[cut, :], (((1,), (1,)), ((), ())), preferred_element_type=F32
        )
        out_ref[:, cut] = jax.nn.gelu(lifted, approximate=True).astype(BF16)

    for copy in copies:
        copy.wait()


def up(parts, sources, w, following, at, shape):
    hidden, width = w.shape
    rows = parts[0].shape[0] if sources is None else sum(high - low for _, low, high in sources)
    out_shape = [jax.ShapeDtypeStruct((rows, hidden), BF16), pltpu.VMEM(shape, BF16)]
    if sources is not None:
        out_shape.append(jax.ShapeDtypeStruct((rows, width), BF16))
    return pl.pallas_call(
        functools.partial(up_kernel, sources=sources, count=len(parts), at=at),
        in_specs=[VMEM] * len(parts) + [VMEM, HBM],
        out_specs=[VMEM] * len(out_shape),
        out_shape=out_shape,
        scratch_shapes=[pltpu.SemaphoreType.DMA((PIECES,))],
        compiler_params=params(12),
        cost_estimate=FREE,
        name="up",
    )(*parts, w, following)


def down_kernel(*refs, count, blocks, at):
    weights = refs[count:count + blocks]
    if at is None:
        keep_ref, send_ref = refs[count + blocks:]
        copies = []
    else:
        next_hbm, keep_ref, send_ref, next_ref, sems = refs[count + blocks:]
        copies = stream(next_hbm, next_ref, sems, at)
    for copy in copies:
        copy.start()
    half = keep_ref.shape[0]
    base = 0
    for w_ref in weights:
        step = w_ref.shape[1]
        tile = step // 2

        @pl.loop(0, 2)
        def _(i):
            cut = pl.ds(pl.multiple_of(i * tile, tile), tile)
            to = pl.ds(pl.multiple_of(base + i * tile, tile), tile)
            low = 0
            out = None
            for h_ref in refs[:count]:
                part = jnp.dot(
                    h_ref[...], w_ref[low:low + h_ref.shape[1], cut], preferred_element_type=F32
                )
                out = part if out is None else out + part
                low += h_ref.shape[1]
            keep_ref[:, to] = out[:half]
            send_ref[:, to] = out[half:].astype(BF16)

        base += step
    for copy in copies:
        copy.wait()


def down(hiddens, weights, following, at, shape):
    half = hiddens[0].shape[0] // 2
    step = sum(w.shape[1] for w in weights)
    more = following is not None
    return pl.pallas_call(
        functools.partial(down_kernel, count=len(hiddens), blocks=len(weights), at=at),
        in_specs=[VMEM] * (len(hiddens) + len(weights)) + [HBM] * more,
        out_specs=[VMEM] * (2 + more),
        out_shape=[
            jax.ShapeDtypeStruct((half, step), F32),
            jax.ShapeDtypeStruct((half, step), BF16),
        ]
        + ([pltpu.VMEM(shape, BF16)] if more else []),
        scratch_shapes=[pltpu.SemaphoreType.DMA((PIECES,))] * more,
        compiler_params=params(12),
        cost_estimate=FREE,
        name="down",
    )(*hiddens, *weights, *([following] if more else []))


def add_kernel(*refs, count, cuts):
    at = 0
    for i in range(count):
        keep_ref, got_ref = refs[2 * i:2 * i + 2]
        step = keep_ref.shape[1]
        for ref, (low, high) in zip(refs[2 * count:], cuts):
            total = keep_ref[low:high] + got_ref[low:high].astype(F32)
            ref[:, at:at + step] = total.astype(ref.dtype)
        at += step


def add(pairs, cuts, kinds):
    width = sum(keep.shape[1] for keep, _ in pairs)
    args = [x for pair in pairs for x in pair]
    return pl.pallas_call(
        functools.partial(add_kernel, count=len(pairs), cuts=cuts),
        in_specs=[VMEM] * len(args),
        out_specs=[VMEM] * len(cuts),
        out_shape=[jax.ShapeDtypeStruct((high - low, width), k) for (low, high), k in zip(cuts, kinds)],
        compiler_params=params(8),
        cost_estimate=FREE,
        name="add",
    )(*args)


def own_kernel(mix_ref, keep_ref, near_ref, got_ref, acc_ref):
    own = (keep_ref[...] + near_ref[...].astype(F32)).astype(BF16)
    values = jnp.concatenate([own, got_ref[...]] * 2, axis=0)
    acc_ref[...] = jnp.dot(mix_ref[...], values, preferred_element_type=F32)


def own_part(mix, keep, near, got):
    return pl.pallas_call(
        own_kernel,
        in_specs=[VMEM] * 4,
        out_specs=VMEM,
        out_shape=jax.ShapeDtypeStruct((mix.shape[0], keep.shape[1]), F32),
        compiler_params=params(12),
        cost_estimate=FREE,
        name="own_part",
    )(mix, keep, near, got)


def post_kernel(mix_ref, table_ref, acc_ref, *refs):
    out_ref = refs[-1]
    step = out_ref.shape[1]
    cut = pl.ds(pl.multiple_of(pl.program_id(0) * step, step), step)
    values = jnp.concatenate([ref[:, cut] for ref in refs[:-1]] * 2, axis=0)
    mixed = acc_ref[:, cut] + jnp.dot(mix_ref[...], values, preferred_element_type=F32)
    out_ref[...] = (table_ref[2:3, cut] * mixed).astype(BF16)


def post(mix, table, acc, parts):
    tok_rows, width = acc.shape
    step = min(2048, width)
    return pl.pallas_call(
        post_kernel,
        grid=(width // step,),
        in_specs=[VMEM] * (3 + len(parts)),
        out_specs=pl.BlockSpec((tok_rows, step), lambda i: (0, i)),
        out_shape=jax.ShapeDtypeStruct((tok_rows, width), BF16),
        compiler_params=params(8),
        cost_estimate=FREE,
        name="post",
    )(mix, table, acc, *parts)


def shards(tokens, shift, scale, gate, w_up, w_down, pick, count, combine):
    tok_rows, width = tokens.shape
    _, experts, slots = pick.shape
    devices = lax.axis_size("expert")
    place = lax.axis_index("expert")
    group = devices // experts
    requests = shift.shape[0]
    hidden = w_up.shape[0]
    info = jnp.stack([place // (devices // requests), place // group]).astype(jnp.int32)
    pick = pick[0]
    comb = combine[0]

    far = [d * group for d in turns(experts)[1:]]
    near = []
    bit = group // 2
    while bit:
        near.append(bit)
        bit //= 2

    def swap(x, mask):
        return lax.ppermute(x, "expert", [(i, i ^ mask) for i in range(devices)])

    tokens, shift, scale, gate, w_up, w_down, pick, comb, count = [
        pltpu.with_memory_space_constraint(x, pltpu.HBM)
        for x in (tokens, shift, scale, gate, w_up, w_down, pick, comb, count)
    ]
    farthest, tok, table, picks, weights = first(info, tokens, pick, shift, scale, gate, comb, count)
    own, *others = rest(tok, table, picks)
    mixes = mixer(picks, weights, own, tok_rows)

    flat = [farthest] + others
    blocks = [own] + [swap(x, mask) for x, mask in zip(flat, far)]
    block_up = (hidden // 2, width)
    ups = [load(w_up, (0, 0), block_up, [blocks[1], mixes[0]])]
    blocks[2] = join([blocks[2]], [ups[0]])
    beside = [swap(block, near[0]) for block in blocks]
    early, late = list(range(experts // 2)), list(range(experts // 2, experts))
    parts = []
    sources = []
    for members in (early, late):
        pieces = [join([x for i in members for x in (blocks[i], beside[i])], ups[1:])]
        if members is early:
            ups.append(load(w_up, (hidden // 2, 0), block_up, [pieces[0], ups[0]]))
        height = pieces[0].shape[0]
        for mask in near[1:]:
            block = pieces[0] if len(pieces) == 1 else join(pieces, [])
            pieces = [block, swap(block, mask)]
        cuts = []
        for piece in pieces:
            cuts += [(len(parts), at, at + height) for at in range(0, piece.shape[0], height)]
            parts.append(piece)
        sources.append(cuts)
    sources = [cut for pair in zip(*sources) for cut in pair]

    step = 3 * width // 8
    last = width - 2 * step
    hid, down_a, rows = up(parts, sources, ups[0], w_down, (0, 0), (hidden, step))
    hid_b, down_b = up([rows], None, ups[1], w_down, (0, step), (hidden, step))

    keep_a, send_a, down_c = down([hid, hid_b], [down_a, down_b], w_down, (0, 2 * step), (hidden, last))
    keep_b, send_b = down([hid, hid_b], [down_c], None, None, None)
    pairs = []
    for keep, send in ((keep_a, send_a), (keep_b, send_b)):
        for i, mask in enumerate(reversed(near[1:])):
            if i:
                half = keep.shape[0] // 2
                keep, send = add([(keep, got)], [(0, half), (half, 2 * half)], [F32, BF16])
            if pairs:
                send = join([send], [pairs[0][1]])
            got = swap(send, mask)
        pairs.append((keep, got))
    keeps = [(2 * i * slots, (2 * i + 1) * slots) for i in range(experts)]
    sends = [(high, high + slots) for _, high in keeps]
    summed = add(pairs, sends + keeps, [BF16] * experts + [F32] * experts)
    sends, keeps = summed[:experts], summed[experts:]
    arrived = {i: swap(sends[i], near[0]) for i in list(range(1, experts)) + [0]}
    back = []
    for i, mask in enumerate(far, 1):
        (part,) = add([(keeps[i], arrived[i])], [(0, slots)], [BF16])
        back.append(swap(part, mask))
    acc = own_part(mixes[0], keeps[0], arrived[0], back[0])
    return post(mixes[1], table, acc, back[1:])


def solution(mesh):
    return jax.shard_map(
        shards,
        mesh=mesh,
        in_specs=(
            P(("groups", "expert"), None),
            P("groups", None),
            P("groups", None),
            P("groups", None),
            P("expert", None),
            P("expert", None),
            P(("groups", "expert"), None, None),
            P(("groups", "expert"), None),
            P(("groups", "expert"), None, None),
        ),
        out_specs=P(("groups", "expert"), None),
        check_vma=False,
    )
```

```python
import functools

import jax
import jax.numpy as jnp
from jax import lax
from jax.experimental import pallas as pl
from jax.experimental.pallas import tpu as pltpu
from jax.sharding import PartitionSpec as P

PIECES = 8
MIB = 1024 * 1024
F32 = jnp.float32
BF16 = jnp.bfloat16

SMEM = pl.BlockSpec(memory_space=pltpu.SMEM)
VMEM = pl.BlockSpec(memory_space=pltpu.VMEM)
HBM = pl.BlockSpec(memory_space=pltpu.HBM)
ANY = pl.BlockSpec(memory_space=pl.ANY)


FREE = pl.CostEstimate(flops=1, bytes_accessed=1, transcendentals=0)


def params(mib):
    return pltpu.CompilerParams(vmem_limit_bytes=mib * MIB)


def stream(w_hbm, out_ref, sems, at):
    rows, columns = out_ref.shape
    pieces = sems.shape[0]
    part = rows // pieces
    return [
        pltpu.make_async_copy(
            w_hbm.at[pl.ds(at[0] + p * part, part), pl.ds(at[1], columns)],
            out_ref.at[pl.ds(p * part, part), :],
            sems.at[p],
        )
        for p in range(pieces)
    ]


def turns(experts):
    return [0] + list(range(experts - 1, 0, -1))


def hot_rows(picks, tok_rows):
    return lax.broadcasted_iota(jnp.int32, (tok_rows, picks.shape[1]), 0) == picks


def modulate(picks, tok_ref, table_ref):
    hot = hot_rows(picks, tok_ref.shape[0]).astype(F32).astype(BF16)
    values = lax.dot_general(hot, tok_ref[...], (((0,), (0,)), ((), ())), preferred_element_type=F32)
    center = values - jnp.mean(values, axis=1, keepdims=True)
    spread = jnp.mean(center * center, axis=1, keepdims=True)
    normed = center * (1.0 / jnp.sqrt(spread + 1e-06))
    return (normed * table_ref[0:1, :] + table_ref[1:2, :]).astype(BF16)


def first_kernel(info_ref, w_hbm, *refs):
    sources = refs[:7]
    far_ref, tok_ref, table_ref, picks_ref, weights_ref, w_ref = refs[7:13]
    pick_ref, comb_ref, count_ref, shift_ref, scale_ref, gate_ref, sems, w_sems = refs[13:]
    targets = (tok_ref, pick_ref, shift_ref, scale_ref, gate_ref, comb_ref, count_ref)
    copies = [
        pltpu.make_async_copy(src, dst, sems.at[i])
        for i, (src, dst) in enumerate(zip(sources, targets))
    ]
    loads = stream(w_hbm, w_ref, w_sems, (0, 0))
    for copy in copies + loads:
        copy.start()
    for copy in copies:
        copy.wait()
    experts, slots = pick_ref.shape
    which = pl.ds(info_ref[0], 1)
    table_ref[0:1, :] = 1.0 + scale_ref[which, :]
    table_ref[1:2, :] = shift_ref[which, :]
    table_ref[2:3, :] = gate_ref[which, :]
    lanes = lax.broadcasted_iota(jnp.int32, (1, slots), 1)
    for i, d in enumerate(turns(experts)):
        e = info_ref[1] ^ d
        picks_ref[i:i + 1, :] = pick_ref[pl.ds(e, 1), :]
        weights_ref[i:i + 1, :] = jnp.where(lanes < count_ref[0, e], comb_ref[pl.ds(e, 1), :], 0.0)
    far_ref[...] = modulate(picks_ref[1:2, :], tok_ref, table_ref)
    for copy in loads:
        copy.wait()


def first(info, w, shape, tokens, pick, shift, scale, gate, comb, count):
    experts, slots = pick.shape
    width = tokens.shape[1]
    return pl.pallas_call(
        first_kernel,
        in_specs=[SMEM] + [HBM] * 8,
        out_specs=[VMEM] * 6,
        out_shape=[
            jax.ShapeDtypeStruct((slots, width), BF16),
            jax.ShapeDtypeStruct(tokens.shape, BF16),
            jax.ShapeDtypeStruct((3, width), F32),
            jax.ShapeDtypeStruct(pick.shape, jnp.int32),
            jax.ShapeDtypeStruct(comb.shape, F32),
            pltpu.VMEM(shape, BF16),
        ],
        scratch_shapes=[
            pltpu.VMEM(pick.shape, jnp.int32),
            pltpu.VMEM(comb.shape, F32),
            pltpu.SMEM(count.shape, jnp.int32),
            pltpu.VMEM(shift.shape, F32),
            pltpu.VMEM(scale.shape, F32),
            pltpu.VMEM(gate.shape, F32),
            pltpu.SemaphoreType.DMA((7,)),
            pltpu.SemaphoreType.DMA((PIECES,)),
        ],
        compiler_params=params(8),
        cost_estimate=FREE,
        name="first",
    )(info, w, tokens, pick, shift, scale, gate, comb, count)


def rest_kernel(tok_ref, table_ref, picks_ref, *outs):
    experts, slots = picks_ref.shape
    order = [0] + list(range(2, experts))
    picks = jnp.concatenate([picks_ref[i:i + 1, :] for i in order], axis=1)
    rows = modulate(picks, tok_ref, table_ref)
    for i, out in enumerate(outs):
        out[...] = rows[i * slots:(i + 1) * slots]


def rest(tok, table, picks):
    experts, slots = picks.shape
    return pl.pallas_call(
        rest_kernel,
        in_specs=[VMEM] * 3,
        out_specs=[VMEM] * (experts - 1),
        out_shape=[jax.ShapeDtypeStruct((slots, tok.shape[1]), BF16)] * (experts - 1),
        compiler_params=params(8),
        cost_estimate=FREE,
        name="rest",
    )(tok, table, picks)


def mixer_kernel(picks_ref, weights_ref, after_ref, *outs):
    for i, out in enumerate(outs):
        each = picks_ref.shape[0] // len(outs)
        rows = range(i * each, (i + 1) * each)
        picks = jnp.concatenate([picks_ref[r:r + 1, :] for r in rows], axis=1)
        weights = jnp.concatenate([weights_ref[r:r + 1, :] for r in rows], axis=1)
        mix = jnp.where(hot_rows(picks, out.shape[0]), weights, 0.0)
        high = mix.astype(BF16).astype(F32)
        out[...] = jnp.concatenate([high, mix - high], axis=1).astype(BF16)


def mixer(picks, weights, after, tok_rows):
    experts, slots = picks.shape
    return pl.pallas_call(
        mixer_kernel,
        in_specs=[VMEM] * 2 + [ANY],
        out_specs=[VMEM] * 2,
        out_shape=[jax.ShapeDtypeStruct((tok_rows, experts * slots), BF16)] * 2,
        compiler_params=params(4),
        cost_estimate=FREE,
        name="mixer",
    )(picks, weights, after)


def load_kernel(w_hbm, *refs, at):
    out_ref, sems = refs[-2:]
    copies = stream(w_hbm, out_ref, sems, at)
    for copy in copies:
        copy.start()
    for copy in copies:
        copy.wait()


def load(w, at, shape, after):
    return pl.pallas_call(
        functools.partial(load_kernel, at=at),
        in_specs=[HBM] + [ANY] * len(after),
        out_specs=VMEM,
        out_shape=pltpu.VMEM(shape, w.dtype),
        scratch_shapes=[pltpu.SemaphoreType.DMA((PIECES,))],
        compiler_params=params(2),
        cost_estimate=FREE,
        name="load",
    )(w, *after)


def join_kernel(*refs, count):
    out_ref = refs[-1]
    at = 0
    for ref in refs[:count]:
        out_ref[at:at + ref.shape[0], :] = ref[...]
        at += ref.shape[0]


def join(parts, after):
    return pl.pallas_call(
        functools.partial(join_kernel, count=len(parts)),
        in_specs=[VMEM] * len(parts) + [ANY] * len(after),
        out_specs=VMEM,
        out_shape=jax.ShapeDtypeStruct((sum(p.shape[0] for p in parts), parts[0].shape[1]), BF16),
        compiler_params=params(2),
        cost_estimate=FREE,
        name="join",
    )(*parts, *after)


def up_kernel(*refs, sources, count, blocks, at):
    weights = refs[count:count + blocks]
    next_hbm = refs[count + blocks]
    if sources is None:
        rows_ref = refs[0]
        out_ref, next_ref, sems = refs[-3:]
    else:
        out_ref, next_ref, rows_ref, sems = refs[-4:]
    copies = stream(next_hbm, next_ref, sems, at)
    for copy in copies:
        copy.start()
    if sources is not None:
        to = 0
        for source, low, high in sources:
            rows_ref[to:to + high - low, :] = refs[source][low:high, :]
            to += high - low
    base = 0
    for w_ref in weights:
        hidden = w_ref.shape[0]
        tile = min(512, hidden)

        @pl.loop(0, hidden // tile)
        def _(i):
            lifted = lax.dot_general(
                rows_ref[...],
                w_ref[pl.ds(pl.multiple_of(i * tile, tile), tile), :],
                (((1,), (1,)), ((), ())),
                preferred_element_type=F32,
            )
            to = pl.ds(pl.multiple_of(base + i * tile, tile), tile)
            out_ref[:, to] = jax.nn.gelu(lifted, approximate=True).astype(BF16)

        base += hidden
    for copy in copies:
        copy.wait()


def up(parts, sources, weights, following, at, shape):
    hidden = sum(w.shape[0] for w in weights)
    width = weights[0].shape[1]
    rows = parts[0].shape[0] if sources is None else sum(high - low for _, low, high in sources)
    out_shape = [jax.ShapeDtypeStruct((rows, hidden), BF16), pltpu.VMEM(shape, BF16)]
    if sources is not None:
        out_shape.append(jax.ShapeDtypeStruct((rows, width), BF16))
    return pl.pallas_call(
        functools.partial(
            up_kernel, sources=sources, count=len(parts), blocks=len(weights), at=at
        ),
        in_specs=[VMEM] * (len(parts) + len(weights)) + [HBM],
        out_specs=[VMEM] * len(out_shape),
        out_shape=out_shape,
        scratch_shapes=[pltpu.SemaphoreType.DMA((PIECES,))],
        compiler_params=params(12),
        cost_estimate=FREE,
        name="up",
    )(*parts, *weights, following)


def down_kernel(*refs, count, at):
    hiddens, weights = refs[:count], refs[count:2 * count]
    if at is None:
        keep_ref, send_ref = refs[2 * count:]
        copies = []
    else:
        next_hbm, keep_ref, send_ref = refs[2 * count:2 * count + 3]
        nexts, sems = refs[2 * count + 3:-1], refs[-1]
        copies = []
        for i, ref in enumerate(nexts):
            copies += stream(next_hbm, ref, sems.at[pl.ds(i * PIECES, PIECES)], at[i])
    for copy in copies:
        copy.start()
    half, step = keep_ref.shape
    tile = min(1024, step)

    @pl.loop(0, step // tile)
    def _(i):
        cut = pl.ds(pl.multiple_of(i * tile, tile), tile)
        out = None
        for h_ref, w_ref in zip(hiddens, weights):
            part = jnp.dot(h_ref[...], w_ref[:, cut], preferred_element_type=F32)
            out = part if out is None else out + part
        keep_ref[:, cut] = out[:half]
        send_ref[:, cut] = out[half:].astype(BF16)

    for copy in copies:
        copy.wait()


def down(hiddens, weights, following, at, shapes):
    half = hiddens[0].shape[0] // 2
    step = weights[0].shape[1]
    more = following is not None
    return pl.pallas_call(
        functools.partial(down_kernel, count=len(hiddens), at=at),
        in_specs=[VMEM] * (2 * len(hiddens)) + [HBM] * more,
        out_specs=[VMEM] * (2 + len(shapes)),
        out_shape=[
            jax.ShapeDtypeStruct((half, step), F32),
            jax.ShapeDtypeStruct((half, step), BF16),
        ]
        + [pltpu.VMEM(shape, BF16) for shape in shapes],
        scratch_shapes=[pltpu.SemaphoreType.DMA((len(shapes) * PIECES,))] * more,
        compiler_params=params(12),
        cost_estimate=FREE,
        name="down",
    )(*hiddens, *weights, *([following] if more else []))


def add_kernel(*refs, count, cuts, carried):
    at = 0
    outs = refs[2 * count + carried:]
    for i in range(count):
        keep_ref, got_ref = refs[2 * i:2 * i + 2]
        step = keep_ref.shape[1]
        for ref, (low, high) in zip(outs, cuts):
            total = keep_ref[low:high] + got_ref[low:high].astype(F32)
            ref[:, at:at + step] = total.astype(ref.dtype)
        at += step
    for i in range(carried):
        outs[len(cuts) + i][...] = refs[2 * count + i][...]


def add(pairs, cuts, kinds, carry=()):
    width = sum(keep.shape[1] for keep, _ in pairs)
    args = [x for pair in pairs for x in pair] + list(carry)
    return pl.pallas_call(
        functools.partial(add_kernel, count=len(pairs), cuts=cuts, carried=len(carry)),
        in_specs=[VMEM] * len(args),
        out_specs=[VMEM] * (len(cuts) + len(carry)),
        out_shape=[jax.ShapeDtypeStruct((high - low, width), k) for (low, high), k in zip(cuts, kinds)]
        + [jax.ShapeDtypeStruct(x.shape, x.dtype) for x in carry],
        compiler_params=params(8),
        cost_estimate=FREE,
        name="add",
    )(*args)


def own_kernel(mix_ref, keep_ref, near_ref, got_ref, acc_ref):
    own = (keep_ref[...] + near_ref[near_ref.shape[0] - keep_ref.shape[0]:].astype(F32)).astype(BF16)
    values = jnp.concatenate([own, got_ref[...]] * 2, axis=0)
    acc_ref[...] = jnp.dot(mix_ref[...], values, preferred_element_type=F32)


def own_part(mix, keep, near, got):
    return pl.pallas_call(
        own_kernel,
        in_specs=[VMEM] * 4,
        out_specs=VMEM,
        out_shape=jax.ShapeDtypeStruct((mix.shape[0], keep.shape[1]), F32),
        compiler_params=params(12),
        cost_estimate=FREE,
        name="own_part",
    )(mix, keep, near, got)


def post_kernel(mix_ref, table_ref, acc_ref, *refs):
    out_ref = refs[-1]
    step = out_ref.shape[1]
    cut = pl.ds(pl.multiple_of(pl.program_id(0) * step, step), step)
    values = jnp.concatenate([ref[:, cut] for ref in refs[:-1]] * 2, axis=0)
    mixed = acc_ref[:, cut] + jnp.dot(mix_ref[...], values, preferred_element_type=F32)
    out_ref[...] = (table_ref[2:3, cut] * mixed).astype(BF16)


def post(mix, table, acc, parts):
    tok_rows, width = acc.shape
    step = min(2048, width)
    return pl.pallas_call(
        post_kernel,
        grid=(width // step,),
        in_specs=[VMEM] * (3 + len(parts)),
        out_specs=pl.BlockSpec((tok_rows, step), lambda i: (0, i)),
        out_shape=jax.ShapeDtypeStruct((tok_rows, width), BF16),
        compiler_params=params(8),
        cost_estimate=FREE,
        name="post",
    )(mix, table, acc, *parts)


def shards(tokens, shift, scale, gate, w_up, w_down, pick, count, combine):
    tok_rows, width = tokens.shape
    _, experts, slots = pick.shape
    devices = lax.axis_size("expert")
    place = lax.axis_index("expert")
    group = devices // experts
    requests = shift.shape[0]
    hidden = w_up.shape[0]
    info = jnp.stack([place // (devices // requests), place // group]).astype(jnp.int32)
    pick = pick[0]
    comb = combine[0]

    far = [d * group for d in turns(experts)[1:]]
    near = []
    bit = group // 2
    while bit:
        near.append(bit)
        bit //= 2

    def swap(x, mask):
        return lax.ppermute(x, "expert", [(i, i ^ mask) for i in range(devices)])

    tokens, shift, scale, gate, w_up, w_down, pick, comb, count = [
        pltpu.with_memory_space_constraint(x, pltpu.HBM)
        for x in (tokens, shift, scale, gate, w_up, w_down, pick, comb, count)
    ]
    quarter = hidden // 4
    farthest, tok, table, picks, weights, w_first = first(
        info, w_up, (quarter, width), tokens, pick, shift, scale, gate, comb, count
    )
    own, *others = rest(tok, table, picks)
    mixes = mixer(picks, weights, own, tok_rows)

    flat = [farthest] + others
    blocks = [own] + [swap(x, mask) for x, mask in zip(flat, far)]
    beside = [swap(block, near[0]) for block in blocks]
    w_second = load(w_up, (2 * quarter, 0), (2 * quarter, width), [blocks[2], mixes[0]])
    early, late = list(range(experts // 2)), list(range(experts // 2, experts))
    parts = []
    sources = []
    for members in (early, late):
        after = [] if members is early else [w_second]
        pieces = [join([x for i in members for x in (blocks[i], beside[i])], after)]
        if members is late:
            w_third = load(w_up, (quarter, 0), (quarter, width), [pieces[0]])
        height = pieces[0].shape[0]
        for mask in near[1:]:
            block = pieces[0] if len(pieces) == 1 else join(pieces, [])
            pieces = [block, swap(block, mask)]
        cuts = []
        for piece in pieces:
            cuts += [(len(parts), at, at + height) for at in range(0, piece.shape[0], height)]
            parts.append(piece)
        sources.append(cuts)
    sources = [cut for pair in zip(*sources) for cut in pair]

    half = 2 * quarter
    step = 3 * width // 4
    hid_b, down_b, rows = up(parts, sources, [w_second], w_down, (half, 0), (half, step))
    hid_a, down_a = up([rows], None, [w_first, w_third], w_down, (0, 0), (half, step))

    hiddens = [hid_a, hid_b]
    tall, last = (half, width - step), [(0, step), (half, step)]
    keep_a, send_a, *downs = down(hiddens, [down_a, down_b], w_down, last, [tall, tall])
    keep_b, send_b = down(hiddens, downs, None, None, [])
    pairs = []
    for keep, send in ((keep_a, send_a), (keep_b, send_b)):
        for i, mask in enumerate(reversed(near[1:])):
            if i:
                middle = keep.shape[0] // 2
                keep, send = add(
                    [(keep, got)], [(0, middle), (middle, 2 * middle)], [F32, BF16]
                )
            if pairs:
                send = join([send], [pairs[0][1]])
            got = swap(send, mask)
        pairs.append((keep, got))
    keeps = [(2 * i * slots, (2 * i + 1) * slots) for i in range(experts)]
    sends = [(high, high + slots) for _, high in keeps]
    summed = add(pairs, sends + keeps, [BF16] * experts + [F32] * experts)
    sends, keeps = summed[:experts], summed[experts:]
    arrived = [swap(send, near[0]) for send in sends[1:]]
    parts = [
        add([(keep, got)], [(0, slots)], [BF16])[0] for keep, got in zip(keeps[1:], arrived)
    ]
    back = [swap(part, mask) for part, mask in zip(parts, far)]
    arrived = swap(join([sends[0]], [parts[0]]), near[0])
    acc = own_part(mixes[0], keeps[0], arrived, back[0])
    return post(mixes[1], table, acc, back[1:])


def solution(mesh):
    return jax.shard_map(
        shards,
        mesh=mesh,
        in_specs=(
            P(("groups", "expert"), None),
            P("groups", None),
            P("groups", None),
            P("groups", None),
            P("expert", None),
            P("expert", None),
            P(("groups", "expert"), None, None),
            P(("groups", "expert"), None),
            P(("groups", "expert"), None, None),
        ),
        out_specs=P(("groups", "expert"), None),
        check_vma=False,
    )
```

```python
import functools

import jax
import jax.numpy as jnp
from jax import lax
from jax.experimental import pallas as pl
from jax.experimental.pallas import tpu as pltpu
from jax.sharding import PartitionSpec as P

PIECES = 8
MIB = 1024 * 1024
F32 = jnp.float32
BF16 = jnp.bfloat16

SMEM = pl.BlockSpec(memory_space=pltpu.SMEM)
VMEM = pl.BlockSpec(memory_space=pltpu.VMEM)
HBM = pl.BlockSpec(memory_space=pltpu.HBM)
ANY = pl.BlockSpec(memory_space=pl.ANY)


FREE = pl.CostEstimate(flops=1, bytes_accessed=1, transcendentals=0)


def params(mib):
    return pltpu.CompilerParams(vmem_limit_bytes=mib * MIB)


def fetch(pairs, sems):
    copies = [pltpu.make_async_copy(src, dst, sems.at[i]) for i, (src, dst) in enumerate(pairs)]
    for copy in copies:
        copy.start()
    for copy in copies:
        copy.wait()


def stream(w_hbm, out_ref, sems, at, first=0, rows=None):
    rows = out_ref.shape[0] if rows is None else rows
    columns = out_ref.shape[1]
    part = rows // PIECES
    return [
        pltpu.make_async_copy(
            w_hbm.at[pl.ds(at[0] + p * part, part), pl.ds(at[1], columns)],
            out_ref.at[pl.ds(first + p * part, part), :],
            sems.at[p],
        )
        for p in range(PIECES)
    ]


def turns(experts):
    return [0] + list(range(experts - 1, 0, -1))


def hot_rows(picks, tok_rows):
    return lax.broadcasted_iota(jnp.int32, (tok_rows, picks.shape[1]), 0) == picks


def modulate(picks, tok_ref, table_ref):
    hot = hot_rows(picks, tok_ref.shape[0]).astype(F32).astype(BF16)
    values = lax.dot_general(hot, tok_ref[...], (((0,), (0,)), ((), ())), preferred_element_type=F32)
    center = values - jnp.mean(values, axis=1, keepdims=True)
    spread = jnp.mean(center * center, axis=1, keepdims=True)
    normed = center * (1.0 / jnp.sqrt(spread + 1e-06))
    return (normed * table_ref[0:1, :] + table_ref[1:2, :]).astype(BF16)


def first_kernel(info_ref, *refs):
    sources = refs[:7]
    far_ref, tok_ref, table_ref, picks_ref, weights_ref = refs[7:12]
    pick_ref, comb_ref, count_ref, shift_ref, scale_ref, gate_ref, sems = refs[12:]
    fetch(
        list(zip(sources, (tok_ref, pick_ref, shift_ref, scale_ref, gate_ref, comb_ref, count_ref))),
        sems,
    )
    experts, slots = pick_ref.shape
    which = pl.ds(info_ref[0], 1)
    table_ref[0:1, :] = 1.0 + scale_ref[which, :]
    table_ref[1:2, :] = shift_ref[which, :]
    table_ref[2:3, :] = gate_ref[which, :]
    lanes = lax.broadcasted_iota(jnp.int32, (1, slots), 1)
    for i, d in enumerate(turns(experts)):
        e = info_ref[1] ^ d
        picks_ref[i:i + 1, :] = pick_ref[pl.ds(e, 1), :]
        weights_ref[i:i + 1, :] = jnp.where(lanes < count_ref[0, e], comb_ref[pl.ds(e, 1), :], 0.0)
    far_ref[...] = modulate(picks_ref[1:2, :], tok_ref, table_ref)


def first(info, tokens, pick, shift, scale, gate, comb, count):
    experts, slots = pick.shape
    width = tokens.shape[1]
    return pl.pallas_call(
        first_kernel,
        in_specs=[SMEM] + [HBM] * 7,
        out_specs=[VMEM] * 5,
        out_shape=[
            jax.ShapeDtypeStruct((slots, width), BF16),
            jax.ShapeDtypeStruct(tokens.shape, BF16),
            jax.ShapeDtypeStruct((3, width), F32),
            jax.ShapeDtypeStruct(pick.shape, jnp.int32),
            jax.ShapeDtypeStruct(comb.shape, F32),
        ],
        scratch_shapes=[
            pltpu.VMEM(pick.shape, jnp.int32),
            pltpu.VMEM(comb.shape, F32),
            pltpu.SMEM(count.shape, jnp.int32),
            pltpu.VMEM(shift.shape, F32),
            pltpu.VMEM(scale.shape, F32),
            pltpu.VMEM(gate.shape, F32),
            pltpu.SemaphoreType.DMA((7,)),
        ],
        compiler_params=params(8),
        cost_estimate=FREE,
        name="first",
    )(info, tokens, pick, shift, scale, gate, comb, count)


def rest_kernel(tok_ref, table_ref, picks_ref, w_hbm, *refs):
    outs, w_ref, sems = refs[:-2], refs[-2], refs[-1]
    copies = stream(w_hbm, w_ref, sems, (0, 0), rows=w_ref.shape[0] // 2)
    for copy in copies:
        copy.start()
    experts, slots = picks_ref.shape
    order = [0] + list(range(2, experts))
    picks = jnp.concatenate([picks_ref[i:i + 1, :] for i in order], axis=1)
    rows = modulate(picks, tok_ref, table_ref)
    for i, out in enumerate(outs):
        out[...] = rows[i * slots:(i + 1) * slots]
    for copy in copies:
        copy.wait()


def rest(tok, table, picks, w, shape):
    experts, slots = picks.shape
    return pl.pallas_call(
        rest_kernel,
        in_specs=[VMEM] * 3 + [HBM],
        out_specs=[VMEM] * experts,
        out_shape=[jax.ShapeDtypeStruct((slots, tok.shape[1]), BF16)] * (experts - 1)
        + [pltpu.VMEM(shape, BF16)],
        scratch_shapes=[pltpu.SemaphoreType.DMA((PIECES,))],
        compiler_params=params(8),
        cost_estimate=FREE,
        name="rest",
    )(tok, table, picks, w)


def mixer_kernel(picks_ref, weights_ref, after_ref, *outs):
    for i, out in enumerate(outs):
        each = picks_ref.shape[0] // len(outs)
        rows = range(i * each, (i + 1) * each)
        picks = jnp.concatenate([picks_ref[r:r + 1, :] for r in rows], axis=1)
        weights = jnp.concatenate([weights_ref[r:r + 1, :] for r in rows], axis=1)
        mix = jnp.where(hot_rows(picks, out.shape[0]), weights, 0.0)
        high = mix.astype(BF16).astype(F32)
        out[...] = jnp.concatenate([high, mix - high], axis=1).astype(BF16)


def mixer(picks, weights, after, tok_rows):
    experts, slots = picks.shape
    return pl.pallas_call(
        mixer_kernel,
        in_specs=[VMEM] * 2 + [ANY],
        out_specs=[VMEM] * 2,
        out_shape=[jax.ShapeDtypeStruct((tok_rows, experts * slots), BF16)] * 2,
        compiler_params=params(4),
        cost_estimate=FREE,
        name="mixer",
    )(picks, weights, after)


def load_kernel(w_hbm, *refs, at, first, rows):
    out_ref, sems = refs[-2:]
    copies = stream(w_hbm, out_ref, sems, at, first, rows)
    for copy in copies:
        copy.start()
    for copy in copies:
        copy.wait()


def load(w, at, shape, after):
    return pl.pallas_call(
        functools.partial(load_kernel, at=at, first=0, rows=shape[0]),
        in_specs=[HBM] + [ANY] * len(after),
        out_specs=VMEM,
        out_shape=pltpu.VMEM(shape, w.dtype),
        scratch_shapes=[pltpu.SemaphoreType.DMA((PIECES,))],
        compiler_params=params(2),
        cost_estimate=FREE,
        name="load",
    )(w, *after)


def load_more(w, at, buffer, after):
    rows = buffer.shape[0] // 2
    return pl.pallas_call(
        functools.partial(load_kernel, at=at, first=rows, rows=rows),
        in_specs=[HBM, VMEM] + [ANY] * len(after),
        out_specs=VMEM,
        out_shape=pltpu.VMEM(buffer.shape, w.dtype),
        input_output_aliases={1: 0},
        scratch_shapes=[pltpu.SemaphoreType.DMA((PIECES,))],
        compiler_params=params(2),
        cost_estimate=FREE,
        name="load_more",
    )(w, buffer, *after)


def join_kernel(*refs, count):
    out_ref = refs[-1]
    at = 0
    for ref in refs[:count]:
        out_ref[at:at + ref.shape[0], :] = ref[...]
        at += ref.shape[0]


def join(parts, after):
    return pl.pallas_call(
        functools.partial(join_kernel, count=len(parts)),
        in_specs=[VMEM] * len(parts) + [ANY] * len(after),
        out_specs=VMEM,
        out_shape=jax.ShapeDtypeStruct((sum(p.shape[0] for p in parts), parts[0].shape[1]), BF16),
        compiler_params=params(2),
        cost_estimate=FREE,
        name="join",
    )(*parts, *after)


def up_kernel(*refs, sources, count, at):
    w_ref, next_hbm = refs[count:count + 2]
    if sources is None:
        rows_ref = refs[0]
        out_ref, next_ref, sems = refs[-3:]
    else:
        out_ref, next_ref, rows_ref, sems = refs[-4:]
    copies = stream(next_hbm, next_ref, sems, at)
    for copy in copies:
        copy.start()
    if sources is not None:
        to = 0
        for source, low, high in sources:
            rows_ref[to:to + high - low, :] = refs[source][low:high, :]
            to += high - low
    hidden = w_ref.shape[0]
    tile = min(512, hidden)

    @pl.loop(0, hidden // tile)
    def _(i):
        cut = pl.ds(pl.multiple_of(i * tile, tile), tile)
        lifted = lax.dot_general(
            rows_ref[...], w_ref[cut, :], (((1,), (1,)), ((), ())), preferred_element_type=F32
        )
        out_ref[:, cut] = jax.nn.gelu(lifted, approximate=True).astype(BF16)

    for copy in copies:
        copy.wait()


def up(parts, sources, w, following, at, shape):
    hidden, width = w.shape
    rows = parts[0].shape[0] if sources is None else sum(high - low for _, low, high in sources)
    out_shape = [jax.ShapeDtypeStruct((rows, hidden), BF16), pltpu.VMEM(shape, BF16)]
    if sources is not None:
        out_shape.append(jax.ShapeDtypeStruct((rows, width), BF16))
    return pl.pallas_call(
        functools.partial(up_kernel, sources=sources, count=len(parts), at=at),
        in_specs=[VMEM] * len(parts) + [VMEM, HBM],
        out_specs=[VMEM] * len(out_shape),
        out_shape=out_shape,
        scratch_shapes=[pltpu.SemaphoreType.DMA((PIECES,))],
        compiler_params=params(12),
        cost_estimate=FREE,
        name="up",
    )(*parts, w, following)


def down_kernel(*refs, count, at):
    hiddens, weights = refs[:count], refs[count:2 * count]
    if at is None:
        keep_ref, send_ref = refs[2 * count:]
        copies = []
    else:
        next_hbm, keep_ref, send_ref = refs[2 * count:2 * count + 3]
        nexts, sems = refs[2 * count + 3:-1], refs[-1]
        copies = []
        for i, ref in enumerate(nexts):
            copies += stream(next_hbm, ref, sems.at[pl.ds(i * PIECES, PIECES)], at[i])
    for copy in copies:
        copy.start()
    half, step = keep_ref.shape
    tile = step if step <= 1536 else step // 2

    @pl.loop(0, step // tile)
    def _(i):
        cut = pl.ds(pl.multiple_of(i * tile, tile), tile)
        out = None
        for h_ref, w_ref in zip(hiddens, weights):
            part = jnp.dot(h_ref[...], w_ref[:, cut], preferred_element_type=F32)
            out = part if out is None else out + part
        keep_ref[:, cut] = out[:half]
        send_ref[:, cut] = out[half:].astype(BF16)

    for copy in copies:
        copy.wait()


def down(hiddens, weights, following, at, shapes):
    half = hiddens[0].shape[0] // 2
    step = weights[0].shape[1]
    more = following is not None
    return pl.pallas_call(
        functools.partial(down_kernel, count=len(hiddens), at=at),
        in_specs=[VMEM] * (2 * len(hiddens)) + [HBM] * more,
        out_specs=[VMEM] * (2 + len(shapes)),
        out_shape=[
            jax.ShapeDtypeStruct((half, step), F32),
            jax.ShapeDtypeStruct((half, step), BF16),
        ]
        + [pltpu.VMEM(shape, BF16) for shape in shapes],
        scratch_shapes=[pltpu.SemaphoreType.DMA((len(shapes) * PIECES,))] * more,
        compiler_params=params(12),
        cost_estimate=FREE,
        name="down",
    )(*hiddens, *weights, *([following] if more else []))


def add_kernel(*refs, count, outs):
    for ref, pieces in zip(refs[2 * count:], outs):
        at = 0
        for i, low, high in pieces:
            keep_ref, got_ref = refs[2 * i:2 * i + 2]
            step = keep_ref.shape[1]
            total = keep_ref[low:high] + got_ref[low:high].astype(F32)
            ref[:, at:at + step] = total.astype(ref.dtype)
            at += step


def add(pairs, outs, kinds):
    args = [x for pair in pairs for x in pair]
    shapes = [
        (pieces[0][2] - pieces[0][1], sum(pairs[i][0].shape[1] for i, _, _ in pieces))
        for pieces in outs
    ]
    return pl.pallas_call(
        functools.partial(add_kernel, count=len(pairs), outs=outs),
        in_specs=[VMEM] * len(args),
        out_specs=[VMEM] * len(outs),
        out_shape=[jax.ShapeDtypeStruct(shape, k) for shape, k in zip(shapes, kinds)],
        compiler_params=params(8),
        cost_estimate=FREE,
        name="add",
    )(*args)


def own_kernel(mix_ref, keep_ref, near_ref, got_ref, acc_ref):
    own = (keep_ref[...] + near_ref[...].astype(F32)).astype(BF16)
    values = jnp.concatenate([own, got_ref[...]] * 2, axis=0)
    acc_ref[...] = jnp.dot(mix_ref[...], values, preferred_element_type=F32)


def own_part(mix, keep, near, got):
    return pl.pallas_call(
        own_kernel,
        in_specs=[VMEM] * 4,
        out_specs=VMEM,
        out_shape=jax.ShapeDtypeStruct((mix.shape[0], keep.shape[1]), F32),
        compiler_params=params(12),
        cost_estimate=FREE,
        name="own_part",
    )(mix, keep, near, got)


def post_kernel(mix_ref, table_ref, acc_ref, *refs):
    blocks = refs[:-3]
    out_hbm, out_ref, sems = refs[-3:]
    step = out_ref.shape[1] // sems.shape[0]
    copies = []
    for i in range(sems.shape[0]):
        cut = pl.ds(i * step, step)
        values = jnp.concatenate([ref[:, cut] for ref in blocks] * 2, axis=0)
        mixed = acc_ref[:, cut] + jnp.dot(mix_ref[...], values, preferred_element_type=F32)
        out_ref[:, cut] = (table_ref[2:3, cut] * mixed).astype(BF16)
        copy = pltpu.make_async_copy(out_ref.at[:, cut], out_hbm.at[:, cut], sems.at[i])
        copy.start()
        copies.append(copy)
    for copy in copies:
        copy.wait()


def post(mix, table, acc, blocks):
    tok_rows, width = acc.shape
    return pl.pallas_call(
        post_kernel,
        in_specs=[VMEM] * (3 + len(blocks)),
        out_specs=HBM,
        out_shape=jax.ShapeDtypeStruct((tok_rows, width), BF16),
        scratch_shapes=[pltpu.VMEM((tok_rows, width), BF16), pltpu.SemaphoreType.DMA((4,))],
        compiler_params=params(8),
        cost_estimate=FREE,
        name="post",
    )(mix, table, acc, *blocks)


def shards(tokens, shift, scale, gate, w_up, w_down, pick, count, combine):
    tok_rows, width = tokens.shape
    _, experts, slots = pick.shape
    devices = lax.axis_size("expert")
    place = lax.axis_index("expert")
    group = devices // experts
    requests = shift.shape[0]
    hidden = w_up.shape[0]
    info = jnp.stack([place // (devices // requests), place // group]).astype(jnp.int32)
    pick = pick[0]
    comb = combine[0]

    far = [d * group for d in turns(experts)[1:]]
    near = []
    bit = group // 2
    while bit:
        near.append(bit)
        bit //= 2

    def swap(x, mask):
        return lax.ppermute(x, "expert", [(i, i ^ mask) for i in range(devices)])

    tokens, shift, scale, gate, w_up, w_down, pick, comb, count = [
        pltpu.with_memory_space_constraint(x, pltpu.HBM)
        for x in (tokens, shift, scale, gate, w_up, w_down, pick, comb, count)
    ]
    half = hidden // 2
    farthest, tok, table, picks, weights = first(info, tokens, pick, shift, scale, gate, comb, count)
    own, *others, w_low = rest(tok, table, picks, w_up, (half, width))

    flat = [farthest] + others
    blocks = [own] + [swap(x, mask) for x, mask in zip(flat, far)]
    mixes = mixer(picks, weights, blocks[1], tok_rows)
    blocks[2] = join([blocks[2]], [mixes[0]])
    beside = [swap(block, near[0]) for block in blocks]
    beside[-1] = join([beside[-1]], [])
    early, late = list(range(experts // 2)), list(range(experts // 2, experts))
    parts = []
    sources = []
    for members in (early, late):
        after = [] if members is early else [w_high]
        pieces = [join([x for i in members for x in (blocks[i], beside[i])], after)]
        if members is early:
            w_high = load(w_up, (half, 0), (half, width), [pieces[0]])
        else:
            w_low = load_more(w_up, (half // 2, 0), w_low, [pieces[0]])
        height = pieces[0].shape[0]
        for mask in near[1:]:
            block = pieces[0] if len(pieces) == 1 else join(pieces, [])
            pieces = [block, swap(block, mask)]
        cuts = []
        for piece in pieces:
            cuts += [(len(parts), at, at + height) for at in range(0, piece.shape[0], height)]
            parts.append(piece)
        sources.append(cuts)
    sources = [cut for pair in zip(*sources) for cut in pair]

    step = 5 * width // 8
    hid_high, down_high, rows = up(parts, sources, w_high, w_down, (half, 0), (half, step))
    hid_low, down_low = up([rows], None, w_low, w_down, (0, 0), (half, step))

    hiddens = [hid_low, hid_high]
    tall = (half, width - step)
    keep_a, send_a, *downs = down(
        hiddens, [down_low, down_high], w_down, [(0, step), (half, step)], [tall, tall]
    )
    keep_b, send_b = down(hiddens, downs, None, None, [])
    pairs = []
    for keep, send in ((keep_a, send_a), (keep_b, send_b)):
        for i, mask in enumerate(reversed(near[1:])):
            if i:
                middle = keep.shape[0] // 2
                keep, send = add(
                    [(keep, got)], [[(0, 0, middle)], [(0, middle, 2 * middle)]], [F32, BF16]
                )
            if pairs:
                send = join([send], [pairs[0][1]])
            got = swap(send, mask)
        pairs.append((keep, got))

    def outs(side):
        rows = [(2 * i + side) * slots for i in range(experts)]
        return [[(piece, at, at + slots) for piece in range(len(pairs))] for at in rows]

    sums = add(pairs, outs(1) + outs(0), [BF16] * experts + [F32] * experts)
    sends, keeps = sums[:experts], sums[experts:]
    back = {}
    for i in range(1, experts):
        got = swap(sends[i], near[0])
        (part,) = add([(keeps[i], got)], [[(0, 0, slots)]], [BF16])
        back[i] = swap(part, far[i - 1])
        if i == 1:
            own_send = join(sends[:1], [part])
    got = swap(own_send, near[0])
    acc = own_part(mixes[0], keeps[0], got, back[1])
    return post(mixes[1], table, acc, [back[i] for i in range(2, experts)])


def solution(mesh):
    return jax.shard_map(
        shards,
        mesh=mesh,
        in_specs=(
            P(("groups", "expert"), None),
            P("groups", None),
            P("groups", None),
            P("groups", None),
            P("expert", None),
            P("expert", None),
            P(("groups", "expert"), None, None),
            P(("groups", "expert"), None),
            P(("groups", "expert"), None, None),
        ),
        out_specs=P(("groups", "expert"), None),
        check_vma=False,
    )
```

```python
import functools

import jax
import jax.numpy as jnp
from jax import lax
from jax.experimental import pallas as pl
from jax.experimental.pallas import tpu as pltpu
from jax.sharding import PartitionSpec as P

MIB = 1024 * 1024
F32 = jnp.float32
BF16 = jnp.bfloat16

SMEM = pl.BlockSpec(memory_space=pltpu.SMEM)
VMEM = pl.BlockSpec(memory_space=pltpu.VMEM)
HBM = pl.BlockSpec(memory_space=pltpu.HBM)
ANY = pl.BlockSpec(memory_space=pl.ANY)


FREE = pl.CostEstimate(flops=1, bytes_accessed=1, transcendentals=0)

BUSY = pl.CostEstimate(flops=10**10, bytes_accessed=40 * MIB, transcendentals=0)


def params(mib):
    return pltpu.CompilerParams(vmem_limit_bytes=mib * MIB)


def fetch(pairs, sems):
    copies = [pltpu.make_async_copy(src, dst, sems.at[i]) for i, (src, dst) in enumerate(pairs)]
    for copy in copies:
        copy.start()
    for copy in copies:
        copy.wait()


def turns(experts):
    return [0] + list(range(experts - 1, 0, -1))


def hot_rows(picks, tok_rows):
    return lax.broadcasted_iota(jnp.int32, (tok_rows, picks.shape[1]), 0) == picks


def modulate(picks, tok_ref, table_ref):
    hot = hot_rows(picks, tok_ref.shape[0]).astype(F32).astype(BF16)
    values = lax.dot_general(hot, tok_ref[...], (((0,), (0,)), ((), ())), preferred_element_type=F32)
    center = values - jnp.mean(values, axis=1, keepdims=True)
    spread = jnp.mean(center * center, axis=1, keepdims=True)
    normed = center * (1.0 / jnp.sqrt(spread + 1e-06))
    return (normed * table_ref[0:1, :] + table_ref[1:2, :]).astype(BF16)


def first_kernel(info_ref, *refs):
    sources = refs[:7]
    far_ref, tok_ref, table_ref, picks_ref, weights_ref = refs[7:12]
    pick_ref, comb_ref, count_ref, shift_ref, scale_ref, gate_ref, sems = refs[12:]
    fetch(
        list(zip(sources, (tok_ref, pick_ref, shift_ref, scale_ref, gate_ref, comb_ref, count_ref))),
        sems,
    )
    experts, slots = pick_ref.shape
    which = pl.ds(info_ref[0], 1)
    table_ref[0:1, :] = 1.0 + scale_ref[which, :]
    table_ref[1:2, :] = shift_ref[which, :]
    table_ref[2:3, :] = gate_ref[which, :]
    lanes = lax.broadcasted_iota(jnp.int32, (1, slots), 1)
    for i, d in enumerate(turns(experts)):
        e = info_ref[1] ^ d
        picks_ref[i:i + 1, :] = pick_ref[pl.ds(e, 1), :]
        weights_ref[i:i + 1, :] = jnp.where(lanes < count_ref[0, e], comb_ref[pl.ds(e, 1), :], 0.0)
    far_ref[...] = modulate(picks_ref[1:2, :], tok_ref, table_ref)


def first(info, tokens, pick, shift, scale, gate, comb, count):
    experts, slots = pick.shape
    width = tokens.shape[1]
    return pl.pallas_call(
        first_kernel,
        in_specs=[SMEM] + [HBM] * 7,
        out_specs=[VMEM] * 5,
        out_shape=[
            jax.ShapeDtypeStruct((slots, width), BF16),
            jax.ShapeDtypeStruct(tokens.shape, BF16),
            jax.ShapeDtypeStruct((3, width), F32),
            jax.ShapeDtypeStruct(pick.shape, jnp.int32),
            jax.ShapeDtypeStruct(comb.shape, F32),
        ],
        scratch_shapes=[
            pltpu.VMEM(pick.shape, jnp.int32),
            pltpu.VMEM(comb.shape, F32),
            pltpu.SMEM(count.shape, jnp.int32),
            pltpu.VMEM(shift.shape, F32),
            pltpu.VMEM(scale.shape, F32),
            pltpu.VMEM(gate.shape, F32),
            pltpu.SemaphoreType.DMA((7,)),
        ],
        compiler_params=params(8),
        cost_estimate=BUSY,
        name="first",
    )(info, tokens, pick, shift, scale, gate, comb, count)


def rest_kernel(tok_ref, table_ref, picks_ref, *outs):
    experts, slots = picks_ref.shape
    order = [0] + list(range(2, experts))
    picks = jnp.concatenate([picks_ref[i:i + 1, :] for i in order], axis=1)
    rows = modulate(picks, tok_ref, table_ref)
    for i, out in enumerate(outs):
        out[...] = rows[i * slots:(i + 1) * slots]


def rest(tok, table, picks):
    experts, slots = picks.shape
    return pl.pallas_call(
        rest_kernel,
        in_specs=[VMEM] * 3,
        out_specs=[VMEM] * (experts - 1),
        out_shape=[jax.ShapeDtypeStruct((slots, tok.shape[1]), BF16)] * (experts - 1),
        compiler_params=params(8),
        cost_estimate=BUSY,
        name="rest",
    )(tok, table, picks)


def mixer_kernel(picks_ref, weights_ref, after_ref, *outs):
    for i, out in enumerate(outs):
        each = picks_ref.shape[0] // len(outs)
        rows = range(i * each, (i + 1) * each)
        picks = jnp.concatenate([picks_ref[r:r + 1, :] for r in rows], axis=1)
        weights = jnp.concatenate([weights_ref[r:r + 1, :] for r in rows], axis=1)
        mix = jnp.where(hot_rows(picks, out.shape[0]), weights, 0.0)
        high = mix.astype(BF16).astype(F32)
        out[...] = jnp.concatenate([high, mix - high], axis=1).astype(BF16)


def mixer(picks, weights, after, tok_rows):
    experts, slots = picks.shape
    return pl.pallas_call(
        mixer_kernel,
        in_specs=[VMEM] * 2 + [ANY],
        out_specs=[VMEM] * 2,
        out_shape=[jax.ShapeDtypeStruct((tok_rows, experts * slots), BF16)] * 2,
        compiler_params=params(4),
        cost_estimate=BUSY,
        name="mixer",
    )(picks, weights, after)


def join_kernel(*refs, count):
    out_ref = refs[-1]
    at = 0
    for ref in refs[:count]:
        out_ref[at:at + ref.shape[0], :] = ref[...]
        at += ref.shape[0]


def join(parts, after):
    return pl.pallas_call(
        functools.partial(join_kernel, count=len(parts)),
        in_specs=[VMEM] * len(parts) + [ANY] * len(after),
        out_specs=VMEM,
        out_shape=jax.ShapeDtypeStruct((sum(p.shape[0] for p in parts), parts[0].shape[1]), BF16),
        compiler_params=params(2),
        cost_estimate=FREE,
        name="join",
    )(*parts, *after)


def up_kernel(*refs, sources, count):
    w_ref, out_ref, rows_ref = refs[count:]
    to = 0
    for source, low, high in sources:
        rows_ref[to:to + high - low, :] = refs[source][low:high, :]
        to += high - low
    hidden = w_ref.shape[0]
    tile = min(512, hidden)

    @pl.loop(0, hidden // tile)
    def _(i):
        cut = pl.ds(pl.multiple_of(i * tile, tile), tile)
        lifted = lax.dot_general(
            rows_ref[...], w_ref[cut, :], (((1,), (1,)), ((), ())), preferred_element_type=F32
        )
        out_ref[:, cut] = jax.nn.gelu(lifted, approximate=True).astype(BF16)


def up(parts, sources, w):
    hidden, width = w.shape
    rows = sum(high - low for _, low, high in sources)
    return pl.pallas_call(
        functools.partial(up_kernel, sources=sources, count=len(parts)),
        in_specs=[VMEM] * (len(parts) + 1),
        out_specs=VMEM,
        out_shape=jax.ShapeDtypeStruct((rows, hidden), BF16),
        scratch_shapes=[pltpu.VMEM((rows, width), BF16)],
        compiler_params=params(8),
        cost_estimate=FREE,
        name="up",
    )(*parts, w)


def down_kernel(h_ref, w_ref, keep_ref, send_ref, *, columns):
    half = keep_ref.shape[0]
    first, last, tile = columns

    @pl.loop(0, (last - first) // tile)
    def _(i):
        cut = pl.ds(pl.multiple_of(i * tile, tile), tile)
        from_ = pl.ds(pl.multiple_of(first + i * tile, tile), tile)
        out = jnp.dot(h_ref[...], w_ref[:, from_], preferred_element_type=F32)
        keep_ref[:, cut] = out[:half]
        send_ref[:, cut] = out[half:].astype(BF16)


def down(hid, w, columns):
    half = hid.shape[0] // 2
    step = columns[1] - columns[0]
    return pl.pallas_call(
        functools.partial(down_kernel, columns=columns),
        in_specs=[VMEM] * 2,
        out_specs=[VMEM] * 2,
        out_shape=[
            jax.ShapeDtypeStruct((half, step), F32),
            jax.ShapeDtypeStruct((half, step), BF16),
        ],
        compiler_params=params(8),
        cost_estimate=FREE,
        name="down",
    )(hid, w)


def add_kernel(*refs, count, outs):
    for ref, pieces in zip(refs[2 * count:], outs):
        at = 0
        for i, low, high in pieces:
            keep_ref, got_ref = refs[2 * i:2 * i + 2]
            step = keep_ref.shape[1]
            total = keep_ref[low:high] + got_ref[low:high].astype(F32)
            ref[:, at:at + step] = total.astype(ref.dtype)
            at += step


def add(pairs, outs, kinds):
    args = [x for pair in pairs for x in pair]
    shapes = [
        (pieces[0][2] - pieces[0][1], sum(pairs[i][0].shape[1] for i, _, _ in pieces))
        for pieces in outs
    ]
    return pl.pallas_call(
        functools.partial(add_kernel, count=len(pairs), outs=outs),
        in_specs=[VMEM] * len(args),
        out_specs=[VMEM] * len(outs),
        out_shape=[jax.ShapeDtypeStruct(shape, k) for shape, k in zip(shapes, kinds)],
        compiler_params=params(8),
        cost_estimate=FREE,
        name="add",
    )(*args)


def own_kernel(mix_ref, keep_ref, near_ref, got_ref, acc_ref):
    own = (keep_ref[...] + near_ref[...].astype(F32)).astype(BF16)
    values = jnp.concatenate([own, got_ref[...]] * 2, axis=0)
    acc_ref[...] = jnp.dot(mix_ref[...], values, preferred_element_type=F32)


def own_part(mix, keep, near, got):
    return pl.pallas_call(
        own_kernel,
        in_specs=[VMEM] * 4,
        out_specs=VMEM,
        out_shape=jax.ShapeDtypeStruct((mix.shape[0], keep.shape[1]), F32),
        compiler_params=params(12),
        cost_estimate=FREE,
        name="own_part",
    )(mix, keep, near, got)


def post_kernel(mix_ref, table_ref, acc_ref, *refs):
    blocks = refs[:-3]
    out_hbm, out_ref, sems = refs[-3:]
    step = out_ref.shape[1] // sems.shape[0]
    copies = []
    for i in range(sems.shape[0]):
        cut = pl.ds(i * step, step)
        values = jnp.concatenate([ref[:, cut] for ref in blocks] * 2, axis=0)
        mixed = acc_ref[:, cut] + jnp.dot(mix_ref[...], values, preferred_element_type=F32)
        out_ref[:, cut] = (table_ref[2:3, cut] * mixed).astype(BF16)
        copy = pltpu.make_async_copy(out_ref.at[:, cut], out_hbm.at[:, cut], sems.at[i])
        copy.start()
        copies.append(copy)
    for copy in copies:
        copy.wait()


def post(mix, table, acc, blocks):
    tok_rows, width = acc.shape
    return pl.pallas_call(
        post_kernel,
        in_specs=[VMEM] * (3 + len(blocks)),
        out_specs=HBM,
        out_shape=jax.ShapeDtypeStruct((tok_rows, width), BF16),
        scratch_shapes=[pltpu.VMEM((tok_rows, width), BF16), pltpu.SemaphoreType.DMA((4,))],
        compiler_params=params(8),
        cost_estimate=FREE,
        name="post",
    )(mix, table, acc, *blocks)


def shards(tokens, shift, scale, gate, w_up, w_down, pick, count, combine):
    tok_rows, width = tokens.shape
    _, experts, slots = pick.shape
    devices = lax.axis_size("expert")
    place = lax.axis_index("expert")
    group = devices // experts
    requests = shift.shape[0]
    hidden = w_up.shape[0]
    info = jnp.stack([place // (devices // requests), place // group]).astype(jnp.int32)
    pick = pick[0]
    comb = combine[0]

    far = [d * group for d in turns(experts)[1:]]
    near = []
    bit = group // 2
    while bit:
        near.append(bit)
        bit //= 2

    def swap(x, mask):
        return lax.ppermute(x, "expert", [(i, i ^ mask) for i in range(devices)])

    tokens, shift, scale, gate, pick, comb, count = [
        pltpu.with_memory_space_constraint(x, pltpu.HBM)
        for x in (tokens, shift, scale, gate, pick, comb, count)
    ]
    half = hidden // 2
    farthest, tok, table, picks, weights = first(info, tokens, pick, shift, scale, gate, comb, count)
    own, *others = rest(tok, table, picks)

    flat = [farthest] + others
    blocks = [own] + [swap(x, mask) for x, mask in zip(flat, far)]
    mixes = mixer(picks, weights, blocks[1], tok_rows)
    blocks[2] = join([blocks[2]], [mixes[0]])
    beside = [swap(block, near[0]) for block in blocks]
    beside[-1] = join([beside[-1]], [])
    early, late = list(range(experts // 2)), list(range(experts // 2, experts))
    parts = []
    sources = []
    for members in (early, late):
        pieces = [join([x for i in members for x in (blocks[i], beside[i])], [])]
        height = pieces[0].shape[0]
        for mask in near[1:]:
            block = pieces[0] if len(pieces) == 1 else join(pieces, [])
            pieces = [block, swap(block, mask)]
        cuts = []
        for piece in pieces:
            cuts += [(len(parts), at, at + height) for at in range(0, piece.shape[0], height)]
            parts.append(piece)
        sources.append(cuts)
    sources = [cut for pair in zip(*sources) for cut in pair]

    hid = up(parts, sources, w_up)

    step = 5 * width // 8
    keep_a, send_a = down(hid, w_down, (0, step, step // 2))
    keep_b, send_b = down(hid, w_down, (step, width, (width - step) // 3))
    pairs = []
    for keep, send in ((keep_a, send_a), (keep_b, send_b)):
        for i, mask in enumerate(reversed(near[1:])):
            if i:
                middle = keep.shape[0] // 2
                keep, send = add(
                    [(keep, got)], [[(0, 0, middle)], [(0, middle, 2 * middle)]], [F32, BF16]
                )
            if pairs:
                send = join([send], [pairs[0][1]])
            got = swap(send, mask)
        pairs.append((keep, got))

    def outs(side):
        rows = [(2 * i + side) * slots for i in range(experts)]
        return [[(piece, at, at + slots) for piece in range(len(pairs))] for at in rows]

    sums = add(pairs, outs(1) + outs(0), [BF16] * experts + [F32] * experts)
    sends, keeps = sums[:experts], sums[experts:]
    back = {}
    for i in range(1, experts):
        got = swap(sends[i], near[0])
        (part,) = add([(keeps[i], got)], [[(0, 0, slots)]], [BF16])
        back[i] = swap(part, far[i - 1])
        if i == 1:
            own_send = join(sends[:1], [part])
    got = swap(own_send, near[0])
    acc = own_part(mixes[0], keeps[0], got, back[1])
    return post(mixes[1], table, acc, [back[i] for i in range(2, experts)])


def solution(mesh):
    return jax.shard_map(
        shards,
        mesh=mesh,
        in_specs=(
            P(("groups", "expert"), None),
            P("groups", None),
            P("groups", None),
            P("groups", None),
            P("expert", None),
            P("expert", None),
            P(("groups", "expert"), None, None),
            P(("groups", "expert"), None),
            P(("groups", "expert"), None, None),
        ),
        out_specs=P(("groups", "expert"), None),
        check_vma=False,
    )
```

```python
import functools

import jax
import jax.numpy as jnp
from jax import lax
from jax.experimental import pallas as pl
from jax.experimental.pallas import tpu as pltpu
from jax.sharding import PartitionSpec as P

MIB = 1024 * 1024
F32 = jnp.float32
BF16 = jnp.bfloat16

SMEM = pl.BlockSpec(memory_space=pltpu.SMEM)
VMEM = pl.BlockSpec(memory_space=pltpu.VMEM)
HBM = pl.BlockSpec(memory_space=pltpu.HBM)
ANY = pl.BlockSpec(memory_space=pl.ANY)


FREE = pl.CostEstimate(flops=1, bytes_accessed=1, transcendentals=0)

BUSY = pl.CostEstimate(flops=4 * 10**10, bytes_accessed=128 * MIB, transcendentals=0)


def params(mib):
    return pltpu.CompilerParams(vmem_limit_bytes=mib * MIB)


def fetch(pairs, sems):
    copies = [pltpu.make_async_copy(src, dst, sems.at[i]) for i, (src, dst) in enumerate(pairs)]
    for copy in copies:
        copy.start()
    for copy in copies:
        copy.wait()


def turns(experts):
    return [0] + list(range(experts - 1, 0, -1))


def hot_rows(picks, tok_rows):
    return lax.broadcasted_iota(jnp.int32, (tok_rows, picks.shape[1]), 0) == picks


def modulate(picks, tok_ref, table_ref):
    hot = hot_rows(picks, tok_ref.shape[0]).astype(F32).astype(BF16)
    values = lax.dot_general(hot, tok_ref[...], (((0,), (0,)), ((), ())), preferred_element_type=F32)
    center = values - jnp.mean(values, axis=1, keepdims=True)
    spread = jnp.mean(center * center, axis=1, keepdims=True)
    normed = center * (1.0 / jnp.sqrt(spread + 1e-06))
    return (normed * table_ref[0:1, :] + table_ref[1:2, :]).astype(BF16)


def first_kernel(info_ref, *refs):
    sources = refs[:7]
    far_ref, tok_ref, table_ref, picks_ref, weights_ref = refs[7:12]
    pick_ref, comb_ref, count_ref, shift_ref, scale_ref, gate_ref, sems = refs[12:]
    fetch(
        list(zip(sources, (tok_ref, pick_ref, shift_ref, scale_ref, gate_ref, comb_ref, count_ref))),
        sems,
    )
    experts, slots = pick_ref.shape
    which = pl.ds(info_ref[0], 1)
    table_ref[0:1, :] = 1.0 + scale_ref[which, :]
    table_ref[1:2, :] = shift_ref[which, :]
    table_ref[2:3, :] = gate_ref[which, :]
    lanes = lax.broadcasted_iota(jnp.int32, (1, slots), 1)
    for i, d in enumerate(turns(experts)):
        e = info_ref[1] ^ d
        picks_ref[i:i + 1, :] = pick_ref[pl.ds(e, 1), :]
        weights_ref[i:i + 1, :] = jnp.where(lanes < count_ref[0, e], comb_ref[pl.ds(e, 1), :], 0.0)
    far_ref[...] = modulate(picks_ref[1:2, :], tok_ref, table_ref)


def first(info, tokens, pick, shift, scale, gate, comb, count):
    experts, slots = pick.shape
    width = tokens.shape[1]
    return pl.pallas_call(
        first_kernel,
        in_specs=[SMEM] + [HBM] * 7,
        out_specs=[VMEM] * 5,
        out_shape=[
            jax.ShapeDtypeStruct((slots, width), BF16),
            jax.ShapeDtypeStruct(tokens.shape, BF16),
            jax.ShapeDtypeStruct((3, width), F32),
            jax.ShapeDtypeStruct(pick.shape, jnp.int32),
            jax.ShapeDtypeStruct(comb.shape, F32),
        ],
        scratch_shapes=[
            pltpu.VMEM(pick.shape, jnp.int32),
            pltpu.VMEM(comb.shape, F32),
            pltpu.SMEM(count.shape, jnp.int32),
            pltpu.VMEM(shift.shape, F32),
            pltpu.VMEM(scale.shape, F32),
            pltpu.VMEM(gate.shape, F32),
            pltpu.SemaphoreType.DMA((7,)),
        ],
        compiler_params=params(8),
        cost_estimate=FREE,
        name="first",
    )(info, tokens, pick, shift, scale, gate, comb, count)


def rest_kernel(tok_ref, table_ref, picks_ref, *outs):
    experts, slots = picks_ref.shape
    order = [0] + list(range(2, experts))
    picks = jnp.concatenate([picks_ref[i:i + 1, :] for i in order], axis=1)
    rows = modulate(picks, tok_ref, table_ref)
    for i, out in enumerate(outs):
        out[...] = rows[i * slots:(i + 1) * slots]


def rest(tok, table, picks):
    experts, slots = picks.shape
    return pl.pallas_call(
        rest_kernel,
        in_specs=[VMEM] * 3,
        out_specs=[VMEM] * (experts - 1),
        out_shape=[jax.ShapeDtypeStruct((slots, tok.shape[1]), BF16)] * (experts - 1),
        compiler_params=params(8),
        cost_estimate=BUSY,
        name="rest",
    )(tok, table, picks)


def mixer_kernel(picks_ref, weights_ref, after_ref, *outs):
    for i, out in enumerate(outs):
        each = picks_ref.shape[0] // len(outs)
        rows = range(i * each, (i + 1) * each)
        picks = jnp.concatenate([picks_ref[r:r + 1, :] for r in rows], axis=1)
        weights = jnp.concatenate([weights_ref[r:r + 1, :] for r in rows], axis=1)
        mix = jnp.where(hot_rows(picks, out.shape[0]), weights, 0.0)
        high = mix.astype(BF16).astype(F32)
        out[...] = jnp.concatenate([high, mix - high], axis=1).astype(BF16)


def mixer(picks, weights, after, tok_rows):
    experts, slots = picks.shape
    return pl.pallas_call(
        mixer_kernel,
        in_specs=[VMEM] * 2 + [ANY],
        out_specs=[VMEM] * 2,
        out_shape=[jax.ShapeDtypeStruct((tok_rows, experts * slots), BF16)] * 2,
        compiler_params=params(4),
        cost_estimate=FREE,
        name="mixer",
    )(picks, weights, after)


def join_kernel(*refs, count):
    out_ref = refs[-1]
    at = 0
    for ref in refs[:count]:
        out_ref[at:at + ref.shape[0], :] = ref[...]
        at += ref.shape[0]


def join(parts, after):
    return pl.pallas_call(
        functools.partial(join_kernel, count=len(parts)),
        in_specs=[VMEM] * len(parts) + [ANY] * len(after),
        out_specs=VMEM,
        out_shape=jax.ShapeDtypeStruct((sum(p.shape[0] for p in parts), parts[0].shape[1]), BF16),
        compiler_params=params(2),
        cost_estimate=FREE,
        name="join",
    )(*parts, *after)


def up_kernel(*refs, sources, count):
    w_ref = refs[count]
    out_ref, rows_ref = refs[-2:]
    to = 0
    for source, low, high in sources:
        rows_ref[to:to + high - low, :] = refs[source][low:high, :]
        to += high - low
    hidden = w_ref.shape[0]
    tile = min(512, hidden)

    @pl.loop(0, hidden // tile)
    def _(i):
        cut = pl.ds(pl.multiple_of(i * tile, tile), tile)
        lifted = lax.dot_general(
            rows_ref[...], w_ref[cut, :], (((1,), (1,)), ((), ())), preferred_element_type=F32
        )
        out_ref[:, cut] = jax.nn.gelu(lifted, approximate=True).astype(BF16)


def up(parts, sources, w, after):
    hidden, width = w.shape
    rows = sum(high - low for _, low, high in sources)
    return pl.pallas_call(
        functools.partial(up_kernel, sources=sources, count=len(parts)),
        in_specs=[VMEM] * (len(parts) + 1) + [ANY] * len(after),
        out_specs=VMEM,
        out_shape=jax.ShapeDtypeStruct((rows, hidden), BF16),
        scratch_shapes=[pltpu.VMEM((rows, width), BF16)],
        compiler_params=params(8),
        cost_estimate=FREE,
        name="up",
    )(*parts, w, *after)


def down_kernel(h_ref, w_ref, *refs, columns, groups):
    outs = refs[len(refs) - 2 * groups:]
    first, last, tile = columns
    height = h_ref.shape[0] // groups

    @pl.loop(0, (last - first) // tile)
    def _(i):
        cut = pl.ds(pl.multiple_of(first + i * tile, tile), tile)
        out = jnp.dot(h_ref[...], w_ref[:, cut], preferred_element_type=F32)
        for g in range(groups):
            middle = g * height + height // 2
            outs[2 * g][:, cut] = out[middle - height // 2:middle]
            outs[2 * g + 1][:, cut] = out[middle:middle + height // 2].astype(BF16)


def down(hid, w, columns, groups, after, before):
    half = hid.shape[0] // groups // 2
    width = w.shape[1]
    skip = 2 + len(after)
    return pl.pallas_call(
        functools.partial(down_kernel, columns=columns, groups=groups),
        in_specs=[VMEM] * 2 + [ANY] * len(after) + [VMEM] * len(before),
        out_specs=[VMEM] * (2 * groups),
        out_shape=[
            jax.ShapeDtypeStruct((half, width), F32),
            jax.ShapeDtypeStruct((half, width), BF16),
        ]
        * groups,
        input_output_aliases={skip + i: i for i in range(len(before))},
        compiler_params=params(8),
        cost_estimate=FREE,
        name="down",
    )(hid, w, *after, *before)


def add_kernel(keep_ref, got_ref, *refs, cuts):
    for ref, (low, high) in zip(refs[len(refs) - len(cuts):], cuts):
        ref[...] = (keep_ref[low:high] + got_ref[low:high].astype(F32)).astype(ref.dtype)


def add(keep, got, cuts, kinds, after=()):
    width = keep.shape[1]
    return pl.pallas_call(
        functools.partial(add_kernel, cuts=cuts),
        in_specs=[VMEM] * 2 + [ANY] * len(after),
        out_specs=[VMEM] * len(cuts),
        out_shape=[
            jax.ShapeDtypeStruct((high - low, width), k) for (low, high), k in zip(cuts, kinds)
        ],
        compiler_params=params(8),
        cost_estimate=FREE,
        name="add",
    )(keep, got, *after)


def own_kernel(mix_ref, keep_ref, near_ref, got_ref, acc_ref):
    own = (keep_ref[...] + near_ref[...].astype(F32)).astype(BF16)
    values = jnp.concatenate([own, got_ref[...]] * 2, axis=0)
    acc_ref[...] = jnp.dot(mix_ref[...], values, preferred_element_type=F32)


def own_part(mix, keep, near, got):
    return pl.pallas_call(
        own_kernel,
        in_specs=[VMEM] * 4,
        out_specs=VMEM,
        out_shape=jax.ShapeDtypeStruct((mix.shape[0], keep.shape[1]), F32),
        compiler_params=params(12),
        cost_estimate=FREE,
        name="own_part",
    )(mix, keep, near, got)


def post_kernel(mix_ref, table_ref, acc_ref, *refs):
    blocks = refs[:-3]
    out_hbm, out_ref, sems = refs[-3:]
    step = out_ref.shape[1] // sems.shape[0]
    copies = []
    for i in range(sems.shape[0]):
        cut = pl.ds(i * step, step)
        values = jnp.concatenate([ref[:, cut] for ref in blocks] * 2, axis=0)
        mixed = acc_ref[:, cut] + jnp.dot(mix_ref[...], values, preferred_element_type=F32)
        out_ref[:, cut] = (table_ref[2:3, cut] * mixed).astype(BF16)
        copy = pltpu.make_async_copy(out_ref.at[:, cut], out_hbm.at[:, cut], sems.at[i])
        copy.start()
        copies.append(copy)
    for copy in copies:
        copy.wait()


def post(mix, table, acc, blocks):
    tok_rows, width = acc.shape
    return pl.pallas_call(
        post_kernel,
        in_specs=[VMEM] * (3 + len(blocks)),
        out_specs=HBM,
        out_shape=jax.ShapeDtypeStruct((tok_rows, width), BF16),
        scratch_shapes=[pltpu.VMEM((tok_rows, width), BF16), pltpu.SemaphoreType.DMA((4,))],
        compiler_params=params(8),
        cost_estimate=FREE,
        name="post",
    )(mix, table, acc, *blocks)


def shards(tokens, shift, scale, gate, w_up, w_down, pick, count, combine):
    tok_rows, width = tokens.shape
    _, experts, slots = pick.shape
    devices = lax.axis_size("expert")
    place = lax.axis_index("expert")
    group = devices // experts
    requests = shift.shape[0]
    hidden = w_up.shape[0]
    info = jnp.stack([place // (devices // requests), place // group]).astype(jnp.int32)
    pick = pick[0]
    comb = combine[0]

    far = [d * group for d in turns(experts)[1:]]
    near = []
    bit = group // 2
    while bit:
        near.append(bit)
        bit //= 2

    def swap(x, mask):
        return lax.ppermute(x, "expert", [(i, i ^ mask) for i in range(devices)])

    tokens, shift, scale, gate, pick, comb, count = [
        pltpu.with_memory_space_constraint(x, pltpu.HBM)
        for x in (tokens, shift, scale, gate, pick, comb, count)
    ]
    farthest, tok, table, picks, weights = first(info, tokens, pick, shift, scale, gate, comb, count)
    own, *others = rest(tok, table, picks)

    flat = [farthest] + others
    blocks = [own] + [swap(x, mask) for x, mask in zip(flat, far)]
    mixes = mixer(picks, weights, blocks[1], tok_rows)
    blocks[2] = join([blocks[2]], [mixes[0]])
    beside = [swap(block, near[0]) for block in blocks]
    beside[-1] = join([beside[-1]], [])
    early, late = list(range(experts // 2)), list(range(experts // 2, experts))

    def spread(members, after=()):
        pieces = [join([x for i in members for x in (blocks[i], beside[i])], after)]
        for mask in near[1:]:
            block = pieces[0] if len(pieces) == 1 else join(pieces, [])
            pieces = [block, swap(block, mask)]
        return pieces, [(k, 0, piece.shape[0]) for k, piece in enumerate(pieces)]

    def gather(keep, send, members, after=()):
        for i, mask in enumerate(reversed(near[1:])):
            if i:
                middle = keep.shape[0] // 2
                keep, send = add(keep, got, [(0, middle), (middle, 2 * middle)], [F32, BF16])
            got = swap(send, mask)
        at = [2 * k * slots for k in range(len(members))]
        cuts = [(x + slots, x + 2 * slots) for x in at] + [(x, x + slots) for x in at]
        out = add(keep, got, cuts, [BF16] * len(at) + [F32] * len(at), after)
        return dict(zip(members, zip(out, out[len(at):])))

    def total(i):
        send, keep = block[i]
        return add(keep, swap(send, near[0]), [(0, slots)], [BF16])[0]

    def rows_of(*groups, after=()):
        parts, cuts = [], []
        for members in groups:
            pieces, taken = spread(members, after)
            cuts += [(len(parts) + k, low, high) for k, low, high in taken]
            parts += pieces
        return parts, cuts

    width_a = 7 * width // 8
    links = [blocks[2], blocks[3]]
    parts, sources = rows_of([1], after=links)
    own_parts, own_sources = rows_of([0])
    sources = sources + [(len(parts) + k, low, high) for k, low, high in own_sources]
    hid = up(parts + own_parts, sources, w_up, [])
    keep, send, keep_own, send_own = down(hid, w_down, (0, width, min(1024, width)), 2, [], [])
    hid_late = up(*rows_of(late, after=[hid]), w_up, [keep])
    block = gather(keep, send, [1], [hid_late])
    hid = hid_late
    before = down(hid, w_down, (0, width_a, width_a // 4), 1, [block[1][0]], [])
    part = total(1)
    keep, send = down(hid, w_down, (width_a, width, width - width_a), 1, [part], before)
    block.update(gather(keep, send, late))
    block.update(gather(keep_own, send_own, [0]))
    back = {1: swap(part, far[0])}
    link = back[1]
    link = join([link], [])

    for i in late:
        part = total(i)
        if i == 2:
            part = join([part], [link])
        back[i] = swap(part, far[i - 1])
    send, keep = block[0]
    acc = own_part(mixes[0], keep, swap(send, near[0]), back[1])
    return post(mixes[1], table, acc, [back[i] for i in late])


def solution(mesh):
    return jax.shard_map(
        shards,
        mesh=mesh,
        in_specs=(
            P(("groups", "expert"), None),
            P("groups", None),
            P("groups", None),
            P("groups", None),
            P("expert", None),
            P("expert", None),
            P(("groups", "expert"), None, None),
            P(("groups", "expert"), None),
            P(("groups", "expert"), None, None),
        ),
        out_specs=P(("groups", "expert"), None),
        check_vma=False,
    )
```

```python
import functools

import jax
import jax.numpy as jnp
from jax import lax
from jax.experimental import pallas as pl
from jax.experimental.pallas import tpu as pltpu
from jax.sharding import PartitionSpec as P

MIB = 1024 * 1024
F32 = jnp.float32
BF16 = jnp.bfloat16

SMEM = pl.BlockSpec(memory_space=pltpu.SMEM)
VMEM = pl.BlockSpec(memory_space=pltpu.VMEM)
HBM = pl.BlockSpec(memory_space=pltpu.HBM)
ANY = pl.BlockSpec(memory_space=pl.ANY)


FREE = pl.CostEstimate(flops=1, bytes_accessed=1, transcendentals=0)

BUSY = pl.CostEstimate(flops=4 * 10**10, bytes_accessed=128 * MIB, transcendentals=0)


def params(mib):
    return pltpu.CompilerParams(vmem_limit_bytes=mib * MIB)


def fetch(pairs, sems):
    copies = [pltpu.make_async_copy(src, dst, sems.at[i]) for i, (src, dst) in enumerate(pairs)]
    for copy in copies:
        copy.start()
    for copy in copies:
        copy.wait()


def turns(experts):
    return [0] + list(range(experts - 1, 0, -1))


def hot_rows(picks, tok_rows):
    return lax.broadcasted_iota(jnp.int32, (tok_rows, picks.shape[1]), 0) == picks


def modulate(picks, tok_ref, table_ref):
    hot = hot_rows(picks, tok_ref.shape[0]).astype(F32).astype(BF16)
    values = lax.dot_general(hot, tok_ref[...], (((0,), (0,)), ((), ())), preferred_element_type=F32)
    center = values - jnp.mean(values, axis=1, keepdims=True)
    spread = jnp.mean(center * center, axis=1, keepdims=True)
    normed = center * (1.0 / jnp.sqrt(spread + 1e-06))
    return (normed * table_ref[0:1, :] + table_ref[1:2, :]).astype(BF16)


def first_kernel(info_ref, *refs):
    sources = refs[:7]
    far_ref, tok_ref, table_ref, picks_ref, weights_ref = refs[7:12]
    pick_ref, comb_ref, count_ref, shift_ref, scale_ref, gate_ref, sems = refs[12:]
    fetch(
        list(zip(sources, (tok_ref, pick_ref, shift_ref, scale_ref, gate_ref, comb_ref, count_ref))),
        sems,
    )
    experts, slots = pick_ref.shape
    which = pl.ds(info_ref[0], 1)
    table_ref[0:1, :] = 1.0 + scale_ref[which, :]
    table_ref[1:2, :] = shift_ref[which, :]
    table_ref[2:3, :] = gate_ref[which, :]
    lanes = lax.broadcasted_iota(jnp.int32, (1, slots), 1)
    for i, d in enumerate(turns(experts)):
        e = info_ref[1] ^ d
        picks_ref[i:i + 1, :] = pick_ref[pl.ds(e, 1), :]
        weights_ref[i:i + 1, :] = jnp.where(lanes < count_ref[0, e], comb_ref[pl.ds(e, 1), :], 0.0)
    far_ref[...] = modulate(picks_ref[1:2, :], tok_ref, table_ref)


def first(info, tokens, pick, shift, scale, gate, comb, count):
    experts, slots = pick.shape
    width = tokens.shape[1]
    return pl.pallas_call(
        first_kernel,
        in_specs=[SMEM] + [HBM] * 7,
        out_specs=[VMEM] * 5,
        out_shape=[
            jax.ShapeDtypeStruct((slots, width), BF16),
            jax.ShapeDtypeStruct(tokens.shape, BF16),
            jax.ShapeDtypeStruct((3, width), F32),
            jax.ShapeDtypeStruct(pick.shape, jnp.int32),
            jax.ShapeDtypeStruct(comb.shape, F32),
        ],
        scratch_shapes=[
            pltpu.VMEM(pick.shape, jnp.int32),
            pltpu.VMEM(comb.shape, F32),
            pltpu.SMEM(count.shape, jnp.int32),
            pltpu.VMEM(shift.shape, F32),
            pltpu.VMEM(scale.shape, F32),
            pltpu.VMEM(gate.shape, F32),
            pltpu.SemaphoreType.DMA((7,)),
        ],
        compiler_params=params(8),
        cost_estimate=FREE,
        name="first",
    )(info, tokens, pick, shift, scale, gate, comb, count)


def rest_kernel(tok_ref, table_ref, picks_ref, *outs):
    experts, slots = picks_ref.shape
    order = [0] + list(range(2, experts))
    picks = jnp.concatenate([picks_ref[i:i + 1, :] for i in order], axis=1)
    rows = modulate(picks, tok_ref, table_ref)
    for i, out in enumerate(outs):
        out[...] = rows[i * slots:(i + 1) * slots]


def rest(tok, table, picks):
    experts, slots = picks.shape
    return pl.pallas_call(
        rest_kernel,
        in_specs=[VMEM] * 3,
        out_specs=[VMEM] * (experts - 1),
        out_shape=[jax.ShapeDtypeStruct((slots, tok.shape[1]), BF16)] * (experts - 1),
        compiler_params=params(8),
        cost_estimate=BUSY,
        name="rest",
    )(tok, table, picks)


def mixer_kernel(picks_ref, weights_ref, after_ref, *outs):
    for i, out in enumerate(outs):
        each = picks_ref.shape[0] // len(outs)
        rows = range(i * each, (i + 1) * each)
        picks = jnp.concatenate([picks_ref[r:r + 1, :] for r in rows], axis=1)
        weights = jnp.concatenate([weights_ref[r:r + 1, :] for r in rows], axis=1)
        mix = jnp.where(hot_rows(picks, out.shape[0]), weights, 0.0)
        high = mix.astype(BF16).astype(F32)
        out[...] = jnp.concatenate([high, mix - high], axis=1).astype(BF16)


def mixer(picks, weights, after, tok_rows):
    experts, slots = picks.shape
    return pl.pallas_call(
        mixer_kernel,
        in_specs=[VMEM] * 2 + [ANY],
        out_specs=[VMEM] * 2,
        out_shape=[jax.ShapeDtypeStruct((tok_rows, experts * slots), BF16)] * 2,
        compiler_params=params(4),
        cost_estimate=FREE,
        name="mixer",
    )(picks, weights, after)


def join_kernel(*refs, count):
    out_ref = refs[-1]
    at = 0
    for ref in refs[:count]:
        out_ref[at:at + ref.shape[0], :] = ref[...]
        at += ref.shape[0]


def join(parts, after):
    return pl.pallas_call(
        functools.partial(join_kernel, count=len(parts)),
        in_specs=[VMEM] * len(parts) + [ANY] * len(after),
        out_specs=VMEM,
        out_shape=jax.ShapeDtypeStruct((sum(p.shape[0] for p in parts), parts[0].shape[1]), BF16),
        compiler_params=params(2),
        cost_estimate=FREE,
        name="join",
    )(*parts, *after)


def up_kernel(*refs, sources, count):
    w_ref = refs[count]
    out_ref, rows_ref = refs[-2:]
    to = 0
    for source, low, high in sources:
        rows_ref[to:to + high - low, :] = refs[source][low:high, :]
        to += high - low
    hidden = w_ref.shape[0]
    tile = min(512, hidden)

    @pl.loop(0, hidden // tile)
    def _(i):
        cut = pl.ds(pl.multiple_of(i * tile, tile), tile)
        lifted = lax.dot_general(
            rows_ref[...], w_ref[cut, :], (((1,), (1,)), ((), ())), preferred_element_type=F32
        )
        out_ref[:, cut] = jax.nn.gelu(lifted, approximate=True).astype(BF16)


def up(parts, sources, w, after):
    hidden, width = w.shape
    rows = sum(high - low for _, low, high in sources)
    return pl.pallas_call(
        functools.partial(up_kernel, sources=sources, count=len(parts)),
        in_specs=[VMEM] * (len(parts) + 1) + [ANY] * len(after),
        out_specs=VMEM,
        out_shape=jax.ShapeDtypeStruct((rows, hidden), BF16),
        scratch_shapes=[pltpu.VMEM((rows, width), BF16)],
        compiler_params=params(8),
        cost_estimate=FREE,
        name="up",
    )(*parts, w, *after)


def down_kernel(h_ref, w_ref, *refs, columns, low):
    keep_ref, send_ref = refs[-2:]
    first, last, tile = columns
    half = keep_ref.shape[0]

    @pl.loop(0, (last - first) // tile)
    def _(i):
        cut = pl.ds(pl.multiple_of(first + i * tile, tile), tile)
        out = jnp.dot(h_ref[low:low + 2 * half, :], w_ref[:, cut], preferred_element_type=F32)
        keep_ref[:, cut] = out[:half]
        send_ref[:, cut] = out[half:].astype(BF16)


def down(hid, rows, w, columns, after, before):
    half = (rows[1] - rows[0]) // 2
    width = w.shape[1]
    skip = 2 + len(after)
    return pl.pallas_call(
        functools.partial(down_kernel, columns=columns, low=rows[0]),
        in_specs=[VMEM] * 2 + [ANY] * len(after) + [VMEM] * len(before),
        out_specs=[VMEM] * 2,
        out_shape=[
            jax.ShapeDtypeStruct((half, width), F32),
            jax.ShapeDtypeStruct((half, width), BF16),
        ],
        input_output_aliases={skip + i: i for i in range(len(before))},
        compiler_params=params(8),
        cost_estimate=FREE,
        name="down",
    )(hid, w, *after, *before)


def add_kernel(keep_ref, got_ref, *refs, cuts):
    for ref, (low, high) in zip(refs[len(refs) - len(cuts):], cuts):
        ref[...] = (keep_ref[low:high] + got_ref[low:high].astype(F32)).astype(ref.dtype)


def add(keep, got, cuts, kinds, after=()):
    width = keep.shape[1]
    return pl.pallas_call(
        functools.partial(add_kernel, cuts=cuts),
        in_specs=[VMEM] * 2 + [ANY] * len(after),
        out_specs=[VMEM] * len(cuts),
        out_shape=[
            jax.ShapeDtypeStruct((high - low, width), k) for (low, high), k in zip(cuts, kinds)
        ],
        compiler_params=params(8),
        cost_estimate=FREE,
        name="add",
    )(keep, got, *after)


def own_kernel(mix_ref, keep_ref, near_ref, got_ref, acc_ref):
    own = (keep_ref[...] + near_ref[...].astype(F32)).astype(BF16)
    values = jnp.concatenate([own, got_ref[...]] * 2, axis=0)
    acc_ref[...] = jnp.dot(mix_ref[...], values, preferred_element_type=F32)


def own_part(mix, keep, near, got):
    return pl.pallas_call(
        own_kernel,
        in_specs=[VMEM] * 4,
        out_specs=VMEM,
        out_shape=jax.ShapeDtypeStruct((mix.shape[0], keep.shape[1]), F32),
        compiler_params=params(12),
        cost_estimate=FREE,
        name="own_part",
    )(mix, keep, near, got)


def post_kernel(mix_ref, table_ref, acc_ref, *refs):
    blocks = refs[:-3]
    out_hbm, out_ref, sems = refs[-3:]
    step = out_ref.shape[1] // sems.shape[0]
    copies = []
    for i in range(sems.shape[0]):
        cut = pl.ds(i * step, step)
        values = jnp.concatenate([ref[:, cut] for ref in blocks] * 2, axis=0)
        mixed = acc_ref[:, cut] + jnp.dot(mix_ref[...], values, preferred_element_type=F32)
        out_ref[:, cut] = (table_ref[2:3, cut] * mixed).astype(BF16)
        copy = pltpu.make_async_copy(out_ref.at[:, cut], out_hbm.at[:, cut], sems.at[i])
        copy.start()
        copies.append(copy)
    for copy in copies:
        copy.wait()


def post(mix, table, acc, blocks):
    tok_rows, width = acc.shape
    return pl.pallas_call(
        post_kernel,
        in_specs=[VMEM] * (3 + len(blocks)),
        out_specs=HBM,
        out_shape=jax.ShapeDtypeStruct((tok_rows, width), BF16),
        scratch_shapes=[pltpu.VMEM((tok_rows, width), BF16), pltpu.SemaphoreType.DMA((4,))],
        compiler_params=params(8),
        cost_estimate=FREE,
        name="post",
    )(mix, table, acc, *blocks)


def shards(tokens, shift, scale, gate, w_up, w_down, pick, count, combine):
    tok_rows, width = tokens.shape
    _, experts, slots = pick.shape
    devices = lax.axis_size("expert")
    place = lax.axis_index("expert")
    group = devices // experts
    requests = shift.shape[0]
    hidden = w_up.shape[0]
    info = jnp.stack([place // (devices // requests), place // group]).astype(jnp.int32)
    pick = pick[0]
    comb = combine[0]

    far = [d * group for d in turns(experts)[1:]]
    near = []
    bit = group // 2
    while bit:
        near.append(bit)
        bit //= 2

    def swap(x, mask):
        return lax.ppermute(x, "expert", [(i, i ^ mask) for i in range(devices)])

    tokens, shift, scale, gate, pick, comb, count = [
        pltpu.with_memory_space_constraint(x, pltpu.HBM)
        for x in (tokens, shift, scale, gate, pick, comb, count)
    ]
    farthest, tok, table, picks, weights = first(info, tokens, pick, shift, scale, gate, comb, count)
    own, *others = rest(tok, table, picks)

    flat = [farthest] + others
    blocks = [own] + [swap(x, mask) for x, mask in zip(flat, far)]
    mixes = mixer(picks, weights, blocks[1], tok_rows)
    blocks[2] = join([blocks[2]], [mixes[0]])
    beside = [swap(block, near[0]) for block in blocks]
    beside[-1] = join([beside[-1]], [])
    early, late = list(range(experts // 2)), list(range(experts // 2, experts))
    parts = []
    segments = {}
    for members in (early, late):
        pieces = [join([x for i in members for x in (blocks[i], beside[i])], [])]
        height = pieces[0].shape[0]
        for mask in near[1:]:
            block = pieces[0] if len(pieces) == 1 else join(pieces, [])
            pieces = [block, swap(block, mask)]
        for at, i in enumerate(members):
            segments[i] = []
            for k, piece in enumerate(pieces):
                for base in range(2 * at * slots, piece.shape[0], height):
                    segments[i].append((len(parts) + k, base, base + 2 * slots))
        parts += pieces
    others = list(range(2, experts)) + [0]
    sources = segments[1] + [cut for cuts in zip(*[segments[i] for i in others]) for cut in cuts]
    count = sum(high - low for _, low, high in sources)
    skip = 2 * slots * len(segments[1])

    def gather(keep, send, members, after=()):
        for i, mask in enumerate(reversed(near[1:])):
            if i:
                middle = keep.shape[0] // 2
                keep, send = add(keep, got, [(0, middle), (middle, 2 * middle)], [F32, BF16])
            got = swap(send, mask)
        at = [2 * k * slots for k in range(len(members))]
        cuts = [(x + slots, x + 2 * slots) for x in at] + [(x, x + slots) for x in at]
        out = add(keep, got, cuts, [BF16] * len(at) + [F32] * len(at), after)
        return dict(zip(members, zip(out, out[len(at):])))

    def total(i):
        send, keep = block[i]
        return add(keep, swap(send, near[0]), [(0, slots)], [BF16])[0]

    hid = up(parts, sources, w_up, [])

    eighth = width // 8
    ends = [0, 2 * eighth, 7 * eighth, width]
    tiles = [2 * eighth, 5 * eighth // 2, eighth]
    steps = list(zip(ends, ends[1:], tiles))
    keep, send = down(hid, (0, skip), w_down, (0, width, 2 * eighth), [], [])
    before = down(hid, (skip, count), w_down, steps[0], [keep], [])
    block = gather(keep, send, [1], before[:1])
    before = down(hid, (skip, count), w_down, steps[1], [block[1][0]], before)
    part = total(1)
    keep, send = down(hid, (skip, count), w_down, steps[2], [part], before)
    block.update(gather(keep, send, others))
    back = {1: swap(part, far[0])}
    link = join([back[1]], [])
    for i in late:
        part = total(i)
        if i == 2:
            part = join([part], [link])
        back[i] = swap(part, far[i - 1])
    own_send = join([block[0][0]], [part])
    acc = own_part(mixes[0], block[0][1], swap(own_send, near[0]), back[1])
    return post(mixes[1], table, acc, [back[i] for i in late])


def solution(mesh):
    return jax.shard_map(
        shards,
        mesh=mesh,
        in_specs=(
            P(("groups", "expert"), None),
            P("groups", None),
            P("groups", None),
            P("groups", None),
            P("expert", None),
            P("expert", None),
            P(("groups", "expert"), None, None),
            P(("groups", "expert"), None),
            P(("groups", "expert"), None, None),
        ),
        out_specs=P(("groups", "expert"), None),
        check_vma=False,
    )
```

```python
import functools

import jax
import jax.numpy as jnp
from jax import lax
from jax.experimental import pallas as pl
from jax.experimental.pallas import tpu as pltpu
from jax.sharding import PartitionSpec as P

MIB = 1024 * 1024
F32 = jnp.float32
BF16 = jnp.bfloat16

SMEM = pl.BlockSpec(memory_space=pltpu.SMEM)
VMEM = pl.BlockSpec(memory_space=pltpu.VMEM)
HBM = pl.BlockSpec(memory_space=pltpu.HBM)
ANY = pl.BlockSpec(memory_space=pl.ANY)


FREE = pl.CostEstimate(flops=1, bytes_accessed=1, transcendentals=0)

BUSY = pl.CostEstimate(flops=4 * 10**10, bytes_accessed=128 * MIB, transcendentals=0)


def params(mib):
    return pltpu.CompilerParams(vmem_limit_bytes=mib * MIB)


def fetch(pairs, sems):
    copies = [pltpu.make_async_copy(src, dst, sems.at[i]) for i, (src, dst) in enumerate(pairs)]
    for copy in copies:
        copy.start()
    for copy in copies:
        copy.wait()


def turns(experts):
    return [0] + list(range(experts - 1, 0, -1))


def hot_rows(picks, tok_rows):
    return lax.broadcasted_iota(jnp.int32, (tok_rows, picks.shape[1]), 0) == picks


def modulate(picks, tok_ref, table_ref):
    hot = hot_rows(picks, tok_ref.shape[0]).astype(F32).astype(BF16)
    values = lax.dot_general(hot, tok_ref[...], (((0,), (0,)), ((), ())), preferred_element_type=F32)
    center = values - jnp.mean(values, axis=1, keepdims=True)
    spread = jnp.mean(center * center, axis=1, keepdims=True)
    normed = center * (1.0 / jnp.sqrt(spread + 1e-06))
    return (normed * table_ref[0:1, :] + table_ref[1:2, :]).astype(BF16)


def first_kernel(info_ref, *refs):
    sources = refs[:7]
    far_ref, tok_ref, table_ref, picks_ref, weights_ref = refs[7:12]
    pick_ref, comb_ref, count_ref, shift_ref, scale_ref, gate_ref, sems = refs[12:]
    fetch(
        list(zip(sources, (tok_ref, pick_ref, shift_ref, scale_ref, gate_ref, comb_ref, count_ref))),
        sems,
    )
    experts, slots = pick_ref.shape
    which = pl.ds(info_ref[0], 1)
    table_ref[0:1, :] = 1.0 + scale_ref[which, :]
    table_ref[1:2, :] = shift_ref[which, :]
    table_ref[2:3, :] = gate_ref[which, :]
    lanes = lax.broadcasted_iota(jnp.int32, (1, slots), 1)
    for i, d in enumerate(turns(experts)):
        e = info_ref[1] ^ d
        picks_ref[i:i + 1, :] = pick_ref[pl.ds(e, 1), :]
        weights_ref[i:i + 1, :] = jnp.where(lanes < count_ref[0, e], comb_ref[pl.ds(e, 1), :], 0.0)
    far_ref[...] = modulate(picks_ref[1:2, :], tok_ref, table_ref)


def first(info, tokens, pick, shift, scale, gate, comb, count):
    experts, slots = pick.shape
    width = tokens.shape[1]
    return pl.pallas_call(
        first_kernel,
        in_specs=[SMEM] + [HBM] * 7,
        out_specs=[VMEM] * 5,
        out_shape=[
            jax.ShapeDtypeStruct((slots, width), BF16),
            jax.ShapeDtypeStruct(tokens.shape, BF16),
            jax.ShapeDtypeStruct((3, width), F32),
            jax.ShapeDtypeStruct(pick.shape, jnp.int32),
            jax.ShapeDtypeStruct(comb.shape, F32),
        ],
        scratch_shapes=[
            pltpu.VMEM(pick.shape, jnp.int32),
            pltpu.VMEM(comb.shape, F32),
            pltpu.SMEM(count.shape, jnp.int32),
            pltpu.VMEM(shift.shape, F32),
            pltpu.VMEM(scale.shape, F32),
            pltpu.VMEM(gate.shape, F32),
            pltpu.SemaphoreType.DMA((7,)),
        ],
        compiler_params=params(8),
        cost_estimate=FREE,
        name="first",
    )(info, tokens, pick, shift, scale, gate, comb, count)


def rest_kernel(tok_ref, table_ref, picks_ref, *outs):
    experts, slots = picks_ref.shape
    order = [0] + list(range(2, experts))
    picks = jnp.concatenate([picks_ref[i:i + 1, :] for i in order], axis=1)
    rows = modulate(picks, tok_ref, table_ref)
    for i, out in enumerate(outs):
        out[...] = rows[i * slots:(i + 1) * slots]


def rest(tok, table, picks):
    experts, slots = picks.shape
    return pl.pallas_call(
        rest_kernel,
        in_specs=[VMEM] * 3,
        out_specs=[VMEM] * (experts - 1),
        out_shape=[jax.ShapeDtypeStruct((slots, tok.shape[1]), BF16)] * (experts - 1),
        compiler_params=params(8),
        cost_estimate=BUSY,
        name="rest",
    )(tok, table, picks)


def mixer_kernel(picks_ref, weights_ref, after_ref, *outs):
    for i, out in enumerate(outs):
        each = picks_ref.shape[0] // len(outs)
        rows = range(i * each, (i + 1) * each)
        picks = jnp.concatenate([picks_ref[r:r + 1, :] for r in rows], axis=1)
        weights = jnp.concatenate([weights_ref[r:r + 1, :] for r in rows], axis=1)
        mix = jnp.where(hot_rows(picks, out.shape[0]), weights, 0.0)
        high = mix.astype(BF16).astype(F32)
        out[...] = jnp.concatenate([high, mix - high], axis=1).astype(BF16)


def mixer(picks, weights, after, tok_rows):
    experts, slots = picks.shape
    return pl.pallas_call(
        mixer_kernel,
        in_specs=[VMEM] * 2 + [ANY],
        out_specs=[VMEM] * 2,
        out_shape=[jax.ShapeDtypeStruct((tok_rows, experts * slots), BF16)] * 2,
        compiler_params=params(4),
        cost_estimate=FREE,
        name="mixer",
    )(picks, weights, after)


def join_kernel(*refs, count):
    out_ref = refs[-1]
    at = 0
    for ref in refs[:count]:
        out_ref[at:at + ref.shape[0], :] = ref[...]
        at += ref.shape[0]


def join(parts, after):
    return pl.pallas_call(
        functools.partial(join_kernel, count=len(parts)),
        in_specs=[VMEM] * len(parts) + [ANY] * len(after),
        out_specs=VMEM,
        out_shape=jax.ShapeDtypeStruct((sum(p.shape[0] for p in parts), parts[0].shape[1]), BF16),
        compiler_params=params(2),
        cost_estimate=FREE,
        name="join",
    )(*parts, *after)


def up_kernel(*refs, sources, count):
    w_ref = refs[count]
    out_ref, rows_ref = refs[-2:]
    to = 0
    for source, low, high in sources:
        rows_ref[to:to + high - low, :] = refs[source][low:high, :]
        to += high - low
    hidden = w_ref.shape[0]
    tile = min(512, hidden)

    @pl.loop(0, hidden // tile)
    def _(i):
        cut = pl.ds(pl.multiple_of(i * tile, tile), tile)
        lifted = lax.dot_general(
            w_ref[cut, :], rows_ref[...], (((1,), (1,)), ((), ())), preferred_element_type=F32
        )
        out_ref[:, cut] = jax.nn.gelu(lifted, approximate=True).astype(BF16).T


def up(parts, sources, w, after):
    hidden, width = w.shape
    rows = sum(high - low for _, low, high in sources)
    return pl.pallas_call(
        functools.partial(up_kernel, sources=sources, count=len(parts)),
        in_specs=[VMEM] * (len(parts) + 1) + [ANY] * len(after),
        out_specs=VMEM,
        out_shape=jax.ShapeDtypeStruct((rows, hidden), BF16),
        scratch_shapes=[pltpu.VMEM((rows, width), BF16)],
        compiler_params=params(8),
        cost_estimate=FREE,
        name="up",
    )(*parts, w, *after)


def down_kernel(h_ref, w_ref, keep_ref, send_ref, *, columns):
    half = keep_ref.shape[0]
    first, last, tile = columns

    @pl.loop(0, (last - first) // tile)
    def _(i):
        cut = pl.ds(pl.multiple_of(i * tile, tile), tile)
        from_ = pl.ds(pl.multiple_of(first + i * tile, tile), tile)
        out = jnp.dot(h_ref[...], w_ref[:, from_], preferred_element_type=F32)
        keep_ref[:, cut] = out[:half]
        send_ref[:, cut] = out[half:].astype(BF16)


def down(hid, w, columns):
    half = hid.shape[0] // 2
    step = columns[1] - columns[0]
    return pl.pallas_call(
        functools.partial(down_kernel, columns=columns),
        in_specs=[VMEM] * 2,
        out_specs=[VMEM] * 2,
        out_shape=[
            jax.ShapeDtypeStruct((half, step), F32),
            jax.ShapeDtypeStruct((half, step), BF16),
        ],
        compiler_params=params(8),
        cost_estimate=FREE,
        name="down",
    )(hid, w)


def add_kernel(*refs, count, outs):
    for ref, pieces in zip(refs[2 * count:], outs):
        at = 0
        for i, low, high in pieces:
            keep_ref, got_ref = refs[2 * i:2 * i + 2]
            step = keep_ref.shape[1]
            total = keep_ref[low:high] + got_ref[low:high].astype(F32)
            ref[:, at:at + step] = total.astype(ref.dtype)
            at += step


def add(pairs, outs, kinds):
    args = [x for pair in pairs for x in pair]
    shapes = [
        (pieces[0][2] - pieces[0][1], sum(pairs[i][0].shape[1] for i, _, _ in pieces))
        for pieces in outs
    ]
    return pl.pallas_call(
        functools.partial(add_kernel, count=len(pairs), outs=outs),
        in_specs=[VMEM] * len(args),
        out_specs=[VMEM] * len(outs),
        out_shape=[jax.ShapeDtypeStruct(shape, k) for shape, k in zip(shapes, kinds)],
        compiler_params=params(8),
        cost_estimate=FREE,
        name="add",
    )(*args)


def own_kernel(mix_ref, keep_ref, near_ref, got_ref, acc_ref):
    own = (keep_ref[...] + near_ref[...].astype(F32)).astype(BF16)
    values = jnp.concatenate([own, got_ref[...]] * 2, axis=0)
    acc_ref[...] = jnp.dot(mix_ref[...], values, preferred_element_type=F32)


def own_part(mix, keep, near, got):
    return pl.pallas_call(
        own_kernel,
        in_specs=[VMEM] * 4,
        out_specs=VMEM,
        out_shape=jax.ShapeDtypeStruct((mix.shape[0], keep.shape[1]), F32),
        compiler_params=params(12),
        cost_estimate=FREE,
        name="own_part",
    )(mix, keep, near, got)


def post_kernel(mix_ref, table_ref, acc_ref, *refs):
    blocks = refs[:-3]
    out_hbm, out_ref, sems = refs[-3:]
    step = out_ref.shape[1] // sems.shape[0]
    copies = []
    for i in range(sems.shape[0]):
        cut = pl.ds(i * step, step)
        values = jnp.concatenate([ref[:, cut] for ref in blocks] * 2, axis=0)
        mixed = acc_ref[:, cut] + jnp.dot(mix_ref[...], values, preferred_element_type=F32)
        out_ref[:, cut] = (table_ref[2:3, cut] * mixed).astype(BF16)
        copy = pltpu.make_async_copy(out_ref.at[:, cut], out_hbm.at[:, cut], sems.at[i])
        copy.start()
        copies.append(copy)
    for copy in copies:
        copy.wait()


def post(mix, table, acc, blocks):
    tok_rows, width = acc.shape
    return pl.pallas_call(
        post_kernel,
        in_specs=[VMEM] * (3 + len(blocks)),
        out_specs=HBM,
        out_shape=jax.ShapeDtypeStruct((tok_rows, width), BF16),
        scratch_shapes=[pltpu.VMEM((tok_rows, width), BF16), pltpu.SemaphoreType.DMA((4,))],
        compiler_params=params(8),
        cost_estimate=FREE,
        name="post",
    )(mix, table, acc, *blocks)


def shards(tokens, shift, scale, gate, w_up, w_down, pick, count, combine):
    tok_rows, width = tokens.shape
    _, experts, slots = pick.shape
    devices = lax.axis_size("expert")
    place = lax.axis_index("expert")
    group = devices // experts
    requests = shift.shape[0]
    hidden = w_up.shape[0]
    info = jnp.stack([place // (devices // requests), place // group]).astype(jnp.int32)
    pick = pick[0]
    comb = combine[0]

    far = [d * group for d in turns(experts)[1:]]
    near = []
    bit = group // 2
    while bit:
        near.append(bit)
        bit //= 2

    def swap(x, mask):
        return lax.ppermute(x, "expert", [(i, i ^ mask) for i in range(devices)])

    tokens, shift, scale, gate, pick, comb, count = [
        pltpu.with_memory_space_constraint(x, pltpu.HBM)
        for x in (tokens, shift, scale, gate, pick, comb, count)
    ]
    farthest, tok, table, picks, weights = first(info, tokens, pick, shift, scale, gate, comb, count)
    own, *others = rest(tok, table, picks)

    flat = [farthest] + others
    blocks = [own] + [swap(x, mask) for x, mask in zip(flat, far)]
    mixes = mixer(picks, weights, blocks[1], tok_rows)
    blocks[2] = join([blocks[2]], [mixes[0]])
    beside = [swap(block, near[0]) for block in blocks]
    beside[-1] = join([beside[-1]], [])
    early, late = list(range(experts // 2)), list(range(experts // 2, experts))
    parts = []
    sources = []
    for members in (early, late):
        pieces = [join([x for i in members for x in (blocks[i], beside[i])], [])]
        height = pieces[0].shape[0]
        for mask in near[1:]:
            block = pieces[0] if len(pieces) == 1 else join(pieces, [])
            pieces = [block, swap(block, mask)]
        cuts = []
        for piece in pieces:
            cuts += [(len(parts), at, at + height) for at in range(0, piece.shape[0], height)]
            parts.append(piece)
        sources.append(cuts)
    sources = [cut for pair in zip(*sources) for cut in pair]

    hid = up(parts, sources, w_up, [])

    step = 5 * width // 8
    keep_a, send_a = down(hid, w_down, (0, step, step // 2))
    keep_b, send_b = down(hid, w_down, (step, width, width - step))
    pairs = []
    for keep, send in ((keep_a, send_a), (keep_b, send_b)):
        for i, mask in enumerate(reversed(near[1:])):
            if i:
                middle = keep.shape[0] // 2
                keep, send = add(
                    [(keep, got)], [[(0, 0, middle)], [(0, middle, 2 * middle)]], [F32, BF16]
                )
            if pairs:
                send = join([send], [pairs[0][1]])
            got = swap(send, mask)
        pairs.append((keep, got))

    def outs(side):
        rows = [(2 * i + side) * slots for i in range(experts)]
        return [[(piece, at, at + slots) for piece in range(len(pairs))] for at in rows]

    sums = add(pairs, outs(1) + outs(0), [BF16] * experts + [F32] * experts)
    sends, keeps = sums[:experts], sums[experts:]
    back = {}
    for i in range(1, experts):
        got = swap(sends[i], near[0])
        (part,) = add([(keeps[i], got)], [[(0, 0, slots)]], [BF16])
        back[i] = swap(part, far[i - 1])
        if i == 1:
            own_send = join(sends[:1], [part])
    got = swap(own_send, near[0])
    acc = own_part(mixes[0], keeps[0], got, back[1])
    return post(mixes[1], table, acc, [back[i] for i in range(2, experts)])


def solution(mesh):
    return jax.shard_map(
        shards,
        mesh=mesh,
        in_specs=(
            P(("groups", "expert"), None),
            P("groups", None),
            P("groups", None),
            P("groups", None),
            P("expert", None),
            P("expert", None),
            P(("groups", "expert"), None, None),
            P(("groups", "expert"), None),
            P(("groups", "expert"), None, None),
        ),
        out_specs=P(("groups", "expert"), None),
        check_vma=False,
    )
```

```python
import functools

import jax
import jax.numpy as jnp
from jax import lax
from jax.experimental import pallas as pl
from jax.experimental.pallas import tpu as pltpu
from jax.sharding import PartitionSpec as P

MIB = 1024 * 1024
F32 = jnp.float32
BF16 = jnp.bfloat16

SMEM = pl.BlockSpec(memory_space=pltpu.SMEM)
VMEM = pl.BlockSpec(memory_space=pltpu.VMEM)
HBM = pl.BlockSpec(memory_space=pltpu.HBM)
ANY = pl.BlockSpec(memory_space=pl.ANY)


FREE = pl.CostEstimate(flops=1, bytes_accessed=1, transcendentals=0)

BUSY = pl.CostEstimate(flops=4 * 10**10, bytes_accessed=128 * MIB, transcendentals=0)


def params(mib):
    return pltpu.CompilerParams(vmem_limit_bytes=mib * MIB)


def fetch(pairs, sems):
    copies = [pltpu.make_async_copy(src, dst, sems.at[i]) for i, (src, dst) in enumerate(pairs)]
    for copy in copies:
        copy.start()
    for copy in copies:
        copy.wait()


def turns(experts):
    return [0] + list(range(experts - 1, 0, -1))


def hot_rows(picks, tok_rows):
    return lax.broadcasted_iota(jnp.int32, (tok_rows, picks.shape[1]), 0) == picks


def modulate(picks, tok_ref, table_ref):
    hot = hot_rows(picks, tok_ref.shape[0]).astype(F32).astype(BF16)
    values = lax.dot_general(hot, tok_ref[...], (((0,), (0,)), ((), ())), preferred_element_type=F32)
    center = values - jnp.mean(values, axis=1, keepdims=True)
    spread = jnp.mean(center * center, axis=1, keepdims=True)
    normed = center * (1.0 / jnp.sqrt(spread + 1e-06))
    return (normed * table_ref[0:1, :] + table_ref[1:2, :]).astype(BF16)


def first_kernel(info_ref, *refs):
    sources = refs[:7]
    far_ref, tok_ref, table_ref, picks_ref, weights_ref = refs[7:12]
    pick_ref, comb_ref, count_ref, shift_ref, scale_ref, gate_ref, sems = refs[12:]
    fetch(
        list(zip(sources, (tok_ref, pick_ref, shift_ref, scale_ref, gate_ref, comb_ref, count_ref))),
        sems,
    )
    experts, slots = pick_ref.shape
    which = pl.ds(info_ref[0], 1)
    table_ref[0:1, :] = 1.0 + scale_ref[which, :]
    table_ref[1:2, :] = shift_ref[which, :]
    table_ref[2:3, :] = gate_ref[which, :]
    lanes = lax.broadcasted_iota(jnp.int32, (1, slots), 1)
    for i, d in enumerate(turns(experts)):
        e = info_ref[1] ^ d
        picks_ref[i:i + 1, :] = pick_ref[pl.ds(e, 1), :]
        weights_ref[i:i + 1, :] = jnp.where(lanes < count_ref[0, e], comb_ref[pl.ds(e, 1), :], 0.0)
    far_ref[...] = modulate(picks_ref[1:2, :], tok_ref, table_ref)


def first(info, tokens, pick, shift, scale, gate, comb, count):
    experts, slots = pick.shape
    width = tokens.shape[1]
    return pl.pallas_call(
        first_kernel,
        in_specs=[SMEM] + [HBM] * 7,
        out_specs=[VMEM] * 5,
        out_shape=[
            jax.ShapeDtypeStruct((slots, width), BF16),
            jax.ShapeDtypeStruct(tokens.shape, BF16),
            jax.ShapeDtypeStruct((3, width), F32),
            jax.ShapeDtypeStruct(pick.shape, jnp.int32),
            jax.ShapeDtypeStruct(comb.shape, F32),
        ],
        scratch_shapes=[
            pltpu.VMEM(pick.shape, jnp.int32),
            pltpu.VMEM(comb.shape, F32),
            pltpu.SMEM(count.shape, jnp.int32),
            pltpu.VMEM(shift.shape, F32),
            pltpu.VMEM(scale.shape, F32),
            pltpu.VMEM(gate.shape, F32),
            pltpu.SemaphoreType.DMA((7,)),
        ],
        compiler_params=params(8),
        cost_estimate=FREE,
        name="first",
    )(info, tokens, pick, shift, scale, gate, comb, count)


def rest_kernel(tok_ref, table_ref, picks_ref, *outs):
    experts, slots = picks_ref.shape
    order = [0] + list(range(2, experts))
    picks = jnp.concatenate([picks_ref[i:i + 1, :] for i in order], axis=1)
    rows = modulate(picks, tok_ref, table_ref)
    for i, out in enumerate(outs):
        out[...] = rows[i * slots:(i + 1) * slots]


def rest(tok, table, picks):
    experts, slots = picks.shape
    return pl.pallas_call(
        rest_kernel,
        in_specs=[VMEM] * 3,
        out_specs=[VMEM] * (experts - 1),
        out_shape=[jax.ShapeDtypeStruct((slots, tok.shape[1]), BF16)] * (experts - 1),
        compiler_params=params(8),
        cost_estimate=BUSY,
        name="rest",
    )(tok, table, picks)


def mixer_kernel(picks_ref, weights_ref, after_ref, *outs):
    experts = picks_ref.shape[0]
    for members, out in zip((range(2), range(1, experts)), outs):
        picks = jnp.concatenate([picks_ref[r:r + 1, :] for r in members], axis=1)
        weights = jnp.concatenate([weights_ref[r:r + 1, :] for r in members], axis=1)
        mix = jnp.where(hot_rows(picks, out.shape[0]), weights, 0.0)
        high = mix.astype(BF16).astype(F32)
        out[...] = jnp.concatenate([high, mix - high], axis=1).astype(BF16)


def mixer(picks, weights, after, tok_rows):
    experts, slots = picks.shape
    return pl.pallas_call(
        mixer_kernel,
        in_specs=[VMEM] * 2 + [ANY],
        out_specs=[VMEM] * 2,
        out_shape=[
            jax.ShapeDtypeStruct((tok_rows, 4 * slots), BF16),
            jax.ShapeDtypeStruct((tok_rows, 2 * (experts - 1) * slots), BF16),
        ],
        compiler_params=params(4),
        cost_estimate=FREE,
        name="mixer",
    )(picks, weights, after)


def join_kernel(*refs, count):
    out_ref = refs[-1]
    at = 0
    for ref in refs[:count]:
        out_ref[at:at + ref.shape[0], :] = ref[...]
        at += ref.shape[0]


def join(parts, after):
    return pl.pallas_call(
        functools.partial(join_kernel, count=len(parts)),
        in_specs=[VMEM] * len(parts) + [ANY] * len(after),
        out_specs=VMEM,
        out_shape=jax.ShapeDtypeStruct((sum(p.shape[0] for p in parts), parts[0].shape[1]), BF16),
        compiler_params=params(2),
        cost_estimate=FREE,
        name="join",
    )(*parts, *after)


def up_kernel(*refs, sources, count):
    w_ref = refs[count]
    out_ref, rows_ref = refs[-2:]
    to = 0
    for source, low, high in sources:
        rows_ref[to:to + high - low, :] = refs[source][low:high, :]
        to += high - low
    hidden = w_ref.shape[0]
    tile = min(1024, hidden)

    @pl.loop(0, hidden // tile)
    def _(i):
        cut = pl.ds(pl.multiple_of(i * tile, tile), tile)
        lifted = lax.dot_general(
            w_ref[cut, :], rows_ref[...], (((1,), (1,)), ((), ())), preferred_element_type=F32
        )
        out_ref[:, cut] = jax.nn.gelu(lifted, approximate=True).astype(BF16).T


def up(parts, sources, w, after):
    hidden, width = w.shape
    rows = sum(high - low for _, low, high in sources)
    return pl.pallas_call(
        functools.partial(up_kernel, sources=sources, count=len(parts)),
        in_specs=[VMEM] * (len(parts) + 1) + [ANY] * len(after),
        out_specs=VMEM,
        out_shape=jax.ShapeDtypeStruct((rows, hidden), BF16),
        scratch_shapes=[pltpu.VMEM((rows, width), BF16)],
        compiler_params=params(8),
        cost_estimate=FREE,
        name="up",
    )(*parts, w, *after)


def down_kernel(h_ref, w_ref, keep_ref, send_ref, *, columns):
    half = keep_ref.shape[0]
    first, last, tile = columns

    @pl.loop(0, (last - first) // tile)
    def _(i):
        cut = pl.ds(pl.multiple_of(i * tile, tile), tile)
        from_ = pl.ds(pl.multiple_of(first + i * tile, tile), tile)
        out = jnp.dot(h_ref[...], w_ref[:, from_], preferred_element_type=F32)
        keep_ref[:, cut] = out[:half]
        send_ref[:, cut] = out[half:].astype(BF16)


def down(hid, w, columns):
    half = hid.shape[0] // 2
    step = columns[1] - columns[0]
    return pl.pallas_call(
        functools.partial(down_kernel, columns=columns),
        in_specs=[VMEM] * 2,
        out_specs=[VMEM] * 2,
        out_shape=[
            jax.ShapeDtypeStruct((half, step), F32),
            jax.ShapeDtypeStruct((half, step), BF16),
        ],
        compiler_params=params(8),
        cost_estimate=FREE,
        name="down",
    )(hid, w)


def add_kernel(*refs, count, outs):
    for ref, pieces in zip(refs[2 * count:], outs):
        at = 0
        for i, low, high in pieces:
            keep_ref, got_ref = refs[2 * i:2 * i + 2]
            step = keep_ref.shape[1]
            total = keep_ref[low:high] + got_ref[low:high].astype(F32)
            ref[:, at:at + step] = total.astype(ref.dtype)
            at += step


def add(pairs, outs, kinds):
    args = [x for pair in pairs for x in pair]
    shapes = [
        (pieces[0][2] - pieces[0][1], sum(pairs[i][0].shape[1] for i, _, _ in pieces))
        for pieces in outs
    ]
    return pl.pallas_call(
        functools.partial(add_kernel, count=len(pairs), outs=outs),
        in_specs=[VMEM] * len(args),
        out_specs=[VMEM] * len(outs),
        out_shape=[jax.ShapeDtypeStruct(shape, k) for shape, k in zip(shapes, kinds)],
        compiler_params=params(8),
        cost_estimate=FREE,
        name="add",
    )(*args)


def own_kernel(mix_ref, keep_ref, near_ref, got_ref, acc_ref):
    slots = keep_ref.shape[0]
    step = got_ref.shape[1]
    own = (keep_ref[...] + near_ref[...].astype(F32)).astype(BF16)
    values = jnp.concatenate([own[:, :step], got_ref[...]] * 2, axis=0)
    acc_ref[:, :step] = jnp.dot(mix_ref[...], values, preferred_element_type=F32)
    for_own = jnp.concatenate(
        [mix_ref[:, i * slots:(i + 1) * slots] for i in range(0, mix_ref.shape[1] // slots, 2)], axis=1
    )
    values = jnp.concatenate([own[:, step:]] * 2, axis=0)
    acc_ref[:, step:] = jnp.dot(for_own, values, preferred_element_type=F32)


def own_part(mix, keep, near, got):
    return pl.pallas_call(
        own_kernel,
        in_specs=[VMEM] * 4,
        out_specs=VMEM,
        out_shape=jax.ShapeDtypeStruct((mix.shape[0], keep.shape[1]), F32),
        compiler_params=params(12),
        cost_estimate=FREE,
        name="own_part",
    )(mix, keep, near, got)


def post_kernel(mix_ref, table_ref, acc_ref, tail_ref, *refs):
    blocks = refs[:-3]
    out_hbm, out_ref, sems = refs[-3:]
    width = out_ref.shape[1]
    slots = tail_ref.shape[0]
    begin = width - tail_ref.shape[1]
    count = mix_ref.shape[1] // 2
    for_head = jnp.concatenate([mix_ref[:, i + slots:i + count] for i in (0, count)], axis=1)
    step = width // sems.shape[0]
    copies = []
    for i in range(sems.shape[0]):
        cuts = [(i * step, (i + 1) * step)]
        if cuts[0][0] < begin < cuts[0][1]:
            cuts = [(i * step, begin), (begin, (i + 1) * step)]
        for low, high in cuts:
            values = [ref[:, low:high] for ref in blocks]
            mix = for_head
            if low >= begin:
                values = [tail_ref[:, low - begin:high - begin]] + values
                mix = mix_ref[...]
            values = jnp.concatenate(values * 2, axis=0)
            mixed = acc_ref[:, low:high] + jnp.dot(mix, values, preferred_element_type=F32)
            out_ref[:, low:high] = (table_ref[2:3, low:high] * mixed).astype(BF16)
        cut = pl.ds(i * step, step)
        copy = pltpu.make_async_copy(out_ref.at[:, cut], out_hbm.at[:, cut], sems.at[i])
        copy.start()
        copies.append(copy)
    for copy in copies:
        copy.wait()


def post(mix, table, acc, tail, blocks):
    tok_rows, width = acc.shape
    return pl.pallas_call(
        post_kernel,
        in_specs=[VMEM] * (4 + len(blocks)),
        out_specs=HBM,
        out_shape=jax.ShapeDtypeStruct((tok_rows, width), BF16),
        scratch_shapes=[pltpu.VMEM((tok_rows, width), BF16), pltpu.SemaphoreType.DMA((4,))],
        compiler_params=params(8),
        cost_estimate=FREE,
        name="post",
    )(mix, table, acc, tail, *blocks)


def shards(tokens, shift, scale, gate, w_up, w_down, pick, count, combine):
    tok_rows, width = tokens.shape
    _, experts, slots = pick.shape
    devices = lax.axis_size("expert")
    place = lax.axis_index("expert")
    group = devices // experts
    requests = shift.shape[0]
    hidden = w_up.shape[0]
    info = jnp.stack([place // (devices // requests), place // group]).astype(jnp.int32)
    pick = pick[0]
    comb = combine[0]

    far = [d * group for d in turns(experts)[1:]]
    near = []
    bit = group // 2
    while bit:
        near.append(bit)
        bit //= 2

    def swap(x, mask):
        return lax.ppermute(x, "expert", [(i, i ^ mask) for i in range(devices)])

    tokens, shift, scale, gate, pick, comb, count = [
        pltpu.with_memory_space_constraint(x, pltpu.HBM)
        for x in (tokens, shift, scale, gate, pick, comb, count)
    ]
    farthest, tok, table, picks, weights = first(info, tokens, pick, shift, scale, gate, comb, count)
    own, *others = rest(tok, table, picks)

    flat = [farthest] + others
    blocks = [own] + [swap(x, mask) for x, mask in zip(flat, far)]
    mixes = mixer(picks, weights, blocks[1], tok_rows)
    blocks[2] = join([blocks[2]], [mixes[0]])
    beside = [swap(block, near[0]) for block in blocks]
    beside[-1] = join([beside[-1]], [])
    early, late = list(range(experts // 2)), list(range(experts // 2, experts))
    parts = []
    sources = []
    for members in (early, late):
        pieces = [join([x for i in members for x in (blocks[i], beside[i])], [])]
        height = pieces[0].shape[0]
        for mask in near[1:]:
            block = pieces[0] if len(pieces) == 1 else join(pieces, [])
            pieces = [block, swap(block, mask)]
        cuts = []
        for piece in pieces:
            cuts += [(len(parts), at, at + height) for at in range(0, piece.shape[0], height)]
            parts.append(piece)
        sources.append(cuts)
    sources = [cut for pair in zip(*sources) for cut in pair]

    hid = up(parts, sources, w_up, [])

    step = 5 * width // 8
    keep_a, send_a = down(hid, w_down, (0, step, step // 2))
    keep_b, send_b = down(hid, w_down, (step, width, width - step))
    pairs = []
    for keep, send in ((keep_a, send_a), (keep_b, send_b)):
        for i, mask in enumerate(reversed(near[1:])):
            if i:
                middle = keep.shape[0] // 2
                keep, send = add(
                    [(keep, got)], [[(0, 0, middle)], [(0, middle, 2 * middle)]], [F32, BF16]
                )
            if pairs:
                send = join([send], [pairs[0][1]])
            got = swap(send, mask)
        pairs.append((keep, got))

    def outs(i, side, pieces):
        at = (2 * i + side) * slots
        return [(piece, at, at + slots) for piece in pieces]

    rest_of = list(range(2, experts)) + [0]
    head = add(pairs[:1], [outs(1, side, [0]) for side in (1, 0)], [BF16, F32])
    sums = add(
        pairs,
        [outs(i, side, [0, 1]) for i in rest_of for side in (1, 0)]
        + [outs(1, side, [1]) for side in (1, 0)],
        [BF16, F32] * (len(rest_of) + 1),
    )
    block = {i: sums[2 * k:2 * k + 2] for k, i in enumerate(rest_of)}

    def total(send, keep):
        return add([(keep, swap(send, near[0]))], [[(0, 0, slots)]], [BF16])[0]

    head = swap(total(*head), far[0])
    link = head
    back = {}
    for i in range(2, experts):
        part = total(*block[i])
        if i > 2:
            part = join([part], [link])
        back[i] = swap(part, far[i - 1])
        if i == 2:
            first_part = part
    tail_part = total(*sums[-2:])
    tail = swap(tail_part, far[0])
    send, keep = block[0]
    beside_own = swap(join([send], [first_part, tail_part]), near[0])
    acc = own_part(mixes[0], keep, beside_own, head)
    return post(mixes[1], table, acc, tail, [back[i] for i in range(2, experts)])


def solution(mesh):
    return jax.shard_map(
        shards,
        mesh=mesh,
        in_specs=(
            P(("groups", "expert"), None),
            P("groups", None),
            P("groups", None),
            P("groups", None),
            P("expert", None),
            P("expert", None),
            P(("groups", "expert"), None, None),
            P(("groups", "expert"), None),
            P(("groups", "expert"), None, None),
        ),
        out_specs=P(("groups", "expert"), None),
        check_vma=False,
    )
```

```python
import functools

import jax
import jax.numpy as jnp
from jax import lax
from jax.experimental import pallas as pl
from jax.experimental.pallas import tpu as pltpu
from jax.sharding import PartitionSpec as P

MIB = 1024 * 1024
F32 = jnp.float32
BF16 = jnp.bfloat16

SMEM = pl.BlockSpec(memory_space=pltpu.SMEM)
VMEM = pl.BlockSpec(memory_space=pltpu.VMEM)
HBM = pl.BlockSpec(memory_space=pltpu.HBM)
ANY = pl.BlockSpec(memory_space=pl.ANY)


FREE = pl.CostEstimate(flops=1, bytes_accessed=1, transcendentals=0)

BUSY = pl.CostEstimate(flops=4 * 10**10, bytes_accessed=128 * MIB, transcendentals=0)


def params(mib):
    return pltpu.CompilerParams(vmem_limit_bytes=mib * MIB)


def fetch(pairs, sems):
    copies = [pltpu.make_async_copy(src, dst, sems.at[i]) for i, (src, dst) in enumerate(pairs)]
    for copy in copies:
        copy.start()
    for copy in copies:
        copy.wait()


def turns(experts):
    return [0] + list(range(experts - 1, 0, -1))


def hot_rows(picks, tok_rows):
    return lax.broadcasted_iota(jnp.int32, (tok_rows, picks.shape[1]), 0) == picks


def modulate(picks, tok_ref, table_ref):
    hot = hot_rows(picks, tok_ref.shape[0]).astype(F32).astype(BF16)
    values = lax.dot_general(hot, tok_ref[...], (((0,), (0,)), ((), ())), preferred_element_type=F32)
    center = values - jnp.mean(values, axis=1, keepdims=True)
    spread = jnp.mean(center * center, axis=1, keepdims=True)
    normed = center * (1.0 / jnp.sqrt(spread + 1e-06))
    return (normed * table_ref[0:1, :] + table_ref[1:2, :]).astype(BF16)


def first_kernel(info_ref, *refs):
    sources = refs[:7]
    far_ref, tok_ref, table_ref, picks_ref, weights_ref = refs[7:12]
    pick_ref, comb_ref, count_ref, shift_ref, scale_ref, gate_ref, sems = refs[12:]
    fetch(
        list(zip(sources, (tok_ref, pick_ref, shift_ref, scale_ref, gate_ref, comb_ref, count_ref))),
        sems,
    )
    experts, slots = pick_ref.shape
    which = pl.ds(info_ref[0], 1)
    table_ref[0:1, :] = 1.0 + scale_ref[which, :]
    table_ref[1:2, :] = shift_ref[which, :]
    table_ref[2:3, :] = gate_ref[which, :]
    lanes = lax.broadcasted_iota(jnp.int32, (1, slots), 1)
    for i, d in enumerate(turns(experts)):
        e = info_ref[1] ^ d
        picks_ref[i:i + 1, :] = pick_ref[pl.ds(e, 1), :]
        weights_ref[i:i + 1, :] = jnp.where(lanes < count_ref[0, e], comb_ref[pl.ds(e, 1), :], 0.0)
    far_ref[...] = modulate(picks_ref[1:2, :], tok_ref, table_ref)


def first(info, tokens, pick, shift, scale, gate, comb, count):
    experts, slots = pick.shape
    width = tokens.shape[1]
    return pl.pallas_call(
        first_kernel,
        in_specs=[SMEM] + [HBM] * 7,
        out_specs=[VMEM] * 5,
        out_shape=[
            jax.ShapeDtypeStruct((slots, width), BF16),
            jax.ShapeDtypeStruct(tokens.shape, BF16),
            jax.ShapeDtypeStruct((3, width), F32),
            jax.ShapeDtypeStruct(pick.shape, jnp.int32),
            jax.ShapeDtypeStruct(comb.shape, F32),
        ],
        scratch_shapes=[
            pltpu.VMEM(pick.shape, jnp.int32),
            pltpu.VMEM(comb.shape, F32),
            pltpu.SMEM(count.shape, jnp.int32),
            pltpu.VMEM(shift.shape, F32),
            pltpu.VMEM(scale.shape, F32),
            pltpu.VMEM(gate.shape, F32),
            pltpu.SemaphoreType.DMA((7,)),
        ],
        compiler_params=params(8),
        cost_estimate=FREE,
        name="first",
    )(info, tokens, pick, shift, scale, gate, comb, count)


def rest_kernel(tok_ref, table_ref, picks_ref, *outs):
    experts, slots = picks_ref.shape
    order = [0] + list(range(2, experts))
    picks = jnp.concatenate([picks_ref[i:i + 1, :] for i in order], axis=1)
    rows = modulate(picks, tok_ref, table_ref)
    for i, out in enumerate(outs):
        out[...] = rows[i * slots:(i + 1) * slots]


def rest(tok, table, picks):
    experts, slots = picks.shape
    return pl.pallas_call(
        rest_kernel,
        in_specs=[VMEM] * 3,
        out_specs=[VMEM] * (experts - 1),
        out_shape=[jax.ShapeDtypeStruct((slots, tok.shape[1]), BF16)] * (experts - 1),
        compiler_params=params(8),
        cost_estimate=BUSY,
        name="rest",
    )(tok, table, picks)


def mixer_kernel(picks_ref, weights_ref, after_ref, *outs):
    experts = picks_ref.shape[0]
    for members, out in zip((range(2), range(1, experts)), outs):
        picks = jnp.concatenate([picks_ref[r:r + 1, :] for r in members], axis=1)
        weights = jnp.concatenate([weights_ref[r:r + 1, :] for r in members], axis=1)
        mix = jnp.where(hot_rows(picks, out.shape[0]), weights, 0.0)
        high = mix.astype(BF16).astype(F32)
        out[...] = jnp.concatenate([high, mix - high], axis=1).astype(BF16)


def mixer(picks, weights, after, tok_rows):
    experts, slots = picks.shape
    return pl.pallas_call(
        mixer_kernel,
        in_specs=[VMEM] * 2 + [ANY],
        out_specs=[VMEM] * 2,
        out_shape=[
            jax.ShapeDtypeStruct((tok_rows, 4 * slots), BF16),
            jax.ShapeDtypeStruct((tok_rows, 2 * (experts - 1) * slots), BF16),
        ],
        compiler_params=params(4),
        cost_estimate=FREE,
        name="mixer",
    )(picks, weights, after)


def join_kernel(*refs, count):
    out_ref = refs[-1]
    at = 0
    for ref in refs[:count]:
        out_ref[at:at + ref.shape[0], :] = ref[...]
        at += ref.shape[0]


def join(parts, after):
    return pl.pallas_call(
        functools.partial(join_kernel, count=len(parts)),
        in_specs=[VMEM] * len(parts) + [ANY] * len(after),
        out_specs=VMEM,
        out_shape=jax.ShapeDtypeStruct((sum(p.shape[0] for p in parts), parts[0].shape[1]), BF16),
        compiler_params=params(2),
        cost_estimate=FREE,
        name="join",
    )(*parts, *after)


def up_kernel(*refs, sources, count):
    w_ref = refs[count]
    out_ref, rows_ref = refs[-2:]
    to = 0
    for source, low, high in sources:
        rows_ref[to:to + high - low, :] = refs[source][low:high, :]
        to += high - low
    hidden = w_ref.shape[0]
    tile = min(1024, hidden)

    @pl.loop(0, hidden // tile)
    def _(i):
        cut = pl.ds(pl.multiple_of(i * tile, tile), tile)
        lifted = lax.dot_general(
            w_ref[cut, :], rows_ref[...], (((1,), (1,)), ((), ())), preferred_element_type=F32
        )
        out_ref[:, cut] = jax.nn.gelu(lifted, approximate=True).astype(BF16).T


def up(parts, sources, w, after):
    hidden, width = w.shape
    rows = sum(high - low for _, low, high in sources)
    return pl.pallas_call(
        functools.partial(up_kernel, sources=sources, count=len(parts)),
        in_specs=[VMEM] * (len(parts) + 1) + [ANY] * len(after),
        out_specs=VMEM,
        out_shape=jax.ShapeDtypeStruct((rows, hidden), BF16),
        scratch_shapes=[pltpu.VMEM((rows, width), BF16)],
        compiler_params=params(8),
        cost_estimate=FREE,
        name="up",
    )(*parts, w, *after)


def down_kernel(h_ref, w_ref, keep_ref, send_ref, *, columns):
    half = keep_ref.shape[0]
    first, last, tile = columns

    @pl.loop(0, (last - first) // tile)
    def _(i):
        cut = pl.ds(pl.multiple_of(i * tile, tile), tile)
        from_ = pl.ds(pl.multiple_of(first + i * tile, tile), tile)
        out = jnp.dot(h_ref[...], w_ref[:, from_], preferred_element_type=F32)
        keep_ref[:, cut] = out[:half]
        send_ref[:, cut] = out[half:].astype(BF16)


def down(hid, w, columns):
    half = hid.shape[0] // 2
    step = columns[1] - columns[0]
    return pl.pallas_call(
        functools.partial(down_kernel, columns=columns),
        in_specs=[VMEM] * 2,
        out_specs=[VMEM] * 2,
        out_shape=[
            jax.ShapeDtypeStruct((half, step), F32),
            jax.ShapeDtypeStruct((half, step), BF16),
        ],
        compiler_params=params(8),
        cost_estimate=FREE,
        name="down",
    )(hid, w)


def add_kernel(*refs, count, outs):
    for ref, pieces in zip(refs[2 * count:], outs):
        at = 0
        for i, low, high in pieces:
            keep_ref, got_ref = refs[2 * i:2 * i + 2]
            step = keep_ref.shape[1]
            total = keep_ref[low:high] + got_ref[low:high].astype(F32)
            ref[:, at:at + step] = total.astype(ref.dtype)
            at += step


def add(pairs, outs, kinds):
    args = [x for pair in pairs for x in pair]
    shapes = [
        (pieces[0][2] - pieces[0][1], sum(pairs[i][0].shape[1] for i, _, _ in pieces))
        for pieces in outs
    ]
    return pl.pallas_call(
        functools.partial(add_kernel, count=len(pairs), outs=outs),
        in_specs=[VMEM] * len(args),
        out_specs=[VMEM] * len(outs),
        out_shape=[jax.ShapeDtypeStruct(shape, k) for shape, k in zip(shapes, kinds)],
        compiler_params=params(8),
        cost_estimate=FREE,
        name="add",
    )(*args)


def own_kernel(mix_ref, keep_ref, near_ref, got_ref, acc_ref):
    slots = keep_ref.shape[0]
    step = got_ref.shape[1]
    own = (keep_ref[...] + near_ref[...].astype(F32)).astype(BF16)
    values = jnp.concatenate([own[:, :step], got_ref[...]] * 2, axis=0)
    acc_ref[:, :step] = jnp.dot(mix_ref[...], values, preferred_element_type=F32)
    for_own = jnp.concatenate(
        [mix_ref[:, i * slots:(i + 1) * slots] for i in range(0, mix_ref.shape[1] // slots, 2)], axis=1
    )
    values = jnp.concatenate([own[:, step:]] * 2, axis=0)
    acc_ref[:, step:] = jnp.dot(for_own, values, preferred_element_type=F32)


def own_part(mix, keep, near, got):
    return pl.pallas_call(
        own_kernel,
        in_specs=[VMEM] * 4,
        out_specs=VMEM,
        out_shape=jax.ShapeDtypeStruct((mix.shape[0], keep.shape[1]), F32),
        compiler_params=params(12),
        cost_estimate=FREE,
        name="own_part",
    )(mix, keep, near, got)


def post_kernel(mix_ref, table_ref, acc_ref, tail_ref, *refs):
    blocks = refs[:-3]
    out_hbm, out_ref, sems = refs[-3:]
    width = out_ref.shape[1]
    slots = tail_ref.shape[0]
    begin = width - tail_ref.shape[1]
    count = mix_ref.shape[1] // 2
    for_head = jnp.concatenate([mix_ref[:, i + slots:i + count] for i in (0, count)], axis=1)
    step = width // sems.shape[0]
    copies = []
    for i in range(sems.shape[0]):
        cuts = [(i * step, (i + 1) * step)]
        if cuts[0][0] < begin < cuts[0][1]:
            cuts = [(i * step, begin), (begin, (i + 1) * step)]
        for low, high in cuts:
            values = [ref[:, low:high] for ref in blocks]
            mix = for_head
            if low >= begin:
                values = [tail_ref[:, low - begin:high - begin]] + values
                mix = mix_ref[...]
            values = jnp.concatenate(values * 2, axis=0)
            mixed = acc_ref[:, low:high] + jnp.dot(mix, values, preferred_element_type=F32)
            out_ref[:, low:high] = (table_ref[2:3, low:high] * mixed).astype(BF16)
        cut = pl.ds(i * step, step)
        copy = pltpu.make_async_copy(out_ref.at[:, cut], out_hbm.at[:, cut], sems.at[i])
        copy.start()
        copies.append(copy)
    for copy in copies:
        copy.wait()


def post(mix, table, acc, tail, blocks):
    tok_rows, width = acc.shape
    return pl.pallas_call(
        post_kernel,
        in_specs=[VMEM] * (4 + len(blocks)),
        out_specs=HBM,
        out_shape=jax.ShapeDtypeStruct((tok_rows, width), BF16),
        scratch_shapes=[pltpu.VMEM((tok_rows, width), BF16), pltpu.SemaphoreType.DMA((4,))],
        compiler_params=params(8),
        cost_estimate=FREE,
        name="post",
    )(mix, table, acc, tail, *blocks)


def shards(tokens, shift, scale, gate, w_up, w_down, pick, count, combine):
    tok_rows, width = tokens.shape
    _, experts, slots = pick.shape
    devices = lax.axis_size("expert")
    place = lax.axis_index("expert")
    group = devices // experts
    requests = shift.shape[0]
    hidden = w_up.shape[0]
    info = jnp.stack([place // (devices // requests), place // group]).astype(jnp.int32)
    pick = pick[0]
    comb = combine[0]

    far = [d * group for d in turns(experts)[1:]]
    near = []
    bit = group // 2
    while bit:
        near.append(bit)
        bit //= 2

    def swap(x, mask):
        return lax.ppermute(x, "expert", [(i, i ^ mask) for i in range(devices)])

    tokens, shift, scale, gate, pick, comb, count = [
        pltpu.with_memory_space_constraint(x, pltpu.HBM)
        for x in (tokens, shift, scale, gate, pick, comb, count)
    ]
    farthest, tok, table, picks, weights = first(info, tokens, pick, shift, scale, gate, comb, count)
    own, *others = rest(tok, table, picks)

    flat = [farthest] + others
    blocks = [own] + [swap(x, mask) for x, mask in zip(flat, far)]
    mixes = mixer(picks, weights, blocks[1], tok_rows)
    blocks[2] = join([blocks[2]], [mixes[0]])
    beside = [swap(block, near[0]) for block in blocks]
    beside[-1] = join([beside[-1]], [])
    early, late = list(range(experts // 2)), list(range(experts // 2, experts))
    parts = []
    sources = []
    for members in (early, late):
        pieces = [join([x for i in members for x in (blocks[i], beside[i])], [])]
        height = pieces[0].shape[0]
        for mask in near[1:]:
            block = pieces[0] if len(pieces) == 1 else join(pieces, [])
            pieces = [block, swap(block, mask)]
        cuts = []
        for piece in pieces:
            cuts += [(len(parts), at, at + height) for at in range(0, piece.shape[0], height)]
            parts.append(piece)
        sources.append(cuts)
    sources = [cut for pair in zip(*sources) for cut in pair]

    hid = up(parts, sources, w_up, [])

    step = 5 * width // 8
    keep_a, send_a = down(hid, w_down, (0, step, step // 2))
    keep_b, send_b = down(hid, w_down, (step, width, width - step))
    pairs = []
    for keep, send in ((keep_a, send_a), (keep_b, send_b)):
        for i, mask in enumerate(reversed(near[1:])):
            if i:
                middle = keep.shape[0] // 2
                keep, send = add(
                    [(keep, got)], [[(0, 0, middle)], [(0, middle, 2 * middle)]], [F32, BF16]
                )
            if pairs:
                send = join([send], [pairs[0][1]])
            got = swap(send, mask)
        pairs.append((keep, got))

    def outs(i, side, pieces):
        at = (2 * i + side) * slots
        return [(piece, at, at + slots) for piece in pieces]

    rest_of = list(range(2, experts)) + [0]
    head = add(pairs[:1], [outs(1, side, [0]) for side in (1, 0)], [BF16, F32])
    sums = add(
        pairs,
        [outs(i, side, [0, 1]) for i in rest_of for side in (1, 0)]
        + [outs(1, side, [1]) for side in (1, 0)],
        [BF16, F32] * (len(rest_of) + 1),
    )
    block = {i: sums[2 * k:2 * k + 2] for k, i in enumerate(rest_of)}

    def total(send, keep):
        return add([(keep, swap(send, near[0]))], [[(0, 0, slots)]], [BF16])[0]

    head = swap(total(*head), far[0])
    link = head
    back = {}
    for i in range(2, experts):
        part = total(*block[i])
        if i > 2:
            part = join([part], [link])
        back[i] = swap(part, far[i - 1])
        if i == 2:
            first_part = part
    tail = swap(total(*sums[-2:]), far[0])
    send, keep = block[0]
    beside_own = swap(join([send], [first_part]), near[0])
    acc = own_part(mixes[0], keep, beside_own, head)
    return post(mixes[1], table, acc, tail, [back[i] for i in range(2, experts)])


def solution(mesh):
    return jax.shard_map(
        shards,
        mesh=mesh,
        in_specs=(
            P(("groups", "expert"), None),
            P("groups", None),
            P("groups", None),
            P("groups", None),
            P("expert", None),
            P("expert", None),
            P(("groups", "expert"), None, None),
            P(("groups", "expert"), None),
            P(("groups", "expert"), None, None),
        ),
        out_specs=P(("groups", "expert"), None),
        check_vma=False,
    )
```

```python
import functools

import jax
import jax.numpy as jnp
from jax import lax
from jax.experimental import pallas as pl
from jax.experimental.pallas import tpu as pltpu
from jax.sharding import PartitionSpec as P

MIB = 1024 * 1024
F32 = jnp.float32
BF16 = jnp.bfloat16

SMEM = pl.BlockSpec(memory_space=pltpu.SMEM)
VMEM = pl.BlockSpec(memory_space=pltpu.VMEM)
HBM = pl.BlockSpec(memory_space=pltpu.HBM)
ANY = pl.BlockSpec(memory_space=pl.ANY)


FREE = pl.CostEstimate(flops=1, bytes_accessed=1, transcendentals=0)

BUSY = pl.CostEstimate(flops=4 * 10**10, bytes_accessed=128 * MIB, transcendentals=0)


def params(mib):
    return pltpu.CompilerParams(vmem_limit_bytes=mib * MIB)


def fetch(pairs, sems):
    copies = [pltpu.make_async_copy(src, dst, sems.at[i]) for i, (src, dst) in enumerate(pairs)]
    for copy in copies:
        copy.start()
    for copy in copies:
        copy.wait()


def turns(experts):
    return [0] + list(range(experts - 1, 0, -1))


def hot_rows(picks, tok_rows):
    return lax.broadcasted_iota(jnp.int32, (tok_rows, picks.shape[1]), 0) == picks


def modulate(picks, tok_ref, table_ref):
    hot = hot_rows(picks, tok_ref.shape[0]).astype(F32).astype(BF16)
    values = lax.dot_general(hot, tok_ref[...], (((0,), (0,)), ((), ())), preferred_element_type=F32)
    center = values - jnp.mean(values, axis=1, keepdims=True)
    spread = jnp.mean(center * center, axis=1, keepdims=True)
    normed = center * (1.0 / jnp.sqrt(spread + 1e-06))
    return (normed * table_ref[0:1, :] + table_ref[1:2, :]).astype(BF16)


def first_kernel(info_ref, *refs):
    sources = refs[:7]
    far_ref, tok_ref, table_ref, picks_ref, weights_ref = refs[7:12]
    pick_ref, comb_ref, count_ref, shift_ref, scale_ref, gate_ref, sems = refs[12:]
    fetch(
        list(zip(sources, (tok_ref, pick_ref, shift_ref, scale_ref, gate_ref, comb_ref, count_ref))),
        sems,
    )
    experts, slots = pick_ref.shape
    which = pl.ds(info_ref[0], 1)
    table_ref[0:1, :] = 1.0 + scale_ref[which, :]
    table_ref[1:2, :] = shift_ref[which, :]
    table_ref[2:3, :] = gate_ref[which, :]
    lanes = lax.broadcasted_iota(jnp.int32, (1, slots), 1)
    for i, d in enumerate(turns(experts)):
        e = info_ref[1] ^ d
        picks_ref[i:i + 1, :] = pick_ref[pl.ds(e, 1), :]
        weights_ref[i:i + 1, :] = jnp.where(lanes < count_ref[0, e], comb_ref[pl.ds(e, 1), :], 0.0)
    far_ref[...] = modulate(picks_ref[1:2, :], tok_ref, table_ref)


def first(info, tokens, pick, shift, scale, gate, comb, count):
    experts, slots = pick.shape
    width = tokens.shape[1]
    return pl.pallas_call(
        first_kernel,
        in_specs=[SMEM] + [HBM] * 7,
        out_specs=[VMEM] * 5,
        out_shape=[
            jax.ShapeDtypeStruct((slots, width), BF16),
            jax.ShapeDtypeStruct(tokens.shape, BF16),
            jax.ShapeDtypeStruct((3, width), F32),
            jax.ShapeDtypeStruct(pick.shape, jnp.int32),
            jax.ShapeDtypeStruct(comb.shape, F32),
        ],
        scratch_shapes=[
            pltpu.VMEM(pick.shape, jnp.int32),
            pltpu.VMEM(comb.shape, F32),
            pltpu.SMEM(count.shape, jnp.int32),
            pltpu.VMEM(shift.shape, F32),
            pltpu.VMEM(scale.shape, F32),
            pltpu.VMEM(gate.shape, F32),
            pltpu.SemaphoreType.DMA((7,)),
        ],
        compiler_params=params(8),
        cost_estimate=FREE,
        name="first",
    )(info, tokens, pick, shift, scale, gate, comb, count)


def rest_kernel(tok_ref, table_ref, picks_ref, *outs):
    experts, slots = picks_ref.shape
    order = [0] + list(range(2, experts))
    picks = jnp.concatenate([picks_ref[i:i + 1, :] for i in order], axis=1)
    rows = modulate(picks, tok_ref, table_ref)
    for i, out in enumerate(outs):
        out[...] = rows[i * slots:(i + 1) * slots]


def rest(tok, table, picks):
    experts, slots = picks.shape
    return pl.pallas_call(
        rest_kernel,
        in_specs=[VMEM] * 3,
        out_specs=[VMEM] * (experts - 1),
        out_shape=[jax.ShapeDtypeStruct((slots, tok.shape[1]), BF16)] * (experts - 1),
        compiler_params=params(8),
        cost_estimate=BUSY,
        name="rest",
    )(tok, table, picks)


def mixer_kernel(picks_ref, weights_ref, after_ref, *outs):
    for i, out in enumerate(outs):
        each = picks_ref.shape[0] // len(outs)
        rows = range(i * each, (i + 1) * each)
        picks = jnp.concatenate([picks_ref[r:r + 1, :] for r in rows], axis=1)
        weights = jnp.concatenate([weights_ref[r:r + 1, :] for r in rows], axis=1)
        mix = jnp.where(hot_rows(picks, out.shape[0]), weights, 0.0)
        high = mix.astype(BF16).astype(F32)
        out[...] = jnp.concatenate([high, mix - high], axis=1).astype(BF16)


def mixer(picks, weights, after, tok_rows):
    experts, slots = picks.shape
    return pl.pallas_call(
        mixer_kernel,
        in_specs=[VMEM] * 2 + [ANY],
        out_specs=[VMEM] * 2,
        out_shape=[jax.ShapeDtypeStruct((tok_rows, experts * slots), BF16)] * 2,
        compiler_params=params(4),
        cost_estimate=FREE,
        name="mixer",
    )(picks, weights, after)


def join_kernel(*refs, count):
    out_ref = refs[-1]
    at = 0
    for ref in refs[:count]:
        out_ref[at:at + ref.shape[0], :] = ref[...]
        at += ref.shape[0]


def join(parts, after):
    return pl.pallas_call(
        functools.partial(join_kernel, count=len(parts)),
        in_specs=[VMEM] * len(parts) + [ANY] * len(after),
        out_specs=VMEM,
        out_shape=jax.ShapeDtypeStruct((sum(p.shape[0] for p in parts), parts[0].shape[1]), BF16),
        compiler_params=params(2),
        cost_estimate=FREE,
        name="join",
    )(*parts, *after)


def up_kernel(*refs, sources, count):
    w_ref = refs[count]
    out_ref, rows_ref = refs[-2:]
    to = 0
    for source, low, high in sources:
        rows_ref[to:to + high - low, :] = refs[source][low:high, :]
        to += high - low
    hidden = w_ref.shape[0]
    tile = min(1024, hidden)

    @pl.loop(0, hidden // tile)
    def _(i):
        cut = pl.ds(pl.multiple_of(i * tile, tile), tile)
        lifted = lax.dot_general(
            w_ref[cut, :], rows_ref[...], (((1,), (1,)), ((), ())), preferred_element_type=F32
        )
        out_ref[:, cut] = jax.nn.gelu(lifted, approximate=True).astype(BF16).T


def up(parts, sources, w, after):
    hidden, width = w.shape
    rows = sum(high - low for _, low, high in sources)
    return pl.pallas_call(
        functools.partial(up_kernel, sources=sources, count=len(parts)),
        in_specs=[VMEM] * (len(parts) + 1) + [ANY] * len(after),
        out_specs=VMEM,
        out_shape=jax.ShapeDtypeStruct((rows, hidden), BF16),
        scratch_shapes=[pltpu.VMEM((rows, width), BF16)],
        compiler_params=params(8),
        cost_estimate=FREE,
        name="up",
    )(*parts, w, *after)


def down_kernel(h_ref, w_ref, *refs, low, columns, pieces):
    keep_ref, sends = refs[-pieces - 1], refs[-pieces:]
    half = keep_ref.shape[0]
    height = half // pieces
    first, last, tile = columns

    @pl.loop(0, (last - first) // tile)
    def _(i):
        cut = pl.ds(pl.multiple_of(first + i * tile, tile), tile)
        out = jnp.dot(h_ref[low:low + 2 * half, :], w_ref[:, cut], preferred_element_type=F32)
        keep_ref[:, cut] = out[:half]
        for k, send_ref in enumerate(sends):
            at = half + k * height
            send_ref[:, cut] = out[at:at + height].astype(BF16)


def down(hid, rows, w, columns, pieces, after, before):
    half = (rows[1] - rows[0]) // 2
    width = w.shape[1]
    return pl.pallas_call(
        functools.partial(down_kernel, low=rows[0], columns=columns, pieces=pieces),
        in_specs=[VMEM] * 2 + [ANY] * len(after) + [VMEM] * len(before),
        out_specs=[VMEM] * (1 + pieces),
        out_shape=[jax.ShapeDtypeStruct((half, width), F32)]
        + [jax.ShapeDtypeStruct((half // pieces, width), BF16)] * pieces,
        input_output_aliases={2 + len(after) + i: i for i in range(len(before))},
        compiler_params=params(8),
        cost_estimate=FREE,
        name="down",
    )(hid, w, *after, *before)


def add_kernel(keep_ref, *refs, pieces, cuts):
    gots, outs = refs[:pieces], refs[len(refs) - len(cuts):]
    height = gots[0].shape[0]
    for ref, (low, high, first, last) in zip(outs, cuts):
        step = min(height, high - low)
        for at in range(low, high, step):
            from_ = at % height
            total = keep_ref[at:at + step, first:last] + gots[at // height][
                from_:from_ + step, first:last
            ].astype(F32)
            ref[at - low:at - low + step, :] = total.astype(ref.dtype)


def add(keep, gots, cuts, kinds):
    return pl.pallas_call(
        functools.partial(add_kernel, pieces=len(gots), cuts=cuts),
        in_specs=[VMEM] * (1 + len(gots)),
        out_specs=[VMEM] * len(cuts),
        out_shape=[
            jax.ShapeDtypeStruct((high - low, last - first), k)
            for (low, high, first, last), k in zip(cuts, kinds)
        ],
        compiler_params=params(8),
        cost_estimate=FREE,
        name="add",
    )(keep, *gots)


def own_kernel(mix_ref, keep_ref, near_ref, got_ref, acc_ref):
    own = (keep_ref[...] + near_ref[...].astype(F32)).astype(BF16)
    values = jnp.concatenate([own, got_ref[...]] * 2, axis=0)
    acc_ref[...] = jnp.dot(mix_ref[...], values, preferred_element_type=F32)


def own_part(mix, keep, near, got):
    return pl.pallas_call(
        own_kernel,
        in_specs=[VMEM] * 4,
        out_specs=VMEM,
        out_shape=jax.ShapeDtypeStruct((mix.shape[0], keep.shape[1]), F32),
        compiler_params=params(12),
        cost_estimate=FREE,
        name="own_part",
    )(mix, keep, near, got)


def post_kernel(mix_ref, table_ref, acc_ref, *refs, counts):
    out_hbm, out_ref, sems = refs[-3:]
    step = out_ref.shape[1] // sems.shape[0]
    copies = []
    for i in range(sems.shape[0]):
        values = []
        at = 0
        for count in counts:
            each = out_ref.shape[1] // count
            piece, low = divmod(i * step, each)
            values.append(refs[at + piece][:, low:low + step])
            at += count
        values = jnp.concatenate(values * 2, axis=0)
        cut = pl.ds(i * step, step)
        mixed = acc_ref[:, cut] + jnp.dot(mix_ref[...], values, preferred_element_type=F32)
        out_ref[:, cut] = (table_ref[2:3, cut] * mixed).astype(BF16)
        copy = pltpu.make_async_copy(out_ref.at[:, cut], out_hbm.at[:, cut], sems.at[i])
        copy.start()
        copies.append(copy)
    for copy in copies:
        copy.wait()


def post(mix, table, acc, blocks):
    tok_rows, width = acc.shape
    args = [x for block in blocks for x in block]
    return pl.pallas_call(
        functools.partial(post_kernel, counts=[len(block) for block in blocks]),
        in_specs=[VMEM] * (3 + len(args)),
        out_specs=HBM,
        out_shape=jax.ShapeDtypeStruct((tok_rows, width), BF16),
        scratch_shapes=[pltpu.VMEM((tok_rows, width), BF16), pltpu.SemaphoreType.DMA((4,))],
        compiler_params=params(8),
        cost_estimate=FREE,
        name="post",
    )(mix, table, acc, *args)


def shards(tokens, shift, scale, gate, w_up, w_down, pick, count, combine):
    tok_rows, width = tokens.shape
    _, experts, slots = pick.shape
    devices = lax.axis_size("expert")
    place = lax.axis_index("expert")
    group = devices // experts
    requests = shift.shape[0]
    hidden = w_up.shape[0]
    info = jnp.stack([place // (devices // requests), place // group]).astype(jnp.int32)
    pick = pick[0]
    comb = combine[0]

    far = [d * group for d in turns(experts)[1:]]
    near = []
    bit = group // 2
    while bit:
        near.append(bit)
        bit //= 2

    def swap(x, mask):
        return lax.ppermute(x, "expert", [(i, i ^ mask) for i in range(devices)])

    tokens, shift, scale, gate, pick, comb, count = [
        pltpu.with_memory_space_constraint(x, pltpu.HBM)
        for x in (tokens, shift, scale, gate, pick, comb, count)
    ]
    farthest, tok, table, picks, weights = first(info, tokens, pick, shift, scale, gate, comb, count)
    own, *others = rest(tok, table, picks)

    flat = [farthest] + others
    blocks = [own] + [swap(x, mask) for x, mask in zip(flat, far)]
    mixes = mixer(picks, weights, blocks[1], tok_rows)
    blocks[2] = join([blocks[2]], [mixes[0]])
    beside = [swap(block, near[0]) for block in blocks]
    beside[-1] = join([beside[-1]], [])
    early, late = list(range(experts // 2)), list(range(experts // 2, experts))
    parts = []
    segments = {}
    for members in (early, late):
        pieces = [join([x for i in members for x in (blocks[i], beside[i])], [])]
        height = pieces[0].shape[0]
        for mask in near[1:]:
            block = pieces[0] if len(pieces) == 1 else join(pieces, [])
            pieces = [block, swap(block, mask)]
        for at, i in enumerate(members):
            segments[i] = []
            for k, piece in enumerate(pieces):
                for base in range(2 * at * slots, piece.shape[0], height):
                    segments[i].append((len(parts) + k, base, base + 2 * slots))
        parts += pieces
    far_blocks, near_blocks = [2, 1], list(range(3, experts)) + [0]
    sources = [
        cut
        for members in (far_blocks, near_blocks)
        for cuts in zip(*[segments[i] for i in members])
        for cut in cuts
    ]
    count = sum(high - low for _, low, high in sources)
    skip = 2 * slots * len(far_blocks) * len(segments[1])
    hid = up(parts, sources, w_up, [])

    def gather(keep, sends, columns):
        for i, mask in enumerate(reversed(near[1:])):
            if i:
                middle = keep.shape[0] // 2
                height = middle // len(sends)
                cuts = [(0, middle, 0, width)] + [
                    (at, at + height, 0, width) for at in range(middle, 2 * middle, height)
                ]
                keep, *sends = add(keep, gots, cuts, [F32] + [BF16] * len(sends))
            gots = [swap(send, mask) for send in sends]
        cuts = []
        for at, pieces in enumerate(columns):
            each = width // pieces
            for c in range(pieces):
                for side in (1, 0):
                    low = (2 * at + side) * slots
                    cuts.append((low, low + slots, c * each, (c + 1) * each))
        out = add(keep, gots, cuts, [BF16, F32] * (len(cuts) // 2))
        split = []
        for pieces in columns:
            split.append([out[2 * c:2 * c + 2] for c in range(pieces)])
            out = out[2 * pieces:]
        return split

    def total(send, keep):
        cuts = [(0, slots, 0, keep.shape[1])]
        return add(keep, [swap(send, near[0])], cuts, [BF16])[0]

    tile = width // 4
    keep, *sends = down(hid, (0, skip), w_down, (0, width, tile), 1, [], [])
    far_rows = gather(keep, sends, [1, 1])
    after = [far_rows[0][0][0]]
    keep, *sends = down(hid, (skip, count), w_down, (0, width, tile), 4, after, [])
    near_rows = gather(keep, sends, [2] * (experts - 3) + [1])
    back = []
    for block, mask in zip(far_rows[::-1] + near_rows[:-1], far):
        parts_of = [total(*piece) for piece in block]
        back.append([swap(part, mask) for part in parts_of])
        if mask == far[1]:
            far_part = parts_of[0]
    for i in range(2):
        for _ in range(2):
            back[i] = [join(back[i], [])]
    ((send, keep),) = near_rows[-1]
    acc = own_part(mixes[0], keep, swap(join([send], [far_part]), near[0]), back[0][0])
    return post(mixes[1], table, acc, back[1:])


def solution(mesh):
    return jax.shard_map(
        shards,
        mesh=mesh,
        in_specs=(
            P(("groups", "expert"), None),
            P("groups", None),
            P("groups", None),
            P("groups", None),
            P("expert", None),
            P("expert", None),
            P(("groups", "expert"), None, None),
            P(("groups", "expert"), None),
            P(("groups", "expert"), None, None),
        ),
        out_specs=P(("groups", "expert"), None),
        check_vma=False,
    )
```

```python
import functools

import jax
import jax.numpy as jnp
from jax import lax
from jax.experimental import pallas as pl
from jax.experimental.pallas import tpu as pltpu
from jax.sharding import PartitionSpec as P

MIB = 1024 * 1024
F32 = jnp.float32
BF16 = jnp.bfloat16

SMEM = pl.BlockSpec(memory_space=pltpu.SMEM)
VMEM = pl.BlockSpec(memory_space=pltpu.VMEM)
HBM = pl.BlockSpec(memory_space=pltpu.HBM)
ANY = pl.BlockSpec(memory_space=pl.ANY)


FREE = pl.CostEstimate(flops=1, bytes_accessed=1, transcendentals=0)

BUSY = pl.CostEstimate(flops=4 * 10**10, bytes_accessed=128 * MIB, transcendentals=0)


def params(mib):
    return pltpu.CompilerParams(vmem_limit_bytes=mib * MIB)


def fetch(pairs, sems):
    copies = [pltpu.make_async_copy(src, dst, sems.at[i]) for i, (src, dst) in enumerate(pairs)]
    for copy in copies:
        copy.start()
    for copy in copies:
        copy.wait()


def turns(experts):
    return [0] + list(range(experts - 1, 0, -1))


def hot_rows(picks, tok_rows):
    return lax.broadcasted_iota(jnp.int32, (tok_rows, picks.shape[1]), 0) == picks


def modulate(picks, tok_ref, table_ref):
    hot = hot_rows(picks, tok_ref.shape[0]).astype(F32).astype(BF16)
    values = lax.dot_general(hot, tok_ref[...], (((0,), (0,)), ((), ())), preferred_element_type=F32)
    center = values - jnp.mean(values, axis=1, keepdims=True)
    spread = jnp.mean(center * center, axis=1, keepdims=True)
    normed = center * (1.0 / jnp.sqrt(spread + 1e-06))
    return (normed * table_ref[0:1, :] + table_ref[1:2, :]).astype(BF16)


def first_kernel(info_ref, *refs):
    sources = refs[:7]
    far_ref, tok_ref, table_ref, picks_ref, weights_ref = refs[7:12]
    pick_ref, comb_ref, count_ref, shift_ref, scale_ref, gate_ref, sems = refs[12:]
    fetch(
        list(zip(sources, (tok_ref, pick_ref, shift_ref, scale_ref, gate_ref, comb_ref, count_ref))),
        sems,
    )
    experts, slots = pick_ref.shape
    which = pl.ds(info_ref[0], 1)
    table_ref[0:1, :] = 1.0 + scale_ref[which, :]
    table_ref[1:2, :] = shift_ref[which, :]
    table_ref[2:3, :] = gate_ref[which, :]
    lanes = lax.broadcasted_iota(jnp.int32, (1, slots), 1)
    for i, d in enumerate(turns(experts)):
        e = info_ref[1] ^ d
        picks_ref[i:i + 1, :] = pick_ref[pl.ds(e, 1), :]
        weights_ref[i:i + 1, :] = jnp.where(lanes < count_ref[0, e], comb_ref[pl.ds(e, 1), :], 0.0)
    far_ref[...] = modulate(picks_ref[1:2, :], tok_ref, table_ref)


def first(info, tokens, pick, shift, scale, gate, comb, count):
    experts, slots = pick.shape
    width = tokens.shape[1]
    return pl.pallas_call(
        first_kernel,
        in_specs=[SMEM] + [HBM] * 7,
        out_specs=[VMEM] * 5,
        out_shape=[
            jax.ShapeDtypeStruct((slots, width), BF16),
            jax.ShapeDtypeStruct(tokens.shape, BF16),
            jax.ShapeDtypeStruct((3, width), F32),
            jax.ShapeDtypeStruct(pick.shape, jnp.int32),
            jax.ShapeDtypeStruct(comb.shape, F32),
        ],
        scratch_shapes=[
            pltpu.VMEM(pick.shape, jnp.int32),
            pltpu.VMEM(comb.shape, F32),
            pltpu.SMEM(count.shape, jnp.int32),
            pltpu.VMEM(shift.shape, F32),
            pltpu.VMEM(scale.shape, F32),
            pltpu.VMEM(gate.shape, F32),
            pltpu.SemaphoreType.DMA((7,)),
        ],
        compiler_params=params(8),
        cost_estimate=FREE,
        name="first",
    )(info, tokens, pick, shift, scale, gate, comb, count)


def rest_kernel(tok_ref, table_ref, picks_ref, *outs):
    experts, slots = picks_ref.shape
    order = [0] + list(range(2, experts))
    picks = jnp.concatenate([picks_ref[i:i + 1, :] for i in order], axis=1)
    rows = modulate(picks, tok_ref, table_ref)
    for i, out in enumerate(outs):
        out[...] = rows[i * slots:(i + 1) * slots]


def rest(tok, table, picks):
    experts, slots = picks.shape
    return pl.pallas_call(
        rest_kernel,
        in_specs=[VMEM] * 3,
        out_specs=[VMEM] * (experts - 1),
        out_shape=[jax.ShapeDtypeStruct((slots, tok.shape[1]), BF16)] * (experts - 1),
        compiler_params=params(8),
        cost_estimate=BUSY,
        name="rest",
    )(tok, table, picks)


def mixer_kernel(picks_ref, weights_ref, after_ref, *outs):
    for i, out in enumerate(outs):
        each = picks_ref.shape[0] // len(outs)
        rows = range(i * each, (i + 1) * each)
        picks = jnp.concatenate([picks_ref[r:r + 1, :] for r in rows], axis=1)
        weights = jnp.concatenate([weights_ref[r:r + 1, :] for r in rows], axis=1)
        mix = jnp.where(hot_rows(picks, out.shape[0]), weights, 0.0)
        high = mix.astype(BF16).astype(F32)
        out[...] = jnp.concatenate([high, mix - high], axis=1).astype(BF16)


def mixer(picks, weights, after, tok_rows):
    experts, slots = picks.shape
    return pl.pallas_call(
        mixer_kernel,
        in_specs=[VMEM] * 2 + [ANY],
        out_specs=[VMEM] * 2,
        out_shape=[jax.ShapeDtypeStruct((tok_rows, experts * slots), BF16)] * 2,
        compiler_params=params(4),
        cost_estimate=FREE,
        name="mixer",
    )(picks, weights, after)


def join_kernel(*refs, count):
    out_ref = refs[-1]
    at = 0
    for ref in refs[:count]:
        out_ref[at:at + ref.shape[0], :] = ref[...]
        at += ref.shape[0]


def join(parts, after):
    return pl.pallas_call(
        functools.partial(join_kernel, count=len(parts)),
        in_specs=[VMEM] * len(parts) + [ANY] * len(after),
        out_specs=VMEM,
        out_shape=jax.ShapeDtypeStruct((sum(p.shape[0] for p in parts), parts[0].shape[1]), BF16),
        compiler_params=params(2),
        cost_estimate=FREE,
        name="join",
    )(*parts, *after)


def up_kernel(*refs, sources, count):
    w_ref = refs[count]
    out_ref, rows_ref = refs[-2:]
    to = 0
    for source, low, high in sources:
        rows_ref[to:to + high - low, :] = refs[source][low:high, :]
        to += high - low
    hidden = w_ref.shape[0]
    tile = min(1024, hidden)

    @pl.loop(0, hidden // tile)
    def _(i):
        cut = pl.ds(pl.multiple_of(i * tile, tile), tile)
        lifted = lax.dot_general(
            w_ref[cut, :], rows_ref[...], (((1,), (1,)), ((), ())), preferred_element_type=F32
        )
        out_ref[:, cut] = jax.nn.gelu(lifted, approximate=True).astype(BF16).T


def up(parts, sources, w, after):
    hidden, width = w.shape
    rows = sum(high - low for _, low, high in sources)
    return pl.pallas_call(
        functools.partial(up_kernel, sources=sources, count=len(parts)),
        in_specs=[VMEM] * (len(parts) + 1) + [ANY] * len(after),
        out_specs=VMEM,
        out_shape=jax.ShapeDtypeStruct((rows, hidden), BF16),
        scratch_shapes=[pltpu.VMEM((rows, width), BF16)],
        compiler_params=params(8),
        cost_estimate=FREE,
        name="up",
    )(*parts, w, *after)


def down_kernel(h_ref, w_ref, *outs, columns, low):
    first, last, tile = columns
    groups = len(outs) // 2
    half = outs[0].shape[0]

    @pl.loop(0, (last - first) // tile)
    def _(i):
        to = pl.ds(pl.multiple_of(i * tile, tile), tile)
        cut = pl.ds(pl.multiple_of(first + i * tile, tile), tile)
        rows = slice(low, low + 2 * half * groups)
        out = jnp.dot(h_ref[rows, :], w_ref[:, cut], preferred_element_type=F32)
        for g in range(groups):
            at = 2 * half * g
            outs[2 * g][:, to] = out[at:at + half]
            outs[2 * g + 1][:, to] = out[at + half:at + 2 * half].astype(BF16)


def down(hid, low, groups, w, columns):
    half = hid.shape[0] // 4
    step = columns[1] - columns[0]
    return pl.pallas_call(
        functools.partial(down_kernel, columns=columns, low=low),
        in_specs=[VMEM] * 2,
        out_specs=[VMEM] * (2 * groups),
        out_shape=[
            jax.ShapeDtypeStruct((half, step), F32),
            jax.ShapeDtypeStruct((half, step), BF16),
        ]
        * groups,
        compiler_params=params(8),
        cost_estimate=FREE,
        name="down",
    )(hid, w)


def add_kernel(*refs, count, outs):
    for ref, pieces in zip(refs[2 * count:], outs):
        at = 0
        for i, low, high in pieces:
            keep_ref, got_ref = refs[2 * i:2 * i + 2]
            step = keep_ref.shape[1]
            total = keep_ref[low:high] + got_ref[low:high].astype(F32)
            ref[:, at:at + step] = total.astype(ref.dtype)
            at += step


def add(pairs, outs, kinds):
    args = [x for pair in pairs for x in pair]
    shapes = [
        (pieces[0][2] - pieces[0][1], sum(pairs[i][0].shape[1] for i, _, _ in pieces))
        for pieces in outs
    ]
    return pl.pallas_call(
        functools.partial(add_kernel, count=len(pairs), outs=outs),
        in_specs=[VMEM] * len(args),
        out_specs=[VMEM] * len(outs),
        out_shape=[jax.ShapeDtypeStruct(shape, k) for shape, k in zip(shapes, kinds)],
        compiler_params=params(8),
        cost_estimate=FREE,
        name="add",
    )(*args)


def own_kernel(mix_ref, keep_ref, near_ref, got_ref, acc_ref):
    own = (keep_ref[...] + near_ref[...].astype(F32)).astype(BF16)
    values = jnp.concatenate([own, got_ref[...]] * 2, axis=0)
    acc_ref[...] = jnp.dot(mix_ref[...], values, preferred_element_type=F32)


def own_part(mix, keep, near, got):
    return pl.pallas_call(
        own_kernel,
        in_specs=[VMEM] * 4,
        out_specs=VMEM,
        out_shape=jax.ShapeDtypeStruct((mix.shape[0], keep.shape[1]), F32),
        compiler_params=params(12),
        cost_estimate=FREE,
        name="own_part",
    )(mix, keep, near, got)


def post_kernel(mix_ref, table_ref, acc_ref, *refs):
    blocks = refs[:-3]
    out_hbm, out_ref, sems = refs[-3:]
    step = out_ref.shape[1] // sems.shape[0]
    copies = []
    for i in range(sems.shape[0]):
        cut = pl.ds(i * step, step)
        values = jnp.concatenate([ref[:, cut] for ref in blocks] * 2, axis=0)
        mixed = acc_ref[:, cut] + jnp.dot(mix_ref[...], values, preferred_element_type=F32)
        out_ref[:, cut] = (table_ref[2:3, cut] * mixed).astype(BF16)
        copy = pltpu.make_async_copy(out_ref.at[:, cut], out_hbm.at[:, cut], sems.at[i])
        copy.start()
        copies.append(copy)
    for copy in copies:
        copy.wait()


def post(mix, table, acc, blocks):
    tok_rows, width = acc.shape
    return pl.pallas_call(
        post_kernel,
        in_specs=[VMEM] * (3 + len(blocks)),
        out_specs=HBM,
        out_shape=jax.ShapeDtypeStruct((tok_rows, width), BF16),
        scratch_shapes=[pltpu.VMEM((tok_rows, width), BF16), pltpu.SemaphoreType.DMA((4,))],
        compiler_params=params(8),
        cost_estimate=FREE,
        name="post",
    )(mix, table, acc, *blocks)


def shards(tokens, shift, scale, gate, w_up, w_down, pick, count, combine):
    tok_rows, width = tokens.shape
    _, experts, slots = pick.shape
    devices = lax.axis_size("expert")
    place = lax.axis_index("expert")
    group = devices // experts
    requests = shift.shape[0]
    hidden = w_up.shape[0]
    info = jnp.stack([place // (devices // requests), place // group]).astype(jnp.int32)
    pick = pick[0]
    comb = combine[0]

    far = [d * group for d in turns(experts)[1:]]
    near = []
    bit = group // 2
    while bit:
        near.append(bit)
        bit //= 2

    def swap(x, mask):
        return lax.ppermute(x, "expert", [(i, i ^ mask) for i in range(devices)])

    tokens, shift, scale, gate, pick, comb, count = [
        pltpu.with_memory_space_constraint(x, pltpu.HBM)
        for x in (tokens, shift, scale, gate, pick, comb, count)
    ]
    farthest, tok, table, picks, weights = first(info, tokens, pick, shift, scale, gate, comb, count)
    own, *others = rest(tok, table, picks)

    flat = [farthest] + others
    blocks = [own] + [swap(x, mask) for x, mask in zip(flat, far)]
    mixes = mixer(picks, weights, blocks[1], tok_rows)
    blocks[2] = join([blocks[2]], [mixes[0]])
    beside = [swap(block, near[0]) for block in blocks]
    beside[-1] = join([beside[-1]], [])
    early, late = list(range(experts // 2)), list(range(experts // 2, experts))
    parts = []
    segments = {}
    for members in (early, late):
        pieces = [join([x for i in members for x in (blocks[i], beside[i])], [])]
        height = pieces[0].shape[0]
        for mask in near[1:]:
            block = pieces[0] if len(pieces) == 1 else join(pieces, [])
            pieces = [block, swap(block, mask)]
        for at, i in enumerate(members):
            segments[i] = []
            for k, piece in enumerate(pieces):
                for base in range(2 * at * slots, piece.shape[0], height):
                    segments[i].append((len(parts) + k, base, base + 2 * slots))
        parts += pieces
    groups = [[1, 2], list(range(3, experts)) + [0]]
    sources = [
        cut for members in groups for cuts in zip(*[segments[i] for i in members]) for cut in cuts
    ]
    hid = up(parts, sources, w_up, [])

    def gather(keep, send):
        for i, mask in enumerate(reversed(near[1:])):
            if i:
                middle = keep.shape[0] // 2
                keep, send = add(
                    [(keep, got)], [[(0, 0, middle)], [(0, middle, 2 * middle)]], [F32, BF16]
                )
            got = swap(send, mask)
        return keep, got

    half = hid.shape[0] // 2
    step = 5 * width // 8
    keep, send, *others = down(hid, 0, 2, w_down, (0, step, step // 2))
    heads = [gather(keep, send), gather(*others)]
    tails = []
    for g in range(2):
        keep, send = down(hid, g * half, 1, w_down, (step, width, width - step))
        tails.append(gather(keep, send))
    block = {}
    for members, head, tail in zip(groups, heads, tails):
        outs = []
        for at in range(len(members)):
            for side in (1, 0):
                low = (2 * at + side) * slots
                outs.append([(piece, low, low + slots) for piece in range(2)])
        sums = add([head, tail], outs, [BF16, F32] * len(members))
        block.update((i, sums[2 * at:2 * at + 2]) for at, i in enumerate(members))

    def total(send, keep):
        return add([(keep, swap(send, near[0]))], [[(0, 0, slots)]], [BF16])[0]

    sums = [total(*block[i]) for i in range(1, experts)]
    back = [swap(part, mask) for part, mask in zip(sums, far)]
    send, keep = block[0]
    acc = own_part(mixes[0], keep, swap(join([send], [sums[0]]), near[0]), back[0])
    return post(mixes[1], table, acc, back[1:])


def solution(mesh):
    return jax.shard_map(
        shards,
        mesh=mesh,
        in_specs=(
            P(("groups", "expert"), None),
            P("groups", None),
            P("groups", None),
            P("groups", None),
            P("expert", None),
            P("expert", None),
            P(("groups", "expert"), None, None),
            P(("groups", "expert"), None),
            P(("groups", "expert"), None, None),
        ),
        out_specs=P(("groups", "expert"), None),
        check_vma=False,
    )
```

```python
import functools

import jax
import jax.numpy as jnp
from jax import lax
from jax.experimental import pallas as pl
from jax.experimental.pallas import tpu as pltpu
from jax.sharding import PartitionSpec as P

MIB = 1024 * 1024
F32 = jnp.float32
BF16 = jnp.bfloat16

SMEM = pl.BlockSpec(memory_space=pltpu.SMEM)
VMEM = pl.BlockSpec(memory_space=pltpu.VMEM)
HBM = pl.BlockSpec(memory_space=pltpu.HBM)
ANY = pl.BlockSpec(memory_space=pl.ANY)


FREE = pl.CostEstimate(flops=1, bytes_accessed=1, transcendentals=0)

BUSY = pl.CostEstimate(flops=4 * 10**10, bytes_accessed=128 * MIB, transcendentals=0)


def params(mib):
    return pltpu.CompilerParams(vmem_limit_bytes=mib * MIB)


def fetch(pairs, sems):
    copies = [pltpu.make_async_copy(src, dst, sems.at[i]) for i, (src, dst) in enumerate(pairs)]
    for copy in copies:
        copy.start()
    for copy in copies:
        copy.wait()


def turns(experts):
    return [0] + list(range(experts - 1, 0, -1))


def hot_rows(picks, tok_rows):
    return lax.broadcasted_iota(jnp.int32, (tok_rows, picks.shape[1]), 0) == picks


def modulate(picks, tok_ref, table_ref):
    hot = hot_rows(picks, tok_ref.shape[0]).astype(F32).astype(BF16)
    values = lax.dot_general(hot, tok_ref[...], (((0,), (0,)), ((), ())), preferred_element_type=F32)
    center = values - jnp.mean(values, axis=1, keepdims=True)
    spread = jnp.mean(center * center, axis=1, keepdims=True)
    normed = center * (1.0 / jnp.sqrt(spread + 1e-06))
    return (normed * table_ref[0:1, :] + table_ref[1:2, :]).astype(BF16)


def first_kernel(info_ref, *refs):
    sources = refs[:7]
    far_ref, tok_ref, table_ref, picks_ref, weights_ref = refs[7:12]
    pick_ref, comb_ref, count_ref, shift_ref, scale_ref, gate_ref, sems = refs[12:]
    fetch(
        list(zip(sources, (tok_ref, pick_ref, shift_ref, scale_ref, gate_ref, comb_ref, count_ref))),
        sems,
    )
    experts, slots = pick_ref.shape
    which = pl.ds(info_ref[0], 1)
    table_ref[0:1, :] = 1.0 + scale_ref[which, :]
    table_ref[1:2, :] = shift_ref[which, :]
    table_ref[2:3, :] = gate_ref[which, :]
    lanes = lax.broadcasted_iota(jnp.int32, (1, slots), 1)
    for i, d in enumerate(turns(experts)):
        e = info_ref[1] ^ d
        picks_ref[i:i + 1, :] = pick_ref[pl.ds(e, 1), :]
        weights_ref[i:i + 1, :] = jnp.where(lanes < count_ref[0, e], comb_ref[pl.ds(e, 1), :], 0.0)
    far_ref[...] = modulate(picks_ref[1:2, :], tok_ref, table_ref)


def first(info, tokens, pick, shift, scale, gate, comb, count):
    experts, slots = pick.shape
    width = tokens.shape[1]
    return pl.pallas_call(
        first_kernel,
        in_specs=[SMEM] + [HBM] * 7,
        out_specs=[VMEM] * 5,
        out_shape=[
            jax.ShapeDtypeStruct((slots, width), BF16),
            jax.ShapeDtypeStruct(tokens.shape, BF16),
            jax.ShapeDtypeStruct((3, width), F32),
            jax.ShapeDtypeStruct(pick.shape, jnp.int32),
            jax.ShapeDtypeStruct(comb.shape, F32),
        ],
        scratch_shapes=[
            pltpu.VMEM(pick.shape, jnp.int32),
            pltpu.VMEM(comb.shape, F32),
            pltpu.SMEM(count.shape, jnp.int32),
            pltpu.VMEM(shift.shape, F32),
            pltpu.VMEM(scale.shape, F32),
            pltpu.VMEM(gate.shape, F32),
            pltpu.SemaphoreType.DMA((7,)),
        ],
        compiler_params=params(8),
        cost_estimate=FREE,
        name="first",
    )(info, tokens, pick, shift, scale, gate, comb, count)


def rest_kernel(tok_ref, table_ref, picks_ref, *outs):
    experts, slots = picks_ref.shape
    order = [0] + list(range(2, experts))
    picks = jnp.concatenate([picks_ref[i:i + 1, :] for i in order], axis=1)
    rows = modulate(picks, tok_ref, table_ref)
    for i, out in enumerate(outs):
        out[...] = rows[i * slots:(i + 1) * slots]


def rest(tok, table, picks):
    experts, slots = picks.shape
    return pl.pallas_call(
        rest_kernel,
        in_specs=[VMEM] * 3,
        out_specs=[VMEM] * (experts - 1),
        out_shape=[jax.ShapeDtypeStruct((slots, tok.shape[1]), BF16)] * (experts - 1),
        compiler_params=params(8),
        cost_estimate=BUSY,
        name="rest",
    )(tok, table, picks)


def mixer_kernel(picks_ref, weights_ref, after_ref, *outs):
    for i, out in enumerate(outs):
        each = picks_ref.shape[0] // len(outs)
        rows = range(i * each, (i + 1) * each)
        picks = jnp.concatenate([picks_ref[r:r + 1, :] for r in rows], axis=1)
        weights = jnp.concatenate([weights_ref[r:r + 1, :] for r in rows], axis=1)
        mix = jnp.where(hot_rows(picks, out.shape[0]), weights, 0.0)
        high = mix.astype(BF16).astype(F32)
        out[...] = jnp.concatenate([high, mix - high], axis=1).astype(BF16)


def mixer(picks, weights, after, tok_rows):
    experts, slots = picks.shape
    return pl.pallas_call(
        mixer_kernel,
        in_specs=[VMEM] * 2 + [ANY],
        out_specs=[VMEM] * 2,
        out_shape=[jax.ShapeDtypeStruct((tok_rows, experts * slots), BF16)] * 2,
        compiler_params=params(4),
        cost_estimate=FREE,
        name="mixer",
    )(picks, weights, after)


def join_kernel(*refs, count):
    out_ref = refs[-1]
    at = 0
    for ref in refs[:count]:
        out_ref[at:at + ref.shape[0], :] = ref[...]
        at += ref.shape[0]


def join(parts, after):
    return pl.pallas_call(
        functools.partial(join_kernel, count=len(parts)),
        in_specs=[VMEM] * len(parts) + [ANY] * len(after),
        out_specs=VMEM,
        out_shape=jax.ShapeDtypeStruct((sum(p.shape[0] for p in parts), parts[0].shape[1]), BF16),
        compiler_params=params(2),
        cost_estimate=FREE,
        name="join",
    )(*parts, *after)


def up_kernel(*refs, sources, count):
    w_ref = refs[count]
    out_ref, rows_ref = refs[-2:]
    to = 0
    for source, low, high in sources:
        rows_ref[to:to + high - low, :] = refs[source][low:high, :]
        to += high - low
    hidden = w_ref.shape[0]
    tile = min(1024, hidden)

    @pl.loop(0, hidden // tile)
    def _(i):
        cut = pl.ds(pl.multiple_of(i * tile, tile), tile)
        lifted = lax.dot_general(
            w_ref[cut, :], rows_ref[...], (((1,), (1,)), ((), ())), preferred_element_type=F32
        )
        out_ref[:, cut] = jax.nn.gelu(lifted, approximate=True).astype(BF16).T


def up(parts, sources, w, after):
    hidden, width = w.shape
    rows = sum(high - low for _, low, high in sources)
    return pl.pallas_call(
        functools.partial(up_kernel, sources=sources, count=len(parts)),
        in_specs=[VMEM] * (len(parts) + 1) + [ANY] * len(after),
        out_specs=VMEM,
        out_shape=jax.ShapeDtypeStruct((rows, hidden), BF16),
        scratch_shapes=[pltpu.VMEM((rows, width), BF16)],
        compiler_params=params(8),
        cost_estimate=FREE,
        name="up",
    )(*parts, w, *after)


def down_kernel(h_ref, w_ref, *refs, columns, low, groups):
    first, last, tile = columns
    outs = refs[len(refs) - 2 * groups:]
    half = outs[0].shape[0]

    @pl.loop(0, (last - first) // tile)
    def _(i):
        to = pl.ds(pl.multiple_of(i * tile, tile), tile)
        cut = pl.ds(pl.multiple_of(first + i * tile, tile), tile)
        rows = slice(low, low + 2 * half * groups)
        out = jnp.dot(h_ref[rows, :], w_ref[:, cut], preferred_element_type=F32)
        for g in range(groups):
            at = 2 * half * g
            outs[2 * g][:, to] = out[at:at + half]
            outs[2 * g + 1][:, to] = out[at + half:at + 2 * half].astype(BF16)


def down(hid, low, groups, w, columns, after):
    half = hid.shape[0] // 4
    step = columns[1] - columns[0]
    return pl.pallas_call(
        functools.partial(down_kernel, columns=columns, low=low, groups=groups),
        in_specs=[VMEM] * 2 + [ANY] * len(after),
        out_specs=[VMEM] * (2 * groups),
        out_shape=[
            jax.ShapeDtypeStruct((half, step), F32),
            jax.ShapeDtypeStruct((half, step), BF16),
        ]
        * groups,
        compiler_params=params(8),
        cost_estimate=FREE,
        name="down",
    )(hid, w, *after)


def add_kernel(*refs, count, outs):
    for ref, pieces in zip(refs[2 * count:], outs):
        at = 0
        for i, low, high in pieces:
            keep_ref, got_ref = refs[2 * i:2 * i + 2]
            step = keep_ref.shape[1]
            total = keep_ref[low:high] + got_ref[low:high].astype(F32)
            ref[:, at:at + step] = total.astype(ref.dtype)
            at += step


def add(pairs, outs, kinds):
    args = [x for pair in pairs for x in pair]
    shapes = [
        (pieces[0][2] - pieces[0][1], sum(pairs[i][0].shape[1] for i, _, _ in pieces))
        for pieces in outs
    ]
    return pl.pallas_call(
        functools.partial(add_kernel, count=len(pairs), outs=outs),
        in_specs=[VMEM] * len(args),
        out_specs=[VMEM] * len(outs),
        out_shape=[jax.ShapeDtypeStruct(shape, k) for shape, k in zip(shapes, kinds)],
        compiler_params=params(8),
        cost_estimate=FREE,
        name="add",
    )(*args)


def own_kernel(mix_ref, keep_ref, near_ref, got_ref, acc_ref):
    own = (keep_ref[...] + near_ref[...].astype(F32)).astype(BF16)
    values = jnp.concatenate([own, got_ref[...]] * 2, axis=0)
    acc_ref[...] = jnp.dot(mix_ref[...], values, preferred_element_type=F32)


def own_part(mix, keep, near, got):
    return pl.pallas_call(
        own_kernel,
        in_specs=[VMEM] * 4,
        out_specs=VMEM,
        out_shape=jax.ShapeDtypeStruct((mix.shape[0], keep.shape[1]), F32),
        compiler_params=params(12),
        cost_estimate=FREE,
        name="own_part",
    )(mix, keep, near, got)


def post_kernel(mix_ref, table_ref, acc_ref, *refs):
    blocks = refs[:-3]
    out_hbm, out_ref, sems = refs[-3:]
    step = out_ref.shape[1] // sems.shape[0]
    copies = []
    for i in range(sems.shape[0]):
        cut = pl.ds(i * step, step)
        values = jnp.concatenate([ref[:, cut] for ref in blocks] * 2, axis=0)
        mixed = acc_ref[:, cut] + jnp.dot(mix_ref[...], values, preferred_element_type=F32)
        out_ref[:, cut] = (table_ref[2:3, cut] * mixed).astype(BF16)
        copy = pltpu.make_async_copy(out_ref.at[:, cut], out_hbm.at[:, cut], sems.at[i])
        copy.start()
        copies.append(copy)
    for copy in copies:
        copy.wait()


def post(mix, table, acc, blocks):
    tok_rows, width = acc.shape
    return pl.pallas_call(
        post_kernel,
        in_specs=[VMEM] * (3 + len(blocks)),
        out_specs=HBM,
        out_shape=jax.ShapeDtypeStruct((tok_rows, width), BF16),
        scratch_shapes=[pltpu.VMEM((tok_rows, width), BF16), pltpu.SemaphoreType.DMA((4,))],
        compiler_params=params(8),
        cost_estimate=FREE,
        name="post",
    )(mix, table, acc, *blocks)


def shards(tokens, shift, scale, gate, w_up, w_down, pick, count, combine):
    tok_rows, width = tokens.shape
    _, experts, slots = pick.shape
    devices = lax.axis_size("expert")
    place = lax.axis_index("expert")
    group = devices // experts
    requests = shift.shape[0]
    hidden = w_up.shape[0]
    info = jnp.stack([place // (devices // requests), place // group]).astype(jnp.int32)
    pick = pick[0]
    comb = combine[0]

    far = [d * group for d in turns(experts)[1:]]
    near = []
    bit = group // 2
    while bit:
        near.append(bit)
        bit //= 2

    def swap(x, mask):
        return lax.ppermute(x, "expert", [(i, i ^ mask) for i in range(devices)])

    tokens, shift, scale, gate, pick, comb, count = [
        pltpu.with_memory_space_constraint(x, pltpu.HBM)
        for x in (tokens, shift, scale, gate, pick, comb, count)
    ]
    farthest, tok, table, picks, weights = first(info, tokens, pick, shift, scale, gate, comb, count)
    own, *others = rest(tok, table, picks)

    flat = [farthest] + others
    blocks = [own] + [swap(x, mask) for x, mask in zip(flat, far)]
    mixes = mixer(picks, weights, blocks[1], tok_rows)
    blocks[2] = join([blocks[2]], [mixes[0]])
    beside = [swap(block, near[0]) for block in blocks]
    beside[-1] = join([beside[-1]], [])
    early, late = list(range(experts // 2)), list(range(experts // 2, experts))
    parts = []
    segments = {}
    for members in (early, late):
        pieces = [join([x for i in members for x in (blocks[i], beside[i])], [])]
        height = pieces[0].shape[0]
        for mask in near[1:]:
            block = pieces[0] if len(pieces) == 1 else join(pieces, [])
            pieces = [block, swap(block, mask)]
        for at, i in enumerate(members):
            segments[i] = []
            for k, piece in enumerate(pieces):
                for base in range(2 * at * slots, piece.shape[0], height):
                    segments[i].append((len(parts) + k, base, base + 2 * slots))
        parts += pieces
    groups = [[1, 2], list(range(3, experts)) + [0]]
    sources = [
        cut for members in groups for cuts in zip(*[segments[i] for i in members]) for cut in cuts
    ]
    hid = up(parts, sources, w_up, [])

    def gather(keep, send):
        for i, mask in enumerate(reversed(near[1:])):
            if i:
                middle = keep.shape[0] // 2
                keep, send = add(
                    [(keep, got)], [[(0, 0, middle)], [(0, middle, 2 * middle)]], [F32, BF16]
                )
            got = swap(send, mask)
        return keep, got

    half = hid.shape[0] // 2
    step = 5 * width // 8
    keep, send, *others = down(hid, 0, 2, w_down, (0, step, step // 2), [])
    heads = [gather(keep, send), gather(*others)]
    def sums_of(members, pairs):
        outs = []
        for at in range(len(members)):
            for side in (1, 0):
                low = (2 * at + side) * slots
                outs.append([(piece, low, low + slots) for piece in range(len(pairs))])
        sums = add(pairs, outs, [BF16, F32] * len(members))
        return {i: sums[2 * at:2 * at + 2] for at, i in enumerate(members)}

    tail = gather(*down(hid, 0, 1, w_down, (step, width, width - step), []))
    block = sums_of(groups[0], [heads[0], tail])
    tails = []
    after = []
    part = (width - step) // 2
    for low in range(step, width, part):
        tails.append(gather(*down(hid, half, 1, w_down, (low, low + part, part), after)))
    block.update(sums_of(groups[1], [heads[1]] + tails))

    def total(send, keep):
        return add([(keep, swap(send, near[0]))], [[(0, 0, slots)]], [BF16])[0]

    sums = [total(*block[i]) for i in range(1, experts)]
    back = [swap(sums[0], far[0])]
    for k in range(1, experts - 1):
        part = sums[k] if k == 1 else join([sums[k]], back[:1])
        back.append(swap(part, far[k]))
    send, keep = block[0]
    acc = own_part(mixes[0], keep, swap(join([send], [sums[1]]), near[0]), back[0])
    return post(mixes[1], table, acc, back[1:])


def solution(mesh):
    return jax.shard_map(
        shards,
        mesh=mesh,
        in_specs=(
            P(("groups", "expert"), None),
            P("groups", None),
            P("groups", None),
            P("groups", None),
            P("expert", None),
            P("expert", None),
            P(("groups", "expert"), None, None),
            P(("groups", "expert"), None),
            P(("groups", "expert"), None, None),
        ),
        out_specs=P(("groups", "expert"), None),
        check_vma=False,
    )
```

```python
import functools

import jax
import jax.numpy as jnp
from jax import lax
from jax.experimental import pallas as pl
from jax.experimental.pallas import tpu as pltpu
from jax.sharding import PartitionSpec as P

MIB = 1024 * 1024
F32 = jnp.float32
BF16 = jnp.bfloat16

SMEM = pl.BlockSpec(memory_space=pltpu.SMEM)
VMEM = pl.BlockSpec(memory_space=pltpu.VMEM)
HBM = pl.BlockSpec(memory_space=pltpu.HBM)
ANY = pl.BlockSpec(memory_space=pl.ANY)


FREE = pl.CostEstimate(flops=1, bytes_accessed=1, transcendentals=0)

BUSY = pl.CostEstimate(flops=4 * 10**10, bytes_accessed=128 * MIB, transcendentals=0)


def params(mib):
    return pltpu.CompilerParams(vmem_limit_bytes=mib * MIB)


def fetch(pairs, sems):
    copies = [pltpu.make_async_copy(src, dst, sems.at[i]) for i, (src, dst) in enumerate(pairs)]
    for copy in copies:
        copy.start()
    for copy in copies:
        copy.wait()


def turns(experts):
    return [0] + list(range(experts - 1, 0, -1))


def hot_rows(picks, tok_rows):
    return lax.broadcasted_iota(jnp.int32, (tok_rows, picks.shape[1]), 0) == picks


def modulate(picks, tok_ref, table_ref):
    hot = hot_rows(picks, tok_ref.shape[0]).astype(F32).astype(BF16)
    values = lax.dot_general(hot, tok_ref[...], (((0,), (0,)), ((), ())), preferred_element_type=F32)
    center = values - jnp.mean(values, axis=1, keepdims=True)
    spread = jnp.mean(center * center, axis=1, keepdims=True)
    normed = center * (1.0 / jnp.sqrt(spread + 1e-06))
    return (normed * table_ref[0:1, :] + table_ref[1:2, :]).astype(BF16)


def first_kernel(info_ref, *refs):
    sources = refs[:7]
    far_ref, tok_ref, table_ref, picks_ref, weights_ref = refs[7:12]
    pick_ref, comb_ref, count_ref, shift_ref, scale_ref, gate_ref, sems = refs[12:]
    fetch(
        list(zip(sources, (tok_ref, pick_ref, shift_ref, scale_ref, gate_ref, comb_ref, count_ref))),
        sems,
    )
    experts, slots = pick_ref.shape
    which = pl.ds(info_ref[0], 1)
    table_ref[0:1, :] = 1.0 + scale_ref[which, :]
    table_ref[1:2, :] = shift_ref[which, :]
    table_ref[2:3, :] = gate_ref[which, :]
    lanes = lax.broadcasted_iota(jnp.int32, (1, slots), 1)
    for i, d in enumerate(turns(experts)):
        e = info_ref[1] ^ d
        picks_ref[i:i + 1, :] = pick_ref[pl.ds(e, 1), :]
        weights_ref[i:i + 1, :] = jnp.where(lanes < count_ref[0, e], comb_ref[pl.ds(e, 1), :], 0.0)
    far_ref[...] = modulate(picks_ref[1:2, :], tok_ref, table_ref)


def first(info, tokens, pick, shift, scale, gate, comb, count):
    experts, slots = pick.shape
    width = tokens.shape[1]
    return pl.pallas_call(
        first_kernel,
        in_specs=[SMEM] + [HBM] * 7,
        out_specs=[VMEM] * 5,
        out_shape=[
            jax.ShapeDtypeStruct((slots, width), BF16),
            jax.ShapeDtypeStruct(tokens.shape, BF16),
            jax.ShapeDtypeStruct((3, width), F32),
            jax.ShapeDtypeStruct(pick.shape, jnp.int32),
            jax.ShapeDtypeStruct(comb.shape, F32),
        ],
        scratch_shapes=[
            pltpu.VMEM(pick.shape, jnp.int32),
            pltpu.VMEM(comb.shape, F32),
            pltpu.SMEM(count.shape, jnp.int32),
            pltpu.VMEM(shift.shape, F32),
            pltpu.VMEM(scale.shape, F32),
            pltpu.VMEM(gate.shape, F32),
            pltpu.SemaphoreType.DMA((7,)),
        ],
        compiler_params=params(8),
        cost_estimate=FREE,
        name="first",
    )(info, tokens, pick, shift, scale, gate, comb, count)


def rest_kernel(tok_ref, table_ref, picks_ref, *outs):
    experts, slots = picks_ref.shape
    order = [0] + list(range(2, experts))
    picks = jnp.concatenate([picks_ref[i:i + 1, :] for i in order], axis=1)
    rows = modulate(picks, tok_ref, table_ref)
    for i, out in enumerate(outs):
        out[...] = rows[i * slots:(i + 1) * slots]


def rest(tok, table, picks):
    experts, slots = picks.shape
    return pl.pallas_call(
        rest_kernel,
        in_specs=[VMEM] * 3,
        out_specs=[VMEM] * (experts - 1),
        out_shape=[jax.ShapeDtypeStruct((slots, tok.shape[1]), BF16)] * (experts - 1),
        compiler_params=params(8),
        cost_estimate=BUSY,
        name="rest",
    )(tok, table, picks)


def mixer_kernel(picks_ref, weights_ref, after_ref, *outs):
    for i, out in enumerate(outs):
        each = picks_ref.shape[0] // len(outs)
        rows = range(i * each, (i + 1) * each)
        picks = jnp.concatenate([picks_ref[r:r + 1, :] for r in rows], axis=1)
        weights = jnp.concatenate([weights_ref[r:r + 1, :] for r in rows], axis=1)
        mix = jnp.where(hot_rows(picks, out.shape[0]), weights, 0.0)
        high = mix.astype(BF16).astype(F32)
        out[...] = jnp.concatenate([high, mix - high], axis=1).astype(BF16)


def mixer(picks, weights, after, tok_rows):
    experts, slots = picks.shape
    return pl.pallas_call(
        mixer_kernel,
        in_specs=[VMEM] * 2 + [ANY],
        out_specs=[VMEM] * 2,
        out_shape=[jax.ShapeDtypeStruct((tok_rows, experts * slots), BF16)] * 2,
        compiler_params=params(4),
        cost_estimate=FREE,
        name="mixer",
    )(picks, weights, after)


def join_kernel(*refs, count):
    out_ref = refs[-1]
    at = 0
    for ref in refs[:count]:
        out_ref[at:at + ref.shape[0], :] = ref[...]
        at += ref.shape[0]


def join(parts, after):
    return pl.pallas_call(
        functools.partial(join_kernel, count=len(parts)),
        in_specs=[VMEM] * len(parts) + [ANY] * len(after),
        out_specs=VMEM,
        out_shape=jax.ShapeDtypeStruct((sum(p.shape[0] for p in parts), parts[0].shape[1]), BF16),
        compiler_params=params(2),
        cost_estimate=FREE,
        name="join",
    )(*parts, *after)


def up_kernel(*refs, sources, count):
    w_ref = refs[count]
    out_ref, rows_ref = refs[-2:]
    to = 0
    for source, low, high in sources:
        rows_ref[to:to + high - low, :] = refs[source][low:high, :]
        to += high - low
    hidden = w_ref.shape[0]
    tile = min(1024, hidden)

    @pl.loop(0, hidden // tile)
    def _(i):
        cut = pl.ds(pl.multiple_of(i * tile, tile), tile)
        lifted = lax.dot_general(
            w_ref[cut, :], rows_ref[...], (((1,), (1,)), ((), ())), preferred_element_type=F32
        )
        out_ref[:, cut] = jax.nn.gelu(lifted, approximate=True).astype(BF16).T


def up(parts, sources, w, after):
    hidden, width = w.shape
    rows = sum(high - low for _, low, high in sources)
    return pl.pallas_call(
        functools.partial(up_kernel, sources=sources, count=len(parts)),
        in_specs=[VMEM] * (len(parts) + 1) + [ANY] * len(after),
        out_specs=VMEM,
        out_shape=jax.ShapeDtypeStruct((rows, hidden), BF16),
        scratch_shapes=[pltpu.VMEM((rows, width), BF16)],
        compiler_params=params(8),
        cost_estimate=FREE,
        name="up",
    )(*parts, w, *after)


def down_kernel(h_ref, w_ref, *refs, columns, low, groups):
    first, last, tile = columns
    outs = refs[len(refs) - 2 * groups:]
    half = outs[0].shape[0]

    @pl.loop(0, (last - first) // tile)
    def _(i):
        to = pl.ds(pl.multiple_of(i * tile, tile), tile)
        cut = pl.ds(pl.multiple_of(first + i * tile, tile), tile)
        rows = slice(low, low + 2 * half * groups)
        out = jnp.dot(h_ref[rows, :], w_ref[:, cut], preferred_element_type=F32)
        for g in range(groups):
            at = 2 * half * g
            outs[2 * g][:, to] = out[at:at + half]
            outs[2 * g + 1][:, to] = out[at + half:at + 2 * half].astype(BF16)


def down(hid, low, groups, w, columns, after):
    half = hid.shape[0] // 4
    step = columns[1] - columns[0]
    return pl.pallas_call(
        functools.partial(down_kernel, columns=columns, low=low, groups=groups),
        in_specs=[VMEM] * 2 + [ANY] * len(after),
        out_specs=[VMEM] * (2 * groups),
        out_shape=[
            jax.ShapeDtypeStruct((half, step), F32),
            jax.ShapeDtypeStruct((half, step), BF16),
        ]
        * groups,
        compiler_params=params(8),
        cost_estimate=FREE,
        name="down",
    )(hid, w, *after)


def add_kernel(*refs, count, outs):
    for ref, pieces in zip(refs[2 * count:], outs):
        at = 0
        for i, low, high in pieces:
            keep_ref, got_ref = refs[2 * i:2 * i + 2]
            step = keep_ref.shape[1]
            total = keep_ref[low:high] + got_ref[low:high].astype(F32)
            ref[:, at:at + step] = total.astype(ref.dtype)
            at += step


def add(pairs, outs, kinds):
    args = [x for pair in pairs for x in pair]
    shapes = [
        (pieces[0][2] - pieces[0][1], sum(pairs[i][0].shape[1] for i, _, _ in pieces))
        for pieces in outs
    ]
    return pl.pallas_call(
        functools.partial(add_kernel, count=len(pairs), outs=outs),
        in_specs=[VMEM] * len(args),
        out_specs=[VMEM] * len(outs),
        out_shape=[jax.ShapeDtypeStruct(shape, k) for shape, k in zip(shapes, kinds)],
        compiler_params=params(8),
        cost_estimate=FREE,
        name="add",
    )(*args)


def own_kernel(mix_ref, got_ref, *refs):
    acc_ref = refs[-1]
    own = [ref[...] for ref in refs[:-1]]
    own = own[0] if len(own) == 1 else jnp.concatenate(own, axis=1)
    values = jnp.concatenate([own, got_ref[...]] * 2, axis=0)
    acc_ref[...] = jnp.dot(mix_ref[...], values, preferred_element_type=F32)


def own_part(mix, got, own):
    return pl.pallas_call(
        own_kernel,
        in_specs=[VMEM] * (2 + len(own)),
        out_specs=VMEM,
        out_shape=jax.ShapeDtypeStruct((mix.shape[0], got.shape[1]), F32),
        compiler_params=params(12),
        cost_estimate=FREE,
        name="own_part",
    )(mix, got, *own)


def post_kernel(mix_ref, table_ref, acc_ref, *refs, counts):
    out_hbm, out_ref, sems = refs[-3:]
    step = out_ref.shape[1] // sems.shape[0]
    copies = []
    for i in range(sems.shape[0]):
        values = []
        at = 0
        for count in counts:
            pieces = []
            base = 0
            for ref in refs[at:at + count]:
                low = max(i * step - base, 0)
                high = min((i + 1) * step - base, ref.shape[1])
                if low < high:
                    pieces.append(ref[:, low:high])
                base += ref.shape[1]
            values.append(pieces[0] if len(pieces) == 1 else jnp.concatenate(pieces, axis=1))
            at += count
        values = jnp.concatenate(values * 2, axis=0)
        cut = pl.ds(i * step, step)
        mixed = acc_ref[:, cut] + jnp.dot(mix_ref[...], values, preferred_element_type=F32)
        out_ref[:, cut] = (table_ref[2:3, cut] * mixed).astype(BF16)
        copy = pltpu.make_async_copy(out_ref.at[:, cut], out_hbm.at[:, cut], sems.at[i])
        copy.start()
        copies.append(copy)
    for copy in copies:
        copy.wait()


def post(mix, table, acc, blocks):
    tok_rows, width = acc.shape
    args = [x for block in blocks for x in block]
    return pl.pallas_call(
        functools.partial(post_kernel, counts=[len(block) for block in blocks]),
        in_specs=[VMEM] * (3 + len(args)),
        out_specs=HBM,
        out_shape=jax.ShapeDtypeStruct((tok_rows, width), BF16),
        scratch_shapes=[pltpu.VMEM((tok_rows, width), BF16), pltpu.SemaphoreType.DMA((4,))],
        compiler_params=params(8),
        cost_estimate=FREE,
        name="post",
    )(mix, table, acc, *args)


def shards(tokens, shift, scale, gate, w_up, w_down, pick, count, combine):
    tok_rows, width = tokens.shape
    _, experts, slots = pick.shape
    devices = lax.axis_size("expert")
    place = lax.axis_index("expert")
    group = devices // experts
    requests = shift.shape[0]
    hidden = w_up.shape[0]
    info = jnp.stack([place // (devices // requests), place // group]).astype(jnp.int32)
    pick = pick[0]
    comb = combine[0]

    far = [d * group for d in turns(experts)[1:]]
    near = []
    bit = group // 2
    while bit:
        near.append(bit)
        bit //= 2

    def swap(x, mask):
        return lax.ppermute(x, "expert", [(i, i ^ mask) for i in range(devices)])

    tokens, shift, scale, gate, pick, comb, count = [
        pltpu.with_memory_space_constraint(x, pltpu.HBM)
        for x in (tokens, shift, scale, gate, pick, comb, count)
    ]
    farthest, tok, table, picks, weights = first(info, tokens, pick, shift, scale, gate, comb, count)
    own, *others = rest(tok, table, picks)

    flat = [farthest] + others
    blocks = [own] + [swap(x, mask) for x, mask in zip(flat, far)]
    mixes = mixer(picks, weights, blocks[1], tok_rows)
    blocks[2] = join([blocks[2]], [mixes[0]])
    beside = [swap(block, near[0]) for block in blocks]
    beside[-1] = join([beside[-1]], [])
    early, late = list(range(experts // 2)), list(range(experts // 2, experts))
    parts = []
    segments = {}
    for members in (early, late):
        pieces = [join([x for i in members for x in (blocks[i], beside[i])], [])]
        height = pieces[0].shape[0]
        for mask in near[1:]:
            block = pieces[0] if len(pieces) == 1 else join(pieces, [])
            pieces = [block, swap(block, mask)]
        for at, i in enumerate(members):
            segments[i] = []
            for k, piece in enumerate(pieces):
                for base in range(2 * at * slots, piece.shape[0], height):
                    segments[i].append((len(parts) + k, base, base + 2 * slots))
        parts += pieces
    groups = [[1, 2], list(range(3, experts)) + [0]]
    sources = [
        cut for cuts in zip(*[segments[i] for i in groups[0]]) for cut in cuts
    ]
    for cuts in zip(*[segments[i] for i in groups[1]]):
        sources += [(k, low, low + slots) for k, low, _ in cuts]
        sources += [(k, low + slots, high) for k, low, high in cuts]
    hid = up(parts, sources, w_up, [])

    def gather(keep, send):
        for i, mask in enumerate(reversed(near[1:])):
            if i:
                middle = keep.shape[0] // 2
                keep, send = add(
                    [(keep, got)], [[(0, 0, middle)], [(0, middle, 2 * middle)]], [F32, BF16]
                )
            got = swap(send, mask)
        return keep, got

    half = hid.shape[0] // 2
    step = 5 * width // 8
    keep, send, *others = down(hid, 0, 2, w_down, (0, step, step // 2), [])
    heads = [gather(keep, send), gather(*others)]
    def both(low, height, pieces):
        return [[(piece, at, at + height) for piece in pieces] for at in (low + height, low)]

    def total(send, keep, cuts):
        return add([(keep, swap(send, near[0]))], [[(0, *cut)] for cut in cuts], [BF16] * len(cuts))

    tail = gather(*down(hid, 0, 1, w_down, (step, width, width - step), []))
    outs = both(0, slots, [0, 1]) + both(2 * slots, slots, [0, 1])
    sums = add([heads[0], tail], outs, [BF16, F32] * 2)
    part = (width - step) // 1
    tails = []
    for low in range(step, width, part):
        tails.append(gather(*down(hid, half, 1, w_down, (low, low + part, part), [])))
    height = len(groups[1]) * slots
    every = list(range(1 + 1))
    outs = both(0, height, every[:1]) + both(0, height, every[1:])
    near_sums = add([heads[1]] + tails, outs, [BF16, F32] * 2)

    back = []
    for k in range(2):
        (summed,) = total(*sums[2 * k:2 * k + 2], [(0, slots)])
        back.append([swap(summed, far[k])])
    cuts = [(at, at + slots) for at in range(0, height, slots)]
    columns = [total(*near_sums[2 * k:2 * k + 2], cuts) for k in range(2)]
    for k, mask in enumerate(far[2:]):
        back.append([swap(rows[k], mask) for rows in columns])
    acc = own_part(mixes[0], back[0][0], [rows[-1] for rows in columns])
    return post(mixes[1], table, acc, back[1:])


def solution(mesh):
    return jax.shard_map(
        shards,
        mesh=mesh,
        in_specs=(
            P(("groups", "expert"), None),
            P("groups", None),
            P("groups", None),
            P("groups", None),
            P("expert", None),
            P("expert", None),
            P(("groups", "expert"), None, None),
            P(("groups", "expert"), None),
            P(("groups", "expert"), None, None),
        ),
        out_specs=P(("groups", "expert"), None),
        check_vma=False,
    )
```

```python
import functools

import jax
import jax.numpy as jnp
from jax import lax
from jax.experimental import pallas as pl
from jax.experimental.pallas import tpu as pltpu
from jax.sharding import PartitionSpec as P

MIB = 1024 * 1024
F32 = jnp.float32
BF16 = jnp.bfloat16

SMEM = pl.BlockSpec(memory_space=pltpu.SMEM)
VMEM = pl.BlockSpec(memory_space=pltpu.VMEM)
HBM = pl.BlockSpec(memory_space=pltpu.HBM)
ANY = pl.BlockSpec(memory_space=pl.ANY)


FREE = pl.CostEstimate(flops=1, bytes_accessed=1, transcendentals=0)

BUSY = pl.CostEstimate(flops=4 * 10**10, bytes_accessed=128 * MIB, transcendentals=0)


def params(mib):
    return pltpu.CompilerParams(vmem_limit_bytes=mib * MIB)


def fetch(pairs, sems):
    copies = [pltpu.make_async_copy(src, dst, sems.at[i]) for i, (src, dst) in enumerate(pairs)]
    for copy in copies:
        copy.start()
    for copy in copies:
        copy.wait()


def turns(experts):
    return [0] + list(range(experts - 1, 0, -1))


def hot_rows(picks, tok_rows):
    return lax.broadcasted_iota(jnp.int32, (tok_rows, picks.shape[1]), 0) == picks


def modulate(picks, tok_ref, table_ref):
    hot = hot_rows(picks, tok_ref.shape[0]).astype(F32).astype(BF16)
    values = lax.dot_general(hot, tok_ref[...], (((0,), (0,)), ((), ())), preferred_element_type=F32)
    center = values - jnp.mean(values, axis=1, keepdims=True)
    spread = jnp.mean(center * center, axis=1, keepdims=True)
    normed = center * (1.0 / jnp.sqrt(spread + 1e-06))
    return (normed * table_ref[0:1, :] + table_ref[1:2, :]).astype(BF16)


def first_kernel(info_ref, *refs):
    sources = refs[:7]
    far_ref, tok_ref, table_ref, picks_ref, weights_ref = refs[7:12]
    pick_ref, comb_ref, count_ref, shift_ref, scale_ref, gate_ref, sems = refs[12:]
    fetch(
        list(zip(sources, (tok_ref, pick_ref, shift_ref, scale_ref, gate_ref, comb_ref, count_ref))),
        sems,
    )
    experts, slots = pick_ref.shape
    which = pl.ds(info_ref[0], 1)
    table_ref[0:1, :] = 1.0 + scale_ref[which, :]
    table_ref[1:2, :] = shift_ref[which, :]
    table_ref[2:3, :] = gate_ref[which, :]
    lanes = lax.broadcasted_iota(jnp.int32, (1, slots), 1)
    for i, d in enumerate(turns(experts)):
        e = info_ref[1] ^ d
        picks_ref[i:i + 1, :] = pick_ref[pl.ds(e, 1), :]
        weights_ref[i:i + 1, :] = jnp.where(lanes < count_ref[0, e], comb_ref[pl.ds(e, 1), :], 0.0)
    far_ref[...] = modulate(picks_ref[1:2, :], tok_ref, table_ref)


def first(info, tokens, pick, shift, scale, gate, comb, count):
    experts, slots = pick.shape
    width = tokens.shape[1]
    return pl.pallas_call(
        first_kernel,
        in_specs=[SMEM] + [HBM] * 7,
        out_specs=[VMEM] * 5,
        out_shape=[
            jax.ShapeDtypeStruct((slots, width), BF16),
            jax.ShapeDtypeStruct(tokens.shape, BF16),
            jax.ShapeDtypeStruct((3, width), F32),
            jax.ShapeDtypeStruct(pick.shape, jnp.int32),
            jax.ShapeDtypeStruct(comb.shape, F32),
        ],
        scratch_shapes=[
            pltpu.VMEM(pick.shape, jnp.int32),
            pltpu.VMEM(comb.shape, F32),
            pltpu.SMEM(count.shape, jnp.int32),
            pltpu.VMEM(shift.shape, F32),
            pltpu.VMEM(scale.shape, F32),
            pltpu.VMEM(gate.shape, F32),
            pltpu.SemaphoreType.DMA((7,)),
        ],
        compiler_params=params(8),
        cost_estimate=FREE,
        name="first",
    )(info, tokens, pick, shift, scale, gate, comb, count)


def rest_kernel(tok_ref, table_ref, picks_ref, *outs):
    experts, slots = picks_ref.shape
    order = [0] + list(range(2, experts))
    picks = jnp.concatenate([picks_ref[i:i + 1, :] for i in order], axis=1)
    rows = modulate(picks, tok_ref, table_ref)
    for i, out in enumerate(outs):
        out[...] = rows[i * slots:(i + 1) * slots]


def rest(tok, table, picks):
    experts, slots = picks.shape
    return pl.pallas_call(
        rest_kernel,
        in_specs=[VMEM] * 3,
        out_specs=[VMEM] * (experts - 1),
        out_shape=[jax.ShapeDtypeStruct((slots, tok.shape[1]), BF16)] * (experts - 1),
        compiler_params=params(8),
        cost_estimate=BUSY,
        name="rest",
    )(tok, table, picks)


def mixer_kernel(picks_ref, weights_ref, after_ref, *outs):
    for i, out in enumerate(outs):
        each = picks_ref.shape[0] // len(outs)
        rows = range(i * each, (i + 1) * each)
        picks = jnp.concatenate([picks_ref[r:r + 1, :] for r in rows], axis=1)
        weights = jnp.concatenate([weights_ref[r:r + 1, :] for r in rows], axis=1)
        mix = jnp.where(hot_rows(picks, out.shape[0]), weights, 0.0)
        high = mix.astype(BF16).astype(F32)
        out[...] = jnp.concatenate([high, mix - high], axis=1).astype(BF16)


def mixer(picks, weights, after, tok_rows):
    experts, slots = picks.shape
    return pl.pallas_call(
        mixer_kernel,
        in_specs=[VMEM] * 2 + [ANY],
        out_specs=[VMEM] * 2,
        out_shape=[jax.ShapeDtypeStruct((tok_rows, experts * slots), BF16)] * 2,
        compiler_params=params(4),
        cost_estimate=FREE,
        name="mixer",
    )(picks, weights, after)


def join_kernel(*refs, count):
    out_ref = refs[-1]
    at = 0
    for ref in refs[:count]:
        out_ref[at:at + ref.shape[0], :] = ref[...]
        at += ref.shape[0]


def join(parts, after):
    return pl.pallas_call(
        functools.partial(join_kernel, count=len(parts)),
        in_specs=[VMEM] * len(parts) + [ANY] * len(after),
        out_specs=VMEM,
        out_shape=jax.ShapeDtypeStruct((sum(p.shape[0] for p in parts), parts[0].shape[1]), BF16),
        compiler_params=params(2),
        cost_estimate=FREE,
        name="join",
    )(*parts, *after)


def up_kernel(*refs, sources, count):
    w_ref = refs[count]
    out_ref, rows_ref = refs[-2:]
    to = 0
    for source, low, high in sources:
        rows_ref[to:to + high - low, :] = refs[source][low:high, :]
        to += high - low
    hidden = w_ref.shape[0]
    tile = min(1024, hidden)

    @pl.loop(0, hidden // tile)
    def _(i):
        cut = pl.ds(pl.multiple_of(i * tile, tile), tile)
        lifted = lax.dot_general(
            w_ref[cut, :], rows_ref[...], (((1,), (1,)), ((), ())), preferred_element_type=F32
        )
        out_ref[:, cut] = jax.nn.gelu(lifted, approximate=True).astype(BF16).T


def up(parts, sources, w, after):
    hidden, width = w.shape
    rows = sum(high - low for _, low, high in sources)
    return pl.pallas_call(
        functools.partial(up_kernel, sources=sources, count=len(parts)),
        in_specs=[VMEM] * (len(parts) + 1) + [ANY] * len(after),
        out_specs=VMEM,
        out_shape=jax.ShapeDtypeStruct((rows, hidden), BF16),
        scratch_shapes=[pltpu.VMEM((rows, width), BF16)],
        compiler_params=params(8),
        cost_estimate=FREE,
        name="up",
    )(*parts, w, *after)


def down_kernel(h_ref, w_ref, *outs, columns, low):
    first, last, tile = columns
    groups = len(outs) // 2
    half = outs[0].shape[0]

    @pl.loop(0, (last - first) // tile)
    def _(i):
        to = pl.ds(pl.multiple_of(i * tile, tile), tile)
        cut = pl.ds(pl.multiple_of(first + i * tile, tile), tile)
        rows = slice(low, low + 2 * half * groups)
        out = jnp.dot(h_ref[rows, :], w_ref[:, cut], preferred_element_type=F32)
        for g in range(groups):
            at = 2 * half * g
            outs[2 * g][:, to] = out[at:at + half]
            outs[2 * g + 1][:, to] = out[at + half:at + 2 * half].astype(BF16)


def down(hid, low, groups, w, columns):
    half = hid.shape[0] // 4
    step = columns[1] - columns[0]
    return pl.pallas_call(
        functools.partial(down_kernel, columns=columns, low=low),
        in_specs=[VMEM] * 2,
        out_specs=[VMEM] * (2 * groups),
        out_shape=[
            jax.ShapeDtypeStruct((half, step), F32),
            jax.ShapeDtypeStruct((half, step), BF16),
        ]
        * groups,
        compiler_params=params(8),
        cost_estimate=FREE,
        name="down",
    )(hid, w)


def add_kernel(*refs, count, outs):
    for ref, pieces in zip(refs[2 * count:], outs):
        at = 0
        for i, low, high in pieces:
            keep_ref, got_ref = refs[2 * i:2 * i + 2]
            step = keep_ref.shape[1]
            total = keep_ref[low:high] + got_ref[low:high].astype(F32)
            ref[:, at:at + step] = total.astype(ref.dtype)
            at += step


def add(pairs, outs, kinds):
    args = [x for pair in pairs for x in pair]
    shapes = [
        (pieces[0][2] - pieces[0][1], sum(pairs[i][0].shape[1] for i, _, _ in pieces))
        for pieces in outs
    ]
    return pl.pallas_call(
        functools.partial(add_kernel, count=len(pairs), outs=outs),
        in_specs=[VMEM] * len(args),
        out_specs=[VMEM] * len(outs),
        out_shape=[jax.ShapeDtypeStruct(shape, k) for shape, k in zip(shapes, kinds)],
        compiler_params=params(8),
        cost_estimate=FREE,
        name="add",
    )(*args)


def own_kernel(mix_ref, keep_ref, near_ref, got_ref, acc_ref):
    own = (keep_ref[...] + near_ref[...].astype(F32)).astype(BF16)
    values = jnp.concatenate([own, got_ref[...]] * 2, axis=0)
    acc_ref[...] = jnp.dot(mix_ref[...], values, preferred_element_type=F32)


def own_part(mix, keep, near, got):
    return pl.pallas_call(
        own_kernel,
        in_specs=[VMEM] * 4,
        out_specs=VMEM,
        out_shape=jax.ShapeDtypeStruct((mix.shape[0], keep.shape[1]), F32),
        compiler_params=params(12),
        cost_estimate=FREE,
        name="own_part",
    )(mix, keep, near, got)


def post_kernel(mix_ref, table_ref, acc_ref, *refs):
    blocks = refs[:-3]
    out_hbm, out_ref, sems = refs[-3:]
    step = out_ref.shape[1] // sems.shape[0]
    copies = []
    for i in range(sems.shape[0]):
        cut = pl.ds(i * step, step)
        values = jnp.concatenate([ref[:, cut] for ref in blocks] * 2, axis=0)
        mixed = acc_ref[:, cut] + jnp.dot(mix_ref[...], values, preferred_element_type=F32)
        out_ref[:, cut] = (table_ref[2:3, cut] * mixed).astype(BF16)
        copy = pltpu.make_async_copy(out_ref.at[:, cut], out_hbm.at[:, cut], sems.at[i])
        copy.start()
        copies.append(copy)
    for copy in copies:
        copy.wait()


def post(mix, table, acc, blocks):
    tok_rows, width = acc.shape
    return pl.pallas_call(
        post_kernel,
        in_specs=[VMEM] * (3 + len(blocks)),
        out_specs=HBM,
        out_shape=jax.ShapeDtypeStruct((tok_rows, width), BF16),
        scratch_shapes=[pltpu.VMEM((tok_rows, width), BF16), pltpu.SemaphoreType.DMA((4,))],
        compiler_params=params(8),
        cost_estimate=FREE,
        name="post",
    )(mix, table, acc, *blocks)


def shards(tokens, shift, scale, gate, w_up, w_down, pick, count, combine):
    tok_rows, width = tokens.shape
    _, experts, slots = pick.shape
    devices = lax.axis_size("expert")
    place = lax.axis_index("expert")
    group = devices // experts
    requests = shift.shape[0]
    hidden = w_up.shape[0]
    info = jnp.stack([place // (devices // requests), place // group]).astype(jnp.int32)
    pick = pick[0]
    comb = combine[0]

    far = [d * group for d in turns(experts)[1:]]
    near = []
    bit = group // 2
    while bit:
        near.append(bit)
        bit //= 2

    def swap(x, mask):
        return lax.ppermute(x, "expert", [(i, i ^ mask) for i in range(devices)])

    tokens, shift, scale, gate, pick, comb, count = [
        pltpu.with_memory_space_constraint(x, pltpu.HBM)
        for x in (tokens, shift, scale, gate, pick, comb, count)
    ]
    farthest, tok, table, picks, weights = first(info, tokens, pick, shift, scale, gate, comb, count)
    own, *others = rest(tok, table, picks)

    flat = [farthest] + others
    blocks = [own] + [swap(x, mask) for x, mask in zip(flat, far)]
    mixes = mixer(picks, weights, blocks[1], tok_rows)
    blocks[2] = join([blocks[2]], [mixes[0]])
    beside = [swap(block, near[0]) for block in blocks]
    early, late = list(range(experts // 2)), list(range(experts // 2, experts))
    parts = []
    segments = {}
    for members in [[i] for i in early + late]:
        pieces = [join([x for i in members for x in (blocks[i], beside[i])], [])]
        height = pieces[0].shape[0]
        for mask in near[1:]:
            block = pieces[0] if len(pieces) == 1 else join(pieces, [])
            pieces = [block, swap(block, mask)]
        for at, i in enumerate(members):
            segments[i] = []
            for k, piece in enumerate(pieces):
                for base in range(2 * at * slots, piece.shape[0], height):
                    segments[i].append((len(parts) + k, base, base + 2 * slots))
        parts += pieces
    groups = [[1, 2], list(range(3, experts)) + [0]]
    sources = [
        cut for members in groups for cuts in zip(*[segments[i] for i in members]) for cut in cuts
    ]
    hid = up(parts, sources, w_up, [])

    def gather(keep, send):
        for i, mask in enumerate(reversed(near[1:])):
            if i:
                middle = keep.shape[0] // 2
                keep, send = add(
                    [(keep, got)], [[(0, 0, middle)], [(0, middle, 2 * middle)]], [F32, BF16]
                )
            got = swap(send, mask)
        return keep, got

    half = hid.shape[0] // 2
    step = 5 * width // 8
    keep, send, *others = down(hid, 0, 2, w_down, (0, step, step // 2))
    heads = [gather(keep, send), gather(*others)]
    tails = []
    for g in range(2):
        keep, send = down(hid, g * half, 1, w_down, (step, width, width - step))
        tails.append(gather(keep, send))
    block = {}
    for members, head, tail in zip(groups, heads, tails):
        outs = []
        for at in range(len(members)):
            for side in (1, 0):
                low = (2 * at + side) * slots
                outs.append([(piece, low, low + slots) for piece in range(2)])
        sums = add([head, tail], outs, [BF16, F32] * len(members))
        block.update((i, sums[2 * at:2 * at + 2]) for at, i in enumerate(members))

    def total(send, keep):
        return add([(keep, swap(send, near[0]))], [[(0, 0, slots)]], [BF16])[0]

    sums = [total(*block[i]) for i in range(1, experts)]
    back = [swap(part, mask) for part, mask in zip(sums, far)]
    send, keep = block[0]
    acc = own_part(mixes[0], keep, swap(join([send], [sums[0]]), near[0]), back[0])
    return post(mixes[1], table, acc, back[1:])


def solution(mesh):
    return jax.shard_map(
        shards,
        mesh=mesh,
        in_specs=(
            P(("groups", "expert"), None),
            P("groups", None),
            P("groups", None),
            P("groups", None),
            P("expert", None),
            P("expert", None),
            P(("groups", "expert"), None, None),
            P(("groups", "expert"), None),
            P(("groups", "expert"), None, None),
        ),
        out_specs=P(("groups", "expert"), None),
        check_vma=False,
    )
```

```python
import functools

import jax
import jax.numpy as jnp
from jax import lax
from jax.experimental import pallas as pl
from jax.experimental.pallas import tpu as pltpu
from jax.sharding import PartitionSpec as P

MIB = 1024 * 1024
F32 = jnp.float32
BF16 = jnp.bfloat16

SMEM = pl.BlockSpec(memory_space=pltpu.SMEM)
VMEM = pl.BlockSpec(memory_space=pltpu.VMEM)
HBM = pl.BlockSpec(memory_space=pltpu.HBM)
ANY = pl.BlockSpec(memory_space=pl.ANY)


FREE = pl.CostEstimate(flops=1, bytes_accessed=1, transcendentals=0)

BUSY = pl.CostEstimate(flops=4 * 10**10, bytes_accessed=128 * MIB, transcendentals=0)


def params(mib):
    return pltpu.CompilerParams(vmem_limit_bytes=mib * MIB)


def turns(experts):
    return [0] + list(range(experts - 1, 0, -1))


def hot_rows(picks, tok_rows):
    return lax.broadcasted_iota(jnp.int32, (tok_rows, picks.shape[1]), 0) == picks


def one_hot(picks, tok_rows):
    return hot_rows(picks, tok_rows).astype(F32).astype(BF16)


def modulate(hot, tok_ref, table_ref):
    values = lax.dot_general(hot, tok_ref[...], (((0,), (0,)), ((), ())), preferred_element_type=F32)
    center = values - jnp.mean(values, axis=1, keepdims=True)
    spread = jnp.mean(center * center, axis=1, keepdims=True)
    normed = center * (1.0 / jnp.sqrt(spread + 1e-06))
    return (normed * table_ref[0:1, :] + table_ref[1:2, :]).astype(BF16)


def first_kernel(info_ref, *refs):
    sources = refs[:7]
    far_ref, tok_ref, table_ref, picks_ref, weights_ref = refs[7:12]
    pick_ref, comb_ref, count_ref, shift_ref, scale_ref, gate_ref, sems = refs[12:]
    targets = (tok_ref, pick_ref, shift_ref, scale_ref, gate_ref, comb_ref, count_ref)
    copies = [
        pltpu.make_async_copy(src, dst, sems.at[i])
        for i, (src, dst) in enumerate(zip(sources, targets))
    ]
    for copy in copies:
        copy.start()
    for copy in copies[1:]:
        copy.wait()
    experts, slots = pick_ref.shape
    which = pl.ds(info_ref[0], 1)
    table_ref[0:1, :] = 1.0 + scale_ref[which, :]
    table_ref[1:2, :] = shift_ref[which, :]
    table_ref[2:3, :] = gate_ref[which, :]
    lanes = lax.broadcasted_iota(jnp.int32, (1, slots), 1)
    for i, d in enumerate(turns(experts)):
        e = info_ref[1] ^ d
        picks_ref[i:i + 1, :] = pick_ref[pl.ds(e, 1), :]
        weights_ref[i:i + 1, :] = jnp.where(lanes < count_ref[0, e], comb_ref[pl.ds(e, 1), :], 0.0)
    hot = one_hot(picks_ref[1:2, :], tok_ref.shape[0])
    copies[0].wait()
    far_ref[...] = modulate(hot, tok_ref, table_ref)


def first(info, tokens, pick, shift, scale, gate, comb, count):
    experts, slots = pick.shape
    width = tokens.shape[1]
    return pl.pallas_call(
        first_kernel,
        in_specs=[SMEM] + [HBM] * 7,
        out_specs=[VMEM] * 5,
        out_shape=[
            jax.ShapeDtypeStruct((slots, width), BF16),
            jax.ShapeDtypeStruct(tokens.shape, BF16),
            jax.ShapeDtypeStruct((3, width), F32),
            jax.ShapeDtypeStruct(pick.shape, jnp.int32),
            jax.ShapeDtypeStruct(comb.shape, F32),
        ],
        scratch_shapes=[
            pltpu.VMEM(pick.shape, jnp.int32),
            pltpu.VMEM(comb.shape, F32),
            pltpu.SMEM(count.shape, jnp.int32),
            pltpu.VMEM(shift.shape, F32),
            pltpu.VMEM(scale.shape, F32),
            pltpu.VMEM(gate.shape, F32),
            pltpu.SemaphoreType.DMA((7,)),
        ],
        compiler_params=params(8),
        cost_estimate=FREE,
        name="first",
    )(info, tokens, pick, shift, scale, gate, comb, count)


def rest_kernel(tok_ref, table_ref, picks_ref, *outs):
    experts, slots = picks_ref.shape
    order = [0] + list(range(2, experts))
    picks = jnp.concatenate([picks_ref[i:i + 1, :] for i in order], axis=1)
    rows = modulate(one_hot(picks, tok_ref.shape[0]), tok_ref, table_ref)
    for i, out in enumerate(outs):
        out[...] = rows[i * slots:(i + 1) * slots]


def rest(tok, table, picks):
    experts, slots = picks.shape
    return pl.pallas_call(
        rest_kernel,
        in_specs=[VMEM] * 3,
        out_specs=[VMEM] * (experts - 1),
        out_shape=[jax.ShapeDtypeStruct((slots, tok.shape[1]), BF16)] * (experts - 1),
        compiler_params=params(8),
        cost_estimate=BUSY,
        name="rest",
    )(tok, table, picks)


def mixer_kernel(picks_ref, weights_ref, after_ref, *outs):
    for i, out in enumerate(outs):
        each = picks_ref.shape[0] // len(outs)
        rows = range(i * each, (i + 1) * each)
        picks = jnp.concatenate([picks_ref[r:r + 1, :] for r in rows], axis=1)
        weights = jnp.concatenate([weights_ref[r:r + 1, :] for r in rows], axis=1)
        mix = jnp.where(hot_rows(picks, out.shape[0]), weights, 0.0)
        high = mix.astype(BF16).astype(F32)
        out[...] = jnp.concatenate([high, mix - high], axis=1).astype(BF16)


def mixer(picks, weights, after, tok_rows):
    experts, slots = picks.shape
    return pl.pallas_call(
        mixer_kernel,
        in_specs=[VMEM] * 2 + [ANY],
        out_specs=[VMEM] * 2,
        out_shape=[jax.ShapeDtypeStruct((tok_rows, experts * slots), BF16)] * 2,
        compiler_params=params(4),
        cost_estimate=FREE,
        name="mixer",
    )(picks, weights, after)


def join_kernel(*refs, count):
    out_ref = refs[-1]
    at = 0
    for ref in refs[:count]:
        out_ref[at:at + ref.shape[0], :] = ref[...]
        at += ref.shape[0]


def join(parts, after):
    return pl.pallas_call(
        functools.partial(join_kernel, count=len(parts)),
        in_specs=[VMEM] * len(parts) + [ANY] * len(after),
        out_specs=VMEM,
        out_shape=jax.ShapeDtypeStruct((sum(p.shape[0] for p in parts), parts[0].shape[1]), BF16),
        compiler_params=params(2),
        cost_estimate=FREE,
        name="join",
    )(*parts, *after)


def up_kernel(*refs, sources, count):
    w_ref = refs[count]
    out_ref, rows_ref = refs[-2:]
    to = 0
    for source, low, high in sources:
        rows_ref[to:to + high - low, :] = refs[source][low:high, :]
        to += high - low
    hidden = w_ref.shape[0]
    tile = min(1024, hidden)

    @pl.loop(0, hidden // tile, unroll=True)
    def _(i):
        cut = pl.ds(pl.multiple_of(i * tile, tile), tile)
        lifted = lax.dot_general(
            w_ref[cut, :], rows_ref[...], (((1,), (1,)), ((), ())), preferred_element_type=F32
        )
        out_ref[:, cut] = jax.nn.gelu(lifted, approximate=True).astype(BF16).T


def up(parts, sources, w, after):
    hidden, width = w.shape
    rows = sum(high - low for _, low, high in sources)
    return pl.pallas_call(
        functools.partial(up_kernel, sources=sources, count=len(parts)),
        in_specs=[VMEM] * (len(parts) + 1) + [ANY] * len(after),
        out_specs=VMEM,
        out_shape=jax.ShapeDtypeStruct((rows, hidden), BF16),
        scratch_shapes=[pltpu.VMEM((rows, width), BF16)],
        compiler_params=params(8),
        cost_estimate=FREE,
        name="up",
    )(*parts, w, *after)


def down_kernel(h_ref, w_ref, *outs, columns, low):
    first, last, tile = columns
    groups = len(outs) // 2
    half = outs[0].shape[0]

    @pl.loop(0, (last - first) // tile)
    def _(i):
        to = pl.ds(pl.multiple_of(i * tile, tile), tile)
        cut = pl.ds(pl.multiple_of(first + i * tile, tile), tile)
        rows = slice(low, low + 2 * half * groups)
        out = jnp.dot(h_ref[rows, :], w_ref[:, cut], preferred_element_type=F32)
        for g in range(groups):
            at = 2 * half * g
            outs[2 * g][:, to] = out[at:at + half]
            outs[2 * g + 1][:, to] = out[at + half:at + 2 * half].astype(BF16)


def down(hid, low, groups, w, columns):
    half = hid.shape[0] // 4
    step = columns[1] - columns[0]
    return pl.pallas_call(
        functools.partial(down_kernel, columns=columns, low=low),
        in_specs=[VMEM] * 2,
        out_specs=[VMEM] * (2 * groups),
        out_shape=[
            jax.ShapeDtypeStruct((half, step), F32),
            jax.ShapeDtypeStruct((half, step), BF16),
        ]
        * groups,
        compiler_params=params(8),
        cost_estimate=FREE,
        name="down",
    )(hid, w)


def add_kernel(*refs, count, outs):
    for ref, pieces in zip(refs[2 * count:], outs):
        at = 0
        for i, low, high in pieces:
            keep_ref, got_ref = refs[2 * i:2 * i + 2]
            step = keep_ref.shape[1]
            total = keep_ref[low:high] + got_ref[low:high].astype(F32)
            ref[:, at:at + step] = total.astype(ref.dtype)
            at += step


def add(pairs, outs, kinds):
    args = [x for pair in pairs for x in pair]
    shapes = [
        (pieces[0][2] - pieces[0][1], sum(pairs[i][0].shape[1] for i, _, _ in pieces))
        for pieces in outs
    ]
    return pl.pallas_call(
        functools.partial(add_kernel, count=len(pairs), outs=outs),
        in_specs=[VMEM] * len(args),
        out_specs=[VMEM] * len(outs),
        out_shape=[jax.ShapeDtypeStruct(shape, k) for shape, k in zip(shapes, kinds)],
        compiler_params=params(8),
        cost_estimate=FREE,
        name="add",
    )(*args)


def own_kernel(mix_ref, keep_ref, near_ref, got_ref, acc_ref):
    own = (keep_ref[...] + near_ref[...].astype(F32)).astype(BF16)
    values = jnp.concatenate([own, got_ref[...]] * 2, axis=0)
    acc_ref[...] = jnp.dot(mix_ref[...], values, preferred_element_type=F32)


def own_part(mix, keep, near, got):
    return pl.pallas_call(
        own_kernel,
        in_specs=[VMEM] * 4,
        out_specs=VMEM,
        out_shape=jax.ShapeDtypeStruct((mix.shape[0], keep.shape[1]), F32),
        compiler_params=params(12),
        cost_estimate=FREE,
        name="own_part",
    )(mix, keep, near, got)


def post_kernel(mix_ref, table_ref, acc_ref, *refs):
    blocks = refs[:-3]
    out_hbm, out_ref, sems = refs[-3:]
    step = out_ref.shape[1] // sems.shape[0]
    copies = []
    for i in range(sems.shape[0]):
        cut = pl.ds(i * step, step)
        values = jnp.concatenate([ref[:, cut] for ref in blocks] * 2, axis=0)
        mixed = acc_ref[:, cut] + jnp.dot(mix_ref[...], values, preferred_element_type=F32)
        out_ref[:, cut] = (table_ref[2:3, cut] * mixed).astype(BF16)
        copy = pltpu.make_async_copy(out_ref.at[:, cut], out_hbm.at[:, cut], sems.at[i])
        copy.start()
        copies.append(copy)
    for copy in copies:
        copy.wait()


def post(mix, table, acc, blocks):
    tok_rows, width = acc.shape
    return pl.pallas_call(
        post_kernel,
        in_specs=[VMEM] * (3 + len(blocks)),
        out_specs=HBM,
        out_shape=jax.ShapeDtypeStruct((tok_rows, width), BF16),
        scratch_shapes=[pltpu.VMEM((tok_rows, width), BF16), pltpu.SemaphoreType.DMA((4,))],
        compiler_params=params(8),
        cost_estimate=FREE,
        name="post",
    )(mix, table, acc, *blocks)


def shards(tokens, shift, scale, gate, w_up, w_down, pick, count, combine):
    tok_rows, width = tokens.shape
    _, experts, slots = pick.shape
    devices = lax.axis_size("expert")
    place = lax.axis_index("expert")
    group = devices // experts
    requests = shift.shape[0]
    hidden = w_up.shape[0]
    info = jnp.stack([place // (devices // requests), place // group]).astype(jnp.int32)
    pick = pick[0]
    comb = combine[0]

    far = [d * group for d in turns(experts)[1:]]
    near = []
    bit = group // 2
    while bit:
        near.append(bit)
        bit //= 2

    def swap(x, mask):
        return lax.ppermute(x, "expert", [(i, i ^ mask) for i in range(devices)])

    tokens, shift, scale, gate, pick, comb, count = [
        pltpu.with_memory_space_constraint(x, pltpu.HBM)
        for x in (tokens, shift, scale, gate, pick, comb, count)
    ]
    farthest, tok, table, picks, weights = first(info, tokens, pick, shift, scale, gate, comb, count)
    own, *others = rest(tok, table, picks)

    flat = [farthest] + others
    blocks = [own] + [swap(x, mask) for x, mask in zip(flat, far)]
    mixes = mixer(picks, weights, blocks[1], tok_rows)
    blocks[2] = join([blocks[2]], [mixes[0]])
    beside = [swap(block, near[0]) for block in blocks]
    early, late = list(range(experts // 2)), list(range(experts // 2, experts))
    parts = []
    segments = {}
    for members in [[i] for i in early + late]:
        pieces = [join([x for i in members for x in (blocks[i], beside[i])], [])]
        height = pieces[0].shape[0]
        for mask in near[1:]:
            block = pieces[0] if len(pieces) == 1 else join(pieces, [])
            pieces = [block, swap(block, mask)]
        for at, i in enumerate(members):
            segments[i] = []
            for k, piece in enumerate(pieces):
                for base in range(2 * at * slots, piece.shape[0], height):
                    segments[i].append((len(parts) + k, base, base + 2 * slots))
        parts += pieces
    groups = [[1, 2], list(range(3, experts)) + [0]]
    sources = [
        cut for members in groups for cuts in zip(*[segments[i] for i in members]) for cut in cuts
    ]
    hid = up(parts, sources, w_up, [])

    def gather(keep, send):
        for i, mask in enumerate(reversed(near[1:])):
            if i:
                middle = keep.shape[0] // 2
                keep, send = add(
                    [(keep, got)], [[(0, 0, middle)], [(0, middle, 2 * middle)]], [F32, BF16]
                )
            got = swap(send, mask)
        return keep, got

    half = hid.shape[0] // 2
    step = 5 * width // 8
    keep, send, *others = down(hid, 0, 2, w_down, (0, step, step // 2))
    heads = [gather(keep, send), gather(*others)]
    tails = []
    for g in range(2):
        keep, send = down(hid, g * half, 1, w_down, (step, width, width - step))
        tails.append(gather(keep, send))
    block = {}
    for members, head, tail in zip(groups, heads, tails):
        outs = []
        for at in range(len(members)):
            for side in (1, 0):
                low = (2 * at + side) * slots
                outs.append([(piece, low, low + slots) for piece in range(2)])
        sums = add([head, tail], outs, [BF16, F32] * len(members))
        block.update((i, sums[2 * at:2 * at + 2]) for at, i in enumerate(members))

    def total(send, keep):
        return add([(keep, swap(send, near[0]))], [[(0, 0, slots)]], [BF16])[0]

    sums = [total(*block[i]) for i in range(1, experts)]
    back = [swap(part, mask) for part, mask in zip(sums, far)]
    send, keep = block[0]
    acc = own_part(mixes[0], keep, swap(join([send], [sums[0]]), near[0]), back[0])
    return post(mixes[1], table, acc, back[1:])


def solution(mesh):
    return jax.shard_map(
        shards,
        mesh=mesh,
        in_specs=(
            P(("groups", "expert"), None),
            P("groups", None),
            P("groups", None),
            P("groups", None),
            P("expert", None),
            P("expert", None),
            P(("groups", "expert"), None, None),
            P(("groups", "expert"), None),
            P(("groups", "expert"), None, None),
        ),
        out_specs=P(("groups", "expert"), None),
        check_vma=False,
    )
```

```python
import functools

import jax
import jax.numpy as jnp
from jax import lax
from jax.experimental import pallas as pl
from jax.experimental.pallas import tpu as pltpu
from jax.sharding import PartitionSpec as P

MIB = 1024 * 1024
PIECES = 4
F32 = jnp.float32
BF16 = jnp.bfloat16

SMEM = pl.BlockSpec(memory_space=pltpu.SMEM)
VMEM = pl.BlockSpec(memory_space=pltpu.VMEM)
HBM = pl.BlockSpec(memory_space=pltpu.HBM)
ANY = pl.BlockSpec(memory_space=pl.ANY)


FREE = pl.CostEstimate(flops=1, bytes_accessed=1, transcendentals=0)

BUSY = pl.CostEstimate(flops=4 * 10**10, bytes_accessed=128 * MIB, transcendentals=0)


def params(mib):
    return pltpu.CompilerParams(vmem_limit_bytes=mib * MIB)


def turns(experts):
    return [0] + list(range(experts - 1, 0, -1))


def hot_rows(picks, tok_rows):
    return lax.broadcasted_iota(jnp.int32, (tok_rows, picks.shape[1]), 0) == picks


def one_hot(picks, tok_rows):
    return hot_rows(picks, tok_rows).astype(F32).astype(BF16)


def modulate(hot, tok_ref, table_ref):
    values = lax.dot_general(hot, tok_ref[...], (((0,), (0,)), ((), ())), preferred_element_type=F32)
    center = values - jnp.mean(values, axis=1, keepdims=True)
    spread = jnp.mean(center * center, axis=1, keepdims=True)
    normed = center * (1.0 / jnp.sqrt(spread + 1e-06))
    return (normed * table_ref[0:1, :] + table_ref[1:2, :]).astype(BF16)


def first_kernel(info_ref, *refs):
    sources = refs[:7]
    far_ref, tok_ref, table_ref, picks_ref, weights_ref = refs[7:12]
    pick_ref, comb_ref, count_ref, shift_ref, scale_ref, gate_ref, sems = refs[12:]
    targets = (tok_ref, pick_ref, shift_ref, scale_ref, gate_ref, comb_ref, count_ref)
    part = tok_ref.shape[0] // PIECES
    tokens = [
        pltpu.make_async_copy(
            sources[0].at[pl.ds(p * part, part), :],
            tok_ref.at[pl.ds(p * part, part), :],
            sems.at[len(sources) + p],
        )
        for p in range(PIECES)
    ]
    copies = [
        pltpu.make_async_copy(src, dst, sems.at[i])
        for i, (src, dst) in enumerate(zip(sources, targets))
    ][1:]
    for copy in tokens + copies:
        copy.start()
    for copy in copies:
        copy.wait()
    experts, slots = pick_ref.shape
    which = pl.ds(info_ref[0], 1)
    table_ref[0:1, :] = 1.0 + scale_ref[which, :]
    table_ref[1:2, :] = shift_ref[which, :]
    table_ref[2:3, :] = gate_ref[which, :]
    lanes = lax.broadcasted_iota(jnp.int32, (1, slots), 1)
    for i, d in enumerate(turns(experts)):
        e = info_ref[1] ^ d
        picks_ref[i:i + 1, :] = pick_ref[pl.ds(e, 1), :]
        weights_ref[i:i + 1, :] = jnp.where(lanes < count_ref[0, e], comb_ref[pl.ds(e, 1), :], 0.0)
    hot = one_hot(picks_ref[1:2, :], tok_ref.shape[0])
    for copy in tokens:
        copy.wait()
    far_ref[...] = modulate(hot, tok_ref, table_ref)


def first(info, tokens, pick, shift, scale, gate, comb, count):
    experts, slots = pick.shape
    width = tokens.shape[1]
    return pl.pallas_call(
        first_kernel,
        in_specs=[SMEM] + [HBM] * 7,
        out_specs=[VMEM] * 5,
        out_shape=[
            jax.ShapeDtypeStruct((slots, width), BF16),
            jax.ShapeDtypeStruct(tokens.shape, BF16),
            jax.ShapeDtypeStruct((3, width), F32),
            jax.ShapeDtypeStruct(pick.shape, jnp.int32),
            jax.ShapeDtypeStruct(comb.shape, F32),
        ],
        scratch_shapes=[
            pltpu.VMEM(pick.shape, jnp.int32),
            pltpu.VMEM(comb.shape, F32),
            pltpu.SMEM(count.shape, jnp.int32),
            pltpu.VMEM(shift.shape, F32),
            pltpu.VMEM(scale.shape, F32),
            pltpu.VMEM(gate.shape, F32),
            pltpu.SemaphoreType.DMA((7 + PIECES,)),
        ],
        compiler_params=params(8),
        cost_estimate=FREE,
        name="first",
    )(info, tokens, pick, shift, scale, gate, comb, count)


def rest_kernel(tok_ref, table_ref, picks_ref, *outs):
    experts, slots = picks_ref.shape
    order = [0] + list(range(2, experts))
    picks = jnp.concatenate([picks_ref[i:i + 1, :] for i in order], axis=1)
    rows = modulate(one_hot(picks, tok_ref.shape[0]), tok_ref, table_ref)
    for i, out in enumerate(outs):
        out[...] = rows[i * slots:(i + 1) * slots]


def rest(tok, table, picks):
    experts, slots = picks.shape
    return pl.pallas_call(
        rest_kernel,
        in_specs=[VMEM] * 3,
        out_specs=[VMEM] * (experts - 1),
        out_shape=[jax.ShapeDtypeStruct((slots, tok.shape[1]), BF16)] * (experts - 1),
        compiler_params=params(8),
        cost_estimate=BUSY,
        name="rest",
    )(tok, table, picks)


def mixer_kernel(picks_ref, weights_ref, after_ref, *outs):
    for i, out in enumerate(outs):
        each = picks_ref.shape[0] // len(outs)
        rows = range(i * each, (i + 1) * each)
        picks = jnp.concatenate([picks_ref[r:r + 1, :] for r in rows], axis=1)
        weights = jnp.concatenate([weights_ref[r:r + 1, :] for r in rows], axis=1)
        mix = jnp.where(hot_rows(picks, out.shape[0]), weights, 0.0)
        high = mix.astype(BF16).astype(F32)
        out[...] = jnp.concatenate([high, mix - high], axis=1).astype(BF16)


def mixer(picks, weights, after, tok_rows):
    experts, slots = picks.shape
    return pl.pallas_call(
        mixer_kernel,
        in_specs=[VMEM] * 2 + [ANY],
        out_specs=[VMEM] * 2,
        out_shape=[jax.ShapeDtypeStruct((tok_rows, experts * slots), BF16)] * 2,
        compiler_params=params(4),
        cost_estimate=FREE,
        name="mixer",
    )(picks, weights, after)


def join_kernel(*refs, count):
    out_ref = refs[-1]
    at = 0
    for ref in refs[:count]:
        out_ref[at:at + ref.shape[0], :] = ref[...]
        at += ref.shape[0]


def join(parts, after):
    return pl.pallas_call(
        functools.partial(join_kernel, count=len(parts)),
        in_specs=[VMEM] * len(parts) + [ANY] * len(after),
        out_specs=VMEM,
        out_shape=jax.ShapeDtypeStruct((sum(p.shape[0] for p in parts), parts[0].shape[1]), BF16),
        compiler_params=params(2),
        cost_estimate=FREE,
        name="join",
    )(*parts, *after)


def up_kernel(*refs, sources, count):
    w_ref = refs[count]
    out_ref, rows_ref = refs[-2:]
    to = 0
    for source, low, high in sources:
        rows_ref[to:to + high - low, :] = refs[source][low:high, :]
        to += high - low
    hidden = w_ref.shape[0]
    tile = min(1024, hidden)

    @pl.loop(0, hidden // tile, unroll=True)
    def _(i):
        cut = pl.ds(pl.multiple_of(i * tile, tile), tile)
        lifted = lax.dot_general(
            w_ref[cut, :], rows_ref[...], (((1,), (1,)), ((), ())), preferred_element_type=F32
        )
        out_ref[:, cut] = jax.nn.gelu(lifted, approximate=True).astype(BF16).T


def up(parts, sources, w, after):
    hidden, width = w.shape
    rows = sum(high - low for _, low, high in sources)
    return pl.pallas_call(
        functools.partial(up_kernel, sources=sources, count=len(parts)),
        in_specs=[VMEM] * (len(parts) + 1) + [ANY] * len(after),
        out_specs=VMEM,
        out_shape=jax.ShapeDtypeStruct((rows, hidden), BF16),
        scratch_shapes=[pltpu.VMEM((rows, width), BF16)],
        compiler_params=params(8),
        cost_estimate=FREE,
        name="up",
    )(*parts, w, *after)


def down_kernel(h_ref, w_ref, *outs, columns, low):
    first, last, tile = columns
    groups = len(outs) // 2
    half = outs[0].shape[0]

    @pl.loop(0, (last - first) // tile)
    def _(i):
        to = pl.ds(pl.multiple_of(i * tile, tile), tile)
        cut = pl.ds(pl.multiple_of(first + i * tile, tile), tile)
        rows = slice(low, low + 2 * half * groups)
        out = jnp.dot(h_ref[rows, :], w_ref[:, cut], preferred_element_type=F32)
        for g in range(groups):
            at = 2 * half * g
            outs[2 * g][:, to] = out[at:at + half]
            outs[2 * g + 1][:, to] = out[at + half:at + 2 * half].astype(BF16)


def down(hid, low, groups, w, columns):
    half = hid.shape[0] // 4
    step = columns[1] - columns[0]
    return pl.pallas_call(
        functools.partial(down_kernel, columns=columns, low=low),
        in_specs=[VMEM] * 2,
        out_specs=[VMEM] * (2 * groups),
        out_shape=[
            jax.ShapeDtypeStruct((half, step), F32),
            jax.ShapeDtypeStruct((half, step), BF16),
        ]
        * groups,
        compiler_params=params(8),
        cost_estimate=FREE,
        name="down",
    )(hid, w)


def add_kernel(*refs, count, outs):
    for ref, pieces in zip(refs[2 * count:], outs):
        at = 0
        for i, low, high in pieces:
            keep_ref, got_ref = refs[2 * i:2 * i + 2]
            step = keep_ref.shape[1]
            total = keep_ref[low:high] + got_ref[low:high].astype(F32)
            ref[:, at:at + step] = total.astype(ref.dtype)
            at += step


def add(pairs, outs, kinds):
    args = [x for pair in pairs for x in pair]
    shapes = [
        (pieces[0][2] - pieces[0][1], sum(pairs[i][0].shape[1] for i, _, _ in pieces))
        for pieces in outs
    ]
    return pl.pallas_call(
        functools.partial(add_kernel, count=len(pairs), outs=outs),
        in_specs=[VMEM] * len(args),
        out_specs=[VMEM] * len(outs),
        out_shape=[jax.ShapeDtypeStruct(shape, k) for shape, k in zip(shapes, kinds)],
        compiler_params=params(8),
        cost_estimate=FREE,
        name="add",
    )(*args)


def own_kernel(mix_ref, keep_ref, near_ref, got_ref, acc_ref):
    own = (keep_ref[...] + near_ref[...].astype(F32)).astype(BF16)
    values = jnp.concatenate([own, got_ref[...]] * 2, axis=0)
    acc_ref[...] = jnp.dot(mix_ref[...], values, preferred_element_type=F32)


def own_part(mix, keep, near, got):
    return pl.pallas_call(
        own_kernel,
        in_specs=[VMEM] * 4,
        out_specs=VMEM,
        out_shape=jax.ShapeDtypeStruct((mix.shape[0], keep.shape[1]), F32),
        compiler_params=params(12),
        cost_estimate=FREE,
        name="own_part",
    )(mix, keep, near, got)


def post_kernel(mix_ref, table_ref, acc_ref, *refs):
    blocks = refs[:-3]
    out_hbm, out_ref, sems = refs[-3:]
    step = out_ref.shape[1] // sems.shape[0]
    copies = []
    for i in range(sems.shape[0]):
        cut = pl.ds(i * step, step)
        values = jnp.concatenate([ref[:, cut] for ref in blocks] * 2, axis=0)
        mixed = acc_ref[:, cut] + jnp.dot(mix_ref[...], values, preferred_element_type=F32)
        out_ref[:, cut] = (table_ref[2:3, cut] * mixed).astype(BF16)
        copy = pltpu.make_async_copy(out_ref.at[:, cut], out_hbm.at[:, cut], sems.at[i])
        copy.start()
        copies.append(copy)
    for copy in copies:
        copy.wait()


def post(mix, table, acc, blocks):
    tok_rows, width = acc.shape
    return pl.pallas_call(
        post_kernel,
        in_specs=[VMEM] * (3 + len(blocks)),
        out_specs=HBM,
        out_shape=jax.ShapeDtypeStruct((tok_rows, width), BF16),
        scratch_shapes=[pltpu.VMEM((tok_rows, width), BF16), pltpu.SemaphoreType.DMA((4,))],
        compiler_params=params(8),
        cost_estimate=FREE,
        name="post",
    )(mix, table, acc, *blocks)


def shards(tokens, shift, scale, gate, w_up, w_down, pick, count, combine):
    tok_rows, width = tokens.shape
    _, experts, slots = pick.shape
    devices = lax.axis_size("expert")
    place = lax.axis_index("expert")
    group = devices // experts
    requests = shift.shape[0]
    hidden = w_up.shape[0]
    info = jnp.stack([place // (devices // requests), place // group]).astype(jnp.int32)
    pick = pick[0]
    comb = combine[0]

    far = [d * group for d in turns(experts)[1:]]
    near = []
    bit = group // 2
    while bit:
        near.append(bit)
        bit //= 2

    def swap(x, mask):
        return lax.ppermute(x, "expert", [(i, i ^ mask) for i in range(devices)])

    tokens, shift, scale, gate, pick, comb, count = [
        pltpu.with_memory_space_constraint(x, pltpu.HBM)
        for x in (tokens, shift, scale, gate, pick, comb, count)
    ]
    farthest, tok, table, picks, weights = first(info, tokens, pick, shift, scale, gate, comb, count)
    own, *others = rest(tok, table, picks)

    flat = [farthest] + others
    blocks = [own] + [swap(x, mask) for x, mask in zip(flat, far)]
    mixes = mixer(picks, weights, blocks[1], tok_rows)
    blocks[2] = join([blocks[2]], [mixes[0]])
    beside = [swap(block, near[0]) for block in blocks]
    early, late = list(range(experts // 2)), list(range(experts // 2, experts))
    parts = []
    segments = {}
    for members in [[i] for i in early + late]:
        pieces = [join([x for i in members for x in (blocks[i], beside[i])], [])]
        height = pieces[0].shape[0]
        for mask in near[1:]:
            block = pieces[0] if len(pieces) == 1 else join(pieces, [])
            pieces = [block, swap(block, mask)]
        for at, i in enumerate(members):
            segments[i] = []
            for k, piece in enumerate(pieces):
                for base in range(2 * at * slots, piece.shape[0], height):
                    segments[i].append((len(parts) + k, base, base + 2 * slots))
        parts += pieces
    groups = [[1, 2], list(range(3, experts)) + [0]]
    sources = [
        cut for members in groups for cuts in zip(*[segments[i] for i in members]) for cut in cuts
    ]
    hid = up(parts, sources, w_up, [])

    def gather(keep, send):
        for i, mask in enumerate(reversed(near[1:])):
            if i:
                middle = keep.shape[0] // 2
                keep, send = add(
                    [(keep, got)], [[(0, 0, middle)], [(0, middle, 2 * middle)]], [F32, BF16]
                )
            got = swap(send, mask)
        return keep, got

    half = hid.shape[0] // 2
    step = 5 * width // 8
    keep, send, *others = down(hid, 0, 2, w_down, (0, step, step // 2))
    heads = [gather(keep, send), gather(*others)]
    tails = []
    for g in range(2):
        keep, send = down(hid, g * half, 1, w_down, (step, width, width - step))
        tails.append(gather(keep, send))
    block = {}
    for members, head, tail in zip(groups, heads, tails):
        outs = []
        for at in range(len(members)):
            for side in (1, 0):
                low = (2 * at + side) * slots
                outs.append([(piece, low, low + slots) for piece in range(2)])
        sums = add([head, tail], outs, [BF16, F32] * len(members))
        block.update((i, sums[2 * at:2 * at + 2]) for at, i in enumerate(members))

    def total(send, keep):
        return add([(keep, swap(send, near[0]))], [[(0, 0, slots)]], [BF16])[0]

    sums = [total(*block[i]) for i in range(1, experts)]
    back = [swap(part, mask) for part, mask in zip(sums, far)]
    send, keep = block[0]
    acc = own_part(mixes[0], keep, swap(join([send], [sums[0]]), near[0]), back[0])
    return post(mixes[1], table, acc, back[1:])


def solution(mesh):
    return jax.shard_map(
        shards,
        mesh=mesh,
        in_specs=(
            P(("groups", "expert"), None),
            P("groups", None),
            P("groups", None),
            P("groups", None),
            P("expert", None),
            P("expert", None),
            P(("groups", "expert"), None, None),
            P(("groups", "expert"), None),
            P(("groups", "expert"), None, None),
        ),
        out_specs=P(("groups", "expert"), None),
        check_vma=False,
    )
```

```python
import functools

import jax
import jax.numpy as jnp
from jax import lax
from jax.experimental import pallas as pl
from jax.experimental.pallas import tpu as pltpu
from jax.sharding import PartitionSpec as P

MIB = 1024 * 1024
PIECES = 4
F32 = jnp.float32
BF16 = jnp.bfloat16

SMEM = pl.BlockSpec(memory_space=pltpu.SMEM)
VMEM = pl.BlockSpec(memory_space=pltpu.VMEM)
HBM = pl.BlockSpec(memory_space=pltpu.HBM)
ANY = pl.BlockSpec(memory_space=pl.ANY)


FREE = pl.CostEstimate(flops=1, bytes_accessed=1, transcendentals=0)

BUSY = pl.CostEstimate(flops=4 * 10**10, bytes_accessed=128 * MIB, transcendentals=0)


def params(mib):
    return pltpu.CompilerParams(vmem_limit_bytes=mib * MIB)


def turns(experts):
    return [0] + list(range(experts - 1, 0, -1))


def hot_rows(picks, tok_rows):
    return lax.broadcasted_iota(jnp.int32, (tok_rows, picks.shape[1]), 0) == picks


def one_hot(picks, tok_rows):
    return hot_rows(picks, tok_rows).astype(F32).astype(BF16)


def modulate(hot, tok_ref, table_ref):
    values = lax.dot_general(hot, tok_ref[...], (((0,), (0,)), ((), ())), preferred_element_type=F32)
    center = values - jnp.mean(values, axis=1, keepdims=True)
    spread = jnp.mean(center * center, axis=1, keepdims=True)
    normed = center * (1.0 / jnp.sqrt(spread + 1e-06))
    return (normed * table_ref[0:1, :] + table_ref[1:2, :]).astype(BF16)


def first_kernel(info_ref, *refs):
    sources = refs[:7]
    far_ref, tok_ref, table_ref, picks_ref, weights_ref = refs[7:12]
    pick_ref, comb_ref, count_ref, shift_ref, scale_ref, gate_ref, sems = refs[12:]
    targets = (tok_ref, pick_ref, shift_ref, scale_ref, gate_ref, comb_ref, count_ref)
    part = tok_ref.shape[0] // PIECES
    tokens = [
        pltpu.make_async_copy(
            sources[0].at[pl.ds(p * part, part), :],
            tok_ref.at[pl.ds(p * part, part), :],
            sems.at[len(sources) + p],
        )
        for p in range(PIECES)
    ]
    copies = [
        pltpu.make_async_copy(src, dst, sems.at[i])
        for i, (src, dst) in enumerate(zip(sources, targets))
    ][1:]
    for copy in tokens + copies:
        copy.start()
    for copy in copies:
        copy.wait()
    experts, slots = pick_ref.shape
    which = pl.ds(info_ref[0], 1)
    table_ref[0:1, :] = 1.0 + scale_ref[which, :]
    table_ref[1:2, :] = shift_ref[which, :]
    table_ref[2:3, :] = gate_ref[which, :]
    lanes = lax.broadcasted_iota(jnp.int32, (1, slots), 1)
    for i, d in enumerate(turns(experts)):
        e = info_ref[1] ^ d
        picks_ref[i:i + 1, :] = pick_ref[pl.ds(e, 1), :]
        weights_ref[i:i + 1, :] = jnp.where(lanes < count_ref[0, e], comb_ref[pl.ds(e, 1), :], 0.0)
    hot = one_hot(picks_ref[1:2, :], tok_ref.shape[0])
    for copy in tokens:
        copy.wait()
    far_ref[...] = modulate(hot, tok_ref, table_ref)


def first(info, tokens, pick, shift, scale, gate, comb, count):
    experts, slots = pick.shape
    width = tokens.shape[1]
    return pl.pallas_call(
        first_kernel,
        in_specs=[SMEM] + [HBM] * 7,
        out_specs=[VMEM] * 5,
        out_shape=[
            jax.ShapeDtypeStruct((slots, width), BF16),
            jax.ShapeDtypeStruct(tokens.shape, BF16),
            jax.ShapeDtypeStruct((3, width), F32),
            jax.ShapeDtypeStruct(pick.shape, jnp.int32),
            jax.ShapeDtypeStruct(comb.shape, F32),
        ],
        scratch_shapes=[
            pltpu.VMEM(pick.shape, jnp.int32),
            pltpu.VMEM(comb.shape, F32),
            pltpu.SMEM(count.shape, jnp.int32),
            pltpu.VMEM(shift.shape, F32),
            pltpu.VMEM(scale.shape, F32),
            pltpu.VMEM(gate.shape, F32),
            pltpu.SemaphoreType.DMA((7 + PIECES,)),
        ],
        compiler_params=params(8),
        cost_estimate=FREE,
        name="first",
    )(info, tokens, pick, shift, scale, gate, comb, count)


def rest_kernel(tok_ref, table_ref, picks_ref, *outs):
    experts, slots = picks_ref.shape
    order = [0] + list(range(2, experts))
    picks = jnp.concatenate([picks_ref[i:i + 1, :] for i in order], axis=1)
    rows = modulate(one_hot(picks, tok_ref.shape[0]), tok_ref, table_ref)
    for i, out in enumerate(outs):
        out[...] = rows[i * slots:(i + 1) * slots]


def rest(tok, table, picks):
    experts, slots = picks.shape
    return pl.pallas_call(
        rest_kernel,
        in_specs=[VMEM] * 3,
        out_specs=[VMEM] * (experts - 1),
        out_shape=[jax.ShapeDtypeStruct((slots, tok.shape[1]), BF16)] * (experts - 1),
        compiler_params=params(8),
        cost_estimate=BUSY,
        name="rest",
    )(tok, table, picks)


def mixer_kernel(picks_ref, weights_ref, after_ref, *outs):
    for i, out in enumerate(outs):
        each = picks_ref.shape[0] // len(outs)
        rows = range(i * each, (i + 1) * each)
        picks = jnp.concatenate([picks_ref[r:r + 1, :] for r in rows], axis=1)
        weights = jnp.concatenate([weights_ref[r:r + 1, :] for r in rows], axis=1)
        mix = jnp.where(hot_rows(picks, out.shape[0]), weights, 0.0)
        high = mix.astype(BF16).astype(F32)
        out[...] = jnp.concatenate([high, mix - high], axis=1).astype(BF16)


def mixer(picks, weights, after, tok_rows):
    experts, slots = picks.shape
    return pl.pallas_call(
        mixer_kernel,
        in_specs=[VMEM] * 2 + [ANY],
        out_specs=[VMEM] * 2,
        out_shape=[jax.ShapeDtypeStruct((tok_rows, experts * slots), BF16)] * 2,
        compiler_params=params(4),
        cost_estimate=FREE,
        name="mixer",
    )(picks, weights, after)


def join_kernel(*refs, count):
    out_ref = refs[-1]
    at = 0
    for ref in refs[:count]:
        out_ref[at:at + ref.shape[0], :] = ref[...]
        at += ref.shape[0]


def join(parts, after):
    return pl.pallas_call(
        functools.partial(join_kernel, count=len(parts)),
        in_specs=[VMEM] * len(parts) + [ANY] * len(after),
        out_specs=VMEM,
        out_shape=jax.ShapeDtypeStruct((sum(p.shape[0] for p in parts), parts[0].shape[1]), BF16),
        compiler_params=params(2),
        cost_estimate=FREE,
        name="join",
    )(*parts, *after)


def up_kernel(*refs, sources, count):
    w_ref = refs[count]
    out_ref, rows_ref = refs[-2:]
    to = 0
    for source, low, high in sources:
        rows_ref[to:to + high - low, :] = refs[source][low:high, :]
        to += high - low
    hidden = w_ref.shape[0]
    tile = min(1024, hidden)

    @pl.loop(0, hidden // tile, unroll=True)
    def _(i):
        cut = pl.ds(pl.multiple_of(i * tile, tile), tile)
        lifted = lax.dot_general(
            w_ref[cut, :], rows_ref[...], (((1,), (1,)), ((), ())), preferred_element_type=F32
        )
        out_ref[:, cut] = jax.nn.gelu(lifted, approximate=True).astype(BF16).T


def up(parts, sources, w, after):
    hidden, width = w.shape
    rows = sum(high - low for _, low, high in sources)
    return pl.pallas_call(
        functools.partial(up_kernel, sources=sources, count=len(parts)),
        in_specs=[VMEM] * (len(parts) + 1) + [ANY] * len(after),
        out_specs=VMEM,
        out_shape=jax.ShapeDtypeStruct((rows, hidden), BF16),
        scratch_shapes=[pltpu.VMEM((rows, width), BF16)],
        compiler_params=params(8),
        cost_estimate=FREE,
        name="up",
    )(*parts, w, *after)


def down_kernel(h_ref, w_ref, *outs, columns, low, groups):
    first, last, tile = columns
    pairs = len(outs) // 2
    half = outs[0].shape[0] * pairs // groups

    @pl.loop(0, (last - first) // tile)
    def _(i):
        to = pl.ds(pl.multiple_of(i * tile, tile), tile)
        cut = pl.ds(pl.multiple_of(first + i * tile, tile), tile)
        rows = slice(low, low + 2 * half * groups)
        out = jnp.dot(h_ref[rows, :], w_ref[:, cut], preferred_element_type=F32)
        for g in range(groups):
            at = 2 * half * g
            keep_ref, send_ref = outs[2 * (g % pairs):2 * (g % pairs) + 2]
            into = slice(g // pairs * half, (g // pairs + 1) * half)
            keep_ref[into, to] = out[at:at + half]
            send_ref[into, to] = out[at + half:at + 2 * half].astype(BF16)


def down(hid, low, groups, w, columns, joint=False):
    half = hid.shape[0] // 4 * (groups if joint else 1)
    pairs = 1 if joint else groups
    step = columns[1] - columns[0]
    return pl.pallas_call(
        functools.partial(down_kernel, columns=columns, low=low, groups=groups),
        in_specs=[VMEM] * 2,
        out_specs=[VMEM] * (2 * pairs),
        out_shape=[
            jax.ShapeDtypeStruct((half, step), F32),
            jax.ShapeDtypeStruct((half, step), BF16),
        ]
        * pairs,
        compiler_params=params(8),
        cost_estimate=FREE,
        name="down",
    )(hid, w)


def add_kernel(*refs, count, outs):
    for ref, pieces in zip(refs[2 * count:], outs):
        at = 0
        for i, low, high in pieces:
            keep_ref, got_ref = refs[2 * i:2 * i + 2]
            step = keep_ref.shape[1]
            total = keep_ref[low:high] + got_ref[low:high].astype(F32)
            ref[:, at:at + step] = total.astype(ref.dtype)
            at += step


def add(pairs, outs, kinds):
    args = [x for pair in pairs for x in pair]
    shapes = [
        (pieces[0][2] - pieces[0][1], sum(pairs[i][0].shape[1] for i, _, _ in pieces))
        for pieces in outs
    ]
    return pl.pallas_call(
        functools.partial(add_kernel, count=len(pairs), outs=outs),
        in_specs=[VMEM] * len(args),
        out_specs=[VMEM] * len(outs),
        out_shape=[jax.ShapeDtypeStruct(shape, k) for shape, k in zip(shapes, kinds)],
        compiler_params=params(8),
        cost_estimate=FREE,
        name="add",
    )(*args)


def own_kernel(mix_ref, keep_ref, near_ref, got_ref, acc_ref):
    own = (keep_ref[...] + near_ref[...].astype(F32)).astype(BF16)
    values = jnp.concatenate([own, got_ref[...]] * 2, axis=0)
    acc_ref[...] = jnp.dot(mix_ref[...], values, preferred_element_type=F32)


def own_part(mix, keep, near, got):
    return pl.pallas_call(
        own_kernel,
        in_specs=[VMEM] * 4,
        out_specs=VMEM,
        out_shape=jax.ShapeDtypeStruct((mix.shape[0], keep.shape[1]), F32),
        compiler_params=params(12),
        cost_estimate=FREE,
        name="own_part",
    )(mix, keep, near, got)


def post_kernel(mix_ref, table_ref, acc_ref, *refs):
    blocks = refs[:-3]
    out_hbm, out_ref, sems = refs[-3:]
    step = out_ref.shape[1] // sems.shape[0]
    copies = []
    for i in range(sems.shape[0]):
        cut = pl.ds(i * step, step)
        values = jnp.concatenate([ref[:, cut] for ref in blocks] * 2, axis=0)
        mixed = acc_ref[:, cut] + jnp.dot(mix_ref[...], values, preferred_element_type=F32)
        out_ref[:, cut] = (table_ref[2:3, cut] * mixed).astype(BF16)
        copy = pltpu.make_async_copy(out_ref.at[:, cut], out_hbm.at[:, cut], sems.at[i])
        copy.start()
        copies.append(copy)
    for copy in copies:
        copy.wait()


def post(mix, table, acc, blocks):
    tok_rows, width = acc.shape
    return pl.pallas_call(
        post_kernel,
        in_specs=[VMEM] * (3 + len(blocks)),
        out_specs=HBM,
        out_shape=jax.ShapeDtypeStruct((tok_rows, width), BF16),
        scratch_shapes=[pltpu.VMEM((tok_rows, width), BF16), pltpu.SemaphoreType.DMA((4,))],
        compiler_params=params(8),
        cost_estimate=FREE,
        name="post",
    )(mix, table, acc, *blocks)


def shards(tokens, shift, scale, gate, w_up, w_down, pick, count, combine):
    tok_rows, width = tokens.shape
    _, experts, slots = pick.shape
    devices = lax.axis_size("expert")
    place = lax.axis_index("expert")
    group = devices // experts
    requests = shift.shape[0]
    hidden = w_up.shape[0]
    info = jnp.stack([place // (devices // requests), place // group]).astype(jnp.int32)
    pick = pick[0]
    comb = combine[0]

    far = [d * group for d in turns(experts)[1:]]
    near = []
    bit = group // 2
    while bit:
        near.append(bit)
        bit //= 2

    def swap(x, mask):
        return lax.ppermute(x, "expert", [(i, i ^ mask) for i in range(devices)])

    tokens, shift, scale, gate, pick, comb, count = [
        pltpu.with_memory_space_constraint(x, pltpu.HBM)
        for x in (tokens, shift, scale, gate, pick, comb, count)
    ]
    farthest, tok, table, picks, weights = first(info, tokens, pick, shift, scale, gate, comb, count)
    own, *others = rest(tok, table, picks)

    flat = [farthest] + others
    blocks = [own] + [swap(x, mask) for x, mask in zip(flat, far)]
    mixes = mixer(picks, weights, blocks[1], tok_rows)
    blocks[2] = join([blocks[2]], [mixes[0]])
    beside = [swap(block, near[0]) for block in blocks]
    early, late = list(range(experts // 2)), list(range(experts // 2, experts))
    parts = []
    segments = {}
    for members in [[i] for i in early + late]:
        pieces = [join([x for i in members for x in (blocks[i], beside[i])], [])]
        height = pieces[0].shape[0]
        for mask in near[1:]:
            block = pieces[0] if len(pieces) == 1 else join(pieces, [])
            pieces = [block, swap(block, mask)]
        for at, i in enumerate(members):
            segments[i] = []
            for k, piece in enumerate(pieces):
                for base in range(2 * at * slots, piece.shape[0], height):
                    segments[i].append((len(parts) + k, base, base + 2 * slots))
        parts += pieces
    groups = [[1, 2], list(range(3, experts)) + [0]]
    sources = [
        cut for members in groups for cuts in zip(*[segments[i] for i in members]) for cut in cuts
    ]
    hid = up(parts, sources, w_up, [])

    def gather(keep, send):
        for i, mask in enumerate(reversed(near[1:])):
            if i:
                middle = keep.shape[0] // 2
                keep, send = add(
                    [(keep, got)], [[(0, 0, middle)], [(0, middle, 2 * middle)]], [F32, BF16]
                )
            got = swap(send, mask)
        return keep, got

    half = hid.shape[0] // 2
    step = 5 * width // 8
    joint = len(near) == 2
    made = down(hid, 0, 2, w_down, (0, step, step // 2), joint)
    heads = [gather(*made)] * 2 if joint else [gather(*made[:2]), gather(*made[2:])]
    tails = []
    for g in range(2):
        keep, send = down(hid, g * half, 1, w_down, (step, width, width - step))
        tails.append(gather(keep, send))
    block = {}
    for g, members, head, tail in zip(range(2), groups, heads, tails):
        shift = g * half // 2 if joint else 0
        outs = []
        for at in range(len(members)):
            for side in (1, 0):
                low = (2 * at + side) * slots
                outs.append([(0, low + shift, low + shift + slots), (1, low, low + slots)])
        sums = add([head, tail], outs, [BF16, F32] * len(members))
        block.update((i, sums[2 * at:2 * at + 2]) for at, i in enumerate(members))

    def total(send, keep):
        return add([(keep, swap(send, near[0]))], [[(0, 0, slots)]], [BF16])[0]

    sums = [total(*block[i]) for i in range(1, experts)]
    back = [swap(part, mask) for part, mask in zip(sums, far)]
    send, keep = block[0]
    acc = own_part(mixes[0], keep, swap(join([send], [sums[0]]), near[0]), back[0])
    return post(mixes[1], table, acc, back[1:])


def solution(mesh):
    return jax.shard_map(
        shards,
        mesh=mesh,
        in_specs=(
            P(("groups", "expert"), None),
            P("groups", None),
            P("groups", None),
            P("groups", None),
            P("expert", None),
            P("expert", None),
            P(("groups", "expert"), None, None),
            P(("groups", "expert"), None),
            P(("groups", "expert"), None, None),
        ),
        out_specs=P(("groups", "expert"), None),
        check_vma=False,
    )
```

```python
import functools

import jax
import jax.numpy as jnp
from jax import lax
from jax.experimental import pallas as pl
from jax.experimental.pallas import tpu as pltpu
from jax.sharding import PartitionSpec as P

MIB = 1024 * 1024
PIECES = 4
F32 = jnp.float32
BF16 = jnp.bfloat16

SMEM = pl.BlockSpec(memory_space=pltpu.SMEM)
VMEM = pl.BlockSpec(memory_space=pltpu.VMEM)
HBM = pl.BlockSpec(memory_space=pltpu.HBM)
ANY = pl.BlockSpec(memory_space=pl.ANY)


FREE = pl.CostEstimate(flops=1, bytes_accessed=1, transcendentals=0)

BUSY = pl.CostEstimate(flops=4 * 10**10, bytes_accessed=128 * MIB, transcendentals=0)


def params(mib):
    return pltpu.CompilerParams(vmem_limit_bytes=mib * MIB)


def turns(experts):
    return [0] + list(range(experts - 1, 0, -1))


def hot_rows(picks, tok_rows):
    return lax.broadcasted_iota(jnp.int32, (tok_rows, picks.shape[1]), 0) == picks


def one_hot(picks, tok_rows):
    return hot_rows(picks, tok_rows).astype(F32).astype(BF16)


def modulate(hot, tok_ref, table_ref):
    values = lax.dot_general(hot, tok_ref[...], (((0,), (0,)), ((), ())), preferred_element_type=F32)
    center = values - jnp.mean(values, axis=1, keepdims=True)
    spread = jnp.mean(center * center, axis=1, keepdims=True)
    normed = center * (1.0 / jnp.sqrt(spread + 1e-06))
    return (normed * table_ref[0:1, :] + table_ref[1:2, :]).astype(BF16)


def first_kernel(info_ref, *refs):
    sources = refs[:7]
    far_ref, tok_ref, table_ref, picks_ref, weights_ref = refs[7:12]
    pick_ref, comb_ref, count_ref, shift_ref, scale_ref, gate_ref, sems = refs[12:]
    targets = (tok_ref, pick_ref, shift_ref, scale_ref, gate_ref, comb_ref, count_ref)
    part = tok_ref.shape[0] // PIECES
    tokens = [
        pltpu.make_async_copy(
            sources[0].at[pl.ds(p * part, part), :],
            tok_ref.at[pl.ds(p * part, part), :],
            sems.at[len(sources) + p],
        )
        for p in range(PIECES)
    ]
    copies = [
        pltpu.make_async_copy(src, dst, sems.at[i])
        for i, (src, dst) in enumerate(zip(sources, targets))
    ][1:]
    for copy in tokens + copies:
        copy.start()
    for copy in copies:
        copy.wait()
    experts, slots = pick_ref.shape
    which = pl.ds(info_ref[0], 1)
    table_ref[0:1, :] = 1.0 + scale_ref[which, :]
    table_ref[1:2, :] = shift_ref[which, :]
    table_ref[2:3, :] = gate_ref[which, :]
    lanes = lax.broadcasted_iota(jnp.int32, (1, slots), 1)
    for i, d in enumerate(turns(experts)):
        e = info_ref[1] ^ d
        picks_ref[i:i + 1, :] = pick_ref[pl.ds(e, 1), :]
        weights_ref[i:i + 1, :] = jnp.where(lanes < count_ref[0, e], comb_ref[pl.ds(e, 1), :], 0.0)
    hot = one_hot(picks_ref[1:2, :], tok_ref.shape[0])
    for copy in tokens:
        copy.wait()
    far_ref[...] = modulate(hot, tok_ref, table_ref)


def first(info, tokens, pick, shift, scale, gate, comb, count):
    experts, slots = pick.shape
    width = tokens.shape[1]
    return pl.pallas_call(
        first_kernel,
        in_specs=[SMEM] + [HBM] * 7,
        out_specs=[VMEM] * 5,
        out_shape=[
            jax.ShapeDtypeStruct((slots, width), BF16),
            jax.ShapeDtypeStruct(tokens.shape, BF16),
            jax.ShapeDtypeStruct((3, width), F32),
            jax.ShapeDtypeStruct(pick.shape, jnp.int32),
            jax.ShapeDtypeStruct(comb.shape, F32),
        ],
        scratch_shapes=[
            pltpu.VMEM(pick.shape, jnp.int32),
            pltpu.VMEM(comb.shape, F32),
            pltpu.SMEM(count.shape, jnp.int32),
            pltpu.VMEM(shift.shape, F32),
            pltpu.VMEM(scale.shape, F32),
            pltpu.VMEM(gate.shape, F32),
            pltpu.SemaphoreType.DMA((7 + PIECES,)),
        ],
        compiler_params=params(8),
        cost_estimate=FREE,
        name="first",
    )(info, tokens, pick, shift, scale, gate, comb, count)


def rest_kernel(tok_ref, table_ref, picks_ref, *outs):
    experts, slots = picks_ref.shape
    order = [0] + list(range(2, experts))
    picks = jnp.concatenate([picks_ref[i:i + 1, :] for i in order], axis=1)
    rows = modulate(one_hot(picks, tok_ref.shape[0]), tok_ref, table_ref)
    for i, out in enumerate(outs):
        out[...] = rows[i * slots:(i + 1) * slots]


def rest(tok, table, picks):
    experts, slots = picks.shape
    return pl.pallas_call(
        rest_kernel,
        in_specs=[VMEM] * 3,
        out_specs=[VMEM] * (experts - 1),
        out_shape=[jax.ShapeDtypeStruct((slots, tok.shape[1]), BF16)] * (experts - 1),
        compiler_params=params(8),
        cost_estimate=BUSY,
        name="rest",
    )(tok, table, picks)


def mixer_kernel(picks_ref, weights_ref, after_ref, *outs):
    for i, out in enumerate(outs):
        each = picks_ref.shape[0] // len(outs)
        rows = range(i * each, (i + 1) * each)
        picks = jnp.concatenate([picks_ref[r:r + 1, :] for r in rows], axis=1)
        weights = jnp.concatenate([weights_ref[r:r + 1, :] for r in rows], axis=1)
        mix = jnp.where(hot_rows(picks, out.shape[0]), weights, 0.0)
        high = mix.astype(BF16).astype(F32)
        out[...] = jnp.concatenate([high, mix - high], axis=1).astype(BF16)


def mixer(picks, weights, after, tok_rows):
    experts, slots = picks.shape
    return pl.pallas_call(
        mixer_kernel,
        in_specs=[VMEM] * 2 + [ANY],
        out_specs=[VMEM] * 2,
        out_shape=[jax.ShapeDtypeStruct((tok_rows, experts * slots), BF16)] * 2,
        compiler_params=params(4),
        cost_estimate=FREE,
        name="mixer",
    )(picks, weights, after)


def join_kernel(*refs, count):
    out_ref = refs[-1]
    at = 0
    for ref in refs[:count]:
        out_ref[at:at + ref.shape[0], :] = ref[...]
        at += ref.shape[0]


def join(parts, after):
    return pl.pallas_call(
        functools.partial(join_kernel, count=len(parts)),
        in_specs=[VMEM] * len(parts) + [ANY] * len(after),
        out_specs=VMEM,
        out_shape=jax.ShapeDtypeStruct((sum(p.shape[0] for p in parts), parts[0].shape[1]), BF16),
        compiler_params=params(2),
        cost_estimate=FREE,
        name="join",
    )(*parts, *after)


def up_kernel(*refs, sources, count):
    w_ref = refs[count]
    out_ref, rows_ref = refs[-2:]
    to = 0
    for source, low, high in sources:
        rows_ref[to:to + high - low, :] = refs[source][low:high, :]
        to += high - low
    hidden = w_ref.shape[0]
    tile = min(1024, hidden)

    @pl.loop(0, hidden // tile, unroll=True)
    def _(i):
        cut = pl.ds(pl.multiple_of(i * tile, tile), tile)
        lifted = lax.dot_general(
            w_ref[cut, :], rows_ref[...], (((1,), (1,)), ((), ())), preferred_element_type=F32
        )
        out_ref[:, cut] = jax.nn.gelu(lifted, approximate=True).astype(BF16).T


def up(parts, sources, w, after):
    hidden, width = w.shape
    rows = sum(high - low for _, low, high in sources)
    return pl.pallas_call(
        functools.partial(up_kernel, sources=sources, count=len(parts)),
        in_specs=[VMEM] * (len(parts) + 1) + [ANY] * len(after),
        out_specs=VMEM,
        out_shape=jax.ShapeDtypeStruct((rows, hidden), BF16),
        scratch_shapes=[pltpu.VMEM((rows, width), BF16)],
        compiler_params=params(8),
        cost_estimate=FREE,
        name="up",
    )(*parts, w, *after)


def down_kernel(h_ref, w_ref, *outs, columns, low, groups):
    first, last, tile = columns
    pairs = len(outs) // 2
    half = outs[0].shape[0] * pairs // groups

    @pl.loop(0, (last - first) // tile, unroll=True)
    def _(i):
        to = pl.ds(pl.multiple_of(i * tile, tile), tile)
        cut = pl.ds(pl.multiple_of(first + i * tile, tile), tile)
        rows = slice(low, low + 2 * half * groups)
        out = jnp.dot(h_ref[rows, :], w_ref[:, cut], preferred_element_type=F32)
        for g in range(groups):
            at = 2 * half * g
            keep_ref, send_ref = outs[2 * (g % pairs):2 * (g % pairs) + 2]
            into = slice(g // pairs * half, (g // pairs + 1) * half)
            keep_ref[into, to] = out[at:at + half]
            send_ref[into, to] = out[at + half:at + 2 * half].astype(BF16)


def down(hid, low, groups, w, columns, joint=False):
    half = hid.shape[0] // 4 * (groups if joint else 1)
    pairs = 1 if joint else groups
    step = columns[1] - columns[0]
    return pl.pallas_call(
        functools.partial(down_kernel, columns=columns, low=low, groups=groups),
        in_specs=[VMEM] * 2,
        out_specs=[VMEM] * (2 * pairs),
        out_shape=[
            jax.ShapeDtypeStruct((half, step), F32),
            jax.ShapeDtypeStruct((half, step), BF16),
        ]
        * pairs,
        compiler_params=params(8),
        cost_estimate=FREE,
        name="down",
    )(hid, w)


def add_kernel(*refs, count, outs):
    for ref, pieces in zip(refs[2 * count:], outs):
        at = 0
        for i, low, high in pieces:
            keep_ref, got_ref = refs[2 * i:2 * i + 2]
            step = keep_ref.shape[1]
            total = keep_ref[low:high] + got_ref[low:high].astype(F32)
            ref[:, at:at + step] = total.astype(ref.dtype)
            at += step


def add(pairs, outs, kinds):
    args = [x for pair in pairs for x in pair]
    shapes = [
        (pieces[0][2] - pieces[0][1], sum(pairs[i][0].shape[1] for i, _, _ in pieces))
        for pieces in outs
    ]
    return pl.pallas_call(
        functools.partial(add_kernel, count=len(pairs), outs=outs),
        in_specs=[VMEM] * len(args),
        out_specs=[VMEM] * len(outs),
        out_shape=[jax.ShapeDtypeStruct(shape, k) for shape, k in zip(shapes, kinds)],
        compiler_params=params(8),
        cost_estimate=FREE,
        name="add",
    )(*args)


def own_kernel(mix_ref, keep_ref, near_ref, got_ref, acc_ref):
    own = (keep_ref[...] + near_ref[...].astype(F32)).astype(BF16)
    values = jnp.concatenate([own, got_ref[...]] * 2, axis=0)
    acc_ref[...] = jnp.dot(mix_ref[...], values, preferred_element_type=F32)


def own_part(mix, keep, near, got):
    return pl.pallas_call(
        own_kernel,
        in_specs=[VMEM] * 4,
        out_specs=VMEM,
        out_shape=jax.ShapeDtypeStruct((mix.shape[0], keep.shape[1]), F32),
        compiler_params=params(12),
        cost_estimate=FREE,
        name="own_part",
    )(mix, keep, near, got)


def post_kernel(mix_ref, table_ref, acc_ref, *refs):
    blocks = refs[:-3]
    out_hbm, out_ref, sems = refs[-3:]
    step = out_ref.shape[1] // sems.shape[0]
    copies = []
    for i in range(sems.shape[0]):
        cut = pl.ds(i * step, step)
        values = jnp.concatenate([ref[:, cut] for ref in blocks] * 2, axis=0)
        mixed = acc_ref[:, cut] + jnp.dot(mix_ref[...], values, preferred_element_type=F32)
        out_ref[:, cut] = (table_ref[2:3, cut] * mixed).astype(BF16)
        copy = pltpu.make_async_copy(out_ref.at[:, cut], out_hbm.at[:, cut], sems.at[i])
        copy.start()
        copies.append(copy)
    for copy in copies:
        copy.wait()


def post(mix, table, acc, blocks):
    tok_rows, width = acc.shape
    return pl.pallas_call(
        post_kernel,
        in_specs=[VMEM] * (3 + len(blocks)),
        out_specs=HBM,
        out_shape=jax.ShapeDtypeStruct((tok_rows, width), BF16),
        scratch_shapes=[pltpu.VMEM((tok_rows, width), BF16), pltpu.SemaphoreType.DMA((4,))],
        compiler_params=params(8),
        cost_estimate=FREE,
        name="post",
    )(mix, table, acc, *blocks)


def shards(tokens, shift, scale, gate, w_up, w_down, pick, count, combine):
    tok_rows, width = tokens.shape
    _, experts, slots = pick.shape
    devices = lax.axis_size("expert")
    place = lax.axis_index("expert")
    group = devices // experts
    requests = shift.shape[0]
    hidden = w_up.shape[0]
    info = jnp.stack([place // (devices // requests), place // group]).astype(jnp.int32)
    pick = pick[0]
    comb = combine[0]

    far = [d * group for d in turns(experts)[1:]]
    near = []
    bit = group // 2
    while bit:
        near.append(bit)
        bit //= 2

    def swap(x, mask):
        return lax.ppermute(x, "expert", [(i, i ^ mask) for i in range(devices)])

    tokens, shift, scale, gate, pick, comb, count = [
        pltpu.with_memory_space_constraint(x, pltpu.HBM)
        for x in (tokens, shift, scale, gate, pick, comb, count)
    ]
    farthest, tok, table, picks, weights = first(info, tokens, pick, shift, scale, gate, comb, count)
    own, *others = rest(tok, table, picks)

    flat = [farthest] + others
    blocks = [own] + [swap(x, mask) for x, mask in zip(flat, far)]
    mixes = mixer(picks, weights, blocks[1], tok_rows)
    blocks[2] = join([blocks[2]], [mixes[0]])
    beside = [swap(block, near[0]) for block in blocks]
    early, late = list(range(experts // 2)), list(range(experts // 2, experts))
    parts = []
    segments = {}
    for members in [[i] for i in early + late]:
        pieces = [join([x for i in members for x in (blocks[i], beside[i])], [])]
        height = pieces[0].shape[0]
        for mask in near[1:]:
            block = pieces[0] if len(pieces) == 1 else join(pieces, [])
            pieces = [block, swap(block, mask)]
        for at, i in enumerate(members):
            segments[i] = []
            for k, piece in enumerate(pieces):
                for base in range(2 * at * slots, piece.shape[0], height):
                    segments[i].append((len(parts) + k, base, base + 2 * slots))
        parts += pieces
    groups = [[1, 2], list(range(3, experts)) + [0]]
    sources = [
        cut for members in groups for cuts in zip(*[segments[i] for i in members]) for cut in cuts
    ]
    hid = up(parts, sources, w_up, [])

    def gather(keep, send):
        for i, mask in enumerate(reversed(near[1:])):
            if i:
                middle = keep.shape[0] // 2
                keep, send = add(
                    [(keep, got)], [[(0, 0, middle)], [(0, middle, 2 * middle)]], [F32, BF16]
                )
            got = swap(send, mask)
        return keep, got

    half = hid.shape[0] // 2
    step = 5 * width // 8
    joint = len(near) == 2
    made = down(hid, 0, 2, w_down, (0, step, step // 2), joint)
    heads = [gather(*made)] * 2 if joint else [gather(*made[:2]), gather(*made[2:])]
    tails = []
    for g in range(2):
        keep, send = down(hid, g * half, 1, w_down, (step, width, width - step))
        tails.append(gather(keep, send))
    block = {}
    for g, members, head, tail in zip(range(2), groups, heads, tails):
        shift = g * half // 2 if joint else 0
        outs = []
        for at in range(len(members)):
            for side in (1, 0):
                low = (2 * at + side) * slots
                outs.append([(0, low + shift, low + shift + slots), (1, low, low + slots)])
        sums = add([head, tail], outs, [BF16, F32] * len(members))
        block.update((i, sums[2 * at:2 * at + 2]) for at, i in enumerate(members))

    def total(send, keep):
        return add([(keep, swap(send, near[0]))], [[(0, 0, slots)]], [BF16])[0]

    sums = [total(*block[i]) for i in range(1, experts)]
    back = [swap(part, mask) for part, mask in zip(sums, far)]
    send, keep = block[0]
    acc = own_part(mixes[0], keep, swap(join([send], [sums[0]]), near[0]), back[0])
    return post(mixes[1], table, acc, back[1:])


def solution(mesh):
    return jax.shard_map(
        shards,
        mesh=mesh,
        in_specs=(
            P(("groups", "expert"), None),
            P("groups", None),
            P("groups", None),
            P("groups", None),
            P("expert", None),
            P("expert", None),
            P(("groups", "expert"), None, None),
            P(("groups", "expert"), None),
            P(("groups", "expert"), None, None),
        ),
        out_specs=P(("groups", "expert"), None),
        check_vma=False,
    )
```

```python
import functools

import jax
import jax.numpy as jnp
from jax import lax
from jax.experimental import pallas as pl
from jax.experimental.pallas import tpu as pltpu
from jax.sharding import PartitionSpec as P

MIB = 1024 * 1024
PIECES = 4
F32 = jnp.float32
BF16 = jnp.bfloat16

SMEM = pl.BlockSpec(memory_space=pltpu.SMEM)
VMEM = pl.BlockSpec(memory_space=pltpu.VMEM)
HBM = pl.BlockSpec(memory_space=pltpu.HBM)
ANY = pl.BlockSpec(memory_space=pl.ANY)


FREE = pl.CostEstimate(flops=1, bytes_accessed=1, transcendentals=0)

BUSY = pl.CostEstimate(flops=4 * 10**10, bytes_accessed=128 * MIB, transcendentals=0)


def params(mib):
    return pltpu.CompilerParams(vmem_limit_bytes=mib * MIB)


def turns(experts):
    return [0] + list(range(experts - 1, 0, -1))


def hot_rows(picks, tok_rows):
    return lax.broadcasted_iota(jnp.int32, (tok_rows, picks.shape[1]), 0) == picks


def one_hot(picks, tok_rows):
    return hot_rows(picks, tok_rows).astype(F32).astype(BF16)


def modulate(hot, tok_ref, table_ref):
    values = lax.dot_general(hot, tok_ref[...], (((0,), (0,)), ((), ())), preferred_element_type=F32)
    center = values - jnp.mean(values, axis=1, keepdims=True)
    spread = jnp.mean(center * center, axis=1, keepdims=True)
    normed = center * (1.0 / jnp.sqrt(spread + 1e-06))
    return (normed * table_ref[0:1, :] + table_ref[1:2, :]).astype(BF16)


def first_kernel(info_ref, *refs):
    sources = refs[:7]
    far_ref, tok_ref, table_ref, picks_ref, weights_ref = refs[7:12]
    pick_ref, comb_ref, count_ref, shift_ref, scale_ref, gate_ref, sems = refs[12:]
    targets = (tok_ref, pick_ref, shift_ref, scale_ref, gate_ref, comb_ref, count_ref)
    part = tok_ref.shape[0] // PIECES
    tokens = [
        pltpu.make_async_copy(
            sources[0].at[pl.ds(p * part, part), :],
            tok_ref.at[pl.ds(p * part, part), :],
            sems.at[len(sources) + p],
        )
        for p in range(PIECES)
    ]
    copies = [
        pltpu.make_async_copy(src, dst, sems.at[i])
        for i, (src, dst) in enumerate(zip(sources, targets))
    ][1:]
    for copy in tokens + copies:
        copy.start()
    for copy in copies:
        copy.wait()
    experts, slots = pick_ref.shape
    which = pl.ds(info_ref[0], 1)
    table_ref[0:1, :] = 1.0 + scale_ref[which, :]
    table_ref[1:2, :] = shift_ref[which, :]
    table_ref[2:3, :] = gate_ref[which, :]
    lanes = lax.broadcasted_iota(jnp.int32, (1, slots), 1)
    for i, d in enumerate(turns(experts)):
        e = info_ref[1] ^ d
        picks_ref[i:i + 1, :] = pick_ref[pl.ds(e, 1), :]
        weights_ref[i:i + 1, :] = jnp.where(lanes < count_ref[0, e], comb_ref[pl.ds(e, 1), :], 0.0)
    hot = one_hot(picks_ref[1:2, :], tok_ref.shape[0])
    for copy in tokens:
        copy.wait()
    far_ref[...] = modulate(hot, tok_ref, table_ref)


def first(info, tokens, pick, shift, scale, gate, comb, count):
    experts, slots = pick.shape
    width = tokens.shape[1]
    return pl.pallas_call(
        first_kernel,
        in_specs=[SMEM] + [HBM] * 7,
        out_specs=[VMEM] * 5,
        out_shape=[
            jax.ShapeDtypeStruct((slots, width), BF16),
            jax.ShapeDtypeStruct(tokens.shape, BF16),
            jax.ShapeDtypeStruct((3, width), F32),
            jax.ShapeDtypeStruct(pick.shape, jnp.int32),
            jax.ShapeDtypeStruct(comb.shape, F32),
        ],
        scratch_shapes=[
            pltpu.VMEM(pick.shape, jnp.int32),
            pltpu.VMEM(comb.shape, F32),
            pltpu.SMEM(count.shape, jnp.int32),
            pltpu.VMEM(shift.shape, F32),
            pltpu.VMEM(scale.shape, F32),
            pltpu.VMEM(gate.shape, F32),
            pltpu.SemaphoreType.DMA((7 + PIECES,)),
        ],
        compiler_params=params(8),
        cost_estimate=FREE,
        name="first",
    )(info, tokens, pick, shift, scale, gate, comb, count)


def rest_kernel(tok_ref, table_ref, picks_ref, *outs):
    experts, slots = picks_ref.shape
    order = [0] + list(range(2, experts))
    picks = jnp.concatenate([picks_ref[i:i + 1, :] for i in order], axis=1)
    rows = modulate(one_hot(picks, tok_ref.shape[0]), tok_ref, table_ref)
    for i, out in enumerate(outs):
        out[...] = rows[i * slots:(i + 1) * slots]


def rest(tok, table, picks):
    experts, slots = picks.shape
    return pl.pallas_call(
        rest_kernel,
        in_specs=[VMEM] * 3,
        out_specs=[VMEM] * (experts - 1),
        out_shape=[jax.ShapeDtypeStruct((slots, tok.shape[1]), BF16)] * (experts - 1),
        compiler_params=params(8),
        cost_estimate=BUSY,
        name="rest",
    )(tok, table, picks)


def mixer_kernel(picks_ref, weights_ref, after_ref, *outs):
    for i, out in enumerate(outs):
        each = picks_ref.shape[0] // len(outs)
        rows = range(i * each, (i + 1) * each)
        picks = jnp.concatenate([picks_ref[r:r + 1, :] for r in rows], axis=1)
        weights = jnp.concatenate([weights_ref[r:r + 1, :] for r in rows], axis=1)
        mix = jnp.where(hot_rows(picks, out.shape[0]), weights, 0.0)
        high = mix.astype(BF16).astype(F32)
        out[...] = jnp.concatenate([high, mix - high], axis=1).astype(BF16)


def mixer(picks, weights, after, tok_rows):
    experts, slots = picks.shape
    return pl.pallas_call(
        mixer_kernel,
        in_specs=[VMEM] * 2 + [ANY],
        out_specs=[VMEM] * 2,
        out_shape=[jax.ShapeDtypeStruct((tok_rows, experts * slots), BF16)] * 2,
        compiler_params=params(4),
        cost_estimate=FREE,
        name="mixer",
    )(picks, weights, after)


def join_kernel(*refs, count):
    out_ref = refs[-1]
    at = 0
    for ref in refs[:count]:
        out_ref[at:at + ref.shape[0], :] = ref[...]
        at += ref.shape[0]


def join(parts, after):
    return pl.pallas_call(
        functools.partial(join_kernel, count=len(parts)),
        in_specs=[VMEM] * len(parts) + [ANY] * len(after),
        out_specs=VMEM,
        out_shape=jax.ShapeDtypeStruct((sum(p.shape[0] for p in parts), parts[0].shape[1]), BF16),
        compiler_params=params(2),
        cost_estimate=FREE,
        name="join",
    )(*parts, *after)


def up_kernel(*refs, sources, count):
    w_ref = refs[count]
    out_ref, rows_ref = refs[-2:]
    to = 0
    for source, low, high in sources:
        rows_ref[to:to + high - low, :] = refs[source][low:high, :]
        to += high - low
    hidden = w_ref.shape[0]
    tile = min(1024, hidden)

    @pl.loop(0, hidden // tile, unroll=True)
    def _(i):
        cut = pl.ds(pl.multiple_of(i * tile, tile), tile)
        lifted = lax.dot_general(
            w_ref[cut, :], rows_ref[...], (((1,), (1,)), ((), ())), preferred_element_type=F32
        )
        out_ref[:, cut] = jax.nn.gelu(lifted, approximate=True).astype(BF16).T


def up(parts, sources, w, after):
    hidden, width = w.shape
    rows = sum(high - low for _, low, high in sources)
    return pl.pallas_call(
        functools.partial(up_kernel, sources=sources, count=len(parts)),
        in_specs=[VMEM] * (len(parts) + 1) + [ANY] * len(after),
        out_specs=VMEM,
        out_shape=jax.ShapeDtypeStruct((rows, hidden), BF16),
        scratch_shapes=[pltpu.VMEM((rows, width), BF16)],
        compiler_params=params(8),
        cost_estimate=FREE,
        name="up",
    )(*parts, w, *after)


def down_kernel(h_ref, w_ref, *outs, columns, low, groups):
    first, last, tile = columns
    pairs = len(outs) // 2
    half = outs[0].shape[0] * pairs // groups

    @pl.loop(0, (last - first) // tile, unroll=True)
    def _(i):
        to = pl.ds(pl.multiple_of(i * tile, tile), tile)
        cut = pl.ds(pl.multiple_of(first + i * tile, tile), tile)
        rows = slice(low, low + 2 * half * groups)
        out = jnp.dot(h_ref[rows, :], w_ref[:, cut], preferred_element_type=F32)
        for g in range(groups):
            at = 2 * half * g
            keep_ref, send_ref = outs[2 * (g % pairs):2 * (g % pairs) + 2]
            into = slice(g // pairs * half, (g // pairs + 1) * half)
            keep_ref[into, to] = out[at:at + half]
            send_ref[into, to] = out[at + half:at + 2 * half].astype(BF16)


def down(hid, low, groups, w, columns, joint=False):
    half = hid.shape[0] // 4 * (groups if joint else 1)
    pairs = 1 if joint else groups
    step = columns[1] - columns[0]
    return pl.pallas_call(
        functools.partial(down_kernel, columns=columns, low=low, groups=groups),
        in_specs=[VMEM] * 2,
        out_specs=[VMEM] * (2 * pairs),
        out_shape=[
            jax.ShapeDtypeStruct((half, step), F32),
            jax.ShapeDtypeStruct((half, step), BF16),
        ]
        * pairs,
        compiler_params=params(8),
        cost_estimate=FREE,
        name="down",
    )(hid, w)


def add_kernel(*refs, count, outs):
    for ref, pieces in zip(refs[2 * count:], outs):
        at = 0
        for i, low, high in pieces:
            keep_ref, got_ref = refs[2 * i:2 * i + 2]
            step = keep_ref.shape[1]
            total = keep_ref[low:high] + got_ref[low:high].astype(F32)
            ref[:, at:at + step] = total.astype(ref.dtype)
            at += step


def add(pairs, outs, kinds):
    args = [x for pair in pairs for x in pair]
    shapes = [
        (pieces[0][2] - pieces[0][1], sum(pairs[i][0].shape[1] for i, _, _ in pieces))
        for pieces in outs
    ]
    return pl.pallas_call(
        functools.partial(add_kernel, count=len(pairs), outs=outs),
        in_specs=[VMEM] * len(args),
        out_specs=[VMEM] * len(outs),
        out_shape=[jax.ShapeDtypeStruct(shape, k) for shape, k in zip(shapes, kinds)],
        compiler_params=params(8),
        cost_estimate=FREE,
        name="add",
    )(*args)


def own_kernel(mix_ref, keep_ref, near_ref, got_ref, acc_ref):
    own = (keep_ref[...] + near_ref[...].astype(F32)).astype(BF16)
    values = jnp.concatenate([own, got_ref[...]] * 2, axis=0)
    acc_ref[...] = jnp.dot(mix_ref[...], values, preferred_element_type=F32)


def own_part(mix, keep, near, got):
    return pl.pallas_call(
        own_kernel,
        in_specs=[VMEM] * 4,
        out_specs=VMEM,
        out_shape=jax.ShapeDtypeStruct((mix.shape[0], keep.shape[1]), F32),
        compiler_params=params(12),
        cost_estimate=FREE,
        name="own_part",
    )(mix, keep, near, got)


def post_kernel(mix_ref, table_ref, acc_ref, *refs):
    blocks = refs[:-3]
    out_hbm, out_ref, sems = refs[-3:]
    step = out_ref.shape[1] // sems.shape[0]
    copies = []
    for i in range(sems.shape[0]):
        cut = pl.ds(i * step, step)
        values = jnp.concatenate([ref[:, cut] for ref in blocks] * 2, axis=0)
        mixed = acc_ref[:, cut] + jnp.dot(mix_ref[...], values, preferred_element_type=F32)
        out_ref[:, cut] = (table_ref[2:3, cut] * mixed).astype(BF16)
        copy = pltpu.make_async_copy(out_ref.at[:, cut], out_hbm.at[:, cut], sems.at[i])
        copy.start()
        copies.append(copy)
    for copy in copies:
        copy.wait()


def post(mix, table, acc, blocks):
    tok_rows, width = acc.shape
    return pl.pallas_call(
        post_kernel,
        in_specs=[VMEM] * (3 + len(blocks)),
        out_specs=HBM,
        out_shape=jax.ShapeDtypeStruct((tok_rows, width), BF16),
        scratch_shapes=[pltpu.VMEM((tok_rows, width), BF16), pltpu.SemaphoreType.DMA((4,))],
        compiler_params=params(8),
        cost_estimate=FREE,
        name="post",
    )(mix, table, acc, *blocks)


def shards(tokens, shift, scale, gate, w_up, w_down, pick, count, combine):
    tok_rows, width = tokens.shape
    _, experts, slots = pick.shape
    devices = lax.axis_size("expert")
    place = lax.axis_index("expert")
    group = devices // experts
    requests = shift.shape[0]
    hidden = w_up.shape[0]
    info = jnp.stack([place // (devices // requests), place // group]).astype(jnp.int32)
    pick = pick[0]
    comb = combine[0]

    far = [d * group for d in turns(experts)[1:]]
    near = []
    bit = group // 2
    while bit:
        near.append(bit)
        bit //= 2

    def swap(x, mask):
        return lax.ppermute(x, "expert", [(i, i ^ mask) for i in range(devices)])

    tokens, shift, scale, gate, pick, comb, count = [
        pltpu.with_memory_space_constraint(x, pltpu.HBM)
        for x in (tokens, shift, scale, gate, pick, comb, count)
    ]
    farthest, tok, table, picks, weights = first(info, tokens, pick, shift, scale, gate, comb, count)
    own, *others = rest(tok, table, picks)

    flat = [farthest] + others
    blocks = [own] + [swap(x, mask) for x, mask in zip(flat, far)]
    mixes = mixer(picks, weights, blocks[1], tok_rows)
    blocks[2] = join([blocks[2]], [mixes[0]])
    beside = [swap(block, near[0]) for block in blocks]
    early, late = list(range(experts // 2)), list(range(experts // 2, experts))
    parts = []
    segments = {}
    for members in [[i] for i in early + late]:
        pieces = [join([x for i in members for x in (blocks[i], beside[i])], [])]
        height = pieces[0].shape[0]
        for mask in near[1:]:
            block = pieces[0] if len(pieces) == 1 else join(pieces, [])
            pieces = [block, swap(block, mask)]
        for at, i in enumerate(members):
            segments[i] = []
            for k, piece in enumerate(pieces):
                for base in range(2 * at * slots, piece.shape[0], height):
                    segments[i].append((len(parts) + k, base, base + 2 * slots))
        parts += pieces
    groups = [[1, 2], list(range(3, experts)) + [0]]
    sources = [
        cut for members in groups for cuts in zip(*[segments[i] for i in members]) for cut in cuts
    ]
    hid = up(parts, sources, w_up, [])

    def gather(keep, send):
        for i, mask in enumerate(reversed(near[1:])):
            if i:
                middle = keep.shape[0] // 2
                keep, send = add(
                    [(keep, got)], [[(0, 0, middle)], [(0, middle, 2 * middle)]], [F32, BF16]
                )
            got = swap(send, mask)
        return keep, got

    half = hid.shape[0] // 2
    step = 5 * width // 8
    joint = len(near) == 2
    made = down(hid, 0, 2, w_down, (0, step, step // 5), joint)
    heads = [gather(*made)] * 2 if joint else [gather(*made[:2]), gather(*made[2:])]
    tails = []
    for g in range(2):
        keep, send = down(hid, g * half, 1, w_down, (step, width, (width - step) // 3))
        tails.append(gather(keep, send))
    block = {}
    for g, members, head, tail in zip(range(2), groups, heads, tails):
        shift = g * half // 2 if joint else 0
        outs = []
        for at in range(len(members)):
            for side in (1, 0):
                low = (2 * at + side) * slots
                outs.append([(0, low + shift, low + shift + slots), (1, low, low + slots)])
        sums = add([head, tail], outs, [BF16, F32] * len(members))
        block.update((i, sums[2 * at:2 * at + 2]) for at, i in enumerate(members))

    def total(send, keep):
        return add([(keep, swap(send, near[0]))], [[(0, 0, slots)]], [BF16])[0]

    sums = [total(*block[i]) for i in range(1, experts)]
    back = [swap(part, mask) for part, mask in zip(sums, far)]
    send, keep = block[0]
    acc = own_part(mixes[0], keep, swap(join([send], [sums[0]]), near[0]), back[0])
    return post(mixes[1], table, acc, back[1:])


def solution(mesh):
    return jax.shard_map(
        shards,
        mesh=mesh,
        in_specs=(
            P(("groups", "expert"), None),
            P("groups", None),
            P("groups", None),
            P("groups", None),
            P("expert", None),
            P("expert", None),
            P(("groups", "expert"), None, None),
            P(("groups", "expert"), None),
            P(("groups", "expert"), None, None),
        ),
        out_specs=P(("groups", "expert"), None),
        check_vma=False,
    )
```
